32 devices in a mesh: groups: 2 (over x), expert: 16 (over z, y, core).
Axes of the slice: x: 2, y: 2, z: 4, core: 2. Of those that a mesh axis runs over, the one named last changes fastest.
Arguments:
- block_values: bfloat16 [4096, 2048], P(('groups', 'expert')), parts along dimension 0, may hold values from -4 to 4
- block_exps: int32 [4096, 16], P(('groups', 'expert')), parts along dimension 0, may hold values from -3 to 1
- row_ids: int32 [4096], P(('groups', 'expert')), parts along dimension 0, may hold values from 0 to 4095, as said below
- expert_ids: int32 [4096, 4], P(('groups', 'expert')), parts along dimension 0, may hold values from 0 to 63, all different within a row; in each aligned block of 128 rows (0 to 127, 128 to 255, ...) at most 12 rows name the same one
- gate_weights: float32 [4096, 4], P(('groups', 'expert')), parts along dimension 0, may hold values from 0.05 to 0.5
- table: bfloat16 [4096, 2048], P('expert'), may hold values from -4 to 4
- w_gate: bfloat16 [64, 2048, 1408], P('expert'), may hold values from -0.125 to 0.125
- w_up: bfloat16 [64, 2048, 1408], P('expert'), may hold values from -0.125 to 0.125
- w_down: bfloat16 [64, 1408, 2048], P('expert'), may hold values from -0.15625 to 0.15625
- out_grad: bfloat16 [4096, 2048], P(('groups', 'expert')), parts along dimension 0, may hold values from -0.19921875 to 0.19921875
Outputs:
- mixed: bfloat16 [4096, 2048], P(('groups', 'expert')), parts along dimension 0
- gate_grads: float32 [4096, 4], P(('groups', 'expert')), parts along dimension 0
The draws below stay inside these ranges and needn't reach their ends.
There are 2 independent parts, one for each index of `groups`. The reference program is written for one: setup_inputs(seed, part) draws one part's arguments, and reference() takes and returns one part's arrays. A program takes and returns all parts, laid end to end along the dimension named above; an argument that names none is the same for every part. Nothing has to cross between parts.
Inputs may be any that keep to these rules, and one draw needn't show every extreme that they name: `row_ids`: among the 128 tokens of one device at most 16 name rows of any one block of 256 consecutive table rows, and every device has a block named exactly 16 times. `expert_ids`: in the 128 rows of one device no expert is named by more than 12 rows, a bound that some block reaches.
All inputs are finite; a program needn't handle non-finite values.
Results may differ from the reference program's by a relative error of at most 0.0071.
Values may be sent and summed in bfloat16 or wider, within the bound.
No kernel may reach another device: no remote copies, remote signals or barrier semaphores. Data moves between devices by JAX's collectives and lax.ppermute only.
A program may use at most 192 MiB of HBM per device.

```python
import math
import jax
import jax.numpy as jnp
import numpy as np
from jax import lax

D = 2048
FF = 1408
EXPERTS = 64
TOP = 4
BLOCK = 128
TOK_DEV = 128
ROWS_DEV = 256
SPLIT = 1
EXP_DEV = 4
FF_DEV = 1408
NBLK = 16
CAP = 12
LOOK_CAP = 16
TOKENS = 2048
ROWS = 4096
N_EXPERT = 16


def owners_for_device(key):
    key_slots, key_order, key_owner, key_inside = jax.random.split(key, 4)
    remaining = LOOK_CAP + jax.random.permutation(key_slots, N_EXPERT * LOOK_CAP - LOOK_CAP)
    slot_ids = jnp.concatenate([jnp.arange(LOOK_CAP, dtype=jnp.int32), remaining.astype(jnp.int32)])[:TOK_DEV]
    slot_ids = jax.random.permutation(key_order, slot_ids)
    owner_map = jax.random.permutation(key_owner, N_EXPERT).astype(jnp.int32)
    owners = owner_map[slot_ids // LOOK_CAP]
    inside = jax.random.randint(key_inside, (TOK_DEV,), 0, ROWS_DEV, dtype=jnp.int32)
    return owners * ROWS_DEV + inside


def draw_row_ids(key, part):
    key = jax.random.fold_in(key, 7)
    key_list = jax.random.split(key, N_EXPERT)
    return jax.vmap(owners_for_device)(key_list).reshape(TOKENS).astype(jnp.int32)


def set_ends(array, own_key, low, top_value):
    place = [jax.random.randint(jax.random.fold_in(own_key, axis), (), 0, length) for axis, length in enumerate(array.shape)]
    widest = array.shape.index(max(array.shape))
    beside = place[:widest] + [(place[widest] + 1) % array.shape[widest]] + place[widest + 1:]
    return array.at[tuple(place)].set(low).at[tuple(beside)].set(top_value)


def levels(rng, extent, cuts, least, largest):
    loudness = 1.0
    for position, parts in cuts:
        steps = jax.random.uniform(jax.random.fold_in(jax.random.fold_in(rng, 6), position), (parts,), jnp.float32, least / len(cuts), largest / len(cuts))
        loudness = loudness * jnp.repeat(jnp.exp(steps), extent[position] // parts).reshape((-1,) + (1,) * (len(extent) - 1 - position))
    return loudness


def assign_block(key, own, number, rows, count, top, reach, lean):
    order = jax.random.permutation(key, count)
    heavy_load, common = portions_of(count, rows * top, reach, lean, True), portions_of(count, rows * top, reach, lean, False)
    places = jnp.arange(count)

    def named(tallies, rotation):
        used = int((tallies > 0).sum())
        fixed = max(1, used // 4)
        moved = fixed + (places - fixed + rotation * (used - fixed)) % max(1, count - fixed)
        return jnp.zeros((count,), jnp.int32).at[order[jnp.where(places < fixed, places, moved)]].set(jnp.asarray(tallies, jnp.int32))

    tallies = jnp.where(number % 4 == 0, named(heavy_load, number // 4), named(common, number - number // 4 - 1))
    mixed = jax.random.permutation(jax.random.fold_in(own, 3), count)
    donor, receiver = mixed[0:count // 2 * 2:2], mixed[1:count // 2 * 2:2]
    room = jnp.minimum(tallies[donor] - 1, reach - tallies[receiver]) // 2
    room = jnp.where((donor == order[0]) | (receiver == order[0]) | (tallies[receiver] == 0), 0, jnp.maximum(room, 0))
    moved = jax.random.randint(jax.random.fold_in(own, 4), (count // 2,), 0, 1 << 20) % (room + 1)
    tallies = tallies.at[donor].add(-moved).at[receiver].add(moved)
    members = jnp.searchsorted(jnp.cumsum(tallies), jnp.arange(rows * top), side="right").astype(jnp.int32)
    listing = members.reshape(top, rows).T
    listing = listing[jax.random.permutation(jax.random.fold_in(own, 1), rows)]
    rotation = jax.random.randint(jax.random.fold_in(own, 2), (rows, 1), 0, top)
    return jnp.take_along_axis(listing, (jnp.arange(top)[None, :] + rotation) % top, axis=1)


def portions_of(number_of, total, reach, skew, full):
    portions = [(1 << 20) // math.isqrt(grade ** skew) + 1 for grade in range(1, number_of + 1)]
    largest = reach if full else min(reach, max(-(-total // number_of), total * portions[0] // sum(portions)))
    least = 1 if total - largest >= number_of - 1 else 0
    given, spare = [largest] + [least] * (number_of - 1), total - largest - least * (number_of - 1)
    while spare > 0:
        free = [i for i in range(1, number_of) if given[i] < largest] or [i for i in range(1, number_of) if given[i] < reach]
        whole, left = sum([portions[i] for i in free]), spare
        for i in free:
            extra = min(reach - given[i], max(1, left * portions[i] // whole), spare)
            given[i] = given[i] + extra
            spare = spare - extra
    return np.array(given)


def centred(key, dims, width, limit, shards=(), kind=jnp.bfloat16):
    factor_of = levels(key, dims, shards, -0.22, 0.18) if shards else 1.0
    array = jax.random.normal(key, dims, jnp.float32) * width * factor_of
    return jnp.minimum(jnp.maximum(array, -limit), limit).astype(kind)


def setup_inputs(seed: int = 0, part: int = 0) -> dict:
    seeds = jax.random.split(jax.random.key(seed), 11)
    own_keys = jax.random.split(jax.random.fold_in(seeds[10], part), 11)
    block_values = centred(own_keys[0], (TOKENS, D), 1.0, 4.0, ((0, 16),))
    block_exps = set_ends(jax.random.randint(own_keys[1], (TOKENS, NBLK), -3, 2), jax.random.fold_in(own_keys[1], 1), -3, 1).astype(jnp.int32)
    row_ids = draw_row_ids(jax.random.fold_in(jax.random.fold_in(seeds[10], part), 71), part)
    expert_ids_keys = jax.random.split(jax.random.fold_in(own_keys[3], 1), TOKENS // TOK_DEV)
    expert_ids_turns = jax.random.permutation(jax.random.fold_in(own_keys[3], 3), TOKENS // TOK_DEV)
    expert_ids = jax.vmap(lambda own, number: assign_block(jax.random.fold_in(own_keys[3], 2), own, number, TOK_DEV, EXPERTS, TOP, CAP, 2))(expert_ids_keys, expert_ids_turns).reshape((TOKENS, TOP))
    gate_weights = jnp.clip(jnp.exp(math.log(0.5) - 2.3025851 * jax.random.uniform(own_keys[4], (TOKENS, TOP), jnp.float32) ** levels(own_keys[4], (TOKENS, TOP), ((0, 16),), -0.2, 0.2)), 0.05, 0.5)
    table = centred(seeds[5], (ROWS, D), 0.5, 4.0, ((0, 16),))
    w_gate = centred(seeds[6], (N_EXPERT * EXP_DEV, D, FF_DEV), D ** -0.5, 0.125, ((0, 16),))
    w_up = centred(seeds[7], (N_EXPERT * EXP_DEV, D, FF_DEV), D ** -0.5, 0.125, ((0, 16),))
    w_down = centred(seeds[8], (N_EXPERT * EXP_DEV, FF_DEV, D), FF ** -0.5, 0.15625, ((0, 16),))
    out_grad = centred(own_keys[9], (TOKENS, D), 0.03, 0.19921875, ((0, 16),))
    return {"block_values": block_values, "block_exps": block_exps, "row_ids": row_ids, "expert_ids": expert_ids, "gate_weights": gate_weights, "table": table, "w_gate": w_gate, "w_up": w_up, "w_down": w_down, "out_grad": out_grad}


def reference(block_values, block_exps, row_ids, expert_ids, gate_weights, table, w_gate, w_up, w_down, out_grad):
    embedded = jnp.take(table, row_ids, axis=0).astype(jnp.float32)
    scales = jnp.exp2(block_exps.astype(jnp.float32))
    scaled = (block_values.astype(jnp.float32).reshape(TOKENS, NBLK, BLOCK) * scales[:, :, None]).reshape(TOKENS, D)
    token_state = (scaled + embedded).astype(jnp.bfloat16)
    flat_ids = expert_ids.reshape(N_EXPERT, TOK_DEV * TOP).astype(jnp.int32)
    expert_hot = (flat_ids[:, :, None] == jnp.arange(EXPERTS, dtype=jnp.int32)[None, None, :]).astype(jnp.int32)
    rank_in = jnp.sum((jnp.cumsum(expert_hot, axis=1) - 1) * expert_hot, axis=2).astype(jnp.int32)
    device_ids = jnp.arange(N_EXPERT, dtype=jnp.int32)[:, None]
    column = (device_ids * CAP + rank_in).astype(jnp.int32)
    token_of = (device_ids * TOK_DEV + jnp.arange(TOK_DEV * TOP, dtype=jnp.int32)[None, :] // TOP).astype(jnp.int32)
    source = jnp.full((EXPERTS, N_EXPERT * CAP), TOKENS, jnp.int32).at[flat_ids, column].set(token_of)
    padded = jnp.concatenate([token_state, jnp.zeros((1, D), jnp.bfloat16)], axis=0)
    group_count = EXPERTS // EXP_DEV
    gate_full = w_gate.reshape(group_count, SPLIT, EXP_DEV, D, FF_DEV).transpose(0, 2, 3, 1, 4).reshape(EXPERTS, D, FF)
    up_full = w_up.reshape(group_count, SPLIT, EXP_DEV, D, FF_DEV).transpose(0, 2, 3, 1, 4).reshape(EXPERTS, D, FF)
    down_parts = w_down.reshape(group_count, SPLIT, EXP_DEV, FF_DEV, D).transpose(0, 2, 1, 3, 4).reshape(EXPERTS, SPLIT, FF_DEV, D)

    def one_expert(operands):
        indices, gate_weight, up_weight, down_weight = operands
        rows_in = jnp.take(padded, indices, axis=0)
        gate_act = jnp.dot(rows_in, gate_weight, preferred_element_type=jnp.float32)
        up_act = jnp.dot(rows_in, up_weight, preferred_element_type=jnp.float32)
        hidden = (jax.nn.silu(gate_act) * up_act).astype(jnp.bfloat16)
        hidden_split = hidden.reshape(N_EXPERT * CAP, SPLIT, FF_DEV).astype(jnp.float32)
        partial_value = jnp.einsum("rsf,sfd->rsd", hidden_split, down_weight.astype(jnp.float32)).astype(jnp.bfloat16)
        return jnp.sum(partial_value.astype(jnp.float32), axis=1).astype(jnp.bfloat16)

    expert_out = lax.map(one_expert, (source, gate_full, up_full, down_parts))
    chosen = expert_out[flat_ids, column].reshape(TOKENS, TOP, D).astype(jnp.float32)
    mixed = jnp.sum(gate_weights[:, :, None] * chosen, axis=1).astype(jnp.bfloat16)
    gate_grads = jnp.einsum("tkd,td->tk", chosen, out_grad.astype(jnp.float32))
    return mixed, gate_grads
```

```python
import jax
import jax.numpy as jnp
from jax import lax
from jax.sharding import PartitionSpec as P

EXPERTS = 64
TOP = 4
CAP = 12


def expert_work(arrived, w_gate, w_up, w_down):
    gate_act = jnp.einsum("sjcd,jdf->sjcf", arrived, w_gate, preferred_element_type=jnp.float32)
    up_act = jnp.einsum("sjcd,jdf->sjcf", arrived, w_up, preferred_element_type=jnp.float32)
    hidden = (jax.nn.silu(gate_act) * up_act).astype(jnp.bfloat16)
    return jnp.einsum("sjcf,jfd->sjcd", hidden, w_down, preferred_element_type=jnp.float32).astype(
        jnp.bfloat16
    )


def return_path(partial, width_split):
    device_count, exp_dev, cap, features = partial.shape
    returned_out = lax.all_to_all(partial, "expert", split_axis=0, concat_axis=0, tiled=True)
    group_count = device_count // width_split
    pieces = returned_out.reshape(group_count, width_split, exp_dev, cap, features)
    if width_split == 1:
        return pieces.reshape(EXPERTS * CAP, features)
    return (
        jnp.sum(pieces.astype(jnp.float32), axis=1)
        .astype(jnp.bfloat16)
        .reshape(EXPERTS * CAP, features)
    )


def gathered_rows(token_state, expert_ids, exp_dev, width_split):
    states = lax.all_gather(token_state, "expert", axis=0, tiled=False)
    ids = lax.all_gather(expert_ids, "expert", axis=0, tiled=False)
    device_count, tok_rows, features = states.shape
    first = lax.axis_index("expert") // width_split * exp_dev
    mine = first + jnp.arange(exp_dev, dtype=jnp.int32)
    hit = jnp.any(ids[:, :, :, None] == mine, axis=2)
    rank = jnp.cumsum(hit.astype(jnp.int32), axis=1) - 1
    slot = jnp.arange(CAP, dtype=jnp.int32)
    chosen = hit[:, :, :, None] & (rank[:, :, :, None] == slot)
    return jnp.einsum(
        "stjc,std->sjcd", chosen.astype(jnp.bfloat16), states, preferred_element_type=jnp.float32
    ).astype(jnp.bfloat16)


def sent_rows(token_state, slot_of, device_count, exp_dev, width_split):
    tok_rows, features = token_state.shape
    token_index = jnp.arange(tok_rows * TOP, dtype=jnp.int32) // TOP
    source = jnp.full((EXPERTS * CAP,), tok_rows, jnp.int32).at[slot_of].set(token_index)
    padded = jnp.concatenate([token_state, jnp.zeros((1, features), jnp.bfloat16)], axis=0)
    buffer = jnp.take(padded, source, axis=0)
    group_count = EXPERTS // exp_dev
    grouped = buffer.reshape(group_count, 1, exp_dev, CAP, features)
    outgoing = jnp.broadcast_to(
        grouped, (group_count, width_split, exp_dev, CAP, features)
    ).reshape(device_count, exp_dev, CAP, features)
    return lax.all_to_all(outgoing, "expert", split_axis=0, concat_axis=0, tiled=True)


def local(
    block_values,
    block_exps,
    row_ids,
    expert_ids,
    gate_weights,
    table,
    w_gate,
    w_up,
    w_down,
    out_grad,
):
    device_count = lax.axis_size("expert")
    tok_rows = block_values.shape[0]
    features = block_values.shape[1]
    rows_held = table.shape[0]
    look_cap = max(2, 2 * tok_rows // device_count)
    exp_dev = w_gate.shape[0]
    width_split = device_count * exp_dev // EXPERTS
    owners = row_ids // rows_held
    local_row = row_ids % rows_held
    owner_hot = (owners[:, None] == jnp.arange(device_count, dtype=jnp.int32)[None, :]).astype(
        jnp.int32
    )
    owner_rank = jnp.sum((jnp.cumsum(owner_hot, axis=0) - 1) * owner_hot, axis=1)
    placed = owners * look_cap + owner_rank
    wanted = jnp.zeros((device_count * look_cap,), jnp.int32).at[placed].set(local_row)
    requested = lax.all_to_all(
        wanted.reshape(device_count, look_cap), "expert", split_axis=0, concat_axis=0, tiled=True
    )
    fetched = jnp.take(table, requested.reshape(-1), axis=0).reshape(
        device_count, look_cap, features
    )
    rows_returned = lax.all_to_all(fetched, "expert", split_axis=0, concat_axis=0, tiled=True)
    embedded = jnp.take(rows_returned.reshape(device_count * look_cap, features), placed, axis=0)
    scales = jnp.exp2(block_exps.astype(jnp.float32))
    blocks = (
        block_values.reshape(tok_rows, scales.shape[1], -1).astype(jnp.float32) * scales[:, :, None]
    )
    token_state = (blocks.reshape(tok_rows, features) + embedded.astype(jnp.float32)).astype(
        jnp.bfloat16
    )
    flat_ids = expert_ids.reshape(-1)
    expert_hot = (flat_ids[:, None] == jnp.arange(EXPERTS, dtype=jnp.int32)[None, :]).astype(
        jnp.int32
    )
    expert_rank = jnp.sum((jnp.cumsum(expert_hot, axis=0) - 1) * expert_hot, axis=1)
    slot_of = flat_ids * CAP + expert_rank
    if device_count <= 32:
        arrived = gathered_rows(token_state, expert_ids, exp_dev, width_split)
    else:
        arrived = sent_rows(token_state, slot_of, device_count, exp_dev, width_split)
    expert_out = return_path(expert_work(arrived, w_gate, w_up, w_down), width_split)
    chosen = jnp.take(expert_out, slot_of, axis=0).reshape(tok_rows, TOP, features)
    mixed = jnp.sum(gate_weights[:, :, None] * chosen.astype(jnp.float32), axis=1).astype(
        jnp.bfloat16
    )
    gate_grads = jnp.einsum("tkd,td->tk", chosen, out_grad, preferred_element_type=jnp.float32)
    return (mixed, gate_grads)


def solution(mesh):
    return jax.shard_map(
        local,
        mesh=mesh,
        in_specs=(
            P(("groups", "expert"), None),
            P(("groups", "expert"), None),
            P(("groups", "expert")),
            P(("groups", "expert"), None),
            P(("groups", "expert"), None),
            P("expert", None),
            P("expert", None, None),
            P("expert", None, None),
            P("expert", None, None),
            P(("groups", "expert"), None),
        ),
        out_specs=(P(("groups", "expert"), None), P(("groups", "expert"), None)),
        check_vma=False,
    )
```

```python
import functools

import jax
import jax.numpy as jnp
from jax import lax
from jax.experimental import pallas as pl
from jax.experimental.pallas import tpu as pltpu
from jax.sharding import PartitionSpec as P

EXPERTS = 64
TOP = 4
CAP = 12
BLOCK = 128
PAIR = 2 * CAP
VMEM = pltpu.VMEM
F32 = jnp.float32
BF16 = jnp.bfloat16


def dot(a, b):
    return jnp.dot(a, b, preferred_element_type=F32)


def earlier(length):
    row = lax.broadcasted_iota(jnp.int32, (length, length), 0)
    column = lax.broadcasted_iota(jnp.int32, (length, length), 1)
    return (row < column).astype(BF16)


def fetch_kernel(me_ref, rows_ref, table_ref, out_ref):
    device_count, tok_rows = rows_ref.shape
    held = table_ref.shape[0]
    look_cap = out_ref.shape[0] // device_count
    start = me_ref[0] * held
    local = rows_ref[...] - start
    hit = (local >= 0) & (local < held)
    rank = dot(hit.astype(F32).astype(BF16), earlier(tok_rows)).astype(jnp.int32)
    rank = jnp.where(hit, rank, -1)
    slot = lax.broadcasted_iota(jnp.int32, (look_cap, tok_rows), 0)
    place = lax.broadcasted_iota(jnp.int32, (look_cap, held), 1)
    picks = []
    for source in range(device_count):
        mine = jnp.where(slot == rank[source : source + 1], local[source : source + 1], 0)
        wanted = jnp.sum(mine, axis=1, keepdims=True)
        picks.append((place == wanted).astype(F32).astype(BF16))
    pick = jnp.concatenate(picks, axis=0)
    out_ref[...] = dot(pick, table_ref[...]).astype(BF16)


def state_kernel(rows_ref, returned_ref, values_ref, scales_ref, out_ref):
    slots = returned_ref.shape[0]
    tok_rows, features = values_ref.shape
    held = rows_ref.shape[0]
    owner_of = rows_ref[...]
    look_cap = slots // held
    owner = lax.broadcasted_iota(jnp.int32, (held, tok_rows), 0)
    hit = owner_of == owner
    rank = dot(hit.astype(F32).astype(BF16), earlier(tok_rows)).astype(jnp.int32)
    rank = jnp.where(hit, rank, -1)
    slot = lax.broadcasted_iota(jnp.int32, (look_cap, tok_rows), 0)
    put = jnp.concatenate(
        [(slot == rank[o : o + 1]).astype(F32) for o in range(held)], axis=0
    )
    put = put.T.astype(BF16)
    width = 512
    for left in range(0, features, width):
        found = dot(put, returned_ref[:, left : left + width])
        for b in range(width // BLOCK):
            at = left + b * BLOCK
            scaled = values_ref[:, at : at + BLOCK].astype(F32) * scales_ref[
                :, at // BLOCK : at // BLOCK + 1
            ]
            out_ref[:, at : at + BLOCK] = (
                scaled + found[:, b * BLOCK : (b + 1) * BLOCK]
            ).astype(BF16)


def gather_slots(states, ids_ref, source_of, core, first, exp_dev):
    tok_rows = ids_ref.shape[2]
    hits = []
    for part in range(4):
        ids = ids_ref[source_of[part]]
        for j in range(exp_dev):
            hits.append(jnp.max((ids == first + j).astype(F32), axis=0, keepdims=True))
    hits = jnp.concatenate(hits, axis=0)
    rank = dot(hits.astype(BF16), earlier(tok_rows)).astype(jnp.int32)
    rank = jnp.where(hits > 0, rank, -1000)
    row = lax.broadcasted_iota(jnp.int32, (2 * PAIR, tok_rows), 0)
    lines = []
    for j in range(exp_dev):
        cells = []
        for part in range(4):
            flip = (core + part + j) % 2
            base = (part // 2) * PAIR + CAP * flip
            k = part * exp_dev + j
            cells.append((row == rank[k : k + 1] + base).astype(F32).astype(BF16))
        lines.append(jnp.concatenate(cells, axis=1))
    pick = jnp.concatenate(lines, axis=0)
    return dot(pick, states)


def expert_kernel(
    gather,
    first_held,
    place_ref,
    *refs,
):
    if gather:
        ids_ref = refs[0]
        pieces = refs[1:29]
        wg_hbm, wu_hbm, wd_hbm, out_ref, later_ref = refs[29:34]
        x_ref, state_ref, wg_ref, wu_ref, wd_ref, hidden_ref, result_ref, sem, state_sem = refs[34:]
    else:
        x_ref, wg_hbm, wu_hbm, wd_hbm, out_ref = refs[:5]
        wg_ref, wu_ref, wd_ref, hidden_ref, result_ref, sem = refs[5:]
    features = wg_ref.shape[1]
    width = wg_ref.shape[2]
    z, y, core = place_ref[0], place_ref[1], place_ref[2]
    count = wg_ref.shape[0]
    up_cuts = ((0, 512), (512, 512), (1024, width - 1024))
    down_cuts = tuple((at, 512) for at in range(0, features, 512))

    def weight_copies(j):
        copies = []
        for at, size in up_cuts:
            for hbm, ref in ((wg_hbm, wg_ref), (wu_hbm, wu_ref)):
                cols = pl.ds(at, size)
                copies.append((hbm.at[first_held + j, :, cols], ref.at[j, :, cols]))
        for at, size in down_cuts:
            cols = pl.ds(at, size)
            copies.append((wd_hbm.at[first_held + j, :, cols], wd_ref.at[j, :, cols]))
        return [
            pltpu.make_async_copy(src, dst, sem.at[j, n]) for n, (src, dst) in enumerate(copies)
        ]

    if gather:
        options = ((0, 0), (1, 6), (2, 5), (3, 4))
        conditions = (z >= 0, z >= 1, z <= 2, z >= 2)
        tok_rows = ids_ref.shape[2]

        def state_copy(kind, slot, part):
            at = pl.ds((slot * 4 + part) * tok_rows, tok_rows)
            return pltpu.make_async_copy(
                pieces[kind * 4 + part], state_ref.at[at], state_sem.at[slot, part]
            )

        for slot in range(4):
            yes, no = options[slot]
            for part in range(4):
                if yes == no:
                    state_copy(yes, slot, part).start()
                else:

                    @pl.when(conditions[slot])
                    def _(slot=slot, part=part, yes=yes):
                        state_copy(yes, slot, part).start()

                    @pl.when(jnp.logical_not(conditions[slot]))
                    def _(slot=slot, part=part, no=no):
                        state_copy(no, slot, part).start()

    for j in range(count):
        for copy in weight_copies(j):
            copy.start()

    plane = (
        z,
        jnp.where(z >= 1, z - 1, 3),
        jnp.where(z <= 2, z + 1, 0),
        jnp.where(z >= 2, z - 2, z + 2),
    )
    if gather:
        exp_dev = 2 * count
        first = place_ref[3]
        for slot in range(4):
            source_of = [
                plane[slot] * 4 + ((y + part // 2) % 2) * 2 + (core + part) % 2 for part in range(4)
            ]
            for part in range(4):
                state_copy(0, slot, part).wait()
            at = slot * 4 * tok_rows
            rows = gather_slots(
                state_ref[at : at + 4 * tok_rows, :], ids_ref, source_of, core, first, exp_dev
            ).astype(BF16)
            for j in range(exp_dev):
                block = rows[j * 2 * PAIR : (j + 1) * 2 * PAIR]
                if j < count:
                    x_ref[j, slot * 2 * PAIR : (slot + 1) * 2 * PAIR, :] = block
                else:
                    later_ref[j - count, slot * 2 * PAIR : (slot + 1) * 2 * PAIR, :] = block

    @pl.loop(0, count)
    def _(j):
        copies = weight_copies(j)
        n = 0
        for at, size in up_cuts:
            copies[n].wait()
            copies[n + 1].wait()
            n += 2
            x = x_ref[j]
            gate = dot(x, wg_ref[j, :, at : at + size])
            up = dot(x, wu_ref[j, :, at : at + size])
            hidden_ref[:, at : at + size] = (gate / (1.0 + jnp.exp(-gate)) * up).astype(BF16)
        for at, size in down_cuts:
            copies[n].wait()
            n += 1
            result_ref[j, :, at : at + size] = dot(hidden_ref[...], wd_ref[j, :, at : at + size])

    low = lax.broadcasted_iota(jnp.int32, (PAIR, features), 0) < CAP
    for slot in range(4):
        for other in range(2):
            at = (slot * 2 + other) * PAIR
            pair = plane[slot] * 2 + (y + other) % 2
            one = result_ref[0, at : at + PAIR, :]
            two = result_ref[1, at : at + PAIR, :]
            out_ref[2 * pair] = jnp.where(low, one, two).astype(BF16)
            out_ref[2 * pair + 1] = jnp.where(low, two, one).astype(BF16)


def expert_call(gather, first_held, place, operands, weights, device_count):
    w_gate, w_up, w_down = weights
    exp_dev, features, width = w_gate.shape
    count = exp_dev // 2
    rows = device_count * CAP
    anywhere = pl.BlockSpec(memory_space=pl.ANY)
    smem = pl.BlockSpec(memory_space=pltpu.SMEM)
    vmem = pl.BlockSpec(memory_space=VMEM)
    out_shape = [jax.ShapeDtypeStruct((device_count, PAIR, features), BF16)]
    scratch = [
        VMEM((count, features, width), BF16),
        VMEM((count, features, width), BF16),
        VMEM((count, width, features), BF16),
        VMEM((rows, width), BF16),
        VMEM((count, rows, features), F32),
        pltpu.SemaphoreType.DMA((count, 10)),
    ]
    if gather:
        ids, pieces = operands
        tok_rows = ids.shape[2]
        out_shape.append(jax.ShapeDtypeStruct((count, rows, features), BF16))
        scratch = (
            [VMEM((count, rows, features), BF16), VMEM((device_count * tok_rows, features), BF16)]
            + scratch
            + [pltpu.SemaphoreType.DMA((4, 4))]
        )
        inputs = [ids, *pieces]
        in_specs = [vmem] + [anywhere] * len(pieces)
    else:
        inputs = [operands]
        in_specs = [vmem]
    return pl.pallas_call(
        functools.partial(expert_kernel, gather, first_held),
        out_shape=out_shape,
        in_specs=[smem] + in_specs + [anywhere] * 3,
        out_specs=[vmem] * len(out_shape),
        scratch_shapes=scratch,
        compiler_params=pltpu.CompilerParams(vmem_limit_bytes=60 * 1024 * 1024),
        cost_estimate=pl.CostEstimate(
            flops=6 * count * rows * features * width,
            bytes_accessed=6 * count * features * width,
            transcendentals=count * rows * width,
        ),
        name="experts_first" if gather else "experts_second",
    )(place, *inputs, w_gate, w_up, w_down)


def combine_kernel(slots_ref, weights_ref, first_ref, second_ref, grad_ref, mixed_ref, grads_ref):
    tok_rows, features = grad_ref.shape
    half = first_ref.shape[0]
    column = lax.broadcasted_iota(jnp.int32, (tok_rows, half), 1)
    picked = [jnp.zeros((tok_rows, 1), F32) for _ in range(TOP)]
    spread = []
    for part, ref in enumerate((first_ref, second_ref)):
        inner = lax.dot_general(
            grad_ref[...], ref[...], (((1,), (1,)), ((), ())), preferred_element_type=F32
        )
        total = jnp.zeros((tok_rows, half), F32)
        for k in range(TOP):
            here = column == slots_ref[:, k : k + 1] - part * half
            total = total + jnp.where(here, weights_ref[:, k : k + 1], 0.0)
            picked[k] = picked[k] + jnp.sum(jnp.where(here, inner, 0.0), axis=1, keepdims=True)
        high = total.astype(BF16)
        spread.append((high, (total - high.astype(F32)).astype(BF16)))
    for k in range(TOP):
        grads_ref[:, k : k + 1] = picked[k]
    width = 512
    for at in range(0, features, width):
        value = jnp.zeros((tok_rows, width), F32)
        for (high, low), ref in zip(spread, (first_ref, second_ref)):
            rows = ref[:, at : at + width]
            value = value + dot(high, rows) + dot(low, rows)
        mixed_ref[:, at : at + width] = value.astype(BF16)


def gather_states(state):
    device_count = lax.axis_size("expert")
    planes = device_count // 4

    def along(array, step):
        pairs = [
            (i, i + 4 * step) for i in range(device_count) if 0 <= i // 4 + step < planes
        ]
        return lax.ppermute(array, "expert", pairs)

    def across(array, bit, keep):
        pairs = [(i, i ^ bit) for i in range(device_count) if keep(i // 4)]
        return lax.ppermute(array, "expert", pairs)

    up_1, down_1 = along(state, 1), along(state, -1)
    up_2, down_2 = along(up_1, 1), along(down_1, -1)
    up_3, down_3 = along(up_2, 1), along(down_2, -1)
    kinds = (
        (state, lambda z: True),
        (up_1, lambda z: z >= 1),
        (down_1, lambda z: z <= planes - 2),
        (up_2, lambda z: z >= 2),
        (down_2, lambda z: z <= planes - 3),
        (up_3, lambda z: z >= 3),
        (down_3, lambda z: z <= planes - 4),
    )
    pieces = []
    for array, keep in kinds:
        beside = across(array, 2, keep)
        pieces += [array, across(array, 1, keep), beside, across(beside, 1, keep)]
    return pieces


def near_path(
    block_values,
    block_exps,
    row_ids,
    expert_ids,
    gate_weights,
    table,
    w_gate,
    w_up,
    w_down,
    out_grad,
):
    device_count = lax.axis_size("expert")
    me = lax.axis_index("expert").astype(jnp.int32)
    tok_rows, features = block_values.shape
    rows_held = table.shape[0]
    exp_dev = w_gate.shape[0]
    look_cap = max(2, 2 * tok_rows // device_count)
    vmem = pl.BlockSpec(memory_space=VMEM)
    smem = pl.BlockSpec(memory_space=pltpu.SMEM)

    ids = jnp.concatenate([row_ids[None, :], expert_ids.T], axis=0)
    all_ids = lax.all_to_all(
        jnp.broadcast_to(ids[None], (device_count, 1 + TOP, tok_rows)),
        "expert",
        split_axis=0,
        concat_axis=0,
        tiled=True,
    )
    fetched = pl.pallas_call(
        fetch_kernel,
        out_shape=jax.ShapeDtypeStruct((device_count * look_cap, features), BF16),
        in_specs=[smem, vmem, vmem],
        out_specs=vmem,
        name="fetch_rows",
    )(me[None], all_ids[:, 0, :], table)
    returned = lax.all_to_all(
        fetched.reshape(device_count, look_cap, features),
        "expert",
        split_axis=0,
        concat_axis=0,
        tiled=True,
    ).reshape(device_count * look_cap, features)
    scales = jnp.exp2(block_exps.astype(F32))
    owners = jnp.broadcast_to((row_ids // rows_held)[None, :], (device_count, tok_rows))
    state = pl.pallas_call(
        state_kernel,
        out_shape=jax.ShapeDtypeStruct((tok_rows, features), BF16),
        in_specs=[vmem] * 4,
        out_specs=vmem,
        name="token_state",
    )(owners, returned, block_values, scales)
    pieces = gather_states(state)

    core = me % 2
    place = jnp.stack([me // 4, (me // 2) % 2, core, me * exp_dev])
    weights = (w_gate, w_up, w_down)
    first_out, later = expert_call(
        True, 0, place, (all_ids[:, 1:, :], pieces), weights, device_count
    )
    (second_out,) = expert_call(False, exp_dev // 2, place, later, weights, device_count)
    back = [
        lax.all_to_all(out, "expert", split_axis=0, concat_axis=0, tiled=True).reshape(
            device_count * PAIR, features
        )
        for out in (first_out, second_out)
    ]

    named = (expert_ids[:, :, None] == jnp.arange(EXPERTS, dtype=jnp.int32)).astype(F32)
    counted = dot(earlier(tok_rows).T, jnp.sum(named, axis=1).astype(BF16))
    rank = jnp.sum(counted[:, None, :] * named, axis=2).astype(jnp.int32)
    inside = expert_ids % exp_dev
    slots = (
        (inside // 2) * (device_count * PAIR)
        + (expert_ids // exp_dev) * PAIR
        + ((core + inside) % 2) * CAP
        + rank
    )
    return pl.pallas_call(
        combine_kernel,
        out_shape=(
            jax.ShapeDtypeStruct((tok_rows, features), BF16),
            jax.ShapeDtypeStruct((tok_rows, TOP), F32),
        ),
        in_specs=[vmem] * 5,
        out_specs=(vmem, vmem),
        name="combine",
    )(slots, gate_weights, back[0], back[1], out_grad)


def expert_work(arrived, w_gate, w_up, w_down):
    gate_act = jnp.einsum("sjcd,jdf->sjcf", arrived, w_gate, preferred_element_type=jnp.float32)
    up_act = jnp.einsum("sjcd,jdf->sjcf", arrived, w_up, preferred_element_type=jnp.float32)
    hidden = (jax.nn.silu(gate_act) * up_act).astype(jnp.bfloat16)
    return jnp.einsum("sjcf,jfd->sjcd", hidden, w_down, preferred_element_type=jnp.float32).astype(
        jnp.bfloat16
    )


def full_path(buffer, w_gate, w_up, w_down, device_count, exp_dev, width_split, features):
    group_count = EXPERTS // exp_dev
    grouped = buffer.reshape(group_count, 1, exp_dev, CAP, features)
    outgoing = jnp.broadcast_to(
        grouped, (group_count, width_split, exp_dev, CAP, features)
    ).reshape(device_count, exp_dev, CAP, features)
    returned_out = lax.all_to_all(
        expert_work(
            lax.all_to_all(outgoing, "expert", split_axis=0, concat_axis=0, tiled=True),
            w_gate,
            w_up,
            w_down,
        ),
        "expert",
        split_axis=0,
        concat_axis=0,
        tiled=True,
    )
    pieces = returned_out.reshape(group_count, width_split, exp_dev, CAP, features).astype(
        jnp.float32
    )
    return jnp.sum(pieces, axis=1).astype(jnp.bfloat16).reshape(EXPERTS * CAP, features)


def far_path(
    block_values,
    block_exps,
    row_ids,
    expert_ids,
    gate_weights,
    table,
    w_gate,
    w_up,
    w_down,
    out_grad,
):
    device_count = lax.axis_size("expert")
    tok_rows = block_values.shape[0]
    features = block_values.shape[1]
    rows_held = table.shape[0]
    look_cap = max(2, 2 * tok_rows // device_count)
    exp_dev = w_gate.shape[0]
    width_split = device_count * exp_dev // EXPERTS
    owners = row_ids // rows_held
    local_row = row_ids % rows_held
    owner_hot = (owners[:, None] == jnp.arange(device_count, dtype=jnp.int32)[None, :]).astype(
        jnp.int32
    )
    owner_rank = jnp.sum((jnp.cumsum(owner_hot, axis=0) - 1) * owner_hot, axis=1)
    placed = owners * look_cap + owner_rank
    wanted = jnp.zeros((device_count * look_cap,), jnp.int32).at[placed].set(local_row)
    requested = lax.all_to_all(
        wanted.reshape(device_count, look_cap), "expert", split_axis=0, concat_axis=0, tiled=True
    )
    fetched = jnp.take(table, requested.reshape(-1), axis=0).reshape(
        device_count, look_cap, features
    )
    rows_returned = lax.all_to_all(fetched, "expert", split_axis=0, concat_axis=0, tiled=True)
    embedded = jnp.take(rows_returned.reshape(device_count * look_cap, features), placed, axis=0)
    scales = jnp.exp2(block_exps.astype(jnp.float32))
    blocks = (
        block_values.reshape(tok_rows, scales.shape[1], -1).astype(jnp.float32) * scales[:, :, None]
    )
    token_state = (blocks.reshape(tok_rows, features) + embedded.astype(jnp.float32)).astype(
        jnp.bfloat16
    )
    flat_ids = expert_ids.reshape(-1)
    expert_hot = (flat_ids[:, None] == jnp.arange(EXPERTS, dtype=jnp.int32)[None, :]).astype(
        jnp.int32
    )
    expert_rank = jnp.sum((jnp.cumsum(expert_hot, axis=0) - 1) * expert_hot, axis=1)
    slot_of = flat_ids * CAP + expert_rank
    token_index = jnp.arange(tok_rows * TOP, dtype=jnp.int32) // TOP
    source = jnp.full((EXPERTS * CAP,), tok_rows, jnp.int32).at[slot_of].set(token_index)
    padded = jnp.concatenate([token_state, jnp.zeros((1, features), jnp.bfloat16)], axis=0)
    buffer = jnp.take(padded, source, axis=0)
    expert_out = full_path(
        buffer, w_gate, w_up, w_down, device_count, exp_dev, width_split, features
    )
    chosen = jnp.take(expert_out, slot_of, axis=0).reshape(tok_rows, TOP, features)
    mixed = jnp.sum(gate_weights[:, :, None] * chosen.astype(jnp.float32), axis=1).astype(
        jnp.bfloat16
    )
    gate_grads = jnp.einsum("tkd,td->tk", chosen, out_grad, preferred_element_type=jnp.float32)
    return (mixed, gate_grads)


def local(*arrays):
    if lax.axis_size("expert") == 16 and arrays[6].shape[0] * 16 == EXPERTS:
        return near_path(*arrays)
    return far_path(*arrays)


def solution(mesh):
    return jax.shard_map(
        local,
        mesh=mesh,
        in_specs=(
            P(("groups", "expert"), None),
            P(("groups", "expert"), None),
            P(("groups", "expert")),
            P(("groups", "expert"), None),
            P(("groups", "expert"), None),
            P("expert", None),
            P("expert", None, None),
            P("expert", None, None),
            P("expert", None, None),
            P(("groups", "expert"), None),
        ),
        out_specs=(P(("groups", "expert"), None), P(("groups", "expert"), None)),
        check_vma=False,
    )
```

```python
import functools

import jax
import jax.numpy as jnp
from jax import lax
from jax.experimental import pallas as pl
from jax.experimental.pallas import tpu as pltpu
from jax.sharding import PartitionSpec as P

EXPERTS = 64
TOP = 4
CAP = 12
BLOCK = 128
PAIR = 2 * CAP
VMEM = pltpu.VMEM
F32 = jnp.float32
BF16 = jnp.bfloat16


def dot(a, b):
    return jnp.dot(a, b, preferred_element_type=F32)


def iota(shape, dimension):
    return lax.broadcasted_iota(jnp.int32, shape, dimension)


def flags(mask):
    return mask.astype(F32).astype(BF16)


def earlier(length):
    return flags(iota((length, length), 0) < iota((length, length), 1))


def fetch_kernel(me_ref, rows_ref, table_ref, out_ref):
    device_count, _, tok_rows = rows_ref.shape
    held = table_ref.shape[0]
    look_cap = out_ref.shape[0] // device_count
    local = rows_ref[:, 0, :] - me_ref[0] * held
    hit = (local >= 0) & (local < held)
    rank = dot(flags(hit), earlier(tok_rows)).astype(jnp.int32)
    rank = jnp.where(hit, rank, -1)
    slot = iota((look_cap, tok_rows), 0)
    place = iota((look_cap, held), 1)
    picks = []
    for source in range(device_count):
        mine = jnp.where(slot == rank[source : source + 1], local[source : source + 1], 0)
        wanted = jnp.sum(mine, axis=1, keepdims=True)
        picks.append(flags(place == wanted))
    out_ref[...] = dot(jnp.concatenate(picks, axis=0), table_ref[...]).astype(BF16)


def plan_kernel(
    me_ref, rows_ref, across_ref, ids_ref, _, put_ref, first_ref, second_ref, slots_ref
):
    tok_rows = rows_ref.shape[1]
    slots = put_ref.shape[1]
    flip = me_ref[0] % 2
    held = me_ref[1]
    owners = me_ref[2]
    device_count = first_ref.shape[0] // PAIR
    exp_dev = EXPERTS // device_count
    look_cap = slots // device_count
    before = earlier(tok_rows)

    row = jnp.broadcast_to(rows_ref[...], (device_count, tok_rows))
    low = iota((device_count, tok_rows), 0) * held
    hit = (row >= low) & (row < low + held) & (low < owners * held)
    rank = jnp.where(hit, dot(flags(hit), before).astype(jnp.int32), -1)
    slot = iota((look_cap, tok_rows), 0)
    put = [(slot == rank[o : o + 1]).astype(F32) for o in range(device_count)]
    put_ref[...] = jnp.concatenate(put, axis=0).T.astype(BF16)

    expert = iota((EXPERTS, tok_rows), 0)
    hit = functools.reduce(
        jnp.logical_or, [across_ref[k : k + 1, :] == expert for k in range(TOP)]
    )
    rank = jnp.where(hit, dot(flags(hit), before).astype(jnp.int32), -1000)
    place = iota((PAIR, tok_rows), 0)
    for chunk, ref in enumerate((first_ref, second_ref)):
        lines = []
        for d in range(device_count):
            at = d * exp_dev + 2 * chunk
            one, two = rank[at : at + 1], rank[at + 1 : at + 2]
            upper = jnp.where(flip == 0, one, two)
            lower = jnp.where(flip == 0, two, one) + CAP
            here = ((place < CAP) & (place == upper)) | ((place >= CAP) & (place == lower))
            lines.append(here.astype(F32))
        ref[...] = jnp.concatenate(lines, axis=0).astype(BF16)

    expert = iota((tok_rows, EXPERTS), 1)
    chosen = [ids_ref[:, k : k + 1] == expert for k in range(TOP)]
    counted = dot(earlier(tok_rows).T, flags(functools.reduce(jnp.logical_or, chosen)))
    shift = exp_dev.bit_length() - 1
    for k in range(TOP):
        ids = ids_ref[:, k : k + 1]
        nth = jnp.sum(jnp.where(chosen[k], counted, 0.0), axis=1, keepdims=True).astype(jnp.int32)
        inside = ids & (exp_dev - 1)
        slots_ref[:, k : k + 1] = (
            (inside >> 1) * (device_count * PAIR)
            + (ids >> shift) * PAIR
            + ((flip + inside) & 1) * CAP
            + nth
        )


def state_kernel(put_ref, pick_ref, returned_ref, values_ref, scales_ref, state_ref, out_ref):
    features = values_ref.shape[1]
    width = 512
    for left in range(0, features, width):
        found = dot(put_ref[...], returned_ref[:, left : left + width])
        for b in range(width // BLOCK):
            at = left + b * BLOCK
            scaled = (
                values_ref[:, at : at + BLOCK].astype(F32)
                * scales_ref[:, at // BLOCK : at // BLOCK + 1]
            )
            state_ref[:, at : at + BLOCK] = (
                scaled + found[:, b * BLOCK : (b + 1) * BLOCK]
            ).astype(BF16)
        cols = slice(left, left + width)
        out_ref[:, cols] = dot(pick_ref[...], state_ref[:, cols]).astype(BF16)


def pick_kernel(pick_ref, state_ref, _, out_ref):
    features = state_ref.shape[1]
    width = 512
    for left in range(0, features, width):
        cols = slice(left, left + width)
        out_ref[:, cols] = dot(pick_ref[...], state_ref[:, cols]).astype(BF16)


def expert_kernel(
    first_held,
    arrived_ref,
    wg_hbm,
    wu_hbm,
    wd_hbm,
    out_ref,
    x_ref,
    wg_ref,
    wu_ref,
    wd_ref,
    hidden_ref,
    result_ref,
    sem,
):
    count, features, width = wg_ref.shape
    device_count = arrived_ref.shape[0]
    up_cuts = ((0, 512), (512, 512), (1024, width - 1024))
    down_cuts = tuple((at, 512) for at in range(0, features, 512))

    def weight_copies(j):
        copies = []
        for at, size in up_cuts:
            for hbm, ref in ((wg_hbm, wg_ref), (wu_hbm, wu_ref)):
                cols = pl.ds(at, size)
                copies.append((hbm.at[first_held + j, :, cols], ref.at[j, :, cols]))
        for at, size in down_cuts:
            cols = pl.ds(at, size)
            copies.append((wd_hbm.at[first_held + j, :, cols], wd_ref.at[j, :, cols]))
        return [
            pltpu.make_async_copy(src, dst, sem.at[j, n]) for n, (src, dst) in enumerate(copies)
        ]

    for j in range(count):
        for copy in weight_copies(j):
            copy.start()

    low = iota((PAIR, features), 0) < CAP
    for quad in range(device_count // 4):
        ones, twos = [], []
        for pair in range(2):
            source = 4 * quad + 2 * pair
            even = arrived_ref[source].astype(F32)
            odd = arrived_ref[source + 1].astype(F32)
            ones.append(jnp.where(low, even, odd))
            twos.append(jnp.where(low, odd, even))
        rows = slice(quad * 2 * PAIR, (quad + 1) * 2 * PAIR)
        x_ref[0, rows, :] = jnp.concatenate(ones, axis=0).astype(BF16)
        x_ref[1, rows, :] = jnp.concatenate(twos, axis=0).astype(BF16)

    @pl.loop(0, count)
    def _(j):
        copies = weight_copies(j)
        n = 0
        for at, size in up_cuts:
            copies[n].wait()
            copies[n + 1].wait()
            n += 2
            x = x_ref[j]
            gate = dot(x, wg_ref[j, :, at : at + size])
            up = dot(x, wu_ref[j, :, at : at + size])
            hidden_ref[:, at : at + size] = (gate / (1.0 + jnp.exp(-gate)) * up).astype(BF16)
        for at, size in down_cuts:
            copies[n].wait()
            n += 1
            result_ref[j, :, at : at + size] = dot(hidden_ref[...], wd_ref[j, :, at : at + size])

    for pair in range(device_count // 2):
        one = result_ref[0, pair * PAIR : (pair + 1) * PAIR, :]
        two = result_ref[1, pair * PAIR : (pair + 1) * PAIR, :]
        out_ref[2 * pair] = jnp.where(low, one, two).astype(BF16)
        out_ref[2 * pair + 1] = jnp.where(low, two, one).astype(BF16)


def expert_call(first_held, arrived, w_gate, w_up, w_down):
    exp_dev, features, width = w_gate.shape
    device_count = arrived.shape[0]
    count = 2
    rows = device_count * CAP
    anywhere = pl.BlockSpec(memory_space=pl.ANY)
    vmem = pl.BlockSpec(memory_space=VMEM)
    return pl.pallas_call(
        functools.partial(expert_kernel, first_held),
        out_shape=jax.ShapeDtypeStruct((device_count, PAIR, features), BF16),
        in_specs=[vmem] + [anywhere] * 3,
        out_specs=vmem,
        scratch_shapes=[
            VMEM((count, rows, features), BF16),
            VMEM((count, features, width), BF16),
            VMEM((count, features, width), BF16),
            VMEM((count, width, features), BF16),
            VMEM((rows, width), BF16),
            VMEM((count, rows, features), F32),
            pltpu.SemaphoreType.DMA((count, 10)),
        ],
        compiler_params=pltpu.CompilerParams(vmem_limit_bytes=52 * 1024 * 1024),
        cost_estimate=pl.CostEstimate(
            flops=6 * count * rows * features * width,
            bytes_accessed=6 * count * features * width,
            transcendentals=count * rows * width,
        ),
        name="experts_second" if first_held else "experts_first",
    )(arrived, w_gate, w_up, w_down)


def combine_kernel(chunk, slots_ref, weights_ref, back_ref, grad_ref, *refs):
    sums = refs[:2] if chunk else None
    mixed_ref, grads_ref = refs[-2:]
    tok_rows, features = grad_ref.shape
    half = back_ref.shape[0]
    column = iota((tok_rows, half), 1) + chunk * half
    inner = lax.dot_general(
        grad_ref[...], back_ref[...], (((1,), (1,)), ((), ())), preferred_element_type=F32
    )
    total = jnp.zeros((tok_rows, half), F32)
    for k in range(TOP):
        here = column == slots_ref[:, k : k + 1]
        total = total + jnp.where(here, weights_ref[:, k : k + 1], 0.0)
        value = jnp.sum(jnp.where(here, inner, 0.0), axis=1, keepdims=True)
        if chunk:
            value = value + sums[1][:, k : k + 1]
        grads_ref[:, k : k + 1] = value
    high = total.astype(BF16)
    rest = (total - high.astype(F32)).astype(BF16)
    width = 512
    for at in range(0, features, width):
        rows = back_ref[:, at : at + width]
        value = dot(high, rows) + dot(rest, rows)
        if chunk:
            value = value + sums[0][:, at : at + width]
        mixed_ref[:, at : at + width] = value.astype(mixed_ref.dtype)


def swap(array):
    return lax.all_to_all(array, "expert", split_axis=0, concat_axis=0, tiled=True)


def near_path(
    block_values,
    block_exps,
    row_ids,
    expert_ids,
    gate_weights,
    table,
    w_gate,
    w_up,
    w_down,
    out_grad,
):
    device_count = lax.axis_size("expert")
    me = lax.axis_index("expert").astype(jnp.int32)
    tok_rows, features = block_values.shape
    rows_held = table.shape[0]
    look_cap = max(2, 2 * tok_rows // device_count)
    slots = device_count * PAIR
    vmem = pl.BlockSpec(memory_space=VMEM)
    smem = pl.BlockSpec(memory_space=pltpu.SMEM)
    anywhere = pl.BlockSpec(memory_space=pl.ANY)
    place = jnp.stack([me, jnp.int32(rows_held), jnp.int32(device_count)])

    def shape(dims, kind):
        return jax.ShapeDtypeStruct(dims, kind)

    all_rows = swap(jnp.broadcast_to(row_ids[None, None, :], (device_count, 1, tok_rows)))
    fetched = pl.pallas_call(
        fetch_kernel,
        out_shape=shape((device_count * look_cap, features), BF16),
        in_specs=[smem, vmem, vmem],
        out_specs=vmem,
        name="fetch_rows",
    )(place, all_rows, table)
    returned = swap(fetched.reshape(device_count, look_cap, features))
    put, first_pick, second_pick, slot_of = pl.pallas_call(
        plan_kernel,
        out_shape=(
            shape((tok_rows, device_count * look_cap), BF16),
            shape((slots, tok_rows), BF16),
            shape((slots, tok_rows), BF16),
            shape((tok_rows, TOP), jnp.int32),
        ),
        in_specs=[smem, vmem, vmem, vmem, anywhere],
        out_specs=(vmem, vmem, vmem, vmem),
        name="plan",
    )(place, row_ids[None, :], expert_ids.T, expert_ids, fetched)
    state, first_sent = pl.pallas_call(
        state_kernel,
        out_shape=(shape((tok_rows, features), BF16), shape((slots, features), BF16)),
        in_specs=[vmem] * 5,
        out_specs=(vmem, vmem),
        name="token_state",
    )(
        put,
        first_pick,
        returned.reshape(device_count * look_cap, features),
        block_values,
        jnp.exp2(block_exps.astype(F32)),
    )
    first_rows = swap(first_sent.reshape(device_count, PAIR, features))
    second_sent = pl.pallas_call(
        pick_kernel,
        out_shape=shape((slots, features), BF16),
        in_specs=[vmem, vmem, anywhere],
        out_specs=vmem,
        name="second_slots",
    )(second_pick, state, first_rows)
    second_rows = swap(second_sent.reshape(device_count, PAIR, features))
    first_out = expert_call(0, first_rows, w_gate, w_up, w_down)
    first_back = swap(first_out)
    second_out = expert_call(2, second_rows, w_gate, w_up, w_down)
    second_back = swap(
        pl.pallas_call(
            lambda second_ref, first_ref, out_ref: None,
            out_shape=shape(second_out.shape, BF16),
            in_specs=[anywhere, anywhere],
            out_specs=anywhere,
            input_output_aliases={0: 0},
            name="after_first",
        )(second_out, first_back)
    )

    def combine(chunk, back, *sums):
        return pl.pallas_call(
            functools.partial(combine_kernel, chunk),
            out_shape=(
                shape((tok_rows, features), BF16 if chunk else F32),
                shape((tok_rows, TOP), F32),
            ),
            in_specs=[vmem] * (4 + len(sums)),
            out_specs=(vmem, vmem),
            cost_estimate=pl.CostEstimate(
                flops=6 * tok_rows * slots * features,
                bytes_accessed=4 * slots * features,
                transcendentals=0,
            ),
            name="combine_second" if chunk else "combine_first",
        )(slot_of, gate_weights, back.reshape(slots, features), out_grad, *sums)

    return combine(1, second_back, *combine(0, first_back))


def expert_work(arrived, w_gate, w_up, w_down):
    gate_act = jnp.einsum("sjcd,jdf->sjcf", arrived, w_gate, preferred_element_type=jnp.float32)
    up_act = jnp.einsum("sjcd,jdf->sjcf", arrived, w_up, preferred_element_type=jnp.float32)
    hidden = (jax.nn.silu(gate_act) * up_act).astype(jnp.bfloat16)
    return jnp.einsum("sjcf,jfd->sjcd", hidden, w_down, preferred_element_type=jnp.float32).astype(
        jnp.bfloat16
    )


def full_path(buffer, w_gate, w_up, w_down, device_count, exp_dev, width_split, features):
    group_count = EXPERTS // exp_dev
    grouped = buffer.reshape(group_count, 1, exp_dev, CAP, features)
    outgoing = jnp.broadcast_to(
        grouped, (group_count, width_split, exp_dev, CAP, features)
    ).reshape(device_count, exp_dev, CAP, features)
    returned_out = lax.all_to_all(
        expert_work(
            lax.all_to_all(outgoing, "expert", split_axis=0, concat_axis=0, tiled=True),
            w_gate,
            w_up,
            w_down,
        ),
        "expert",
        split_axis=0,
        concat_axis=0,
        tiled=True,
    )
    pieces = returned_out.reshape(group_count, width_split, exp_dev, CAP, features).astype(
        jnp.float32
    )
    return jnp.sum(pieces, axis=1).astype(jnp.bfloat16).reshape(EXPERTS * CAP, features)


def far_path(
    block_values,
    block_exps,
    row_ids,
    expert_ids,
    gate_weights,
    table,
    w_gate,
    w_up,
    w_down,
    out_grad,
):
    device_count = lax.axis_size("expert")
    tok_rows = block_values.shape[0]
    features = block_values.shape[1]
    rows_held = table.shape[0]
    look_cap = max(2, 2 * tok_rows // device_count)
    exp_dev = w_gate.shape[0]
    width_split = device_count * exp_dev // EXPERTS
    owners = row_ids // rows_held
    local_row = row_ids % rows_held
    owner_hot = (owners[:, None] == jnp.arange(device_count, dtype=jnp.int32)[None, :]).astype(
        jnp.int32
    )
    owner_rank = jnp.sum((jnp.cumsum(owner_hot, axis=0) - 1) * owner_hot, axis=1)
    placed = owners * look_cap + owner_rank
    wanted = jnp.zeros((device_count * look_cap,), jnp.int32).at[placed].set(local_row)
    requested = lax.all_to_all(
        wanted.reshape(device_count, look_cap), "expert", split_axis=0, concat_axis=0, tiled=True
    )
    fetched = jnp.take(table, requested.reshape(-1), axis=0).reshape(
        device_count, look_cap, features
    )
    rows_returned = lax.all_to_all(fetched, "expert", split_axis=0, concat_axis=0, tiled=True)
    embedded = jnp.take(rows_returned.reshape(device_count * look_cap, features), placed, axis=0)
    scales = jnp.exp2(block_exps.astype(jnp.float32))
    blocks = (
        block_values.reshape(tok_rows, scales.shape[1], -1).astype(jnp.float32) * scales[:, :, None]
    )
    token_state = (blocks.reshape(tok_rows, features) + embedded.astype(jnp.float32)).astype(
        jnp.bfloat16
    )
    flat_ids = expert_ids.reshape(-1)
    expert_hot = (flat_ids[:, None] == jnp.arange(EXPERTS, dtype=jnp.int32)[None, :]).astype(
        jnp.int32
    )
    expert_rank = jnp.sum((jnp.cumsum(expert_hot, axis=0) - 1) * expert_hot, axis=1)
    slot_of = flat_ids * CAP + expert_rank
    token_index = jnp.arange(tok_rows * TOP, dtype=jnp.int32) // TOP
    source = jnp.full((EXPERTS * CAP,), tok_rows, jnp.int32).at[slot_of].set(token_index)
    padded = jnp.concatenate([token_state, jnp.zeros((1, features), jnp.bfloat16)], axis=0)
    buffer = jnp.take(padded, source, axis=0)
    expert_out = full_path(
        buffer, w_gate, w_up, w_down, device_count, exp_dev, width_split, features
    )
    chosen = jnp.take(expert_out, slot_of, axis=0).reshape(tok_rows, TOP, features)
    mixed = jnp.sum(gate_weights[:, :, None] * chosen.astype(jnp.float32), axis=1).astype(
        jnp.bfloat16
    )
    gate_grads = jnp.einsum("tkd,td->tk", chosen, out_grad, preferred_element_type=jnp.float32)
    return (mixed, gate_grads)


def local(*arrays):
    if lax.axis_size("expert") == 16 and arrays[6].shape[0] * 16 == EXPERTS:
        return near_path(*arrays)
    return far_path(*arrays)


def solution(mesh):
    return jax.shard_map(
        local,
        mesh=mesh,
        in_specs=(
            P(("groups", "expert"), None),
            P(("groups", "expert"), None),
            P(("groups", "expert")),
            P(("groups", "expert"), None),
            P(("groups", "expert"), None),
            P("expert", None),
            P("expert", None, None),
            P("expert", None, None),
            P("expert", None, None),
            P(("groups", "expert"), None),
        ),
        out_specs=(P(("groups", "expert"), None), P(("groups", "expert"), None)),
        check_vma=False,
    )
```

```python
import functools

import jax
import jax.numpy as jnp
from jax import lax
from jax.experimental import pallas as pl
from jax.experimental.pallas import tpu as pltpu
from jax.sharding import PartitionSpec as P

EXPERTS = 64
TOP = 4
CAP = 12
BLOCK = 128
PAIR = 2 * CAP
VMEM = pltpu.VMEM
F32 = jnp.float32
BF16 = jnp.bfloat16


def dot(a, b):
    return jnp.dot(a, b, preferred_element_type=F32)


def iota(shape, dimension):
    return lax.broadcasted_iota(jnp.int32, shape, dimension)


def flags(mask):
    return mask.astype(F32).astype(BF16)


def earlier(length):
    return flags(iota((length, length), 0) < iota((length, length), 1))


def fetch_kernel(me_ref, rows_ref, table_ref, out_ref):
    device_count, _, tok_rows = rows_ref.shape
    held = table_ref.shape[0]
    look_cap = out_ref.shape[0] // device_count
    local = rows_ref[:, 0, :] - me_ref[0] * held
    hit = (local >= 0) & (local < held)
    rank = dot(flags(hit), earlier(tok_rows)).astype(jnp.int32)
    rank = jnp.where(hit, rank, -1)
    slot = iota((look_cap, tok_rows), 0)
    place = iota((look_cap, held), 1)
    picks = []
    for source in range(device_count):
        mine = jnp.where(slot == rank[source : source + 1], local[source : source + 1], 0)
        wanted = jnp.sum(mine, axis=1, keepdims=True)
        picks.append(flags(place == wanted))
    out_ref[...] = dot(jnp.concatenate(picks, axis=0), table_ref[...]).astype(BF16)


def turned(rows):
    count, length = rows.shape
    return jnp.concatenate([rows, jnp.zeros((length - count, length), F32)], axis=0).T


def plan_kernel(
    me_ref,
    rows_ref,
    small_ref,
    other_ref,
    scales_ref,
    _,
    put_ref,
    near_ref,
    far_first_ref,
    far_second_ref,
    near_slots_ref,
    far_slots_ref,
    columns_ref,
):
    tok_rows = rows_ref.shape[1]
    slots = put_ref.shape[1]
    half = near_ref.shape[0] // (2 * PAIR)
    device_count = 2 * half
    exp_dev = EXPERTS // device_count
    look_cap = slots // device_count
    me, held = me_ref[0], me_ref[1]
    flip = me % 2
    start = me // half * half * exp_dev
    before = earlier(tok_rows)

    row = jnp.broadcast_to(rows_ref[...], (device_count, tok_rows))
    low = iota((device_count, tok_rows), 0) * held
    hit = (row >= low) & (row < low + held)
    rank = jnp.where(hit, dot(flags(hit), before).astype(jnp.int32), -1)
    slot = iota((look_cap, tok_rows), 0)
    put = [(slot == rank[o : o + 1]).astype(F32) for o in range(device_count)]
    put_ref[...] = jnp.concatenate(put, axis=0).T.astype(BF16)

    expert = iota((half * exp_dev, tok_rows), 0) + start
    place = iota((PAIR, tok_rows), 0)
    inside = iota((half * exp_dev, tok_rows), 0)
    flipped = ((inside + flip) & 1) * CAP
    device = inside // exp_dev
    chunk = (inside % exp_dev) // 2
    for far, ref in enumerate((small_ref, other_ref)):
        ids = [ref[k : k + 1, :].astype(jnp.int32) for k in range(TOP)]
        chosen = [ids[k] == expert for k in range(TOP)]
        hit = functools.reduce(jnp.logical_or, chosen)
        rank = jnp.where(hit, dot(flags(hit), before).astype(jnp.int32), -1000)
        lines = [[], []]
        for d in range(half):
            for c in range(2):
                at = d * exp_dev + 2 * c
                one, two = rank[at : at + 1], rank[at + 1 : at + 2]
                upper = jnp.where(flip == 0, one, two)
                lower = jnp.where(flip == 0, two, one) + CAP
                here = ((place < CAP) & (place == upper)) | ((place >= CAP) & (place == lower))
                lines[c].append(here.astype(F32))
        if far:
            far_first_ref[...] = jnp.concatenate(lines[0], axis=0).astype(BF16)
            far_second_ref[...] = jnp.concatenate(lines[1], axis=0).astype(BF16)
            slot = chunk * (half * PAIR) + device * PAIR + flipped + rank
        else:
            both = [line for pair in zip(*lines) for line in pair]
            near_ref[...] = jnp.concatenate(both, axis=0).astype(BF16)
            slot = device * (2 * PAIR) + chunk * PAIR + flipped + rank
        found = [
            jnp.sum(jnp.where(chosen[k], slot + 1, 0), axis=0, keepdims=True) - 1
            for k in range(TOP)
        ]
        slots_out = far_slots_ref if far else near_slots_ref
        found = turned(jnp.concatenate(found, axis=0).astype(F32))
        slots_out[...] = found.astype(jnp.int32)
    columns_ref[...] = turned(
        jnp.concatenate(
            [small_ref[TOP:, :], other_ref[TOP:, :], scales_ref[...]], axis=0
        )
    )


def state_kernel(put_ref, pick_ref, returned_ref, values_ref, columns_ref, state_ref, out_ref):
    features = values_ref.shape[1]
    width = 512
    for left in range(0, features, width):
        found = dot(put_ref[...], returned_ref[:, left : left + width])
        for b in range(width // BLOCK):
            at = left + b * BLOCK
            scaled = (
                values_ref[:, at : at + BLOCK].astype(F32)
                * columns_ref[:, 2 * TOP + at // BLOCK : 2 * TOP + at // BLOCK + 1]
            )
            state_ref[:, at : at + BLOCK] = (
                scaled + found[:, b * BLOCK : (b + 1) * BLOCK]
            ).astype(BF16)
        cols = slice(left, left + width)
        out_ref[:, cols] = dot(pick_ref[...], state_ref[:, cols]).astype(BF16)


def pick_kernel(pick_ref, state_ref, _, out_ref):
    features = state_ref.shape[1]
    width = 512
    for left in range(0, features, width):
        cols = slice(left, left + width)
        out_ref[:, cols] = dot(pick_ref[...], state_ref[:, cols]).astype(BF16)


def expert_kernel(chunk, near_ref, far_ref, *refs):
    if chunk:
        early_ref, refs = refs[0], refs[1:]
    wg_hbm, wu_hbm, wd_hbm, near_out_ref, far_out_ref = refs[:5]
    x_ref, wg_ref, wu_ref, wd_ref, hidden_ref, result_ref, sem = refs[5:]
    count, features, width = wg_ref.shape
    half = far_ref.shape[0]
    first_held = count * chunk
    up_cuts = ((0, 512), (512, 512), (1024, width - 1024))
    down_cuts = tuple((at, 512) for at in range(0, features, 512))

    def weight_copies(j):
        copies = []
        for at, size in up_cuts:
            for hbm, ref in ((wg_hbm, wg_ref), (wu_hbm, wu_ref)):
                cols = pl.ds(at, size)
                copies.append((hbm.at[first_held + j, :, cols], ref.at[j, :, cols]))
        for at, size in down_cuts:
            cols = pl.ds(at, size)
            copies.append((wd_hbm.at[first_held + j, :, cols], wd_ref.at[j, :, cols]))
        return [
            pltpu.make_async_copy(src, dst, sem.at[j, n]) for n, (src, dst) in enumerate(copies)
        ]

    for j in range(count):
        for copy in weight_copies(j):
            copy.start()

    low = iota((PAIR, features), 0) < CAP
    for quad in range(half // 2):
        ones, twos = [], []
        for pair in range(2):
            source = 4 * quad + 2 * pair
            if source < half:
                rows = slice(chunk * PAIR, (chunk + 1) * PAIR)
                even = near_ref[source, rows, :].astype(F32)
                odd = near_ref[source + 1, rows, :].astype(F32)
            else:
                even = far_ref[source - half].astype(F32)
                odd = far_ref[source + 1 - half].astype(F32)
            ones.append(jnp.where(low, even, odd))
            twos.append(jnp.where(low, odd, even))
        rows = slice(quad * 2 * PAIR, (quad + 1) * 2 * PAIR)
        x_ref[0, rows, :] = jnp.concatenate(ones, axis=0).astype(BF16)
        x_ref[1, rows, :] = jnp.concatenate(twos, axis=0).astype(BF16)

    @pl.loop(0, count)
    def _(j):
        copies = weight_copies(j)
        n = 0
        for at, size in up_cuts:
            copies[n].wait()
            copies[n + 1].wait()
            n += 2
            x = x_ref[j]
            gate = dot(x, wg_ref[j, :, at : at + size])
            up = dot(x, wu_ref[j, :, at : at + size])
            hidden_ref[:, at : at + size] = (gate / (1.0 + jnp.exp(-gate)) * up).astype(BF16)
        for at, size in down_cuts:
            copies[n].wait()
            n += 1
            result_ref[j, :, at : at + size] = dot(hidden_ref[...], wd_ref[j, :, at : at + size])

    for pair in range(half):
        one = result_ref[0, pair * PAIR : (pair + 1) * PAIR, :]
        two = result_ref[1, pair * PAIR : (pair + 1) * PAIR, :]
        even = jnp.where(low, one, two)
        odd = jnp.where(low, two, one)
        source = 2 * pair
        if source >= half:
            far_out_ref[source - half] = even.astype(BF16)
            far_out_ref[source + 1 - half] = odd.astype(BF16)
        elif chunk:
            for n, value in enumerate((even, odd)):
                both = jnp.concatenate([early_ref[source + n].astype(F32), value], axis=0)
                near_out_ref[source + n] = both.astype(BF16)
        else:
            near_out_ref[source] = even.astype(BF16)
            near_out_ref[source + 1] = odd.astype(BF16)


def expert_call(chunk, near, far, early, w_gate, w_up, w_down):
    exp_dev, features, width = w_gate.shape
    half = far.shape[0]
    count = 2
    rows = 2 * half * CAP
    anywhere = pl.BlockSpec(memory_space=pl.ANY)
    vmem = pl.BlockSpec(memory_space=VMEM)
    return pl.pallas_call(
        functools.partial(expert_kernel, chunk),
        out_shape=(
            jax.ShapeDtypeStruct((half, (1 + chunk) * PAIR, features), BF16),
            jax.ShapeDtypeStruct((half, PAIR, features), BF16),
        ),
        in_specs=[vmem] * (2 + len(early)) + [anywhere] * 3,
        out_specs=(vmem, vmem),
        scratch_shapes=[
            VMEM((count, rows, features), BF16),
            VMEM((count, features, width), BF16),
            VMEM((count, features, width), BF16),
            VMEM((count, width, features), BF16),
            VMEM((rows, width), BF16),
            VMEM((count, rows, features), F32),
            pltpu.SemaphoreType.DMA((count, 10)),
        ],
        compiler_params=pltpu.CompilerParams(vmem_limit_bytes=54 * 1024 * 1024),
        cost_estimate=pl.CostEstimate(
            flops=6 * count * rows * features * width,
            bytes_accessed=6 * count * features * width,
            transcendentals=count * rows * width,
        ),
        name="experts_second" if chunk else "experts_first",
    )(near, far, *early, w_gate, w_up, w_down)


def mix(slots_ref, columns_ref, first_column, parts, grad_ref, mixed_ref, far_ref):
    tok_rows, features = grad_ref.shape
    picked = [jnp.zeros((tok_rows, 1), F32) for _ in range(TOP)]
    spread = []
    start = 0
    for ref in parts:
        count = ref.shape[0]
        column = iota((tok_rows, count), 1) + start
        start += count
        inner = lax.dot_general(
            grad_ref[...], ref[...], (((1,), (1,)), ((), ())), preferred_element_type=F32
        )
        total = jnp.zeros((tok_rows, count), F32)
        for k in range(TOP):
            here = column == slots_ref[:, k : k + 1]
            weight = columns_ref[:, first_column + k : first_column + k + 1]
            total = total + jnp.where(here, weight, 0.0)
            picked[k] = picked[k] + jnp.sum(jnp.where(here, inner, 0.0), axis=1, keepdims=True)
        high = total.astype(BF16)
        spread.append((high, (total - high.astype(F32)).astype(BF16)))
    width = 512
    for at in range(0, features, width):
        cols = slice(at, at + width)
        value = 0.0 if far_ref is None else far_ref[:, cols].astype(F32)
        for (high, rest), ref in zip(spread, parts):
            rows = ref[:, cols]
            value = value + dot(high, rows) + dot(rest, rows)
        mixed_ref[:, cols] = value.astype(BF16)
    column = iota((tok_rows, tok_rows), 1)
    wide = jnp.zeros((tok_rows, tok_rows), F32)
    for k in range(TOP):
        wide = wide + jnp.where(column == k, picked[k], 0.0)
    return wide.T


def far_kernel(slots_ref, columns_ref, first_ref, second_ref, grad_ref, mixed_ref, grads_ref):
    turned_grads = mix(
        slots_ref, columns_ref, TOP, (first_ref, second_ref), grad_ref, mixed_ref, None
    )
    grads_ref[...] = turned_grads[: grads_ref.shape[0], :]


def near_kernel(
    slots_ref, columns_ref, back_ref, grad_ref, far_ref, far_grads_ref, mixed_ref, grads_ref
):
    turned_grads = mix(slots_ref, columns_ref, 0, (back_ref,), grad_ref, mixed_ref, far_ref)
    grads_ref[...] = turned_grads[:TOP, :] + far_grads_ref[:TOP, :]


def swap(array, groups=None):
    return lax.all_to_all(
        array, "expert", split_axis=0, concat_axis=0, tiled=True, axis_index_groups=groups
    )


def near_path(
    block_values,
    block_exps,
    row_ids,
    expert_ids,
    gate_weights,
    table,
    w_gate,
    w_up,
    w_down,
    out_grad,
):
    device_count = lax.axis_size("expert")
    half = device_count // 2
    halves = [list(range(half)), list(range(half, device_count))]
    me = lax.axis_index("expert").astype(jnp.int32)
    tok_rows, features = block_values.shape
    rows_held = table.shape[0]
    look_cap = max(2, 2 * tok_rows // device_count)
    near_slots, far_slots = half * 2 * PAIR, half * PAIR
    vmem = pl.BlockSpec(memory_space=VMEM)
    smem = pl.BlockSpec(memory_space=pltpu.SMEM)
    anywhere = pl.BlockSpec(memory_space=pl.ANY)
    place = jnp.stack([me, jnp.int32(rows_held)])

    def shape(dims, kind):
        return jax.ShapeDtypeStruct(dims, kind)

    def mirrored(array):
        pairs = [(i, (i + half) % device_count) for i in range(device_count)]
        return lax.ppermute(array, "expert", pairs)

    def ordered(array, earlier_array):
        return pl.pallas_call(
            lambda array_ref, earlier_ref, out_ref: None,
            out_shape=shape(array.shape, array.dtype),
            in_specs=[anywhere, anywhere],
            out_specs=anywhere,
            input_output_aliases={0: 0},
            name="ordered",
        )(array, earlier_array)

    def picked(pick, states, earlier_array, name):
        return pl.pallas_call(
            pick_kernel,
            out_shape=shape((pick.shape[0], features), BF16),
            in_specs=[vmem, vmem, anywhere],
            out_specs=vmem,
            name=name,
        )(pick, states, earlier_array)

    small = jnp.concatenate([expert_ids.T.astype(F32), gate_weights.T], axis=0)
    other = mirrored(small)
    other_grad = mirrored(out_grad)
    all_rows = swap(jnp.broadcast_to(row_ids[None, None, :], (device_count, 1, tok_rows)))
    fetched = pl.pallas_call(
        fetch_kernel,
        out_shape=shape((device_count * look_cap, features), BF16),
        in_specs=[smem, vmem, vmem],
        out_specs=vmem,
        name="fetch_rows",
    )(place, all_rows, table)
    returned = swap(fetched.reshape(device_count, look_cap, features))
    put, near_pick, far_first_pick, far_second_pick, near_of, far_of, columns = pl.pallas_call(
        plan_kernel,
        out_shape=(
            shape((tok_rows, device_count * look_cap), BF16),
            shape((near_slots, tok_rows), BF16),
            shape((far_slots, tok_rows), BF16),
            shape((far_slots, tok_rows), BF16),
            shape((tok_rows, tok_rows), jnp.int32),
            shape((tok_rows, tok_rows), jnp.int32),
            shape((tok_rows, tok_rows), F32),
        ),
        in_specs=[smem, vmem, vmem, vmem, vmem, anywhere],
        out_specs=(vmem,) * 7,
        name="plan",
    )(place, row_ids[None, :], small, other, jnp.exp2(block_exps.T.astype(F32)), fetched)
    state, near_sent = pl.pallas_call(
        state_kernel,
        out_shape=(shape((tok_rows, features), BF16), shape((near_slots, features), BF16)),
        in_specs=[vmem] * 5,
        out_specs=(vmem, vmem),
        name="token_state",
    )(put, near_pick, returned.reshape(device_count * look_cap, features), block_values, columns)
    other_state = mirrored(state)
    near_rows = swap(near_sent.reshape(half, 2 * PAIR, features), halves)
    far_sent = picked(far_first_pick, other_state, near_rows, "far_first")
    far_rows = swap(far_sent.reshape(half, PAIR, features), halves)
    far_later_sent = picked(far_second_pick, other_state, far_rows, "far_second")
    far_later_rows = swap(far_later_sent.reshape(half, PAIR, features), halves)

    weights = (w_gate, w_up, w_down)
    near_out, far_out = expert_call(0, near_rows, far_rows, (), *weights)
    far_back = swap(far_out, halves)
    near_out, far_later_out = expert_call(1, near_rows, far_later_rows, (near_out,), *weights)
    far_later_back = swap(ordered(far_later_out, far_back), halves)
    near_back = swap(ordered(near_out, far_later_back), halves)

    far_mixed, far_grads = pl.pallas_call(
        far_kernel,
        out_shape=(shape((tok_rows, features), BF16), shape((2 * TOP, tok_rows), F32)),
        in_specs=[vmem] * 5,
        out_specs=(vmem, vmem),
        name="mix_far",
    )(
        far_of,
        columns,
        far_back.reshape(far_slots, features),
        far_later_back.reshape(far_slots, features),
        other_grad,
    )
    mixed, grads = pl.pallas_call(
        near_kernel,
        out_shape=(shape((tok_rows, features), BF16), shape((TOP, tok_rows), F32)),
        in_specs=[vmem] * 6,
        out_specs=(vmem, vmem),
        name="mix_near",
    )(
        near_of,
        columns,
        near_back.reshape(near_slots, features),
        out_grad,
        mirrored(far_mixed),
        mirrored(far_grads),
    )
    return mixed, grads.T


def expert_work(arrived, w_gate, w_up, w_down):
    gate_act = jnp.einsum("sjcd,jdf->sjcf", arrived, w_gate, preferred_element_type=jnp.float32)
    up_act = jnp.einsum("sjcd,jdf->sjcf", arrived, w_up, preferred_element_type=jnp.float32)
    hidden = (jax.nn.silu(gate_act) * up_act).astype(jnp.bfloat16)
    return jnp.einsum("sjcf,jfd->sjcd", hidden, w_down, preferred_element_type=jnp.float32).astype(
        jnp.bfloat16
    )


def full_path(buffer, w_gate, w_up, w_down, device_count, exp_dev, width_split, features):
    group_count = EXPERTS // exp_dev
    grouped = buffer.reshape(group_count, 1, exp_dev, CAP, features)
    outgoing = jnp.broadcast_to(
        grouped, (group_count, width_split, exp_dev, CAP, features)
    ).reshape(device_count, exp_dev, CAP, features)
    returned_out = lax.all_to_all(
        expert_work(
            lax.all_to_all(outgoing, "expert", split_axis=0, concat_axis=0, tiled=True),
            w_gate,
            w_up,
            w_down,
        ),
        "expert",
        split_axis=0,
        concat_axis=0,
        tiled=True,
    )
    pieces = returned_out.reshape(group_count, width_split, exp_dev, CAP, features).astype(
        jnp.float32
    )
    return jnp.sum(pieces, axis=1).astype(jnp.bfloat16).reshape(EXPERTS * CAP, features)


def far_path(
    block_values,
    block_exps,
    row_ids,
    expert_ids,
    gate_weights,
    table,
    w_gate,
    w_up,
    w_down,
    out_grad,
):
    device_count = lax.axis_size("expert")
    tok_rows = block_values.shape[0]
    features = block_values.shape[1]
    rows_held = table.shape[0]
    look_cap = max(2, 2 * tok_rows // device_count)
    exp_dev = w_gate.shape[0]
    width_split = device_count * exp_dev // EXPERTS
    owners = row_ids // rows_held
    local_row = row_ids % rows_held
    owner_hot = (owners[:, None] == jnp.arange(device_count, dtype=jnp.int32)[None, :]).astype(
        jnp.int32
    )
    owner_rank = jnp.sum((jnp.cumsum(owner_hot, axis=0) - 1) * owner_hot, axis=1)
    placed = owners * look_cap + owner_rank
    wanted = jnp.zeros((device_count * look_cap,), jnp.int32).at[placed].set(local_row)
    requested = lax.all_to_all(
        wanted.reshape(device_count, look_cap), "expert", split_axis=0, concat_axis=0, tiled=True
    )
    fetched = jnp.take(table, requested.reshape(-1), axis=0).reshape(
        device_count, look_cap, features
    )
    rows_returned = lax.all_to_all(fetched, "expert", split_axis=0, concat_axis=0, tiled=True)
    embedded = jnp.take(rows_returned.reshape(device_count * look_cap, features), placed, axis=0)
    scales = jnp.exp2(block_exps.astype(jnp.float32))
    blocks = (
        block_values.reshape(tok_rows, scales.shape[1], -1).astype(jnp.float32) * scales[:, :, None]
    )
    token_state = (blocks.reshape(tok_rows, features) + embedded.astype(jnp.float32)).astype(
        jnp.bfloat16
    )
    flat_ids = expert_ids.reshape(-1)
    expert_hot = (flat_ids[:, None] == jnp.arange(EXPERTS, dtype=jnp.int32)[None, :]).astype(
        jnp.int32
    )
    expert_rank = jnp.sum((jnp.cumsum(expert_hot, axis=0) - 1) * expert_hot, axis=1)
    slot_of = flat_ids * CAP + expert_rank
    token_index = jnp.arange(tok_rows * TOP, dtype=jnp.int32) // TOP
    source = jnp.full((EXPERTS * CAP,), tok_rows, jnp.int32).at[slot_of].set(token_index)
    padded = jnp.concatenate([token_state, jnp.zeros((1, features), jnp.bfloat16)], axis=0)
    buffer = jnp.take(padded, source, axis=0)
    expert_out = full_path(
        buffer, w_gate, w_up, w_down, device_count, exp_dev, width_split, features
    )
    chosen = jnp.take(expert_out, slot_of, axis=0).reshape(tok_rows, TOP, features)
    mixed = jnp.sum(gate_weights[:, :, None] * chosen.astype(jnp.float32), axis=1).astype(
        jnp.bfloat16
    )
    gate_grads = jnp.einsum("tkd,td->tk", chosen, out_grad, preferred_element_type=jnp.float32)
    return (mixed, gate_grads)


def local(*arrays):
    if lax.axis_size("expert") == 16 and arrays[6].shape[0] * 16 == EXPERTS:
        return near_path(*arrays)
    return far_path(*arrays)


def solution(mesh):
    return jax.shard_map(
        local,
        mesh=mesh,
        in_specs=(
            P(("groups", "expert"), None),
            P(("groups", "expert"), None),
            P(("groups", "expert")),
            P(("groups", "expert"), None),
            P(("groups", "expert"), None),
            P("expert", None),
            P("expert", None, None),
            P("expert", None, None),
            P("expert", None, None),
            P(("groups", "expert"), None),
        ),
        out_specs=(P(("groups", "expert"), None), P(("groups", "expert"), None)),
        check_vma=False,
    )
```

```python
import functools

import jax
import jax.numpy as jnp
from jax import lax
from jax.experimental import pallas as pl
from jax.experimental.pallas import tpu as pltpu
from jax.sharding import PartitionSpec as P

EXPERTS = 64
TOP = 4
CAP = 12
BLOCK = 128
PAIR = 2 * CAP
VMEM = pltpu.VMEM
F32 = jnp.float32
BF16 = jnp.bfloat16


def dot(a, b):
    return jnp.dot(a, b, preferred_element_type=F32)


def iota(shape, dimension):
    return lax.broadcasted_iota(jnp.int32, shape, dimension)


def flags(mask):
    return mask.astype(F32).astype(BF16)


def earlier(length):
    return flags(iota((length, length), 0) < iota((length, length), 1))


def fetch_kernel(me_ref, rows_ref, table_ref, _, out_ref):
    device_count, _, tok_rows = rows_ref.shape
    held = table_ref.shape[0]
    look_cap = out_ref.shape[0] // device_count
    local = rows_ref[:, 0, :] - me_ref[0] * held
    hit = (local >= 0) & (local < held)
    rank = dot(flags(hit), earlier(tok_rows)).astype(jnp.int32)
    rank = jnp.where(hit, rank, -1)
    slot = iota((look_cap, tok_rows), 0)
    place = iota((look_cap, held), 1)
    picks = []
    for source in range(device_count):
        mine = jnp.where(slot == rank[source : source + 1], local[source : source + 1], 0)
        wanted = jnp.sum(mine, axis=1, keepdims=True)
        picks.append(flags(place == wanted))
    out_ref[...] = dot(jnp.concatenate(picks, axis=0), table_ref[...]).astype(BF16)


def turned(rows):
    count, length = rows.shape
    return jnp.concatenate([rows, jnp.zeros((length - count, length), F32)], axis=0).T


def plan_kernel(
    me_ref,
    rows_ref,
    small_ref,
    other_ref,
    scales_ref,
    _,
    put_ref,
    near_ref,
    far_ref,
    near_slots_ref,
    far_slots_ref,
    columns_ref,
):
    tok_rows = rows_ref.shape[1]
    slots = put_ref.shape[1]
    half = near_ref.shape[0] // (2 * PAIR)
    device_count = 2 * half
    exp_dev = EXPERTS // device_count
    look_cap = slots // device_count
    me, held = me_ref[0], me_ref[1]
    flip = me % 2
    start = me // half * half * exp_dev
    before = earlier(tok_rows)

    row = jnp.broadcast_to(rows_ref[...], (device_count, tok_rows))
    low = iota((device_count, tok_rows), 0) * held
    hit = (row >= low) & (row < low + held)
    rank = jnp.where(hit, dot(flags(hit), before).astype(jnp.int32), -1)
    slot = iota((look_cap, tok_rows), 0)
    put = [(slot == rank[o : o + 1]).astype(F32) for o in range(device_count)]
    put_ref[...] = jnp.concatenate(put, axis=0).T.astype(BF16)

    expert = iota((half * exp_dev, tok_rows), 0) + start
    place = iota((PAIR, tok_rows), 0)
    inside = iota((half * exp_dev, tok_rows), 0)
    flipped = ((inside + flip) & 1) * CAP
    device = inside // exp_dev
    chunk = (inside % exp_dev) // 2
    for far, ref in enumerate((small_ref, other_ref)):
        ids = [ref[k : k + 1, :].astype(jnp.int32) for k in range(TOP)]
        chosen = [ids[k] == expert for k in range(TOP)]
        hit = functools.reduce(jnp.logical_or, chosen)
        rank = jnp.where(hit, dot(flags(hit), before).astype(jnp.int32), -1000)
        lines = [[], []]
        for d in range(half):
            for c in range(2):
                at = d * exp_dev + 2 * c
                one, two = rank[at : at + 1], rank[at + 1 : at + 2]
                upper = jnp.where(flip == 0, one, two)
                lower = jnp.where(flip == 0, two, one) + CAP
                here = ((place < CAP) & (place == upper)) | ((place >= CAP) & (place == lower))
                lines[c].append(here.astype(F32))
        both = [line for pair in zip(*lines) for line in pair]
        pick_ref = far_ref if far else near_ref
        pick_ref[...] = jnp.concatenate(both, axis=0).astype(BF16)
        if far:
            slot = chunk * (half * PAIR) + device * PAIR + flipped + rank
        else:
            slot = device * (2 * PAIR) + chunk * PAIR + flipped + rank
        found = [
            jnp.sum(jnp.where(chosen[k], slot + 1, 0), axis=0, keepdims=True) - 1
            for k in range(TOP)
        ]
        slots_out = far_slots_ref if far else near_slots_ref
        found = turned(jnp.concatenate(found, axis=0).astype(F32))
        slots_out[...] = found.astype(jnp.int32)
    columns_ref[...] = turned(
        jnp.concatenate(
            [small_ref[TOP:, :], other_ref[TOP:, :], scales_ref[...]], axis=0
        )
    )


def state_kernel(put_ref, returned_ref, values_ref, columns_ref, state_ref):
    features = values_ref.shape[1]
    width = 512
    for left in range(0, features, width):
        found = dot(put_ref[...], returned_ref[:, left : left + width])
        for b in range(width // BLOCK):
            at = left + b * BLOCK
            scaled = (
                values_ref[:, at : at + BLOCK].astype(F32)
                * columns_ref[:, 2 * TOP + at // BLOCK : 2 * TOP + at // BLOCK + 1]
            )
            state_ref[:, at : at + BLOCK] = (
                scaled + found[:, b * BLOCK : (b + 1) * BLOCK]
            ).astype(BF16)


def pick_kernel(pick_ref, state_ref, *refs):
    out_ref = refs[-1]
    features = state_ref.shape[1]
    width = 512
    for left in range(0, features, width):
        cols = slice(left, left + width)
        out_ref[:, cols] = dot(pick_ref[...], state_ref[:, cols]).astype(BF16)


def expert_kernel(chunk, join, after, rows_ref, *refs):
    if join:
        early_ref, refs = refs[0], refs[1:]
    wg_hbm, wu_hbm, wd_hbm, out_ref = refs[after : after + 4]
    x_ref, wg_ref, wu_ref, wd_ref, hidden_ref, result_ref, sem = refs[after + 4 :]
    count, features, width = wg_ref.shape
    half = rows_ref.shape[0]
    first_held = count * chunk
    up_cuts = ((0, 512), (512, 512), (1024, width - 1024))
    down_cuts = tuple((at, 512) for at in range(0, features, 512))

    def weight_copies(j):
        copies = []
        for at, size in up_cuts:
            for hbm, ref in ((wg_hbm, wg_ref), (wu_hbm, wu_ref)):
                cols = pl.ds(at, size)
                copies.append((hbm.at[first_held + j, :, cols], ref.at[j, :, cols]))
        for at, size in down_cuts:
            cols = pl.ds(at, size)
            copies.append((wd_hbm.at[first_held + j, :, cols], wd_ref.at[j, :, cols]))
        return [
            pltpu.make_async_copy(src, dst, sem.at[j, n]) for n, (src, dst) in enumerate(copies)
        ]

    for j in range(count):
        for copy in weight_copies(j):
            copy.start()

    low = iota((PAIR, features), 0) < CAP
    here = slice(chunk * PAIR, (chunk + 1) * PAIR)
    for quad in range(half // 4):
        ones, twos = [], []
        for pair in range(2):
            source = 4 * quad + 2 * pair
            even = rows_ref[source, here, :].astype(F32)
            odd = rows_ref[source + 1, here, :].astype(F32)
            ones.append(jnp.where(low, even, odd))
            twos.append(jnp.where(low, odd, even))
        rows = slice(quad * 2 * PAIR, (quad + 1) * 2 * PAIR)
        x_ref[0, rows, :] = jnp.concatenate(ones, axis=0).astype(BF16)
        x_ref[1, rows, :] = jnp.concatenate(twos, axis=0).astype(BF16)

    @pl.loop(0, count)
    def _(j):
        copies = weight_copies(j)
        n = 0
        for at, size in up_cuts:
            copies[n].wait()
            copies[n + 1].wait()
            n += 2
            x = x_ref[j]
            gate = dot(x, wg_ref[j, :, at : at + size])
            up = dot(x, wu_ref[j, :, at : at + size])
            hidden_ref[:, at : at + size] = (gate / (1.0 + jnp.exp(-gate)) * up).astype(BF16)
        for at, size in down_cuts:
            copies[n].wait()
            n += 1
            result_ref[j, :, at : at + size] = dot(hidden_ref[...], wd_ref[j, :, at : at + size])

    for pair in range(half // 2):
        one = result_ref[0, pair * PAIR : (pair + 1) * PAIR, :]
        two = result_ref[1, pair * PAIR : (pair + 1) * PAIR, :]
        for source, value in (
            (2 * pair, jnp.where(low, one, two)),
            (2 * pair + 1, jnp.where(low, two, one)),
        ):
            if join:
                value = jnp.concatenate([early_ref[source].astype(F32), value], axis=0)
            out_ref[source] = value.astype(BF16)


def expert_call(name, chunk, rows_in, weights, early=(), after=()):
    w_gate, w_up, w_down = weights
    exp_dev, features, width = w_gate.shape
    half = rows_in.shape[0]
    count = 2
    rows = half * CAP
    anywhere = pl.BlockSpec(memory_space=pl.ANY)
    vmem = pl.BlockSpec(memory_space=VMEM)
    return pl.pallas_call(
        functools.partial(expert_kernel, chunk, bool(early), len(after)),
        out_shape=jax.ShapeDtypeStruct((half, (1 + len(early)) * PAIR, features), BF16),
        in_specs=[vmem] * (1 + len(early)) + [anywhere] * (3 + len(after)),
        out_specs=vmem,
        scratch_shapes=[
            VMEM((count, rows, features), BF16),
            VMEM((count, features, width), BF16),
            VMEM((count, features, width), BF16),
            VMEM((count, width, features), BF16),
            VMEM((rows, width), BF16),
            VMEM((count, rows, features), F32),
            pltpu.SemaphoreType.DMA((count, 10)),
        ],
        compiler_params=pltpu.CompilerParams(vmem_limit_bytes=48 * 1024 * 1024),
        cost_estimate=pl.CostEstimate(
            flops=12 * count * rows * features * width,
            bytes_accessed=6 * count * features * width,
            transcendentals=count * rows * width,
        ),
        name=name,
    )(rows_in, *early, *after, w_gate, w_up, w_down)


def mix(slots_ref, columns_ref, first_column, parts, grad_ref, mixed_ref, far_ref):
    tok_rows, features = grad_ref.shape
    picked = [jnp.zeros((tok_rows, 1), F32) for _ in range(TOP)]
    spread = []
    start = 0
    for ref in parts:
        count = ref.shape[0]
        column = iota((tok_rows, count), 1) + start
        start += count
        inner = lax.dot_general(
            grad_ref[...], ref[...], (((1,), (1,)), ((), ())), preferred_element_type=F32
        )
        total = jnp.zeros((tok_rows, count), F32)
        for k in range(TOP):
            here = column == slots_ref[:, k : k + 1]
            weight = columns_ref[:, first_column + k : first_column + k + 1]
            total = total + jnp.where(here, weight, 0.0)
            picked[k] = picked[k] + jnp.sum(jnp.where(here, inner, 0.0), axis=1, keepdims=True)
        high = total.astype(BF16)
        spread.append((high, (total - high.astype(F32)).astype(BF16)))
    width = 512
    for at in range(0, features, width):
        cols = slice(at, at + width)
        value = 0.0 if far_ref is None else far_ref[:, cols].astype(F32)
        for (high, rest), ref in zip(spread, parts):
            rows = ref[:, cols]
            value = value + dot(high, rows) + dot(rest, rows)
        mixed_ref[:, cols] = value.astype(BF16)
    column = iota((tok_rows, tok_rows), 1)
    wide = jnp.zeros((tok_rows, tok_rows), F32)
    for k in range(TOP):
        wide = wide + jnp.where(column == k, picked[k], 0.0)
    return wide.T


def far_kernel(slots_ref, columns_ref, first_ref, second_ref, grad_ref, mixed_ref, grads_ref):
    turned_grads = mix(
        slots_ref, columns_ref, TOP, (first_ref, second_ref), grad_ref, mixed_ref, None
    )
    grads_ref[...] = turned_grads[: grads_ref.shape[0], :]


def near_kernel(
    slots_ref, columns_ref, back_ref, grad_ref, far_ref, far_grads_ref, mixed_ref, grads_ref
):
    turned_grads = mix(slots_ref, columns_ref, 0, (back_ref,), grad_ref, mixed_ref, far_ref)
    grads_ref[...] = turned_grads[:TOP, :] + far_grads_ref[:TOP, :]


def swap(array, groups=None):
    return lax.all_to_all(
        array, "expert", split_axis=0, concat_axis=0, tiled=True, axis_index_groups=groups
    )


def near_path(
    block_values,
    block_exps,
    row_ids,
    expert_ids,
    gate_weights,
    table,
    w_gate,
    w_up,
    w_down,
    out_grad,
):
    device_count = lax.axis_size("expert")
    half = device_count // 2
    halves = [list(range(half)), list(range(half, device_count))]
    me = lax.axis_index("expert").astype(jnp.int32)
    tok_rows, features = block_values.shape
    rows_held = table.shape[0]
    look_cap = max(2, 2 * tok_rows // device_count)
    near_slots, far_slots = half * 2 * PAIR, half * PAIR
    vmem = pl.BlockSpec(memory_space=VMEM)
    smem = pl.BlockSpec(memory_space=pltpu.SMEM)
    anywhere = pl.BlockSpec(memory_space=pl.ANY)
    place = jnp.stack([me, jnp.int32(rows_held)])

    def shape(dims, kind):
        return jax.ShapeDtypeStruct(dims, kind)

    def mirrored(array):
        pairs = [(i, (i + half) % device_count) for i in range(device_count)]
        return lax.ppermute(array, "expert", pairs)

    def ordered(array, earlier_array):
        return pl.pallas_call(
            lambda array_ref, earlier_ref, out_ref: None,
            out_shape=shape(array.shape, array.dtype),
            in_specs=[anywhere, anywhere],
            out_specs=anywhere,
            input_output_aliases={0: 0},
            name="ordered",
        )(array, earlier_array)

    def picked(name, pick, states, *after):
        return pl.pallas_call(
            pick_kernel,
            out_shape=shape((pick.shape[0], features), BF16),
            in_specs=[vmem, vmem] + [anywhere] * len(after),
            out_specs=vmem,
            name=name,
        )(pick, states, *after).reshape(half, 2 * PAIR, features)

    small = jnp.concatenate([expert_ids.T.astype(F32), gate_weights.T], axis=0)
    other = mirrored(small)
    other_grad = mirrored(out_grad)
    all_rows = swap(jnp.broadcast_to(row_ids[None, None, :], (device_count, 1, tok_rows)))
    fetched = pl.pallas_call(
        fetch_kernel,
        out_shape=shape((device_count * look_cap, features), BF16),
        in_specs=[smem, vmem, vmem, anywhere],
        out_specs=vmem,
        name="fetch_rows",
    )(place, all_rows, table, other)
    returned = swap(fetched.reshape(device_count, look_cap, features))
    put, near_pick, far_pick, near_of, far_of, columns = pl.pallas_call(
        plan_kernel,
        out_shape=(
            shape((tok_rows, device_count * look_cap), BF16),
            shape((near_slots, tok_rows), BF16),
            shape((near_slots, tok_rows), BF16),
            shape((tok_rows, tok_rows), jnp.int32),
            shape((tok_rows, tok_rows), jnp.int32),
            shape((tok_rows, tok_rows), F32),
        ),
        in_specs=[smem, vmem, vmem, vmem, vmem, anywhere],
        out_specs=(vmem,) * 6,
        name="plan",
    )(place, row_ids[None, :], small, other, jnp.exp2(block_exps.T.astype(F32)), fetched)
    state = pl.pallas_call(
        state_kernel,
        out_shape=shape((tok_rows, features), BF16),
        in_specs=[vmem] * 4,
        out_specs=vmem,
        name="token_state",
    )(put, returned.reshape(device_count * look_cap, features), block_values, columns)
    other_state = mirrored(state)
    near_rows = swap(picked("near_slots", near_pick, state), halves)
    far_sent = picked("far_slots", far_pick, other_state, near_rows)
    far_rows = swap(far_sent, halves)

    weights = (w_gate, w_up, w_down)
    near_out = expert_call("near_first", 0, near_rows, weights, after=(far_sent,))
    near_out = expert_call("near_second", 1, near_rows, weights, early=(near_out,))
    far_out = expert_call("far_first", 0, far_rows, weights, after=(near_out, other_grad))
    far_back = swap(far_out, halves)
    far_later_out = expert_call("far_second", 1, far_rows, weights, after=(far_out,))
    far_later_back = swap(ordered(far_later_out, far_back), halves)

    far_mixed, far_grads = pl.pallas_call(
        far_kernel,
        out_shape=(shape((tok_rows, features), BF16), shape((2 * TOP, tok_rows), F32)),
        in_specs=[vmem] * 5,
        out_specs=(vmem, vmem),
        name="mix_far",
    )(
        far_of,
        columns,
        far_back.reshape(far_slots, features),
        far_later_back.reshape(far_slots, features),
        other_grad,
    )
    near_back = swap(ordered(near_out, far_mixed), halves)
    mixed, grads = pl.pallas_call(
        near_kernel,
        out_shape=(shape((tok_rows, features), BF16), shape((TOP, tok_rows), F32)),
        in_specs=[vmem] * 6,
        out_specs=(vmem, vmem),
        name="mix_near",
    )(
        near_of,
        columns,
        near_back.reshape(near_slots, features),
        out_grad,
        mirrored(far_mixed),
        mirrored(far_grads),
    )
    return mixed, grads.T


def expert_work(arrived, w_gate, w_up, w_down):
    gate_act = jnp.einsum("sjcd,jdf->sjcf", arrived, w_gate, preferred_element_type=jnp.float32)
    up_act = jnp.einsum("sjcd,jdf->sjcf", arrived, w_up, preferred_element_type=jnp.float32)
    hidden = (jax.nn.silu(gate_act) * up_act).astype(jnp.bfloat16)
    return jnp.einsum("sjcf,jfd->sjcd", hidden, w_down, preferred_element_type=jnp.float32).astype(
        jnp.bfloat16
    )


def full_path(buffer, w_gate, w_up, w_down, device_count, exp_dev, width_split, features):
    group_count = EXPERTS // exp_dev
    grouped = buffer.reshape(group_count, 1, exp_dev, CAP, features)
    outgoing = jnp.broadcast_to(
        grouped, (group_count, width_split, exp_dev, CAP, features)
    ).reshape(device_count, exp_dev, CAP, features)
    returned_out = lax.all_to_all(
        expert_work(
            lax.all_to_all(outgoing, "expert", split_axis=0, concat_axis=0, tiled=True),
            w_gate,
            w_up,
            w_down,
        ),
        "expert",
        split_axis=0,
        concat_axis=0,
        tiled=True,
    )
    pieces = returned_out.reshape(group_count, width_split, exp_dev, CAP, features).astype(
        jnp.float32
    )
    return jnp.sum(pieces, axis=1).astype(jnp.bfloat16).reshape(EXPERTS * CAP, features)


def far_path(
    block_values,
    block_exps,
    row_ids,
    expert_ids,
    gate_weights,
    table,
    w_gate,
    w_up,
    w_down,
    out_grad,
):
    device_count = lax.axis_size("expert")
    tok_rows = block_values.shape[0]
    features = block_values.shape[1]
    rows_held = table.shape[0]
    look_cap = max(2, 2 * tok_rows // device_count)
    exp_dev = w_gate.shape[0]
    width_split = device_count * exp_dev // EXPERTS
    owners = row_ids // rows_held
    local_row = row_ids % rows_held
    owner_hot = (owners[:, None] == jnp.arange(device_count, dtype=jnp.int32)[None, :]).astype(
        jnp.int32
    )
    owner_rank = jnp.sum((jnp.cumsum(owner_hot, axis=0) - 1) * owner_hot, axis=1)
    placed = owners * look_cap + owner_rank
    wanted = jnp.zeros((device_count * look_cap,), jnp.int32).at[placed].set(local_row)
    requested = lax.all_to_all(
        wanted.reshape(device_count, look_cap), "expert", split_axis=0, concat_axis=0, tiled=True
    )
    fetched = jnp.take(table, requested.reshape(-1), axis=0).reshape(
        device_count, look_cap, features
    )
    rows_returned = lax.all_to_all(fetched, "expert", split_axis=0, concat_axis=0, tiled=True)
    embedded = jnp.take(rows_returned.reshape(device_count * look_cap, features), placed, axis=0)
    scales = jnp.exp2(block_exps.astype(jnp.float32))
    blocks = (
        block_values.reshape(tok_rows, scales.shape[1], -1).astype(jnp.float32) * scales[:, :, None]
    )
    token_state = (blocks.reshape(tok_rows, features) + embedded.astype(jnp.float32)).astype(
        jnp.bfloat16
    )
    flat_ids = expert_ids.reshape(-1)
    expert_hot = (flat_ids[:, None] == jnp.arange(EXPERTS, dtype=jnp.int32)[None, :]).astype(
        jnp.int32
    )
    expert_rank = jnp.sum((jnp.cumsum(expert_hot, axis=0) - 1) * expert_hot, axis=1)
    slot_of = flat_ids * CAP + expert_rank
    token_index = jnp.arange(tok_rows * TOP, dtype=jnp.int32) // TOP
    source = jnp.full((EXPERTS * CAP,), tok_rows, jnp.int32).at[slot_of].set(token_index)
    padded = jnp.concatenate([token_state, jnp.zeros((1, features), jnp.bfloat16)], axis=0)
    buffer = jnp.take(padded, source, axis=0)
    expert_out = full_path(
        buffer, w_gate, w_up, w_down, device_count, exp_dev, width_split, features
    )
    chosen = jnp.take(expert_out, slot_of, axis=0).reshape(tok_rows, TOP, features)
    mixed = jnp.sum(gate_weights[:, :, None] * chosen.astype(jnp.float32), axis=1).astype(
        jnp.bfloat16
    )
    gate_grads = jnp.einsum("tkd,td->tk", chosen, out_grad, preferred_element_type=jnp.float32)
    return (mixed, gate_grads)


def local(*arrays):
    if lax.axis_size("expert") == 16 and arrays[6].shape[0] * 16 == EXPERTS:
        return near_path(*arrays)
    return far_path(*arrays)


def solution(mesh):
    return jax.shard_map(
        local,
        mesh=mesh,
        in_specs=(
            P(("groups", "expert"), None),
            P(("groups", "expert"), None),
            P(("groups", "expert")),
            P(("groups", "expert"), None),
            P(("groups", "expert"), None),
            P("expert", None),
            P("expert", None, None),
            P("expert", None, None),
            P("expert", None, None),
            P(("groups", "expert"), None),
        ),
        out_specs=(P(("groups", "expert"), None), P(("groups", "expert"), None)),
        check_vma=False,
    )
```

```python
import functools

import jax
import jax.numpy as jnp
from jax import lax
from jax.experimental import pallas as pl
from jax.experimental.pallas import tpu as pltpu
from jax.sharding import PartitionSpec as P

EXPERTS = 64
TOP = 4
CAP = 12
BLOCK = 128
PAIR = 2 * CAP
VMEM = pltpu.VMEM
F32 = jnp.float32
BF16 = jnp.bfloat16


def dot(a, b):
    return jnp.dot(a, b, preferred_element_type=F32)


def iota(shape, dimension):
    return lax.broadcasted_iota(jnp.int32, shape, dimension)


def flags(mask):
    return mask.astype(F32).astype(BF16)


def earlier(length):
    return flags(iota((length, length), 0) < iota((length, length), 1))


def pack_kernel(rows_ref, ids_ref, weights_ref, out_ref):
    count, lines, tok_rows = out_ref.shape
    packed = jnp.concatenate(
        [
            rows_ref[...].astype(F32),
            ids_ref[...].astype(F32),
            weights_ref[...],
            jnp.zeros((lines - 1 - 2 * TOP, tok_rows), F32),
        ],
        axis=0,
    )
    for n in range(count):
        out_ref[n] = packed


def fetch_kernel(me_ref, packed_ref, table_ref, out_ref):
    device_count, _, tok_rows = packed_ref.shape
    held = table_ref.shape[0]
    look_cap = out_ref.shape[0] // device_count
    local = packed_ref[:, 0, :].astype(jnp.int32) - me_ref[0] * held
    hit = (local >= 0) & (local < held)
    rank = dot(flags(hit), earlier(tok_rows)).astype(jnp.int32)
    rank = jnp.where(hit, rank, -1)
    slot = iota((look_cap, tok_rows), 0)
    place = iota((look_cap, held), 1)
    picks = []
    for source in range(device_count):
        mine = jnp.where(slot == rank[source : source + 1], local[source : source + 1], 0)
        wanted = jnp.sum(mine, axis=1, keepdims=True)
        picks.append(flags(place == wanted))
    out_ref[...] = dot(jnp.concatenate(picks, axis=0), table_ref[...]).astype(BF16)


def turned(rows):
    count, length = rows.shape
    return jnp.concatenate([rows, jnp.zeros((length - count, length), F32)], axis=0).T


def plan_kernel(
    me_ref,
    rows_ref,
    packed_ref,
    scales_ref,
    fetched_ref,
    grad_ref,
    put_ref,
    near_ref,
    far_ref,
    near_slots_ref,
    far_slots_ref,
    columns_ref,
):
    tok_rows = rows_ref.shape[1]
    slots = put_ref.shape[1]
    half = near_ref.shape[0] // (2 * PAIR)
    device_count = 2 * half
    exp_dev = EXPERTS // device_count
    look_cap = slots // device_count
    me, held = me_ref[0], me_ref[1]
    flip = me % 2
    start = me // half * half * exp_dev
    before = earlier(tok_rows)

    row = jnp.broadcast_to(rows_ref[...], (device_count, tok_rows))
    low = iota((device_count, tok_rows), 0) * held
    hit = (row >= low) & (row < low + held)
    rank = jnp.where(hit, dot(flags(hit), before).astype(jnp.int32), -1)
    slot = iota((look_cap, tok_rows), 0)
    put = [(slot == rank[o : o + 1]).astype(F32) for o in range(device_count)]
    put_ref[...] = jnp.concatenate(put, axis=0).T.astype(BF16)

    expert = iota((half * exp_dev, tok_rows), 0) + start
    place = iota((PAIR, tok_rows), 0)
    inside = iota((half * exp_dev, tok_rows), 0)
    flipped = ((inside + flip) & 1) * CAP
    device = inside // exp_dev
    chunk = (inside % exp_dev) // 2
    mine = packed_ref[me]
    other = packed_ref[(me + half) % device_count]
    for far, packed in enumerate((mine, other)):
        ids = [packed[1 + k : 2 + k].astype(jnp.int32) for k in range(TOP)]
        chosen = [ids[k] == expert for k in range(TOP)]
        hit = functools.reduce(jnp.logical_or, chosen)
        rank = jnp.where(hit, dot(flags(hit), before).astype(jnp.int32), -1000)
        lines = [[], []]
        for d in range(half):
            for c in range(2):
                at = d * exp_dev + 2 * c
                one, two = rank[at : at + 1], rank[at + 1 : at + 2]
                upper = jnp.where(flip == 0, one, two)
                lower = jnp.where(flip == 0, two, one) + CAP
                here = ((place < CAP) & (place == upper)) | ((place >= CAP) & (place == lower))
                lines[c].append(here.astype(F32))
        both = [line for pair in zip(*lines) for line in pair]
        pick_ref = far_ref if far else near_ref
        pick_ref[...] = jnp.concatenate(both, axis=0).astype(BF16)
        slot = device * (2 * PAIR) + chunk * PAIR + flipped + rank
        found = [
            jnp.sum(jnp.where(chosen[k], slot + 1, 0), axis=0, keepdims=True) - 1
            for k in range(TOP)
        ]
        slots_out = far_slots_ref if far else near_slots_ref
        found = turned(jnp.concatenate(found, axis=0).astype(F32))
        slots_out[...] = found.astype(jnp.int32)
    columns_ref[...] = turned(
        jnp.concatenate(
            [mine[1 + TOP : 1 + 2 * TOP], other[1 + TOP : 1 + 2 * TOP], scales_ref[...]], axis=0
        )
    )


def state_kernel(put_ref, pick_ref, returned_ref, values_ref, columns_ref, state_ref, out_ref):
    features = values_ref.shape[1]
    width = 512
    for left in range(0, features, width):
        found = dot(put_ref[...], returned_ref[:, left : left + width])
        for b in range(width // BLOCK):
            at = left + b * BLOCK
            scaled = (
                values_ref[:, at : at + BLOCK].astype(F32)
                * columns_ref[:, 2 * TOP + at // BLOCK : 2 * TOP + at // BLOCK + 1]
            )
            state_ref[:, at : at + BLOCK] = (
                scaled + found[:, b * BLOCK : (b + 1) * BLOCK]
            ).astype(BF16)
        cols = slice(left, left + width)
        out_ref[:, cols] = dot(pick_ref[...], state_ref[:, cols]).astype(BF16)


def pick_kernel(pick_ref, state_ref, *refs):
    out_ref = refs[-1]
    features = state_ref.shape[1]
    width = 512
    for left in range(0, features, width):
        cols = slice(left, left + width)
        out_ref[:, cols] = dot(pick_ref[...], state_ref[:, cols]).astype(BF16)


def expert_kernel(after, rows_ref, *refs):
    wg_hbm, wu_hbm, wd_hbm, out_ref = refs[after : after + 4]
    x_ref, wg_ref, wu_ref, wd_ref, hidden_ref, result_ref, sem = refs[after + 4 :]
    exp_dev = wg_hbm.shape[0]
    held, features, width = wg_ref.shape
    half = rows_ref.shape[0]
    up_cuts = ((0, 512), (512, 512), (1024, width - 1024))
    down_cuts = tuple((at, 512) for at in range(0, features, 512))

    def weight_copies(j, place):
        copies = []
        for at, size in up_cuts:
            for hbm, ref in ((wg_hbm, wg_ref), (wu_hbm, wu_ref)):
                cols = pl.ds(at, size)
                copies.append((hbm.at[j, :, cols], ref.at[place, :, cols]))
        for at, size in down_cuts:
            cols = pl.ds(at, size)
            copies.append((wd_hbm.at[j, :, cols], wd_ref.at[place, :, cols]))
        return [
            pltpu.make_async_copy(src, dst, sem.at[place, n])
            for n, (src, dst) in enumerate(copies)
        ]

    for j in range(held):
        for copy in weight_copies(j, j):
            copy.start()

    low = iota((PAIR, features), 0) < CAP
    for chunk in range(exp_dev // 2):
        here = slice(chunk * PAIR, (chunk + 1) * PAIR)
        for quad in range(half // 4):
            ones, twos = [], []
            for pair in range(2):
                source = 4 * quad + 2 * pair
                even = rows_ref[source, here, :].astype(F32)
                odd = rows_ref[source + 1, here, :].astype(F32)
                ones.append(jnp.where(low, even, odd))
                twos.append(jnp.where(low, odd, even))
            rows = slice(quad * 2 * PAIR, (quad + 1) * 2 * PAIR)
            x_ref[2 * chunk, rows, :] = jnp.concatenate(ones, axis=0).astype(BF16)
            x_ref[2 * chunk + 1, rows, :] = jnp.concatenate(twos, axis=0).astype(BF16)

    @pl.loop(0, exp_dev)
    def _(j):
        place = j % held
        copies = weight_copies(j, place)
        later = weight_copies(jnp.minimum(j + held, exp_dev - 1), place)

        def refill(first, count):
            @pl.when(j + held < exp_dev)
            def _():
                for n in range(first, first + count):
                    later[n].start()

        n = 0
        for at, size in up_cuts:
            copies[n].wait()
            copies[n + 1].wait()
            x = x_ref[j]
            gate = dot(x, wg_ref[place, :, at : at + size])
            up = dot(x, wu_ref[place, :, at : at + size])
            hidden_ref[:, at : at + size] = (gate / (1.0 + jnp.exp(-gate)) * up).astype(BF16)
            refill(n, 2)
            n += 2
        for at, size in down_cuts:
            copies[n].wait()
            result_ref[j, :, at : at + size] = dot(
                hidden_ref[...], wd_ref[place, :, at : at + size]
            )
            refill(n, 1)
            n += 1

    for pair in range(half // 2):
        rows = slice(pair * PAIR, (pair + 1) * PAIR)
        values = [result_ref[j, rows, :] for j in range(exp_dev)]
        for odd in range(2):
            parts = [
                jnp.where(low, values[j + odd], values[j + 1 - odd]) for j in range(0, exp_dev, 2)
            ]
            out_ref[2 * pair + odd] = jnp.concatenate(parts, axis=0).astype(BF16)


def expert_call(name, rows_in, weights, after=()):
    w_gate, w_up, w_down = weights
    exp_dev, features, width = w_gate.shape
    half = rows_in.shape[0]
    held = 2
    rows = half * CAP
    anywhere = pl.BlockSpec(memory_space=pl.ANY)
    vmem = pl.BlockSpec(memory_space=VMEM)
    return pl.pallas_call(
        functools.partial(expert_kernel, len(after)),
        out_shape=jax.ShapeDtypeStruct((half, exp_dev * CAP, features), BF16),
        in_specs=[vmem] + [anywhere] * (3 + len(after)),
        out_specs=vmem,
        scratch_shapes=[
            VMEM((exp_dev, rows, features), BF16),
            VMEM((held, features, width), BF16),
            VMEM((held, features, width), BF16),
            VMEM((held, width, features), BF16),
            VMEM((rows, width), BF16),
            VMEM((exp_dev, rows, features), F32),
            pltpu.SemaphoreType.DMA((held, 10)),
        ],
        compiler_params=pltpu.CompilerParams(vmem_limit_bytes=50 * 1024 * 1024),
        cost_estimate=pl.CostEstimate(
            flops=12 * exp_dev * rows * features * width,
            bytes_accessed=6 * exp_dev * features * width,
            transcendentals=exp_dev * rows * width,
        ),
        name=name,
    )(rows_in, *after, w_gate, w_up, w_down)


def mix_kernel(first_column, slots_ref, columns_ref, back_ref, grad_ref, mixed_ref, grads_ref):
    tok_rows, features = grad_ref.shape
    count = back_ref.shape[0]
    column = iota((tok_rows, count), 1)
    inner = lax.dot_general(
        grad_ref[...], back_ref[...], (((1,), (1,)), ((), ())), preferred_element_type=F32
    )
    total = jnp.zeros((tok_rows, count), F32)
    place = iota((tok_rows, tok_rows), 1)
    wide = jnp.zeros((tok_rows, tok_rows), F32)
    for k in range(TOP):
        here = column == slots_ref[:, k : k + 1]
        weight = columns_ref[:, first_column + k : first_column + k + 1]
        total = total + jnp.where(here, weight, 0.0)
        value = jnp.sum(jnp.where(here, inner, 0.0), axis=1, keepdims=True)
        wide = wide + jnp.where(place == k, value, 0.0)
    high = total.astype(BF16)
    rest = (total - high.astype(F32)).astype(BF16)
    width = 512
    for at in range(0, features, width):
        rows = back_ref[:, at : at + width]
        mixed_ref[:, at : at + width] = (dot(high, rows) + dot(rest, rows)).astype(mixed_ref.dtype)
    grads_ref[...] = wide.T[: grads_ref.shape[0], :]


def sum_kernel(near_ref, near_grads_ref, far_ref, far_grads_ref, mixed_ref, grads_ref):
    mixed_ref[...] = (near_ref[...] + far_ref[...].astype(F32)).astype(BF16)
    grads_ref[...] = near_grads_ref[:TOP, :] + far_grads_ref[:TOP, :]


def swap(array, groups=None):
    return lax.all_to_all(
        array, "expert", split_axis=0, concat_axis=0, tiled=True, axis_index_groups=groups
    )


def near_path(
    block_values,
    block_exps,
    row_ids,
    expert_ids,
    gate_weights,
    table,
    w_gate,
    w_up,
    w_down,
    out_grad,
):
    device_count = lax.axis_size("expert")
    half = device_count // 2
    halves = [list(range(half)), list(range(half, device_count))]
    me = lax.axis_index("expert").astype(jnp.int32)
    tok_rows, features = block_values.shape
    rows_held = table.shape[0]
    look_cap = max(2, 2 * tok_rows // device_count)
    slots = half * 2 * PAIR
    vmem = pl.BlockSpec(memory_space=VMEM)
    smem = pl.BlockSpec(memory_space=pltpu.SMEM)
    anywhere = pl.BlockSpec(memory_space=pl.ANY)
    place = jnp.stack([me, jnp.int32(rows_held)])

    def shape(dims, kind):
        return jax.ShapeDtypeStruct(dims, kind)

    def mirrored(array):
        pairs = [(i, (i + half) % device_count) for i in range(device_count)]
        return lax.ppermute(array, "expert", pairs)

    def ordered(array, earlier_array):
        return pl.pallas_call(
            lambda array_ref, earlier_ref, out_ref: None,
            out_shape=shape(array.shape, array.dtype),
            in_specs=[anywhere, anywhere],
            out_specs=anywhere,
            input_output_aliases={0: 0},
            name="ordered",
        )(array, earlier_array)

    def picked(name, pick, states, *after):
        return pl.pallas_call(
            pick_kernel,
            out_shape=shape((pick.shape[0], features), BF16),
            in_specs=[vmem, vmem] + [anywhere] * len(after),
            out_specs=vmem,
            name=name,
        )(pick, states, *after).reshape(half, 2 * PAIR, features)

    other_grad = mirrored(out_grad)
    packed = pl.pallas_call(
        pack_kernel,
        out_shape=shape((device_count, 16, tok_rows), F32),
        in_specs=[vmem] * 3,
        out_specs=vmem,
        name="pack",
    )(row_ids[None, :], expert_ids.T, gate_weights.T)
    packed = swap(packed)
    fetched = pl.pallas_call(
        fetch_kernel,
        out_shape=shape((device_count * look_cap, features), BF16),
        in_specs=[smem, vmem, vmem],
        out_specs=vmem,
        name="fetch_rows",
    )(place, packed, table)
    returned = swap(fetched.reshape(device_count, look_cap, features))
    put, near_pick, far_pick, near_of, far_of, columns = pl.pallas_call(
        plan_kernel,
        out_shape=(
            shape((tok_rows, device_count * look_cap), BF16),
            shape((slots, tok_rows), BF16),
            shape((slots, tok_rows), BF16),
            shape((tok_rows, tok_rows), jnp.int32),
            shape((tok_rows, tok_rows), jnp.int32),
            shape((tok_rows, tok_rows), F32),
        ),
        in_specs=[smem, vmem, vmem, vmem, anywhere, anywhere],
        out_specs=(vmem,) * 6,
        name="plan",
    )(place, row_ids[None, :], packed, jnp.exp2(block_exps.T.astype(F32)), fetched, other_grad)
    state, near_sent = pl.pallas_call(
        state_kernel,
        out_shape=(shape((tok_rows, features), BF16), shape((slots, features), BF16)),
        in_specs=[vmem] * 5,
        out_specs=(vmem, vmem),
        name="token_state",
    )(put, near_pick, returned.reshape(device_count * look_cap, features), block_values, columns)
    other_state = mirrored(state)
    near_rows = swap(near_sent.reshape(half, 2 * PAIR, features), halves)
    far_sent = picked("far_slots", far_pick, other_state, near_rows)
    far_rows = swap(far_sent, halves)

    weights = (w_gate, w_up, w_down)
    near_out = expert_call("near_experts", near_rows, weights, after=(far_sent,))
    far_out = expert_call("far_experts", far_rows, weights, after=(near_out,))
    near_back = swap(near_out, halves)
    far_back = swap(ordered(far_out, near_back), halves)

    def mixed_rows(name, first_column, slot_of, back, grad, kind):
        return pl.pallas_call(
            functools.partial(mix_kernel, first_column),
            out_shape=(shape((tok_rows, features), kind), shape((2 * TOP, tok_rows), F32)),
            in_specs=[vmem] * 4,
            out_specs=(vmem, vmem),
            name=name,
        )(slot_of, columns, back.reshape(slots, features), grad)

    near_mixed, near_grads = mixed_rows("mix_near", 0, near_of, near_back, out_grad, F32)
    far_mixed, far_grads = mixed_rows("mix_far", TOP, far_of, far_back, other_grad, BF16)
    mixed, grads = pl.pallas_call(
        sum_kernel,
        out_shape=(shape((tok_rows, features), BF16), shape((TOP, tok_rows), F32)),
        in_specs=[vmem] * 4,
        out_specs=(vmem, vmem),
        name="sum_mixes",
    )(near_mixed, near_grads, mirrored(far_mixed), mirrored(far_grads))
    return mixed, grads.T


def expert_work(arrived, w_gate, w_up, w_down):
    gate_act = jnp.einsum("sjcd,jdf->sjcf", arrived, w_gate, preferred_element_type=jnp.float32)
    up_act = jnp.einsum("sjcd,jdf->sjcf", arrived, w_up, preferred_element_type=jnp.float32)
    hidden = (jax.nn.silu(gate_act) * up_act).astype(jnp.bfloat16)
    return jnp.einsum("sjcf,jfd->sjcd", hidden, w_down, preferred_element_type=jnp.float32).astype(
        jnp.bfloat16
    )


def full_path(buffer, w_gate, w_up, w_down, device_count, exp_dev, width_split, features):
    group_count = EXPERTS // exp_dev
    grouped = buffer.reshape(group_count, 1, exp_dev, CAP, features)
    outgoing = jnp.broadcast_to(
        grouped, (group_count, width_split, exp_dev, CAP, features)
    ).reshape(device_count, exp_dev, CAP, features)
    returned_out = lax.all_to_all(
        expert_work(
            lax.all_to_all(outgoing, "expert", split_axis=0, concat_axis=0, tiled=True),
            w_gate,
            w_up,
            w_down,
        ),
        "expert",
        split_axis=0,
        concat_axis=0,
        tiled=True,
    )
    pieces = returned_out.reshape(group_count, width_split, exp_dev, CAP, features).astype(
        jnp.float32
    )
    return jnp.sum(pieces, axis=1).astype(jnp.bfloat16).reshape(EXPERTS * CAP, features)


def far_path(
    block_values,
    block_exps,
    row_ids,
    expert_ids,
    gate_weights,
    table,
    w_gate,
    w_up,
    w_down,
    out_grad,
):
    device_count = lax.axis_size("expert")
    tok_rows = block_values.shape[0]
    features = block_values.shape[1]
    rows_held = table.shape[0]
    look_cap = max(2, 2 * tok_rows // device_count)
    exp_dev = w_gate.shape[0]
    width_split = device_count * exp_dev // EXPERTS
    owners = row_ids // rows_held
    local_row = row_ids % rows_held
    owner_hot = (owners[:, None] == jnp.arange(device_count, dtype=jnp.int32)[None, :]).astype(
        jnp.int32
    )
    owner_rank = jnp.sum((jnp.cumsum(owner_hot, axis=0) - 1) * owner_hot, axis=1)
    placed = owners * look_cap + owner_rank
    wanted = jnp.zeros((device_count * look_cap,), jnp.int32).at[placed].set(local_row)
    requested = lax.all_to_all(
        wanted.reshape(device_count, look_cap), "expert", split_axis=0, concat_axis=0, tiled=True
    )
    fetched = jnp.take(table, requested.reshape(-1), axis=0).reshape(
        device_count, look_cap, features
    )
    rows_returned = lax.all_to_all(fetched, "expert", split_axis=0, concat_axis=0, tiled=True)
    embedded = jnp.take(rows_returned.reshape(device_count * look_cap, features), placed, axis=0)
    scales = jnp.exp2(block_exps.astype(jnp.float32))
    blocks = (
        block_values.reshape(tok_rows, scales.shape[1], -1).astype(jnp.float32) * scales[:, :, None]
    )
    token_state = (blocks.reshape(tok_rows, features) + embedded.astype(jnp.float32)).astype(
        jnp.bfloat16
    )
    flat_ids = expert_ids.reshape(-1)
    expert_hot = (flat_ids[:, None] == jnp.arange(EXPERTS, dtype=jnp.int32)[None, :]).astype(
        jnp.int32
    )
    expert_rank = jnp.sum((jnp.cumsum(expert_hot, axis=0) - 1) * expert_hot, axis=1)
    slot_of = flat_ids * CAP + expert_rank
    token_index = jnp.arange(tok_rows * TOP, dtype=jnp.int32) // TOP
    source = jnp.full((EXPERTS * CAP,), tok_rows, jnp.int32).at[slot_of].set(token_index)
    padded = jnp.concatenate([token_state, jnp.zeros((1, features), jnp.bfloat16)], axis=0)
    buffer = jnp.take(padded, source, axis=0)
    expert_out = full_path(
        buffer, w_gate, w_up, w_down, device_count, exp_dev, width_split, features
    )
    chosen = jnp.take(expert_out, slot_of, axis=0).reshape(tok_rows, TOP, features)
    mixed = jnp.sum(gate_weights[:, :, None] * chosen.astype(jnp.float32), axis=1).astype(
        jnp.bfloat16
    )
    gate_grads = jnp.einsum("tkd,td->tk", chosen, out_grad, preferred_element_type=jnp.float32)
    return (mixed, gate_grads)


def local(*arrays):
    if lax.axis_size("expert") == 16 and arrays[6].shape[0] * 16 == EXPERTS:
        return near_path(*arrays)
    return far_path(*arrays)


def solution(mesh):
    return jax.shard_map(
        local,
        mesh=mesh,
        in_specs=(
            P(("groups", "expert"), None),
            P(("groups", "expert"), None),
            P(("groups", "expert")),
            P(("groups", "expert"), None),
            P(("groups", "expert"), None),
            P("expert", None),
            P("expert", None, None),
            P("expert", None, None),
            P("expert", None, None),
            P(("groups", "expert"), None),
        ),
        out_specs=(P(("groups", "expert"), None), P(("groups", "expert"), None)),
        check_vma=False,
    )
```

```python
import functools

import jax
import jax.numpy as jnp
from jax import lax
from jax.experimental import pallas as pl
from jax.experimental.pallas import tpu as pltpu
from jax.sharding import PartitionSpec as P

EXPERTS = 64
TOP = 4
CAP = 12
BLOCK = 128
PAIR = 2 * CAP
VMEM = pltpu.VMEM
F32 = jnp.float32
BF16 = jnp.bfloat16
SMALL = pltpu.CompilerParams(vmem_limit_bytes=16 * 1024 * 1024)


def dot(a, b):
    return jnp.dot(a, b, preferred_element_type=F32)


def iota(shape, dimension):
    return lax.broadcasted_iota(jnp.int32, shape, dimension)


def flags(mask):
    return mask.astype(F32).astype(BF16)


def earlier(length):
    return flags(iota((length, length), 0) < iota((length, length), 1))


def pack_kernel(rows_ref, ids_ref, weights_ref, out_ref):
    count, lines, tok_rows = out_ref.shape
    packed = jnp.concatenate(
        [
            rows_ref[...].astype(F32),
            ids_ref[...].astype(F32),
            weights_ref[...],
            jnp.zeros((lines - 1 - 2 * TOP, tok_rows), F32),
        ],
        axis=0,
    )
    for n in range(count):
        out_ref[n] = packed


def fetch_kernel(me_ref, packed_ref, table_ref, out_ref):
    device_count, _, tok_rows = packed_ref.shape
    held = table_ref.shape[0]
    look_cap = out_ref.shape[0] // device_count
    local = packed_ref[:, 0, :].astype(jnp.int32) - me_ref[0] * held
    hit = (local >= 0) & (local < held)
    rank = dot(flags(hit), earlier(tok_rows)).astype(jnp.int32)
    rank = jnp.where(hit, rank, -1)
    slot = iota((look_cap, tok_rows), 0)
    place = iota((look_cap, held), 1)
    picks = []
    for source in range(device_count):
        mine = jnp.where(slot == rank[source : source + 1], local[source : source + 1], 0)
        wanted = jnp.sum(mine, axis=1, keepdims=True)
        picks.append(flags(place == wanted))
    out_ref[...] = dot(jnp.concatenate(picks, axis=0), table_ref[...]).astype(BF16)


def turned(rows):
    count, length = rows.shape
    return jnp.concatenate([rows, jnp.zeros((length - count, length), F32)], axis=0).T


def plan_kernel(
    me_ref,
    rows_ref,
    packed_ref,
    scales_ref,
    fetched_ref,
    put_ref,
    near_ref,
    far_ref,
    near_slots_ref,
    far_slots_ref,
    columns_ref,
):
    tok_rows = rows_ref.shape[1]
    slots = put_ref.shape[1]
    half = near_ref.shape[0] // (2 * PAIR)
    device_count = 2 * half
    exp_dev = EXPERTS // device_count
    look_cap = slots // device_count
    me, held = me_ref[0], me_ref[1]
    flip = me % 2
    start = me // half * half * exp_dev
    before = earlier(tok_rows)

    row = jnp.broadcast_to(rows_ref[...], (device_count, tok_rows))
    low = iota((device_count, tok_rows), 0) * held
    hit = (row >= low) & (row < low + held)
    rank = jnp.where(hit, dot(flags(hit), before).astype(jnp.int32), -1)
    slot = iota((look_cap, tok_rows), 0)
    put = [(slot == rank[o : o + 1]).astype(F32) for o in range(device_count)]
    put_ref[...] = jnp.concatenate(put, axis=0).T.astype(BF16)

    expert = iota((half * exp_dev, tok_rows), 0) + start
    place = iota((PAIR, tok_rows), 0)
    inside = iota((half * exp_dev, tok_rows), 0)
    flipped = ((inside + flip) & 1) * CAP
    device = inside // exp_dev
    chunk = (inside % exp_dev) // 2
    mine = packed_ref[me]
    other = packed_ref[(me + half) % device_count]
    for far, packed in enumerate((mine, other)):
        ids = [packed[1 + k : 2 + k].astype(jnp.int32) for k in range(TOP)]
        chosen = [ids[k] == expert for k in range(TOP)]
        hit = functools.reduce(jnp.logical_or, chosen)
        rank = jnp.where(hit, dot(flags(hit), before).astype(jnp.int32), -1000)
        lines = [[], []]
        for d in range(half):
            for c in range(2):
                at = d * exp_dev + 2 * c
                one, two = rank[at : at + 1], rank[at + 1 : at + 2]
                upper = jnp.where(flip == 0, one, two)
                lower = jnp.where(flip == 0, two, one) + CAP
                here = ((place < CAP) & (place == upper)) | ((place >= CAP) & (place == lower))
                lines[c].append(here.astype(F32))
        both = [line for pair in zip(*lines) for line in pair]
        pick_ref = far_ref if far else near_ref
        pick_ref[...] = jnp.concatenate(both, axis=0).astype(BF16)
        slot = device * (2 * PAIR) + chunk * PAIR + flipped + rank
        found = [
            jnp.sum(jnp.where(chosen[k], slot + 1, 0), axis=0, keepdims=True) - 1
            for k in range(TOP)
        ]
        slots_out = far_slots_ref if far else near_slots_ref
        found = turned(jnp.concatenate(found, axis=0).astype(F32))
        slots_out[...] = found.astype(jnp.int32)
    columns_ref[...] = turned(
        jnp.concatenate(
            [mine[1 + TOP : 1 + 2 * TOP], other[1 + TOP : 1 + 2 * TOP], scales_ref[...]], axis=0
        )
    )


def state_kernel(put_ref, pick_ref, returned_ref, values_ref, columns_ref, state_ref, out_ref):
    features = values_ref.shape[1]
    width = 512
    for left in range(0, features, width):
        found = dot(put_ref[...], returned_ref[:, left : left + width])
        for b in range(width // BLOCK):
            at = left + b * BLOCK
            scaled = (
                values_ref[:, at : at + BLOCK].astype(F32)
                * columns_ref[:, 2 * TOP + at // BLOCK : 2 * TOP + at // BLOCK + 1]
            )
            state_ref[:, at : at + BLOCK] = (
                scaled + found[:, b * BLOCK : (b + 1) * BLOCK]
            ).astype(BF16)
        cols = slice(left, left + width)
        out_ref[:, cols] = dot(pick_ref[...], state_ref[:, cols]).astype(BF16)


def pick_kernel(pick_ref, state_ref, *refs):
    out_ref = refs[-1]
    features = state_ref.shape[1]
    width = 512
    for left in range(0, features, width):
        cols = slice(left, left + width)
        out_ref[:, cols] = dot(pick_ref[...], state_ref[:, cols]).astype(BF16)


def expert_kernel(after, rows_ref, *refs):
    wg_hbm, wu_hbm, wd_hbm, out_ref = refs[after : after + 4]
    x_ref, wg_ref, wu_ref, wd_ref, hidden_ref, result_ref, sem = refs[after + 4 :]
    exp_dev = wg_hbm.shape[0]
    held, features, width = wg_ref.shape
    half = rows_ref.shape[0]
    up_cuts = ((0, 512), (512, 512), (1024, width - 1024))
    down_cuts = tuple((at, 512) for at in range(0, features, 512))

    def weight_copies(j, place):
        copies = []
        for at, size in up_cuts:
            for hbm, ref in ((wg_hbm, wg_ref), (wu_hbm, wu_ref)):
                cols = pl.ds(at, size)
                copies.append((hbm.at[j, :, cols], ref.at[place, :, cols]))
        for at, size in down_cuts:
            cols = pl.ds(at, size)
            copies.append((wd_hbm.at[j, :, cols], wd_ref.at[place, :, cols]))
        return [
            pltpu.make_async_copy(src, dst, sem.at[place, n])
            for n, (src, dst) in enumerate(copies)
        ]

    for j in range(held):
        for copy in weight_copies(j, j):
            copy.start()

    low = iota((PAIR, features), 0) < CAP
    for chunk in range(exp_dev // 2):
        here = slice(chunk * PAIR, (chunk + 1) * PAIR)
        for quad in range(half // 4):
            ones, twos = [], []
            for pair in range(2):
                source = 4 * quad + 2 * pair
                even = rows_ref[source, here, :].astype(F32)
                odd = rows_ref[source + 1, here, :].astype(F32)
                ones.append(jnp.where(low, even, odd))
                twos.append(jnp.where(low, odd, even))
            rows = slice(quad * 2 * PAIR, (quad + 1) * 2 * PAIR)
            x_ref[2 * chunk, rows, :] = jnp.concatenate(ones, axis=0).astype(BF16)
            x_ref[2 * chunk + 1, rows, :] = jnp.concatenate(twos, axis=0).astype(BF16)

    @pl.loop(0, exp_dev)
    def _(j):
        place = j % held
        copies = weight_copies(j, place)
        later = weight_copies(jnp.minimum(j + held, exp_dev - 1), place)

        def refill(first, count):
            @pl.when(j + held < exp_dev)
            def _():
                for n in range(first, first + count):
                    later[n].start()

        n = 0
        for at, size in up_cuts:
            copies[n].wait()
            copies[n + 1].wait()
            x = x_ref[j]
            gate = dot(x, wg_ref[place, :, at : at + size])
            up = dot(x, wu_ref[place, :, at : at + size])
            hidden_ref[:, at : at + size] = (gate / (1.0 + jnp.exp(-gate)) * up).astype(BF16)
            refill(n, 2)
            n += 2
        for at, size in down_cuts:
            copies[n].wait()
            result_ref[j, :, at : at + size] = dot(
                hidden_ref[...], wd_ref[place, :, at : at + size]
            )
            refill(n, 1)
            n += 1

    for pair in range(half // 2):
        rows = slice(pair * PAIR, (pair + 1) * PAIR)
        values = [result_ref[j, rows, :] for j in range(exp_dev)]
        for odd in range(2):
            parts = [
                jnp.where(low, values[j + odd], values[j + 1 - odd]) for j in range(0, exp_dev, 2)
            ]
            out_ref[2 * pair + odd] = jnp.concatenate(parts, axis=0).astype(BF16)


def expert_call(name, rows_in, weights, after=()):
    w_gate, w_up, w_down = weights
    exp_dev, features, width = w_gate.shape
    half = rows_in.shape[0]
    held = 2
    rows = half * CAP
    anywhere = pl.BlockSpec(memory_space=pl.ANY)
    vmem = pl.BlockSpec(memory_space=VMEM)
    return pl.pallas_call(
        functools.partial(expert_kernel, len(after)),
        out_shape=jax.ShapeDtypeStruct((half, exp_dev * CAP, features), BF16),
        in_specs=[vmem] + [anywhere] * (3 + len(after)),
        out_specs=vmem,
        scratch_shapes=[
            VMEM((exp_dev, rows, features), BF16),
            VMEM((held, features, width), BF16),
            VMEM((held, features, width), BF16),
            VMEM((held, width, features), BF16),
            VMEM((rows, width), BF16),
            VMEM((exp_dev, rows, features), F32),
            pltpu.SemaphoreType.DMA((held, 10)),
        ],
        compiler_params=pltpu.CompilerParams(vmem_limit_bytes=50 * 1024 * 1024),
        cost_estimate=pl.CostEstimate(
            flops=12 * exp_dev * rows * features * width,
            bytes_accessed=6 * exp_dev * features * width,
            transcendentals=exp_dev * rows * width,
        ),
        name=name,
    )(rows_in, *after, w_gate, w_up, w_down)


def mix_kernel(first_column, slots_ref, columns_ref, back_ref, *refs):
    mixed_ref, grads_ref = refs[-2:]
    tok_rows = slots_ref.shape[0]
    count, features = back_ref.shape
    grad = jnp.concatenate([ref[...] for ref in refs[:-2]], axis=0)
    column = iota((tok_rows, count), 1)
    inner = lax.dot_general(
        grad, back_ref[...], (((1,), (1,)), ((), ())), preferred_element_type=F32
    )
    total = jnp.zeros((tok_rows, count), F32)
    place = iota((tok_rows, tok_rows), 1)
    wide = jnp.zeros((tok_rows, tok_rows), F32)
    for k in range(TOP):
        here = column == slots_ref[:, k : k + 1]
        weight = columns_ref[:, first_column + k : first_column + k + 1]
        total = total + jnp.where(here, weight, 0.0)
        value = jnp.sum(jnp.where(here, inner, 0.0), axis=1, keepdims=True)
        wide = wide + jnp.where(place == k, value, 0.0)
    high = total.astype(BF16)
    rest = (total - high.astype(F32)).astype(BF16)
    width = 512
    for at in range(0, features, width):
        rows = back_ref[:, at : at + width]
        mixed_ref[:, at : at + width] = (dot(high, rows) + dot(rest, rows)).astype(mixed_ref.dtype)
    grads_ref[...] = wide.T[: grads_ref.shape[0], :]


def swap(array, groups=None):
    return lax.all_to_all(
        array, "expert", split_axis=0, concat_axis=0, tiled=True, axis_index_groups=groups
    )


def near_path(
    block_values,
    block_exps,
    row_ids,
    expert_ids,
    gate_weights,
    table,
    w_gate,
    w_up,
    w_down,
    out_grad,
):
    device_count = lax.axis_size("expert")
    half = device_count // 2
    halves = [list(range(half)), list(range(half, device_count))]
    me = lax.axis_index("expert").astype(jnp.int32)
    tok_rows, features = block_values.shape
    rows_held = table.shape[0]
    look_cap = max(2, 2 * tok_rows // device_count)
    slots = half * 2 * PAIR
    vmem = pl.BlockSpec(memory_space=VMEM)
    smem = pl.BlockSpec(memory_space=pltpu.SMEM)
    anywhere = pl.BlockSpec(memory_space=pl.ANY)
    place = jnp.stack([me, jnp.int32(rows_held)])

    def shape(dims, kind):
        return jax.ShapeDtypeStruct(dims, kind)

    def mirrored(array):
        pairs = [(i, (i + half) % device_count) for i in range(device_count)]
        return lax.ppermute(array, "expert", pairs)

    def ordered(array, *earlier_arrays):
        return pl.pallas_call(
            lambda *refs: None,
            out_shape=shape(array.shape, array.dtype),
            in_specs=[anywhere] * (1 + len(earlier_arrays)),
            out_specs=anywhere,
            input_output_aliases={0: 0},
            compiler_params=SMALL,
            name="ordered",
        )(array, *earlier_arrays)

    def picked(name, pick, states, *after):
        return pl.pallas_call(
            pick_kernel,
            out_shape=shape((pick.shape[0], features), BF16),
            in_specs=[vmem, vmem] + [anywhere] * len(after),
            out_specs=vmem,
            compiler_params=SMALL,
            name=name,
        )(pick, states, *after).reshape(half, 2 * PAIR, features)

    split = tok_rows // 2
    other_grads = (mirrored(out_grad[:split]), mirrored(out_grad[split:]))
    packed = pl.pallas_call(
        pack_kernel,
        out_shape=shape((device_count, 16, tok_rows), F32),
        in_specs=[vmem] * 3,
        out_specs=vmem,
        compiler_params=SMALL,
        name="pack",
    )(row_ids[None, :], expert_ids.T, gate_weights.T)
    packed = swap(packed)
    fetched = pl.pallas_call(
        fetch_kernel,
        out_shape=shape((device_count * look_cap, features), BF16),
        in_specs=[smem, vmem, vmem],
        out_specs=vmem,
        compiler_params=SMALL,
        name="fetch_rows",
    )(place, packed, table)
    returned = swap(fetched.reshape(device_count, look_cap, features))
    put, near_pick, far_pick, near_of, far_of, columns = pl.pallas_call(
        plan_kernel,
        out_shape=(
            shape((tok_rows, device_count * look_cap), BF16),
            shape((slots, tok_rows), BF16),
            shape((slots, tok_rows), BF16),
            shape((tok_rows, tok_rows), jnp.int32),
            shape((tok_rows, tok_rows), jnp.int32),
            shape((tok_rows, tok_rows), F32),
        ),
        in_specs=[smem, vmem, vmem, vmem, anywhere],
        out_specs=(vmem,) * 6,
        compiler_params=SMALL,
        name="plan",
    )(place, row_ids[None, :], packed, jnp.exp2(block_exps.T.astype(F32)), fetched)
    state, near_sent = pl.pallas_call(
        state_kernel,
        out_shape=(shape((tok_rows, features), BF16), shape((slots, features), BF16)),
        in_specs=[vmem] * 5,
        out_specs=(vmem, vmem),
        compiler_params=SMALL,
        name="token_state",
    )(put, near_pick, returned.reshape(device_count * look_cap, features), block_values, columns)
    other_state = mirrored(state)
    near_rows = swap(near_sent.reshape(half, 2 * PAIR, features), halves)
    far_sent = picked("far_slots", far_pick, other_state)
    far_rows = swap(far_sent, halves)

    weights = (w_gate, w_up, w_down)
    near_out = expert_call("near_experts", near_rows, weights, after=(far_sent,))
    far_out = expert_call("far_experts", far_rows, weights, after=(near_out, other_grads[0]))
    near_back = swap(near_out, halves)
    far_back = swap(ordered(far_out, near_back, other_grads[1]), halves)

    def mixed_rows(name, first_column, slot_of, back, grads, kind):
        return pl.pallas_call(
            functools.partial(mix_kernel, first_column),
            out_shape=(shape((tok_rows, features), kind), shape((2 * TOP, tok_rows), F32)),
            in_specs=[vmem] * (3 + len(grads)),
            out_specs=(vmem, vmem),
            compiler_params=SMALL,
            name=name,
        )(slot_of, columns, back.reshape(slots, features), *grads)

    near_mixed, near_grads = mixed_rows("mix_near", 0, near_of, near_back, (out_grad,), F32)
    far_mixed, far_grads = mixed_rows("mix_far", TOP, far_of, far_back, other_grads, BF16)
    mixed = (near_mixed + mirrored(far_mixed).astype(F32)).astype(BF16)
    grads = (near_grads + mirrored(far_grads))[:TOP]
    return mixed, grads.T


def expert_work(arrived, w_gate, w_up, w_down):
    gate_act = jnp.einsum("sjcd,jdf->sjcf", arrived, w_gate, preferred_element_type=jnp.float32)
    up_act = jnp.einsum("sjcd,jdf->sjcf", arrived, w_up, preferred_element_type=jnp.float32)
    hidden = (jax.nn.silu(gate_act) * up_act).astype(jnp.bfloat16)
    return jnp.einsum("sjcf,jfd->sjcd", hidden, w_down, preferred_element_type=jnp.float32).astype(
        jnp.bfloat16
    )


def full_path(buffer, w_gate, w_up, w_down, device_count, exp_dev, width_split, features):
    group_count = EXPERTS // exp_dev
    grouped = buffer.reshape(group_count, 1, exp_dev, CAP, features)
    outgoing = jnp.broadcast_to(
        grouped, (group_count, width_split, exp_dev, CAP, features)
    ).reshape(device_count, exp_dev, CAP, features)
    returned_out = lax.all_to_all(
        expert_work(
            lax.all_to_all(outgoing, "expert", split_axis=0, concat_axis=0, tiled=True),
            w_gate,
            w_up,
            w_down,
        ),
        "expert",
        split_axis=0,
        concat_axis=0,
        tiled=True,
    )
    pieces = returned_out.reshape(group_count, width_split, exp_dev, CAP, features).astype(
        jnp.float32
    )
    return jnp.sum(pieces, axis=1).astype(jnp.bfloat16).reshape(EXPERTS * CAP, features)


def far_path(
    block_values,
    block_exps,
    row_ids,
    expert_ids,
    gate_weights,
    table,
    w_gate,
    w_up,
    w_down,
    out_grad,
):
    device_count = lax.axis_size("expert")
    tok_rows = block_values.shape[0]
    features = block_values.shape[1]
    rows_held = table.shape[0]
    look_cap = max(2, 2 * tok_rows // device_count)
    exp_dev = w_gate.shape[0]
    width_split = device_count * exp_dev // EXPERTS
    owners = row_ids // rows_held
    local_row = row_ids % rows_held
    owner_hot = (owners[:, None] == jnp.arange(device_count, dtype=jnp.int32)[None, :]).astype(
        jnp.int32
    )
    owner_rank = jnp.sum((jnp.cumsum(owner_hot, axis=0) - 1) * owner_hot, axis=1)
    placed = owners * look_cap + owner_rank
    wanted = jnp.zeros((device_count * look_cap,), jnp.int32).at[placed].set(local_row)
    requested = lax.all_to_all(
        wanted.reshape(device_count, look_cap), "expert", split_axis=0, concat_axis=0, tiled=True
    )
    fetched = jnp.take(table, requested.reshape(-1), axis=0).reshape(
        device_count, look_cap, features
    )
    rows_returned = lax.all_to_all(fetched, "expert", split_axis=0, concat_axis=0, tiled=True)
    embedded = jnp.take(rows_returned.reshape(device_count * look_cap, features), placed, axis=0)
    scales = jnp.exp2(block_exps.astype(jnp.float32))
    blocks = (
        block_values.reshape(tok_rows, scales.shape[1], -1).astype(jnp.float32) * scales[:, :, None]
    )
    token_state = (blocks.reshape(tok_rows, features) + embedded.astype(jnp.float32)).astype(
        jnp.bfloat16
    )
    flat_ids = expert_ids.reshape(-1)
    expert_hot = (flat_ids[:, None] == jnp.arange(EXPERTS, dtype=jnp.int32)[None, :]).astype(
        jnp.int32
    )
    expert_rank = jnp.sum((jnp.cumsum(expert_hot, axis=0) - 1) * expert_hot, axis=1)
    slot_of = flat_ids * CAP + expert_rank
    token_index = jnp.arange(tok_rows * TOP, dtype=jnp.int32) // TOP
    source = jnp.full((EXPERTS * CAP,), tok_rows, jnp.int32).at[slot_of].set(token_index)
    padded = jnp.concatenate([token_state, jnp.zeros((1, features), jnp.bfloat16)], axis=0)
    buffer = jnp.take(padded, source, axis=0)
    expert_out = full_path(
        buffer, w_gate, w_up, w_down, device_count, exp_dev, width_split, features
    )
    chosen = jnp.take(expert_out, slot_of, axis=0).reshape(tok_rows, TOP, features)
    mixed = jnp.sum(gate_weights[:, :, None] * chosen.astype(jnp.float32), axis=1).astype(
        jnp.bfloat16
    )
    gate_grads = jnp.einsum("tkd,td->tk", chosen, out_grad, preferred_element_type=jnp.float32)
    return (mixed, gate_grads)


def local(*arrays):
    if lax.axis_size("expert") == 16 and arrays[6].shape[0] * 16 == EXPERTS:
        return near_path(*arrays)
    return far_path(*arrays)


def solution(mesh):
    return jax.shard_map(
        local,
        mesh=mesh,
        in_specs=(
            P(("groups", "expert"), None),
            P(("groups", "expert"), None),
            P(("groups", "expert")),
            P(("groups", "expert"), None),
            P(("groups", "expert"), None),
            P("expert", None),
            P("expert", None, None),
            P("expert", None, None),
            P("expert", None, None),
            P(("groups", "expert"), None),
        ),
        out_specs=(P(("groups", "expert"), None), P(("groups", "expert"), None)),
        check_vma=False,
    )
```

```python
import functools

import jax
import jax.numpy as jnp
from jax import lax
from jax.experimental import pallas as pl
from jax.experimental.pallas import tpu as pltpu
from jax.sharding import PartitionSpec as P

EXPERTS = 64
TOP = 4
CAP = 12
BLOCK = 128
PAIR = 2 * CAP
VMEM = pltpu.VMEM
F32 = jnp.float32
BF16 = jnp.bfloat16
SMALL = pltpu.CompilerParams(vmem_limit_bytes=16 * 1024 * 1024)


def dot(a, b):
    return jnp.dot(a, b, preferred_element_type=F32)


def iota(shape, dimension):
    return lax.broadcasted_iota(jnp.int32, shape, dimension)


def flags(mask):
    return mask.astype(F32).astype(BF16)


def earlier(length):
    return flags(iota((length, length), 0) < iota((length, length), 1))


def pack_kernel(rows_ref, ids_ref, weights_ref, out_ref):
    count, lines, tok_rows = out_ref.shape
    packed = jnp.concatenate(
        [
            rows_ref[...].astype(F32),
            ids_ref[...].astype(F32),
            weights_ref[...],
            jnp.zeros((lines - 1 - 2 * TOP, tok_rows), F32),
        ],
        axis=0,
    )
    for n in range(count):
        out_ref[n] = packed


def fetch_kernel(me_ref, packed_ref, table_ref, out_ref):
    device_count, _, tok_rows = packed_ref.shape
    held = table_ref.shape[0]
    look_cap = out_ref.shape[0] // device_count
    local = packed_ref[:, 0, :].astype(jnp.int32) - me_ref[0] * held
    hit = (local >= 0) & (local < held)
    rank = dot(flags(hit), earlier(tok_rows)).astype(jnp.int32)
    rank = jnp.where(hit, rank, -1)
    slot = iota((look_cap, tok_rows), 0)
    place = iota((look_cap, held), 1)
    picks = []
    for source in range(device_count):
        mine = jnp.where(slot == rank[source : source + 1], local[source : source + 1], 0)
        wanted = jnp.sum(mine, axis=1, keepdims=True)
        picks.append(flags(place == wanted))
    out_ref[...] = dot(jnp.concatenate(picks, axis=0), table_ref[...]).astype(BF16)


def turned(rows):
    count, length = rows.shape
    return jnp.concatenate([rows, jnp.zeros((length - count, length), F32)], axis=0).T


def plan_kernel(
    me_ref,
    rows_ref,
    packed_ref,
    scales_ref,
    fetched_ref,
    put_ref,
    near_ref,
    far_ref,
    near_slots_ref,
    far_slots_ref,
    columns_ref,
):
    tok_rows = rows_ref.shape[1]
    slots = put_ref.shape[1]
    half = near_ref.shape[0] // (2 * PAIR)
    device_count = 2 * half
    exp_dev = EXPERTS // device_count
    look_cap = slots // device_count
    me, held = me_ref[0], me_ref[1]
    flip = me % 2
    start = me // half * half * exp_dev
    before = earlier(tok_rows)

    row = jnp.broadcast_to(rows_ref[...], (device_count, tok_rows))
    low = iota((device_count, tok_rows), 0) * held
    hit = (row >= low) & (row < low + held)
    rank = jnp.where(hit, dot(flags(hit), before).astype(jnp.int32), -1)
    slot = iota((look_cap, tok_rows), 0)
    put = [(slot == rank[o : o + 1]).astype(F32) for o in range(device_count)]
    put_ref[...] = jnp.concatenate(put, axis=0).T.astype(BF16)

    expert = iota((half * exp_dev, tok_rows), 0) + start
    place = iota((PAIR, tok_rows), 0)
    inside = iota((half * exp_dev, tok_rows), 0)
    flipped = ((inside + flip) & 1) * CAP
    device = inside // exp_dev
    chunk = (inside % exp_dev) // 2
    mine = packed_ref[me]
    other = packed_ref[(me + half) % device_count]
    for far, packed in enumerate((mine, other)):
        ids = [packed[1 + k : 2 + k].astype(jnp.int32) for k in range(TOP)]
        chosen = [ids[k] == expert for k in range(TOP)]
        hit = functools.reduce(jnp.logical_or, chosen)
        rank = jnp.where(hit, dot(flags(hit), before).astype(jnp.int32), -1000)
        lines = [[], []]
        for d in range(half):
            for c in range(2):
                at = d * exp_dev + 2 * c
                one, two = rank[at : at + 1], rank[at + 1 : at + 2]
                upper = jnp.where(flip == 0, one, two)
                lower = jnp.where(flip == 0, two, one) + CAP
                here = ((place < CAP) & (place == upper)) | ((place >= CAP) & (place == lower))
                lines[c].append(here.astype(F32))
        both = [line for pair in zip(*lines) for line in pair]
        pick_ref = far_ref if far else near_ref
        pick_ref[...] = jnp.concatenate(both, axis=0).astype(BF16)
        slot = device * (2 * PAIR) + chunk * PAIR + flipped + rank
        found = [
            jnp.sum(jnp.where(chosen[k], slot + 1, 0), axis=0, keepdims=True) - 1
            for k in range(TOP)
        ]
        slots_out = far_slots_ref if far else near_slots_ref
        found = turned(jnp.concatenate(found, axis=0).astype(F32))
        slots_out[...] = found.astype(jnp.int32)
    columns_ref[...] = turned(
        jnp.concatenate(
            [mine[1 + TOP : 1 + 2 * TOP], other[1 + TOP : 1 + 2 * TOP], scales_ref[...]], axis=0
        )
    )


def pick_slots(pick_ref, state_ref, out_hbm, sent_ref, sem, left, width):
    cols = pl.ds(left, width)
    sent_ref[:, cols] = dot(pick_ref[...], state_ref[:, cols]).astype(BF16)
    copy = pltpu.make_async_copy(
        sent_ref.at[:, cols], out_hbm.at[:, cols], sem.at[left // width]
    )
    copy.start()
    return copy


def state_kernel(
    put_ref, pick_ref, returned_ref, values_ref, columns_ref, state_ref, out_hbm, sent_ref, sem
):
    features = values_ref.shape[1]
    width = features // sem.shape[0]
    copies = []
    for left in range(0, features, width):
        found = dot(put_ref[...], returned_ref[:, left : left + width])
        for b in range(width // BLOCK):
            at = left + b * BLOCK
            scaled = (
                values_ref[:, at : at + BLOCK].astype(F32)
                * columns_ref[:, 2 * TOP + at // BLOCK : 2 * TOP + at // BLOCK + 1]
            )
            state_ref[:, at : at + BLOCK] = (
                scaled + found[:, b * BLOCK : (b + 1) * BLOCK]
            ).astype(BF16)
        copies.append(pick_slots(pick_ref, state_ref, out_hbm, sent_ref, sem, left, width))
    for copy in copies:
        copy.wait()


def pick_kernel(pick_ref, state_ref, out_hbm, sent_ref, sem):
    features = state_ref.shape[1]
    width = features // sem.shape[0]
    copies = [
        pick_slots(pick_ref, state_ref, out_hbm, sent_ref, sem, left, width)
        for left in range(0, features, width)
    ]
    for copy in copies:
        copy.wait()


def expert_kernel(after, rows_ref, *refs):
    wg_hbm, wu_hbm, wd_hbm, out_ref = refs[after : after + 4]
    x_ref, wg_ref, wu_ref, wd_ref, hidden_ref, result_ref, sem = refs[after + 4 :]
    exp_dev = wg_hbm.shape[0]
    held, features, width = wg_ref.shape
    half = rows_ref.shape[0]
    up_cuts = ((0, 512), (512, 512), (1024, width - 1024))
    down_cuts = tuple((at, 512) for at in range(0, features, 512))

    def weight_copies(j, place):
        copies = []
        for at, size in up_cuts:
            for hbm, ref in ((wg_hbm, wg_ref), (wu_hbm, wu_ref)):
                cols = pl.ds(at, size)
                copies.append((hbm.at[j, :, cols], ref.at[place, :, cols]))
        for at, size in down_cuts:
            cols = pl.ds(at, size)
            copies.append((wd_hbm.at[j, :, cols], wd_ref.at[place, :, cols]))
        return [
            pltpu.make_async_copy(src, dst, sem.at[place, n])
            for n, (src, dst) in enumerate(copies)
        ]

    for j in range(held):
        for copy in weight_copies(j, j):
            copy.start()

    low = iota((PAIR, features), 0) < CAP
    for chunk in range(exp_dev // 2):
        here = slice(chunk * PAIR, (chunk + 1) * PAIR)
        for quad in range(half // 4):
            ones, twos = [], []
            for pair in range(2):
                source = 4 * quad + 2 * pair
                even = rows_ref[source, here, :].astype(F32)
                odd = rows_ref[source + 1, here, :].astype(F32)
                ones.append(jnp.where(low, even, odd))
                twos.append(jnp.where(low, odd, even))
            rows = slice(quad * 2 * PAIR, (quad + 1) * 2 * PAIR)
            x_ref[2 * chunk, rows, :] = jnp.concatenate(ones, axis=0).astype(BF16)
            x_ref[2 * chunk + 1, rows, :] = jnp.concatenate(twos, axis=0).astype(BF16)

    @pl.loop(0, exp_dev)
    def _(j):
        place = j % held
        copies = weight_copies(j, place)
        later = weight_copies(jnp.minimum(j + held, exp_dev - 1), place)

        def refill(first, count):
            @pl.when(j + held < exp_dev)
            def _():
                for n in range(first, first + count):
                    later[n].start()

        n = 0
        for at, size in up_cuts:
            copies[n].wait()
            copies[n + 1].wait()
            x = x_ref[j]
            gate = dot(x, wg_ref[place, :, at : at + size])
            up = dot(x, wu_ref[place, :, at : at + size])
            hidden_ref[:, at : at + size] = (gate / (1.0 + jnp.exp(-gate)) * up).astype(BF16)
            refill(n, 2)
            n += 2
        for at, size in down_cuts:
            copies[n].wait()
            result_ref[j, :, at : at + size] = dot(
                hidden_ref[...], wd_ref[place, :, at : at + size]
            )
            refill(n, 1)
            n += 1

    for pair in range(half // 2):
        rows = slice(pair * PAIR, (pair + 1) * PAIR)
        values = [result_ref[j, rows, :] for j in range(exp_dev)]
        for odd in range(2):
            parts = [
                jnp.where(low, values[j + odd], values[j + 1 - odd]) for j in range(0, exp_dev, 2)
            ]
            out_ref[2 * pair + odd] = jnp.concatenate(parts, axis=0).astype(BF16)


def expert_call(name, rows_in, weights, after=()):
    w_gate, w_up, w_down = weights
    exp_dev, features, width = w_gate.shape
    half = rows_in.shape[0]
    held = 2
    rows = half * CAP
    anywhere = pl.BlockSpec(memory_space=pl.ANY)
    vmem = pl.BlockSpec(memory_space=VMEM)
    return pl.pallas_call(
        functools.partial(expert_kernel, len(after)),
        out_shape=jax.ShapeDtypeStruct((half, exp_dev * CAP, features), BF16),
        in_specs=[vmem] + [anywhere] * (3 + len(after)),
        out_specs=vmem,
        scratch_shapes=[
            VMEM((exp_dev, rows, features), BF16),
            VMEM((held, features, width), BF16),
            VMEM((held, features, width), BF16),
            VMEM((held, width, features), BF16),
            VMEM((rows, width), BF16),
            VMEM((exp_dev, rows, features), F32),
            pltpu.SemaphoreType.DMA((held, 10)),
        ],
        compiler_params=pltpu.CompilerParams(vmem_limit_bytes=43 * 1024 * 1024),
        cost_estimate=pl.CostEstimate(
            flops=12 * exp_dev * rows * features * width,
            bytes_accessed=6 * exp_dev * features * width,
            transcendentals=exp_dev * rows * width,
        ),
        name=name,
    )(rows_in, *after, w_gate, w_up, w_down)


def mix_kernel(first_column, slots_ref, columns_ref, back_ref, *refs):
    mixed_ref, grads_ref = refs[-2:]
    tok_rows = slots_ref.shape[0]
    count, features = back_ref.shape
    grad = jnp.concatenate([ref[...] for ref in refs[:-2]], axis=0)
    column = iota((tok_rows, count), 1)
    inner = lax.dot_general(
        grad, back_ref[...], (((1,), (1,)), ((), ())), preferred_element_type=F32
    )
    total = jnp.zeros((tok_rows, count), F32)
    place = iota((tok_rows, tok_rows), 1)
    wide = jnp.zeros((tok_rows, tok_rows), F32)
    for k in range(TOP):
        here = column == slots_ref[:, k : k + 1]
        weight = columns_ref[:, first_column + k : first_column + k + 1]
        total = total + jnp.where(here, weight, 0.0)
        value = jnp.sum(jnp.where(here, inner, 0.0), axis=1, keepdims=True)
        wide = wide + jnp.where(place == k, value, 0.0)
    high = total.astype(BF16)
    rest = (total - high.astype(F32)).astype(BF16)
    width = 512
    for at in range(0, features, width):
        rows = back_ref[:, at : at + width]
        mixed_ref[:, at : at + width] = (dot(high, rows) + dot(rest, rows)).astype(mixed_ref.dtype)
    grads_ref[...] = wide.T[: grads_ref.shape[0], :]


def swap(array, groups=None):
    return lax.all_to_all(
        array, "expert", split_axis=0, concat_axis=0, tiled=True, axis_index_groups=groups
    )


def near_path(
    block_values,
    block_exps,
    row_ids,
    expert_ids,
    gate_weights,
    table,
    w_gate,
    w_up,
    w_down,
    out_grad,
):
    device_count = lax.axis_size("expert")
    half = device_count // 2
    halves = [list(range(half)), list(range(half, device_count))]
    me = lax.axis_index("expert").astype(jnp.int32)
    tok_rows, features = block_values.shape
    rows_held = table.shape[0]
    look_cap = max(2, 2 * tok_rows // device_count)
    slots = half * 2 * PAIR
    vmem = pl.BlockSpec(memory_space=VMEM)
    smem = pl.BlockSpec(memory_space=pltpu.SMEM)
    anywhere = pl.BlockSpec(memory_space=pl.ANY)
    place = jnp.stack([me, jnp.int32(rows_held)])

    def shape(dims, kind):
        return jax.ShapeDtypeStruct(dims, kind)

    def mirrored(array):
        pairs = [(i, (i + half) % device_count) for i in range(device_count)]
        return lax.ppermute(array, "expert", pairs)

    def ordered(array, *earlier_arrays):
        return pl.pallas_call(
            lambda *refs: None,
            out_shape=shape(array.shape, array.dtype),
            in_specs=[anywhere] * (1 + len(earlier_arrays)),
            out_specs=anywhere,
            input_output_aliases={0: 0},
            compiler_params=SMALL,
            name="ordered",
        )(array, *earlier_arrays)

    split = tok_rows // 2
    other_grads = (mirrored(out_grad[:split]), mirrored(out_grad[split:]))
    packed = pl.pallas_call(
        pack_kernel,
        out_shape=shape((device_count, 16, tok_rows), F32),
        in_specs=[vmem] * 3,
        out_specs=vmem,
        name="pack",
    )(row_ids[None, :], expert_ids.T, gate_weights.T)
    packed = swap(packed)
    fetched = pl.pallas_call(
        fetch_kernel,
        out_shape=shape((device_count * look_cap, features), BF16),
        in_specs=[smem, vmem, vmem],
        out_specs=vmem,
        compiler_params=SMALL,
        name="fetch_rows",
    )(place, packed, table)
    returned = swap(fetched.reshape(device_count, look_cap, features))
    put, near_pick, far_pick, near_of, far_of, columns = pl.pallas_call(
        plan_kernel,
        out_shape=(
            shape((tok_rows, device_count * look_cap), BF16),
            shape((slots, tok_rows), BF16),
            shape((slots, tok_rows), BF16),
            shape((tok_rows, tok_rows), jnp.int32),
            shape((tok_rows, tok_rows), jnp.int32),
            shape((tok_rows, tok_rows), F32),
        ),
        in_specs=[smem, vmem, vmem, vmem, anywhere],
        out_specs=(vmem,) * 6,
        compiler_params=SMALL,
        name="plan",
    )(place, row_ids[None, :], packed, jnp.exp2(block_exps.T.astype(F32)), fetched)
    sent_shape = pltpu.HBM((slots, features), BF16)
    sent_scratch = [VMEM((slots, features), BF16), pltpu.SemaphoreType.DMA((4,))]
    state, near_sent = pl.pallas_call(
        state_kernel,
        out_shape=(shape((tok_rows, features), BF16), sent_shape),
        in_specs=[vmem] * 5,
        out_specs=(vmem, anywhere),
        scratch_shapes=sent_scratch,
        compiler_params=SMALL,
        name="token_state",
    )(put, near_pick, returned.reshape(device_count * look_cap, features), block_values, columns)
    other_state = mirrored(state)
    near_rows = swap(near_sent.reshape(half, 2 * PAIR, features), halves)
    far_sent = pl.pallas_call(
        pick_kernel,
        out_shape=sent_shape,
        in_specs=[vmem, vmem],
        out_specs=anywhere,
        scratch_shapes=sent_scratch,
        compiler_params=SMALL,
        cost_estimate=pl.CostEstimate(
            flops=20_000_000_000, bytes_accessed=4 * slots * features, transcendentals=0
        ),
        name="far_slots",
    )(far_pick, other_state).reshape(half, 2 * PAIR, features)
    far_rows = swap(far_sent, halves)

    weights = (w_gate, w_up, w_down)
    near_out = expert_call("near_experts", near_rows, weights, after=(far_sent,))
    far_out = expert_call("far_experts", far_rows, weights, after=(near_out,))
    near_back = swap(ordered(near_out, other_grads[0]), halves)
    far_back = swap(ordered(far_out, near_back, other_grads[1]), halves)

    def mixed_rows(name, first_column, slot_of, back, grads, kind):
        return pl.pallas_call(
            functools.partial(mix_kernel, first_column),
            out_shape=(shape((tok_rows, features), kind), shape((2 * TOP, tok_rows), F32)),
            in_specs=[vmem] * (3 + len(grads)),
            out_specs=(vmem, vmem),
            compiler_params=SMALL,
            name=name,
        )(slot_of, columns, back.reshape(slots, features), *grads)

    near_mixed, near_grads = mixed_rows("mix_near", 0, near_of, near_back, (out_grad,), F32)
    far_mixed, far_grads = mixed_rows("mix_far", TOP, far_of, far_back, other_grads, BF16)
    mixed = (near_mixed + mirrored(far_mixed).astype(F32)).astype(BF16)
    grads = (near_grads + mirrored(far_grads))[:TOP]
    return mixed, grads.T


def expert_work(arrived, w_gate, w_up, w_down):
    gate_act = jnp.einsum("sjcd,jdf->sjcf", arrived, w_gate, preferred_element_type=jnp.float32)
    up_act = jnp.einsum("sjcd,jdf->sjcf", arrived, w_up, preferred_element_type=jnp.float32)
    hidden = (jax.nn.silu(gate_act) * up_act).astype(jnp.bfloat16)
    return jnp.einsum("sjcf,jfd->sjcd", hidden, w_down, preferred_element_type=jnp.float32).astype(
        jnp.bfloat16
    )


def full_path(buffer, w_gate, w_up, w_down, device_count, exp_dev, width_split, features):
    group_count = EXPERTS // exp_dev
    grouped = buffer.reshape(group_count, 1, exp_dev, CAP, features)
    outgoing = jnp.broadcast_to(
        grouped, (group_count, width_split, exp_dev, CAP, features)
    ).reshape(device_count, exp_dev, CAP, features)
    returned_out = lax.all_to_all(
        expert_work(
            lax.all_to_all(outgoing, "expert", split_axis=0, concat_axis=0, tiled=True),
            w_gate,
            w_up,
            w_down,
        ),
        "expert",
        split_axis=0,
        concat_axis=0,
        tiled=True,
    )
    pieces = returned_out.reshape(group_count, width_split, exp_dev, CAP, features).astype(
        jnp.float32
    )
    return jnp.sum(pieces, axis=1).astype(jnp.bfloat16).reshape(EXPERTS * CAP, features)


def far_path(
    block_values,
    block_exps,
    row_ids,
    expert_ids,
    gate_weights,
    table,
    w_gate,
    w_up,
    w_down,
    out_grad,
):
    device_count = lax.axis_size("expert")
    tok_rows = block_values.shape[0]
    features = block_values.shape[1]
    rows_held = table.shape[0]
    look_cap = max(2, 2 * tok_rows // device_count)
    exp_dev = w_gate.shape[0]
    width_split = device_count * exp_dev // EXPERTS
    owners = row_ids // rows_held
    local_row = row_ids % rows_held
    owner_hot = (owners[:, None] == jnp.arange(device_count, dtype=jnp.int32)[None, :]).astype(
        jnp.int32
    )
    owner_rank = jnp.sum((jnp.cumsum(owner_hot, axis=0) - 1) * owner_hot, axis=1)
    placed = owners * look_cap + owner_rank
    wanted = jnp.zeros((device_count * look_cap,), jnp.int32).at[placed].set(local_row)
    requested = lax.all_to_all(
        wanted.reshape(device_count, look_cap), "expert", split_axis=0, concat_axis=0, tiled=True
    )
    fetched = jnp.take(table, requested.reshape(-1), axis=0).reshape(
        device_count, look_cap, features
    )
    rows_returned = lax.all_to_all(fetched, "expert", split_axis=0, concat_axis=0, tiled=True)
    embedded = jnp.take(rows_returned.reshape(device_count * look_cap, features), placed, axis=0)
    scales = jnp.exp2(block_exps.astype(jnp.float32))
    blocks = (
        block_values.reshape(tok_rows, scales.shape[1], -1).astype(jnp.float32) * scales[:, :, None]
    )
    token_state = (blocks.reshape(tok_rows, features) + embedded.astype(jnp.float32)).astype(
        jnp.bfloat16
    )
    flat_ids = expert_ids.reshape(-1)
    expert_hot = (flat_ids[:, None] == jnp.arange(EXPERTS, dtype=jnp.int32)[None, :]).astype(
        jnp.int32
    )
    expert_rank = jnp.sum((jnp.cumsum(expert_hot, axis=0) - 1) * expert_hot, axis=1)
    slot_of = flat_ids * CAP + expert_rank
    token_index = jnp.arange(tok_rows * TOP, dtype=jnp.int32) // TOP
    source = jnp.full((EXPERTS * CAP,), tok_rows, jnp.int32).at[slot_of].set(token_index)
    padded = jnp.concatenate([token_state, jnp.zeros((1, features), jnp.bfloat16)], axis=0)
    buffer = jnp.take(padded, source, axis=0)
    expert_out = full_path(
        buffer, w_gate, w_up, w_down, device_count, exp_dev, width_split, features
    )
    chosen = jnp.take(expert_out, slot_of, axis=0).reshape(tok_rows, TOP, features)
    mixed = jnp.sum(gate_weights[:, :, None] * chosen.astype(jnp.float32), axis=1).astype(
        jnp.bfloat16
    )
    gate_grads = jnp.einsum("tkd,td->tk", chosen, out_grad, preferred_element_type=jnp.float32)
    return (mixed, gate_grads)


def local(*arrays):
    if lax.axis_size("expert") == 16 and arrays[6].shape[0] * 16 == EXPERTS:
        return near_path(*arrays)
    return far_path(*arrays)


def solution(mesh):
    return jax.shard_map(
        local,
        mesh=mesh,
        in_specs=(
            P(("groups", "expert"), None),
            P(("groups", "expert"), None),
            P(("groups", "expert")),
            P(("groups", "expert"), None),
            P(("groups", "expert"), None),
            P("expert", None),
            P("expert", None, None),
            P("expert", None, None),
            P("expert", None, None),
            P(("groups", "expert"), None),
        ),
        out_specs=(P(("groups", "expert"), None), P(("groups", "expert"), None)),
        check_vma=False,
    )
```

```python
import functools

import jax
import jax.numpy as jnp
from jax import lax
from jax.experimental import pallas as pl
from jax.experimental.pallas import tpu as pltpu
from jax.sharding import PartitionSpec as P

EXPERTS = 64
TOP = 4
CAP = 12
BLOCK = 128
PAIR = 2 * CAP
VMEM = pltpu.VMEM
F32 = jnp.float32
BF16 = jnp.bfloat16
SMALL = pltpu.CompilerParams(vmem_limit_bytes=16 * 1024 * 1024)


def dot(a, b):
    return jnp.dot(a, b, preferred_element_type=F32)


def iota(shape, dimension):
    return lax.broadcasted_iota(jnp.int32, shape, dimension)


def flags(mask):
    return mask.astype(F32).astype(BF16)


def earlier(length):
    return flags(iota((length, length), 0) < iota((length, length), 1))


def pack_kernel(rows_ref, ids_ref, weights_ref, out_ref):
    count, lines, tok_rows = out_ref.shape
    packed = jnp.concatenate(
        [
            rows_ref[...].astype(F32),
            ids_ref[...].astype(F32),
            weights_ref[...],
            jnp.zeros((lines - 1 - 2 * TOP, tok_rows), F32),
        ],
        axis=0,
    )
    for n in range(count):
        out_ref[n] = packed


def fetch_kernel(me_ref, packed_ref, table_hbm, out_ref, table_ref, sem):
    width = table_ref.shape[1] // sem.shape[0]
    copies = []
    for n in range(sem.shape[0]):
        cols = pl.ds(n * width, width)
        copies.append(
            pltpu.make_async_copy(table_hbm.at[:, cols], table_ref.at[:, cols], sem.at[n])
        )
        copies[-1].start()
    device_count, _, tok_rows = packed_ref.shape
    held = table_ref.shape[0]
    look_cap = out_ref.shape[0] // device_count
    local = packed_ref[:, 0, :].astype(jnp.int32) - me_ref[0] * held
    hit = (local >= 0) & (local < held)
    rank = dot(flags(hit), earlier(tok_rows)).astype(jnp.int32)
    rank = jnp.where(hit, rank, -1)
    slot = iota((look_cap, tok_rows), 0)
    place = iota((look_cap, held), 1)
    picks = []
    for source in range(device_count):
        mine = jnp.where(slot == rank[source : source + 1], local[source : source + 1], 0)
        wanted = jnp.sum(mine, axis=1, keepdims=True)
        picks.append(flags(place == wanted))
    pick = jnp.concatenate(picks, axis=0)
    for n, copy in enumerate(copies):
        copy.wait()
        cols = slice(n * width, (n + 1) * width)
        out_ref[:, cols] = dot(pick, table_ref[:, cols]).astype(BF16)


def turned(rows):
    count, length = rows.shape
    return jnp.concatenate([rows, jnp.zeros((length - count, length), F32)], axis=0).T


def plan_kernel(
    me_ref,
    rows_ref,
    packed_ref,
    scales_ref,
    fetched_ref,
    put_ref,
    near_ref,
    far_ref,
    near_slots_ref,
    far_slots_ref,
    columns_ref,
):
    tok_rows = rows_ref.shape[1]
    slots = put_ref.shape[1]
    half = near_ref.shape[0] // (2 * PAIR)
    device_count = 2 * half
    exp_dev = EXPERTS // device_count
    look_cap = slots // device_count
    me, held = me_ref[0], me_ref[1]
    flip = me % 2
    start = me // half * half * exp_dev
    before = earlier(tok_rows)

    row = jnp.broadcast_to(rows_ref[...], (device_count, tok_rows))
    low = iota((device_count, tok_rows), 0) * held
    hit = (row >= low) & (row < low + held)
    rank = jnp.where(hit, dot(flags(hit), before).astype(jnp.int32), -1)
    slot = iota((look_cap, tok_rows), 0)
    put = [(slot == rank[o : o + 1]).astype(F32) for o in range(device_count)]
    put_ref[...] = jnp.concatenate(put, axis=0).T.astype(BF16)

    expert = iota((half * exp_dev, tok_rows), 0) + start
    place = iota((PAIR, tok_rows), 0)
    inside = iota((half * exp_dev, tok_rows), 0)
    flipped = ((inside + flip) & 1) * CAP
    device = inside // exp_dev
    chunk = (inside % exp_dev) // 2
    mine = packed_ref[me]
    other = packed_ref[(me + half) % device_count]
    for far, packed in enumerate((mine, other)):
        ids = [packed[1 + k : 2 + k].astype(jnp.int32) for k in range(TOP)]
        chosen = [ids[k] == expert for k in range(TOP)]
        hit = functools.reduce(jnp.logical_or, chosen)
        rank = jnp.where(hit, dot(flags(hit), before).astype(jnp.int32), -1000)
        lines = [[], []]
        for d in range(half):
            for c in range(2):
                at = d * exp_dev + 2 * c
                one, two = rank[at : at + 1], rank[at + 1 : at + 2]
                upper = jnp.where(flip == 0, one, two)
                lower = jnp.where(flip == 0, two, one) + CAP
                here = ((place < CAP) & (place == upper)) | ((place >= CAP) & (place == lower))
                lines[c].append(here.astype(F32))
        both = [line for pair in zip(*lines) for line in pair]
        pick_ref = far_ref if far else near_ref
        pick_ref[...] = jnp.concatenate(both, axis=0).astype(BF16)
        slot = device * (2 * PAIR) + chunk * PAIR + flipped + rank
        found = [
            jnp.sum(jnp.where(chosen[k], slot + 1, 0), axis=0, keepdims=True) - 1
            for k in range(TOP)
        ]
        slots_out = far_slots_ref if far else near_slots_ref
        found = turned(jnp.concatenate(found, axis=0).astype(F32))
        slots_out[...] = found.astype(jnp.int32)
    columns_ref[...] = turned(
        jnp.concatenate(
            [mine[1 + TOP : 1 + 2 * TOP], other[1 + TOP : 1 + 2 * TOP], scales_ref[...]], axis=0
        )
    )


def pick_slots(pick_ref, state_ref, out_hbm, sent_ref, sem, left, width):
    cols = pl.ds(left, width)
    sent_ref[:, cols] = dot(pick_ref[...], state_ref[:, cols]).astype(BF16)
    copy = pltpu.make_async_copy(
        sent_ref.at[:, cols], out_hbm.at[:, cols], sem.at[left // width]
    )
    copy.start()
    return copy


def state_kernel(
    put_ref, pick_ref, returned_ref, values_ref, columns_ref, state_ref, out_hbm, sent_ref, sem
):
    features = values_ref.shape[1]
    width = features // sem.shape[0]
    copies = []
    for left in range(0, features, width):
        found = dot(put_ref[...], returned_ref[:, left : left + width])
        for b in range(width // BLOCK):
            at = left + b * BLOCK
            scaled = (
                values_ref[:, at : at + BLOCK].astype(F32)
                * columns_ref[:, 2 * TOP + at // BLOCK : 2 * TOP + at // BLOCK + 1]
            )
            state_ref[:, at : at + BLOCK] = (
                scaled + found[:, b * BLOCK : (b + 1) * BLOCK]
            ).astype(BF16)
        copies.append(pick_slots(pick_ref, state_ref, out_hbm, sent_ref, sem, left, width))
    for copy in copies:
        copy.wait()


def pick_kernel(
    pick_ref, state_ref, grad_ref, out_hbm, upper_grad_ref, lower_grad_ref, sent_ref, sem
):
    tok_rows, features = state_ref.shape
    width = features // sem.shape[0]
    copies = [
        pick_slots(pick_ref, state_ref, out_hbm, sent_ref, sem, left, width)
        for left in range(0, features, width)
    ]
    upper_grad_ref[...] = grad_ref[: tok_rows // 2, :]
    lower_grad_ref[...] = grad_ref[tok_rows // 2 :, :]
    for copy in copies:
        copy.wait()


def expert_kernel(after, rows_ref, *refs):
    wg_hbm, wu_hbm, wd_hbm, out_ref = refs[after : after + 4]
    x_ref, wg_ref, wu_ref, wd_ref, hidden_ref, result_ref, sem = refs[after + 4 :]
    exp_dev = wg_hbm.shape[0]
    held, features, width = wg_ref.shape
    half = rows_ref.shape[0]
    up_cuts = ((0, 512), (512, 512), (1024, width - 1024))
    down_cuts = tuple((at, 512) for at in range(0, features, 512))

    def weight_copies(j, place):
        copies = []
        for at, size in up_cuts:
            for hbm, ref in ((wg_hbm, wg_ref), (wu_hbm, wu_ref)):
                cols = pl.ds(at, size)
                copies.append((hbm.at[j, :, cols], ref.at[place, :, cols]))
        for at, size in down_cuts:
            cols = pl.ds(at, size)
            copies.append((wd_hbm.at[j, :, cols], wd_ref.at[place, :, cols]))
        return [
            pltpu.make_async_copy(src, dst, sem.at[place, n])
            for n, (src, dst) in enumerate(copies)
        ]

    for j in range(held):
        for copy in weight_copies(j, j):
            copy.start()

    low = iota((PAIR, features), 0) < CAP
    for chunk in range(exp_dev // 2):
        here = slice(chunk * PAIR, (chunk + 1) * PAIR)
        for quad in range(half // 4):
            ones, twos = [], []
            for pair in range(2):
                source = 4 * quad + 2 * pair
                even = rows_ref[source, here, :].astype(F32)
                odd = rows_ref[source + 1, here, :].astype(F32)
                ones.append(jnp.where(low, even, odd))
                twos.append(jnp.where(low, odd, even))
            rows = slice(quad * 2 * PAIR, (quad + 1) * 2 * PAIR)
            x_ref[2 * chunk, rows, :] = jnp.concatenate(ones, axis=0).astype(BF16)
            x_ref[2 * chunk + 1, rows, :] = jnp.concatenate(twos, axis=0).astype(BF16)

    @pl.loop(0, exp_dev)
    def _(j):
        place = j % held
        copies = weight_copies(j, place)
        later = weight_copies(jnp.minimum(j + held, exp_dev - 1), place)

        def refill(first, count):
            @pl.when(j + held < exp_dev)
            def _():
                for n in range(first, first + count):
                    later[n].start()

        n = 0
        for at, size in up_cuts:
            copies[n].wait()
            copies[n + 1].wait()
            x = x_ref[j]
            gate = dot(x, wg_ref[place, :, at : at + size])
            up = dot(x, wu_ref[place, :, at : at + size])
            hidden_ref[:, at : at + size] = (gate / (1.0 + jnp.exp(-gate)) * up).astype(BF16)
            refill(n, 2)
            n += 2
        for at, size in down_cuts:
            copies[n].wait()
            result_ref[j, :, at : at + size] = dot(
                hidden_ref[...], wd_ref[place, :, at : at + size]
            )
            refill(n, 1)
            n += 1

    for pair in range(half // 2):
        rows = slice(pair * PAIR, (pair + 1) * PAIR)
        values = [result_ref[j, rows, :] for j in range(exp_dev)]
        for odd in range(2):
            parts = [
                jnp.where(low, values[j + odd], values[j + 1 - odd]) for j in range(0, exp_dev, 2)
            ]
            out_ref[2 * pair + odd] = jnp.concatenate(parts, axis=0).astype(BF16)


def expert_call(name, rows_in, weights, after=()):
    w_gate, w_up, w_down = weights
    exp_dev, features, width = w_gate.shape
    half = rows_in.shape[0]
    held = 1
    rows = half * CAP
    anywhere = pl.BlockSpec(memory_space=pl.ANY)
    vmem = pl.BlockSpec(memory_space=VMEM)
    return pl.pallas_call(
        functools.partial(expert_kernel, len(after)),
        out_shape=jax.ShapeDtypeStruct((half, exp_dev * CAP, features), BF16),
        in_specs=[vmem] + [anywhere] * (3 + len(after)),
        out_specs=vmem,
        scratch_shapes=[
            VMEM((exp_dev, rows, features), BF16),
            VMEM((held, features, width), BF16),
            VMEM((held, features, width), BF16),
            VMEM((held, width, features), BF16),
            VMEM((rows, width), BF16),
            VMEM((exp_dev, rows, features), F32),
            pltpu.SemaphoreType.DMA((held, 10)),
        ],
        compiler_params=pltpu.CompilerParams(vmem_limit_bytes=27 * 1024 * 1024),
        cost_estimate=pl.CostEstimate(
            flops=12 * exp_dev * rows * features * width,
            bytes_accessed=6 * exp_dev * features * width,
            transcendentals=exp_dev * rows * width,
        ),
        name=name,
    )(rows_in, *after, w_gate, w_up, w_down)


def mix_kernel(first_column, slots_ref, columns_ref, back_ref, *refs):
    mixed_ref, grads_ref = refs[-2:]
    tok_rows = slots_ref.shape[0]
    count, features = back_ref.shape
    grad = jnp.concatenate([ref[...] for ref in refs[:-2]], axis=0)
    column = iota((tok_rows, count), 1)
    inner = lax.dot_general(
        grad, back_ref[...], (((1,), (1,)), ((), ())), preferred_element_type=F32
    )
    total = jnp.zeros((tok_rows, count), F32)
    place = iota((tok_rows, tok_rows), 1)
    wide = jnp.zeros((tok_rows, tok_rows), F32)
    for k in range(TOP):
        here = column == slots_ref[:, k : k + 1]
        weight = columns_ref[:, first_column + k : first_column + k + 1]
        total = total + jnp.where(here, weight, 0.0)
        value = jnp.sum(jnp.where(here, inner, 0.0), axis=1, keepdims=True)
        wide = wide + jnp.where(place == k, value, 0.0)
    high = total.astype(BF16)
    rest = (total - high.astype(F32)).astype(BF16)
    width = 512
    for at in range(0, features, width):
        rows = back_ref[:, at : at + width]
        mixed_ref[:, at : at + width] = (dot(high, rows) + dot(rest, rows)).astype(mixed_ref.dtype)
    grads_ref[...] = wide.T[: grads_ref.shape[0], :]


def swap(array, groups=None):
    return lax.all_to_all(
        array, "expert", split_axis=0, concat_axis=0, tiled=True, axis_index_groups=groups
    )


def near_path(
    block_values,
    block_exps,
    row_ids,
    expert_ids,
    gate_weights,
    table,
    w_gate,
    w_up,
    w_down,
    out_grad,
):
    device_count = lax.axis_size("expert")
    half = device_count // 2
    halves = [list(range(half)), list(range(half, device_count))]
    me = lax.axis_index("expert").astype(jnp.int32)
    tok_rows, features = block_values.shape
    rows_held = table.shape[0]
    look_cap = max(2, 2 * tok_rows // device_count)
    slots = half * 2 * PAIR
    vmem = pl.BlockSpec(memory_space=VMEM)
    smem = pl.BlockSpec(memory_space=pltpu.SMEM)
    anywhere = pl.BlockSpec(memory_space=pl.ANY)
    place = jnp.stack([me, jnp.int32(rows_held)])

    def shape(dims, kind):
        return jax.ShapeDtypeStruct(dims, kind)

    def mirrored(array):
        pairs = [(i, (i + half) % device_count) for i in range(device_count)]
        return lax.ppermute(array, "expert", pairs)

    def ordered(array, *earlier_arrays):
        return pl.pallas_call(
            lambda *refs: None,
            out_shape=shape(array.shape, array.dtype),
            in_specs=[anywhere] * (1 + len(earlier_arrays)),
            out_specs=anywhere,
            input_output_aliases={0: 0},
            compiler_params=SMALL,
            name="ordered",
        )(array, *earlier_arrays)

    split = shape((tok_rows // 2, features), BF16)
    packed = pl.pallas_call(
        pack_kernel,
        out_shape=shape((device_count, 16, tok_rows), F32),
        in_specs=[vmem] * 3,
        out_specs=vmem,
        name="pack",
    )(row_ids[None, :], expert_ids.T, gate_weights.T)
    packed = swap(packed)
    fetched = pl.pallas_call(
        fetch_kernel,
        out_shape=shape((device_count * look_cap, features), BF16),
        in_specs=[smem, vmem, pl.BlockSpec(memory_space=pltpu.HBM)],
        out_specs=vmem,
        scratch_shapes=[VMEM(table.shape, BF16), pltpu.SemaphoreType.DMA((4,))],
        compiler_params=SMALL,
        name="fetch_rows",
    )(place, packed, table)
    returned = swap(fetched.reshape(device_count, look_cap, features))
    put, near_pick, far_pick, near_of, far_of, columns = pl.pallas_call(
        plan_kernel,
        out_shape=(
            shape((tok_rows, device_count * look_cap), BF16),
            shape((slots, tok_rows), BF16),
            shape((slots, tok_rows), BF16),
            shape((tok_rows, tok_rows), jnp.int32),
            shape((tok_rows, tok_rows), jnp.int32),
            shape((tok_rows, tok_rows), F32),
        ),
        in_specs=[smem, vmem, vmem, vmem, anywhere],
        out_specs=(vmem,) * 6,
        compiler_params=SMALL,
        name="plan",
    )(place, row_ids[None, :], packed, jnp.exp2(block_exps.T.astype(F32)), fetched)
    sent_shape = pltpu.HBM((slots, features), BF16)
    sent_scratch = [VMEM((slots, features), BF16), pltpu.SemaphoreType.DMA((4,))]
    state, near_sent = pl.pallas_call(
        state_kernel,
        out_shape=(shape((tok_rows, features), BF16), sent_shape),
        in_specs=[vmem] * 5,
        out_specs=(vmem, anywhere),
        scratch_shapes=sent_scratch,
        compiler_params=SMALL,
        name="token_state",
    )(put, near_pick, returned.reshape(device_count * look_cap, features), block_values, columns)
    other_state = mirrored(state)
    near_rows = swap(near_sent.reshape(half, 2 * PAIR, features), halves)
    far_sent, *grad_halves = pl.pallas_call(
        pick_kernel,
        out_shape=(sent_shape, split, split),
        in_specs=[vmem, vmem, vmem],
        out_specs=(anywhere, vmem, vmem),
        scratch_shapes=sent_scratch,
        compiler_params=SMALL,
        cost_estimate=pl.CostEstimate(
            flops=400_000_000_000, bytes_accessed=4 * slots * features, transcendentals=0
        ),
        name="far_slots",
    )(far_pick, other_state, out_grad)
    other_grads = [mirrored(array) for array in grad_halves]
    far_sent = far_sent.reshape(half, 2 * PAIR, features)
    far_rows = swap(far_sent, halves)

    weights = (w_gate, w_up, w_down)
    near_out = expert_call("near_experts", near_rows, weights, after=(far_sent,))
    near_out = ordered(near_out, other_grads[0])
    far_out = expert_call("far_experts", far_rows, weights, after=(near_out,))
    near_back = swap(near_out, halves)
    far_back = swap(ordered(far_out, near_back, other_grads[1]), halves)

    def mixed_rows(name, first_column, slot_of, back, grads, kind):
        return pl.pallas_call(
            functools.partial(mix_kernel, first_column),
            out_shape=(shape((tok_rows, features), kind), shape((2 * TOP, tok_rows), F32)),
            in_specs=[vmem] * (3 + len(grads)),
            out_specs=(vmem, vmem),
            compiler_params=SMALL,
            name=name,
        )(slot_of, columns, back.reshape(slots, features), *grads)

    near_mixed, near_grads = mixed_rows("mix_near", 0, near_of, near_back, (out_grad,), F32)
    far_mixed, far_grads = mixed_rows("mix_far", TOP, far_of, far_back, other_grads, BF16)
    mixed = (near_mixed + mirrored(far_mixed).astype(F32)).astype(BF16)
    grads = (near_grads + mirrored(far_grads))[:TOP]
    return mixed, grads.T


def expert_work(arrived, w_gate, w_up, w_down):
    gate_act = jnp.einsum("sjcd,jdf->sjcf", arrived, w_gate, preferred_element_type=jnp.float32)
    up_act = jnp.einsum("sjcd,jdf->sjcf", arrived, w_up, preferred_element_type=jnp.float32)
    hidden = (jax.nn.silu(gate_act) * up_act).astype(jnp.bfloat16)
    return jnp.einsum("sjcf,jfd->sjcd", hidden, w_down, preferred_element_type=jnp.float32).astype(
        jnp.bfloat16
    )


def full_path(buffer, w_gate, w_up, w_down, device_count, exp_dev, width_split, features):
    group_count = EXPERTS // exp_dev
    grouped = buffer.reshape(group_count, 1, exp_dev, CAP, features)
    outgoing = jnp.broadcast_to(
        grouped, (group_count, width_split, exp_dev, CAP, features)
    ).reshape(device_count, exp_dev, CAP, features)
    returned_out = lax.all_to_all(
        expert_work(
            lax.all_to_all(outgoing, "expert", split_axis=0, concat_axis=0, tiled=True),
            w_gate,
            w_up,
            w_down,
        ),
        "expert",
        split_axis=0,
        concat_axis=0,
        tiled=True,
    )
    pieces = returned_out.reshape(group_count, width_split, exp_dev, CAP, features).astype(
        jnp.float32
    )
    return jnp.sum(pieces, axis=1).astype(jnp.bfloat16).reshape(EXPERTS * CAP, features)


def far_path(
    block_values,
    block_exps,
    row_ids,
    expert_ids,
    gate_weights,
    table,
    w_gate,
    w_up,
    w_down,
    out_grad,
):
    device_count = lax.axis_size("expert")
    tok_rows = block_values.shape[0]
    features = block_values.shape[1]
    rows_held = table.shape[0]
    look_cap = max(2, 2 * tok_rows // device_count)
    exp_dev = w_gate.shape[0]
    width_split = device_count * exp_dev // EXPERTS
    owners = row_ids // rows_held
    local_row = row_ids % rows_held
    owner_hot = (owners[:, None] == jnp.arange(device_count, dtype=jnp.int32)[None, :]).astype(
        jnp.int32
    )
    owner_rank = jnp.sum((jnp.cumsum(owner_hot, axis=0) - 1) * owner_hot, axis=1)
    placed = owners * look_cap + owner_rank
    wanted = jnp.zeros((device_count * look_cap,), jnp.int32).at[placed].set(local_row)
    requested = lax.all_to_all(
        wanted.reshape(device_count, look_cap), "expert", split_axis=0, concat_axis=0, tiled=True
    )
    fetched = jnp.take(table, requested.reshape(-1), axis=0).reshape(
        device_count, look_cap, features
    )
    rows_returned = lax.all_to_all(fetched, "expert", split_axis=0, concat_axis=0, tiled=True)
    embedded = jnp.take(rows_returned.reshape(device_count * look_cap, features), placed, axis=0)
    scales = jnp.exp2(block_exps.astype(jnp.float32))
    blocks = (
        block_values.reshape(tok_rows, scales.shape[1], -1).astype(jnp.float32) * scales[:, :, None]
    )
    token_state = (blocks.reshape(tok_rows, features) + embedded.astype(jnp.float32)).astype(
        jnp.bfloat16
    )
    flat_ids = expert_ids.reshape(-1)
    expert_hot = (flat_ids[:, None] == jnp.arange(EXPERTS, dtype=jnp.int32)[None, :]).astype(
        jnp.int32
    )
    expert_rank = jnp.sum((jnp.cumsum(expert_hot, axis=0) - 1) * expert_hot, axis=1)
    slot_of = flat_ids * CAP + expert_rank
    token_index = jnp.arange(tok_rows * TOP, dtype=jnp.int32) // TOP
    source = jnp.full((EXPERTS * CAP,), tok_rows, jnp.int32).at[slot_of].set(token_index)
    padded = jnp.concatenate([token_state, jnp.zeros((1, features), jnp.bfloat16)], axis=0)
    buffer = jnp.take(padded, source, axis=0)
    expert_out = full_path(
        buffer, w_gate, w_up, w_down, device_count, exp_dev, width_split, features
    )
    chosen = jnp.take(expert_out, slot_of, axis=0).reshape(tok_rows, TOP, features)
    mixed = jnp.sum(gate_weights[:, :, None] * chosen.astype(jnp.float32), axis=1).astype(
        jnp.bfloat16
    )
    gate_grads = jnp.einsum("tkd,td->tk", chosen, out_grad, preferred_element_type=jnp.float32)
    return (mixed, gate_grads)


def local(*arrays):
    if lax.axis_size("expert") == 16 and arrays[6].shape[0] * 16 == EXPERTS:
        return near_path(*arrays)
    return far_path(*arrays)


def solution(mesh):
    return jax.shard_map(
        local,
        mesh=mesh,
        in_specs=(
            P(("groups", "expert"), None),
            P(("groups", "expert"), None),
            P(("groups", "expert")),
            P(("groups", "expert"), None),
            P(("groups", "expert"), None),
            P("expert", None),
            P("expert", None, None),
            P("expert", None, None),
            P("expert", None, None),
            P(("groups", "expert"), None),
        ),
        out_specs=(P(("groups", "expert"), None), P(("groups", "expert"), None)),
        check_vma=False,
    )
```

```python
import functools

import jax
import jax.numpy as jnp
from jax import lax
from jax.experimental import pallas as pl
from jax.experimental.pallas import tpu as pltpu
from jax.sharding import PartitionSpec as P

EXPERTS = 64
TOP = 4
CAP = 12
BLOCK = 128
PAIR = 2 * CAP
VMEM = pltpu.VMEM
F32 = jnp.float32
BF16 = jnp.bfloat16
SMALL = pltpu.CompilerParams(vmem_limit_bytes=16 * 1024 * 1024)


def dot(a, b):
    return jnp.dot(a, b, preferred_element_type=F32)


def in_hbm(array):
    return pltpu.with_memory_space_constraint(array, pltpu.HBM)


def iota(shape, dimension):
    return lax.broadcasted_iota(jnp.int32, shape, dimension)


def flags(mask):
    return mask.astype(F32).astype(BF16)


def earlier(length):
    return flags(iota((length, length), 0) < iota((length, length), 1))


def pack_kernel(rows_ref, ids_ref, weights_ref, out_ref):
    count, lines, tok_rows = out_ref.shape
    packed = jnp.concatenate(
        [
            rows_ref[...].astype(F32),
            ids_ref[...].astype(F32),
            weights_ref[...],
            jnp.zeros((lines - 1 - 2 * TOP, tok_rows), F32),
        ],
        axis=0,
    )
    for n in range(count):
        out_ref[n] = packed


def fetch_kernel(me_ref, packed_ref, table_hbm, out_ref, table_ref, sem):
    width = table_ref.shape[1] // sem.shape[0]
    copies = []
    for n in range(sem.shape[0]):
        cols = pl.ds(n * width, width)
        copies.append(
            pltpu.make_async_copy(table_hbm.at[:, cols], table_ref.at[:, cols], sem.at[n])
        )
        copies[-1].start()
    device_count, _, tok_rows = packed_ref.shape
    held = table_ref.shape[0]
    look_cap = out_ref.shape[0] // device_count
    local = packed_ref[:, 0, :].astype(jnp.int32) - me_ref[0] * held
    hit = (local >= 0) & (local < held)
    rank = dot(flags(hit), earlier(tok_rows)).astype(jnp.int32)
    rank = jnp.where(hit, rank, -1)
    slot = iota((look_cap, tok_rows), 0)
    place = iota((look_cap, held), 1)
    picks = []
    for source in range(device_count):
        mine = jnp.where(slot == rank[source : source + 1], local[source : source + 1], 0)
        wanted = jnp.sum(mine, axis=1, keepdims=True)
        picks.append(flags(place == wanted))
    pick = jnp.concatenate(picks, axis=0)
    for n, copy in enumerate(copies):
        copy.wait()
        cols = slice(n * width, (n + 1) * width)
        out_ref[:, cols] = dot(pick, table_ref[:, cols]).astype(BF16)


def turned(rows):
    count, length = rows.shape
    return jnp.concatenate([rows, jnp.zeros((length - count, length), F32)], axis=0).T


def plan_kernel(
    me_ref,
    rows_ref,
    packed_ref,
    scales_ref,
    fetched_ref,
    put_ref,
    near_ref,
    far_ref,
    near_slots_ref,
    far_slots_ref,
    columns_ref,
):
    tok_rows = rows_ref.shape[1]
    slots = put_ref.shape[1]
    half = near_ref.shape[0] // (2 * PAIR)
    device_count = 2 * half
    exp_dev = EXPERTS // device_count
    look_cap = slots // device_count
    me, held = me_ref[0], me_ref[1]
    flip = me % 2
    start = me // half * half * exp_dev
    before = earlier(tok_rows)

    row = jnp.broadcast_to(rows_ref[...], (device_count, tok_rows))
    low = iota((device_count, tok_rows), 0) * held
    hit = (row >= low) & (row < low + held)
    rank = jnp.where(hit, dot(flags(hit), before).astype(jnp.int32), -1)
    slot = iota((look_cap, tok_rows), 0)
    put = [(slot == rank[o : o + 1]).astype(F32) for o in range(device_count)]
    put_ref[...] = jnp.concatenate(put, axis=0).T.astype(BF16)

    expert = iota((half * exp_dev, tok_rows), 0) + start
    place = iota((PAIR, tok_rows), 0)
    inside = iota((half * exp_dev, tok_rows), 0)
    flipped = ((inside + flip) & 1) * CAP
    device = inside // exp_dev
    chunk = (inside % exp_dev) // 2
    mine = packed_ref[me]
    other = packed_ref[(me + half) % device_count]
    for far, packed in enumerate((mine, other)):
        ids = [packed[1 + k : 2 + k].astype(jnp.int32) for k in range(TOP)]
        chosen = [ids[k] == expert for k in range(TOP)]
        hit = functools.reduce(jnp.logical_or, chosen)
        rank = jnp.where(hit, dot(flags(hit), before).astype(jnp.int32), -1000)
        lines = [[], []]
        for d in range(half):
            for c in range(2):
                at = d * exp_dev + 2 * c
                one, two = rank[at : at + 1], rank[at + 1 : at + 2]
                upper = jnp.where(flip == 0, one, two)
                lower = jnp.where(flip == 0, two, one) + CAP
                here = ((place < CAP) & (place == upper)) | ((place >= CAP) & (place == lower))
                lines[c].append(here.astype(F32))
        both = [line for pair in zip(*lines) for line in pair]
        pick_ref = far_ref if far else near_ref
        pick_ref[...] = jnp.concatenate(both, axis=0).astype(BF16)
        slot = device * (2 * PAIR) + chunk * PAIR + flipped + rank
        found = [
            jnp.sum(jnp.where(chosen[k], slot + 1, 0), axis=0, keepdims=True) - 1
            for k in range(TOP)
        ]
        slots_out = far_slots_ref if far else near_slots_ref
        found = turned(jnp.concatenate(found, axis=0).astype(F32))
        slots_out[...] = found.astype(jnp.int32)
    columns_ref[...] = turned(
        jnp.concatenate(
            [mine[1 + TOP : 1 + 2 * TOP], other[1 + TOP : 1 + 2 * TOP], scales_ref[...]], axis=0
        )
    )


def pick_slots(pick_ref, state_ref, out_hbm, sent_ref, sem, left, width):
    cols = pl.ds(left, width)
    sent_ref[:, cols] = dot(pick_ref[...], state_ref[:, cols]).astype(BF16)
    copy = pltpu.make_async_copy(
        sent_ref.at[:, cols], out_hbm.at[:, cols], sem.at[left // width]
    )
    copy.start()
    return copy


def state_kernel(
    put_ref, pick_ref, returned_ref, values_ref, columns_ref, state_ref, out_hbm, sent_ref, sem
):
    features = values_ref.shape[1]
    width = features // sem.shape[0]
    copies = []
    for left in range(0, features, width):
        found = dot(put_ref[...], returned_ref[:, left : left + width])
        for b in range(width // BLOCK):
            at = left + b * BLOCK
            scaled = (
                values_ref[:, at : at + BLOCK].astype(F32)
                * columns_ref[:, 2 * TOP + at // BLOCK : 2 * TOP + at // BLOCK + 1]
            )
            state_ref[:, at : at + BLOCK] = (
                scaled + found[:, b * BLOCK : (b + 1) * BLOCK]
            ).astype(BF16)
        copies.append(pick_slots(pick_ref, state_ref, out_hbm, sent_ref, sem, left, width))
    for copy in copies:
        copy.wait()


def pick_kernel(
    pick_ref, state_ref, grad_ref, out_hbm, upper_grad_ref, lower_grad_ref, sent_ref, sem
):
    tok_rows, features = state_ref.shape
    width = features // sem.shape[0]
    copies = [
        pick_slots(pick_ref, state_ref, out_hbm, sent_ref, sem, left, width)
        for left in range(0, features, width)
    ]
    upper_grad_ref[...] = grad_ref[: tok_rows // 2, :]
    lower_grad_ref[...] = grad_ref[tok_rows // 2 :, :]
    for copy in copies:
        copy.wait()


def expert_kernel(after, rows_hbm, *refs):
    wg_hbm, wu_hbm, wd_hbm, out_ref = refs[after : after + 4]
    rows_ref, x_ref, wg_ref, wu_ref, both_ref, wd_ref, hidden_ref, result_ref, sem, rows_sem = refs[
        after + 4 :
    ]
    exp_dev, features, width = wg_hbm.shape
    half = rows_ref.shape[0]
    wide = wg_ref.shape[1]
    rest = width - wide
    up_cuts = ((0, 512), (512, 512), (1024, wide - 1024))
    down_cuts = tuple((at, 512) for at in range(0, features, 512))

    def weight_copies(j):
        copies = []
        for at, size in up_cuts:
            cols = pl.ds(at, size)
            copies.append((wg_hbm.at[j, :, cols], wg_ref.at[:, cols]))
            copies.append((wu_hbm.at[j, :, cols], wu_ref.at[:, cols]))
        for n, hbm in enumerate((wg_hbm, wu_hbm)):
            copies.append((hbm.at[j, :, pl.ds(wide, rest)], both_ref.at[:, pl.ds(n * rest, rest)]))
        for at, size in down_cuts:
            cols = pl.ds(at, size)
            copies.append((wd_hbm.at[j, :, cols], wd_ref.at[:, cols]))
        return [
            pltpu.make_async_copy(src, dst, sem.at[n]) for n, (src, dst) in enumerate(copies)
        ]

    rows_copy = pltpu.make_async_copy(rows_hbm, rows_ref, rows_sem)
    rows_copy.start()
    for copy in weight_copies(0):
        copy.start()
    rows_copy.wait()

    low = iota((PAIR, features), 0) < CAP
    for chunk in range(exp_dev // 2):
        here = slice(chunk * PAIR, (chunk + 1) * PAIR)
        for quad in range(half // 4):
            ones, twos = [], []
            for pair in range(2):
                source = 4 * quad + 2 * pair
                even = rows_ref[source, here, :].astype(F32)
                odd = rows_ref[source + 1, here, :].astype(F32)
                ones.append(jnp.where(low, even, odd))
                twos.append(jnp.where(low, odd, even))
            rows = slice(quad * 2 * PAIR, (quad + 1) * 2 * PAIR)
            x_ref[2 * chunk, rows, :] = jnp.concatenate(ones, axis=0).astype(BF16)
            x_ref[2 * chunk + 1, rows, :] = jnp.concatenate(twos, axis=0).astype(BF16)

    @pl.loop(0, exp_dev)
    def _(j):
        copies = weight_copies(j)
        later = weight_copies(jnp.minimum(j + 1, exp_dev - 1))

        def refill(first, count):
            @pl.when(j + 1 < exp_dev)
            def _():
                for n in range(first, first + count):
                    later[n].start()

        def hide(gate, up, at):
            hidden = gate / (1.0 + jnp.exp(-gate)) * up
            hidden_ref[:, at : at + gate.shape[1]] = hidden.astype(BF16)

        n = 0
        for at, size in up_cuts:
            copies[n].wait()
            copies[n + 1].wait()
            gate = dot(x_ref[j], wg_ref[:, at : at + size])
            up = dot(x_ref[j], wu_ref[:, at : at + size])
            hide(gate, up, at)
            refill(n, 2)
            n += 2
        copies[n].wait()
        copies[n + 1].wait()
        both = dot(x_ref[j], both_ref[...])
        hide(both[:, :rest], both[:, rest:], wide)
        refill(n, 2)
        n += 2
        for at, size in down_cuts:
            copies[n].wait()
            result_ref[j, :, at : at + size] = dot(hidden_ref[...], wd_ref[:, at : at + size])
            refill(n, 1)
            n += 1

    for pair in range(half // 2):
        rows = slice(pair * PAIR, (pair + 1) * PAIR)
        values = [result_ref[j, rows, :] for j in range(exp_dev)]
        for odd in range(2):
            parts = [
                jnp.where(low, values[j + odd], values[j + 1 - odd]) for j in range(0, exp_dev, 2)
            ]
            out_ref[2 * pair + odd] = jnp.concatenate(parts, axis=0).astype(BF16)


def expert_call(name, rows_in, weights, after=()):
    w_gate, w_up, w_down = weights
    exp_dev, features, width = w_gate.shape
    half = rows_in.shape[0]
    rows = half * CAP
    rest = 128
    wide = width - rest
    anywhere = pl.BlockSpec(memory_space=pl.ANY)
    hbm = pl.BlockSpec(memory_space=pltpu.HBM)
    vmem = pl.BlockSpec(memory_space=VMEM)
    return pl.pallas_call(
        functools.partial(expert_kernel, len(after)),
        out_shape=jax.ShapeDtypeStruct((half, exp_dev * CAP, features), BF16),
        in_specs=[hbm] + [anywhere] * len(after) + [hbm] * 3,
        out_specs=vmem,
        scratch_shapes=[
            VMEM(rows_in.shape, BF16),
            VMEM((exp_dev, rows, features), BF16),
            VMEM((features, wide), BF16),
            VMEM((features, wide), BF16),
            VMEM((features, 2 * rest), BF16),
            VMEM((width, features), BF16),
            VMEM((rows, width), BF16),
            VMEM((exp_dev, rows, features), F32),
            pltpu.SemaphoreType.DMA((12,)),
            pltpu.SemaphoreType.DMA,
        ],
        compiler_params=pltpu.CompilerParams(vmem_limit_bytes=28 * 1024 * 1024),
        cost_estimate=pl.CostEstimate(
            flops=12 * exp_dev * rows * features * width,
            bytes_accessed=6 * exp_dev * features * width,
            transcendentals=exp_dev * rows * width,
        ),
        name=name,
    )(in_hbm(rows_in), *[in_hbm(array) for array in after], in_hbm(w_gate), in_hbm(w_up), in_hbm(w_down))


def mix_kernel(first_column, slots_ref, columns_ref, back_ref, *refs):
    mixed_ref, grads_ref = refs[-2:]
    tok_rows = slots_ref.shape[0]
    count, features = back_ref.shape
    grad = jnp.concatenate([ref[...] for ref in refs[:-2]], axis=0)
    column = iota((tok_rows, count), 1)
    inner = lax.dot_general(
        grad, back_ref[...], (((1,), (1,)), ((), ())), preferred_element_type=F32
    )
    total = jnp.zeros((tok_rows, count), F32)
    place = iota((tok_rows, tok_rows), 1)
    wide = jnp.zeros((tok_rows, tok_rows), F32)
    for k in range(TOP):
        here = column == slots_ref[:, k : k + 1]
        weight = columns_ref[:, first_column + k : first_column + k + 1]
        total = total + jnp.where(here, weight, 0.0)
        value = jnp.sum(jnp.where(here, inner, 0.0), axis=1, keepdims=True)
        wide = wide + jnp.where(place == k, value, 0.0)
    high = total.astype(BF16)
    rest = (total - high.astype(F32)).astype(BF16)
    width = 512
    for at in range(0, features, width):
        rows = back_ref[:, at : at + width]
        mixed_ref[:, at : at + width] = (dot(high, rows) + dot(rest, rows)).astype(mixed_ref.dtype)
    grads_ref[...] = wide.T[: grads_ref.shape[0], :]


def swap(array, groups=None):
    return lax.all_to_all(
        array, "expert", split_axis=0, concat_axis=0, tiled=True, axis_index_groups=groups
    )


def near_path(
    block_values,
    block_exps,
    row_ids,
    expert_ids,
    gate_weights,
    table,
    w_gate,
    w_up,
    w_down,
    out_grad,
):
    device_count = lax.axis_size("expert")
    half = device_count // 2
    halves = [list(range(half)), list(range(half, device_count))]
    me = lax.axis_index("expert").astype(jnp.int32)
    tok_rows, features = block_values.shape
    rows_held = table.shape[0]
    look_cap = max(2, 2 * tok_rows // device_count)
    slots = half * 2 * PAIR
    vmem = pl.BlockSpec(memory_space=VMEM)
    smem = pl.BlockSpec(memory_space=pltpu.SMEM)
    anywhere = pl.BlockSpec(memory_space=pl.ANY)
    place = jnp.stack([me, jnp.int32(rows_held)])

    def shape(dims, kind):
        return jax.ShapeDtypeStruct(dims, kind)

    def mirrored(array):
        pairs = [(i, (i + half) % device_count) for i in range(device_count)]
        return lax.ppermute(array, "expert", pairs)

    def ordered(array, *earlier_arrays):
        return pl.pallas_call(
            lambda *refs: None,
            out_shape=shape(array.shape, array.dtype),
            in_specs=[anywhere] * (1 + len(earlier_arrays)),
            out_specs=anywhere,
            input_output_aliases={0: 0},
            compiler_params=SMALL,
            name="ordered",
        )(array, *earlier_arrays)

    split = shape((tok_rows // 2, features), BF16)
    packed = pl.pallas_call(
        pack_kernel,
        out_shape=shape((device_count, 16, tok_rows), F32),
        in_specs=[vmem] * 3,
        out_specs=vmem,
        name="pack",
    )(row_ids[None, :], expert_ids.T, gate_weights.T)
    packed = swap(packed)
    fetched = pl.pallas_call(
        fetch_kernel,
        out_shape=shape((device_count * look_cap, features), BF16),
        in_specs=[smem, vmem, pl.BlockSpec(memory_space=pltpu.HBM)],
        out_specs=vmem,
        scratch_shapes=[VMEM(table.shape, BF16), pltpu.SemaphoreType.DMA((4,))],
        compiler_params=SMALL,
        name="fetch_rows",
    )(place, packed, in_hbm(table))
    returned = swap(fetched.reshape(device_count, look_cap, features))
    put, near_pick, far_pick, near_of, far_of, columns = pl.pallas_call(
        plan_kernel,
        out_shape=(
            shape((tok_rows, device_count * look_cap), BF16),
            shape((slots, tok_rows), BF16),
            shape((slots, tok_rows), BF16),
            shape((tok_rows, tok_rows), jnp.int32),
            shape((tok_rows, tok_rows), jnp.int32),
            shape((tok_rows, tok_rows), F32),
        ),
        in_specs=[smem, vmem, vmem, vmem, anywhere],
        out_specs=(vmem,) * 6,
        compiler_params=SMALL,
        name="plan",
    )(place, row_ids[None, :], packed, jnp.exp2(block_exps.T.astype(F32)), fetched)
    sent_shape = pltpu.HBM((slots, features), BF16)
    sent_scratch = [VMEM((slots, features), BF16), pltpu.SemaphoreType.DMA((4,))]
    state, near_sent = pl.pallas_call(
        state_kernel,
        out_shape=(shape((tok_rows, features), BF16), sent_shape),
        in_specs=[vmem] * 5,
        out_specs=(vmem, anywhere),
        scratch_shapes=sent_scratch,
        compiler_params=SMALL,
        name="token_state",
    )(put, near_pick, returned.reshape(device_count * look_cap, features), block_values, columns)
    other_state = mirrored(state)
    near_rows = swap(near_sent.reshape(half, 2 * PAIR, features), halves)
    far_sent, *grad_halves = pl.pallas_call(
        pick_kernel,
        out_shape=(sent_shape, split, split),
        in_specs=[vmem, vmem, vmem],
        out_specs=(anywhere, vmem, vmem),
        scratch_shapes=sent_scratch,
        compiler_params=SMALL,
        cost_estimate=pl.CostEstimate(
            flops=400_000_000_000, bytes_accessed=4 * slots * features, transcendentals=0
        ),
        name="far_slots",
    )(far_pick, other_state, out_grad)
    other_grads = [mirrored(array) for array in grad_halves]
    far_sent = far_sent.reshape(half, 2 * PAIR, features)
    far_rows = swap(far_sent, halves)

    weights = (w_gate, w_up, w_down)
    near_out = expert_call("near_experts", near_rows, weights, after=(far_sent,))
    near_out = ordered(near_out, other_grads[0])
    far_out = expert_call("far_experts", far_rows, weights, after=(near_out,))
    near_back = swap(near_out, halves)
    far_back = swap(ordered(far_out, near_back, other_grads[1]), halves)

    def mixed_rows(name, first_column, slot_of, back, grads, kind):
        return pl.pallas_call(
            functools.partial(mix_kernel, first_column),
            out_shape=(shape((tok_rows, features), kind), shape((2 * TOP, tok_rows), F32)),
            in_specs=[vmem] * (3 + len(grads)),
            out_specs=(vmem, vmem),
            compiler_params=SMALL,
            name=name,
        )(slot_of, columns, back.reshape(slots, features), *grads)

    near_mixed, near_grads = mixed_rows("mix_near", 0, near_of, near_back, (out_grad,), F32)
    far_mixed, far_grads = mixed_rows("mix_far", TOP, far_of, far_back, other_grads, BF16)
    mixed = (near_mixed + mirrored(far_mixed).astype(F32)).astype(BF16)
    grads = (near_grads + mirrored(far_grads))[:TOP]
    return mixed, grads.T


def expert_work(arrived, w_gate, w_up, w_down):
    gate_act = jnp.einsum("sjcd,jdf->sjcf", arrived, w_gate, preferred_element_type=jnp.float32)
    up_act = jnp.einsum("sjcd,jdf->sjcf", arrived, w_up, preferred_element_type=jnp.float32)
    hidden = (jax.nn.silu(gate_act) * up_act).astype(jnp.bfloat16)
    return jnp.einsum("sjcf,jfd->sjcd", hidden, w_down, preferred_element_type=jnp.float32).astype(
        jnp.bfloat16
    )


def full_path(buffer, w_gate, w_up, w_down, device_count, exp_dev, width_split, features):
    group_count = EXPERTS // exp_dev
    grouped = buffer.reshape(group_count, 1, exp_dev, CAP, features)
    outgoing = jnp.broadcast_to(
        grouped, (group_count, width_split, exp_dev, CAP, features)
    ).reshape(device_count, exp_dev, CAP, features)
    returned_out = lax.all_to_all(
        expert_work(
            lax.all_to_all(outgoing, "expert", split_axis=0, concat_axis=0, tiled=True),
            w_gate,
            w_up,
            w_down,
        ),
        "expert",
        split_axis=0,
        concat_axis=0,
        tiled=True,
    )
    pieces = returned_out.reshape(group_count, width_split, exp_dev, CAP, features).astype(
        jnp.float32
    )
    return jnp.sum(pieces, axis=1).astype(jnp.bfloat16).reshape(EXPERTS * CAP, features)


def far_path(
    block_values,
    block_exps,
    row_ids,
    expert_ids,
    gate_weights,
    table,
    w_gate,
    w_up,
    w_down,
    out_grad,
):
    device_count = lax.axis_size("expert")
    tok_rows = block_values.shape[0]
    features = block_values.shape[1]
    rows_held = table.shape[0]
    look_cap = max(2, 2 * tok_rows // device_count)
    exp_dev = w_gate.shape[0]
    width_split = device_count * exp_dev // EXPERTS
    owners = row_ids // rows_held
    local_row = row_ids % rows_held
    owner_hot = (owners[:, None] == jnp.arange(device_count, dtype=jnp.int32)[None, :]).astype(
        jnp.int32
    )
    owner_rank = jnp.sum((jnp.cumsum(owner_hot, axis=0) - 1) * owner_hot, axis=1)
    placed = owners * look_cap + owner_rank
    wanted = jnp.zeros((device_count * look_cap,), jnp.int32).at[placed].set(local_row)
    requested = lax.all_to_all(
        wanted.reshape(device_count, look_cap), "expert", split_axis=0, concat_axis=0, tiled=True
    )
    fetched = jnp.take(table, requested.reshape(-1), axis=0).reshape(
        device_count, look_cap, features
    )
    rows_returned = lax.all_to_all(fetched, "expert", split_axis=0, concat_axis=0, tiled=True)
    embedded = jnp.take(rows_returned.reshape(device_count * look_cap, features), placed, axis=0)
    scales = jnp.exp2(block_exps.astype(jnp.float32))
    blocks = (
        block_values.reshape(tok_rows, scales.shape[1], -1).astype(jnp.float32) * scales[:, :, None]
    )
    token_state = (blocks.reshape(tok_rows, features) + embedded.astype(jnp.float32)).astype(
        jnp.bfloat16
    )
    flat_ids = expert_ids.reshape(-1)
    expert_hot = (flat_ids[:, None] == jnp.arange(EXPERTS, dtype=jnp.int32)[None, :]).astype(
        jnp.int32
    )
    expert_rank = jnp.sum((jnp.cumsum(expert_hot, axis=0) - 1) * expert_hot, axis=1)
    slot_of = flat_ids * CAP + expert_rank
    token_index = jnp.arange(tok_rows * TOP, dtype=jnp.int32) // TOP
    source = jnp.full((EXPERTS * CAP,), tok_rows, jnp.int32).at[slot_of].set(token_index)
    padded = jnp.concatenate([token_state, jnp.zeros((1, features), jnp.bfloat16)], axis=0)
    buffer = jnp.take(padded, source, axis=0)
    expert_out = full_path(
        buffer, w_gate, w_up, w_down, device_count, exp_dev, width_split, features
    )
    chosen = jnp.take(expert_out, slot_of, axis=0).reshape(tok_rows, TOP, features)
    mixed = jnp.sum(gate_weights[:, :, None] * chosen.astype(jnp.float32), axis=1).astype(
        jnp.bfloat16
    )
    gate_grads = jnp.einsum("tkd,td->tk", chosen, out_grad, preferred_element_type=jnp.float32)
    return (mixed, gate_grads)


def local(*arrays):
    if lax.axis_size("expert") == 16 and arrays[6].shape[0] * 16 == EXPERTS:
        return near_path(*arrays)
    return far_path(*arrays)


def solution(mesh):
    return jax.shard_map(
        local,
        mesh=mesh,
        in_specs=(
            P(("groups", "expert"), None),
            P(("groups", "expert"), None),
            P(("groups", "expert")),
            P(("groups", "expert"), None),
            P(("groups", "expert"), None),
            P("expert", None),
            P("expert", None, None),
            P("expert", None, None),
            P("expert", None, None),
            P(("groups", "expert"), None),
        ),
        out_specs=(P(("groups", "expert"), None), P(("groups", "expert"), None)),
        check_vma=False,
    )
```

```python
import functools

import jax
import jax.numpy as jnp
from jax import lax
from jax.experimental import pallas as pl
from jax.experimental.pallas import tpu as pltpu
from jax.sharding import PartitionSpec as P

EXPERTS = 64
TOP = 4
CAP = 12
BLOCK = 128
PAIR = 2 * CAP
VMEM = pltpu.VMEM
F32 = jnp.float32
BF16 = jnp.bfloat16
SMALL = pltpu.CompilerParams(vmem_limit_bytes=16 * 1024 * 1024)


def dot(a, b):
    return jnp.dot(a, b, preferred_element_type=F32)


def in_hbm(array):
    return pltpu.with_memory_space_constraint(array, pltpu.HBM)


def iota(shape, dimension):
    return lax.broadcasted_iota(jnp.int32, shape, dimension)


def flags(mask):
    return mask.astype(F32).astype(BF16)


def earlier(length):
    return flags(iota((length, length), 0) < iota((length, length), 1))


def repeat_kernel(rows_ref, out_ref):
    for n in range(out_ref.shape[0]):
        out_ref[n] = rows_ref[...]


def fetch_kernel(me_ref, rows_ref, table_hbm, out_ref, table_ref, sem):
    copy = pltpu.make_async_copy(table_hbm, table_ref, sem)
    copy.start()
    device_count, _, tok_rows = rows_ref.shape
    held = table_ref.shape[0]
    look_cap = out_ref.shape[0] // device_count
    local = rows_ref[:, 0, :] - me_ref[0] * held
    hit = (local >= 0) & (local < held)
    rank = dot(flags(hit), earlier(tok_rows)).astype(jnp.int32)
    rank = jnp.where(hit, rank, -1)
    slot = iota((look_cap, tok_rows), 0)
    place = iota((look_cap, held), 1)
    picks = []
    for source in range(device_count):
        mine = jnp.where(slot == rank[source : source + 1], local[source : source + 1], 0)
        wanted = jnp.sum(mine, axis=1, keepdims=True)
        picks.append(flags(place == wanted))
    pick = jnp.concatenate(picks, axis=0)
    copy.wait()
    out_ref[...] = dot(pick, table_ref[...]).astype(BF16)


def turned(rows):
    count, length = rows.shape
    return jnp.concatenate([rows, jnp.zeros((length - count, length), F32)], axis=0).T


def plan_slots(me, ids_ref, pick_ref, slots_ref):
    tok_rows = ids_ref.shape[1]
    half = pick_ref.shape[0] // (2 * PAIR)
    exp_dev = EXPERTS // (2 * half)
    flip = me % 2
    inside = iota((half * exp_dev, tok_rows), 0)
    expert = inside + me // half * half * exp_dev
    place = iota((PAIR, tok_rows), 0)
    ids = ids_ref[...]
    chosen = [ids[k : k + 1] == expert for k in range(TOP)]
    hit = functools.reduce(jnp.logical_or, chosen)
    rank = jnp.where(hit, dot(flags(hit), earlier(tok_rows)).astype(jnp.int32), -1000)
    lines = []
    for at in range(0, half * exp_dev, 2):
        one, two = rank[at : at + 1], rank[at + 1 : at + 2]
        upper = jnp.where(flip == 0, one, two)
        lower = jnp.where(flip == 0, two, one) + CAP
        here = ((place < CAP) & (place == upper)) | ((place >= CAP) & (place == lower))
        lines.append(here.astype(F32))
    pick_ref[...] = jnp.concatenate(lines, axis=0).astype(BF16)
    slot = (inside // 2) * PAIR + ((inside + flip) & 1) * CAP + rank
    found = [
        jnp.sum(jnp.where(chosen[k], slot + 1, 0), axis=0, keepdims=True) - 1 for k in range(TOP)
    ]
    slots_ref[...] = turned(jnp.concatenate(found, axis=0).astype(F32)).astype(jnp.int32)


def near_plan_kernel(
    me_ref,
    rows_ref,
    ids_ref,
    weights_ref,
    scales_ref,
    _,
    put_ref,
    pick_ref,
    slots_ref,
    columns_ref,
    ids_out_ref,
    weights_out_ref,
):
    ids_out_ref[...] = ids_ref[...]
    weights_out_ref[...] = weights_ref[...]
    tok_rows = rows_ref.shape[1]
    me, held = me_ref[0], me_ref[1]
    device_count = pick_ref.shape[0] // PAIR
    look_cap = put_ref.shape[1] // device_count
    row = jnp.broadcast_to(rows_ref[...], (device_count, tok_rows))
    low = iota((device_count, tok_rows), 0) * held
    hit = (row >= low) & (row < low + held)
    rank = jnp.where(hit, dot(flags(hit), earlier(tok_rows)).astype(jnp.int32), -1)
    slot = iota((look_cap, tok_rows), 0)
    put = [(slot == rank[o : o + 1]).astype(F32) for o in range(device_count)]
    put_ref[...] = jnp.concatenate(put, axis=0).T.astype(BF16)
    plan_slots(me, ids_ref, pick_ref, slots_ref)
    columns_ref[...] = turned(jnp.concatenate([weights_ref[...], scales_ref[...]], axis=0))


def far_plan_kernel(me_ref, ids_ref, weights_ref, pick_ref, slots_ref, columns_ref):
    plan_slots(me_ref[0], ids_ref, pick_ref, slots_ref)
    columns_ref[...] = turned(weights_ref[...])


def pick_slots(pick_ref, state_ref, out_hbm, sent_ref, sem, left, width):
    cols = pl.ds(left, width)
    sent_ref[:, cols] = dot(pick_ref[...], state_ref[:, cols]).astype(BF16)
    copy = pltpu.make_async_copy(
        sent_ref.at[:, cols], out_hbm.at[:, cols], sem.at[left // width]
    )
    copy.start()
    return copy


def state_kernel(
    put_ref, pick_ref, returned_ref, values_ref, columns_ref, _, state_ref, out_hbm, sent_ref, sem
):
    features = values_ref.shape[1]
    width = features // sem.shape[0]
    copies = []
    for left in range(0, features, width):
        found = dot(put_ref[...], returned_ref[:, left : left + width])
        for b in range(width // BLOCK):
            at = left + b * BLOCK
            scaled = (
                values_ref[:, at : at + BLOCK].astype(F32)
                * columns_ref[:, TOP + at // BLOCK : TOP + at // BLOCK + 1]
            )
            state_ref[:, at : at + BLOCK] = (
                scaled + found[:, b * BLOCK : (b + 1) * BLOCK]
            ).astype(BF16)
        copies.append(pick_slots(pick_ref, state_ref, out_hbm, sent_ref, sem, left, width))
    for copy in copies:
        copy.wait()


def pick_kernel(pick_ref, state_ref, out_hbm, sent_ref, sem):
    features = state_ref.shape[1]
    width = features // sem.shape[0]
    copies = [
        pick_slots(pick_ref, state_ref, out_hbm, sent_ref, sem, left, width)
        for left in range(0, features, width)
    ]
    for copy in copies:
        copy.wait()


def expert_kernel(after, rows_hbm, *refs):
    wg_hbm, wu_hbm, wd_hbm, out_ref = refs[after : after + 4]
    rows_ref, x_ref, wg_ref, wu_ref, both_ref, wd_ref, hidden_ref, result_ref, sem, rows_sem = refs[
        after + 4 :
    ]
    exp_dev, features, width = wg_hbm.shape
    half = rows_ref.shape[0]
    held = wg_ref.shape[0]
    wide = wg_ref.shape[2]
    rest = width - wide
    up_cuts = ((0, 512), (512, 512), (1024, wide - 1024))
    down_cuts = tuple((at, 512) for at in range(0, features, 512))

    def weight_copies(j, place):
        copies = []
        for at, size in up_cuts:
            cols = pl.ds(at, size)
            copies.append((wg_hbm.at[j, :, cols], wg_ref.at[place, :, cols]))
            copies.append((wu_hbm.at[j, :, cols], wu_ref.at[place, :, cols]))
        for n, hbm in enumerate((wg_hbm, wu_hbm)):
            last = both_ref.at[place, :, pl.ds(n * rest, rest)]
            copies.append((hbm.at[j, :, pl.ds(wide, rest)], last))
        for at, size in down_cuts:
            cols = pl.ds(at, size)
            copies.append((wd_hbm.at[j, :, cols], wd_ref.at[place, :, cols]))
        return [
            pltpu.make_async_copy(src, dst, sem.at[place, n])
            for n, (src, dst) in enumerate(copies)
        ]

    rows_copy = pltpu.make_async_copy(rows_hbm, rows_ref, rows_sem)
    rows_copy.start()
    for j in range(held):
        for copy in weight_copies(j, j):
            copy.start()
    rows_copy.wait()

    low = iota((PAIR, features), 0) < CAP
    for chunk in range(exp_dev // 2):
        here = slice(chunk * PAIR, (chunk + 1) * PAIR)
        for quad in range(half // 4):
            ones, twos = [], []
            for pair in range(2):
                source = 4 * quad + 2 * pair
                even = rows_ref[source, here, :].astype(F32)
                odd = rows_ref[source + 1, here, :].astype(F32)
                ones.append(jnp.where(low, even, odd))
                twos.append(jnp.where(low, odd, even))
            rows = slice(quad * 2 * PAIR, (quad + 1) * 2 * PAIR)
            x_ref[2 * chunk, rows, :] = jnp.concatenate(ones, axis=0).astype(BF16)
            x_ref[2 * chunk + 1, rows, :] = jnp.concatenate(twos, axis=0).astype(BF16)

    @pl.loop(0, exp_dev)
    def _(j):
        place = j % held
        copies = weight_copies(j, place)
        later = weight_copies(jnp.minimum(j + held, exp_dev - 1), place)

        def refill(first, count):
            @pl.when(j + held < exp_dev)
            def _():
                for n in range(first, first + count):
                    later[n].start()

        def hide(gate, up, at):
            hidden = gate / (1.0 + jnp.exp(-gate)) * up
            hidden_ref[:, at : at + gate.shape[1]] = hidden.astype(BF16)

        n = 0
        for at, size in up_cuts:
            copies[n].wait()
            copies[n + 1].wait()
            gate = dot(x_ref[j], wg_ref[place, :, at : at + size])
            up = dot(x_ref[j], wu_ref[place, :, at : at + size])
            hide(gate, up, at)
            refill(n, 2)
            n += 2
        copies[n].wait()
        copies[n + 1].wait()
        both = dot(x_ref[j], both_ref[place])
        hide(both[:, :rest], both[:, rest:], wide)
        refill(n, 2)
        n += 2
        for at, size in down_cuts:
            copies[n].wait()
            result_ref[j, :, at : at + size] = dot(
                hidden_ref[...], wd_ref[place, :, at : at + size]
            )
            refill(n, 1)
            n += 1

    for pair in range(half // 2):
        rows = slice(pair * PAIR, (pair + 1) * PAIR)
        values = [result_ref[j, rows, :] for j in range(exp_dev)]
        for odd in range(2):
            parts = [
                jnp.where(low, values[j + odd], values[j + 1 - odd]) for j in range(0, exp_dev, 2)
            ]
            out_ref[2 * pair + odd] = jnp.concatenate(parts, axis=0).astype(BF16)


def expert_call(name, rows_in, weights, after=()):
    w_gate, w_up, w_down = weights
    exp_dev, features, width = w_gate.shape
    half = rows_in.shape[0]
    rows = half * CAP
    held = 2
    rest = 128
    wide = width - rest
    anywhere = pl.BlockSpec(memory_space=pl.ANY)
    hbm = pl.BlockSpec(memory_space=pltpu.HBM)
    vmem = pl.BlockSpec(memory_space=VMEM)
    return pl.pallas_call(
        functools.partial(expert_kernel, len(after)),
        out_shape=pltpu.HBM((half, exp_dev * CAP, features), BF16),
        in_specs=[hbm] + [anywhere] * len(after) + [hbm] * 3,
        out_specs=vmem,
        scratch_shapes=[
            VMEM(rows_in.shape, BF16),
            VMEM((exp_dev, rows, features), BF16),
            VMEM((held, features, wide), BF16),
            VMEM((held, features, wide), BF16),
            VMEM((held, features, 2 * rest), BF16),
            VMEM((held, width, features), BF16),
            VMEM((rows, width), BF16),
            VMEM((exp_dev, rows, features), F32),
            pltpu.SemaphoreType.DMA((held, 12)),
            pltpu.SemaphoreType.DMA,
        ],
        compiler_params=pltpu.CompilerParams(vmem_limit_bytes=46 * 1024 * 1024),
        cost_estimate=pl.CostEstimate(
            flops=12 * exp_dev * rows * features * width,
            bytes_accessed=6 * exp_dev * features * width,
            transcendentals=exp_dev * rows * width,
        ),
        name=name,
    )(in_hbm(rows_in), *[in_hbm(array) for array in after], in_hbm(w_gate), in_hbm(w_up), in_hbm(w_down))


def mix_kernel(after, slots_ref, columns_ref, back_ref, grad_ref, *refs):
    refs = refs[after:]
    mixed_ref, grads_ref = refs[-2:]
    tok_rows, features = grad_ref.shape
    count = back_ref.shape[0]
    column = iota((tok_rows, count), 1)
    inner = lax.dot_general(
        grad_ref[...], back_ref[...], (((1,), (1,)), ((), ())), preferred_element_type=F32
    )
    total = jnp.zeros((tok_rows, count), F32)
    place = iota((tok_rows, tok_rows), 1)
    wide = jnp.zeros((tok_rows, tok_rows), F32)
    for k in range(TOP):
        here = column == slots_ref[:, k : k + 1]
        total = total + jnp.where(here, columns_ref[:, k : k + 1], 0.0)
        value = jnp.sum(jnp.where(here, inner, 0.0), axis=1, keepdims=True)
        wide = wide + jnp.where(place == k, value, 0.0)
    high = total.astype(BF16)
    rest = (total - high.astype(F32)).astype(BF16)
    width = 512
    for at in range(0, features, width):
        cols = slice(at, at + width)
        value = dot(high, back_ref[:, cols]) + dot(rest, back_ref[:, cols])
        if len(refs) > 2:
            value = value + refs[0][:, cols].astype(F32)
        mixed_ref[:, cols] = value.astype(BF16)
    lines = grads_ref.shape[0]
    grads = wide.T[:lines, :]
    if len(refs) > 2:
        grads = grads + refs[1][:lines, :]
    grads_ref[...] = grads


def after_far_kernel(sent_hbm, far_hbm, grad_ref, sent_out_hbm, grad_out_ref):
    grad_out_ref[...] = grad_ref[...]


def swap(array, groups=None):
    return lax.all_to_all(
        array, "expert", split_axis=0, concat_axis=0, tiled=True, axis_index_groups=groups
    )


def near_path(
    block_values,
    block_exps,
    row_ids,
    expert_ids,
    gate_weights,
    table,
    w_gate,
    w_up,
    w_down,
    out_grad,
):
    device_count = lax.axis_size("expert")
    half = device_count // 2
    halves = [list(range(half)), list(range(half, device_count))]
    me = lax.axis_index("expert").astype(jnp.int32)
    tok_rows, features = block_values.shape
    rows_held = table.shape[0]
    look_cap = max(2, 2 * tok_rows // device_count)
    slots = half * 2 * PAIR
    vmem = pl.BlockSpec(memory_space=VMEM)
    smem = pl.BlockSpec(memory_space=pltpu.SMEM)
    anywhere = pl.BlockSpec(memory_space=pl.ANY)
    place = jnp.stack([me, jnp.int32(rows_held)])

    def shape(dims, kind):
        return jax.ShapeDtypeStruct(dims, kind)

    def mirrored(array):
        pairs = [(i, (i + half) % device_count) for i in range(device_count)]
        return lax.ppermute(array, "expert", pairs)

    def ordered(array, *earlier_arrays, flops=0):
        return pl.pallas_call(
            lambda *refs: None,
            out_shape=shape(array.shape, array.dtype),
            in_specs=[anywhere] * (1 + len(earlier_arrays)),
            out_specs=anywhere,
            input_output_aliases={0: 0},
            compiler_params=SMALL,
            cost_estimate=pl.CostEstimate(flops=flops, bytes_accessed=0, transcendentals=0),
            name="ordered",
        )(array, *earlier_arrays)

    all_rows = pl.pallas_call(
        repeat_kernel,
        out_shape=shape((device_count, 1, tok_rows), jnp.int32),
        in_specs=[vmem],
        out_specs=vmem,
        name="repeat_rows",
    )(row_ids[None, :])
    fetched = pl.pallas_call(
        fetch_kernel,
        out_shape=shape((device_count * look_cap, features), BF16),
        in_specs=[smem, vmem, pl.BlockSpec(memory_space=pltpu.HBM)],
        out_specs=vmem,
        scratch_shapes=[VMEM(table.shape, BF16), pltpu.SemaphoreType.DMA],
        compiler_params=SMALL,
        name="fetch_rows",
    )(place, swap(all_rows), in_hbm(table))
    returned = swap(fetched.reshape(device_count, look_cap, features))
    turned_ids, turned_weights = expert_ids.T, gate_weights.T
    pick_shape = shape((slots, tok_rows), BF16)
    square = (tok_rows, tok_rows)
    put, near_pick, near_of, near_columns, sent_ids, sent_weights = pl.pallas_call(
        near_plan_kernel,
        out_shape=(
            shape((tok_rows, device_count * look_cap), BF16),
            pick_shape,
            shape(square, jnp.int32),
            shape(square, F32),
            shape(turned_ids.shape, jnp.int32),
            shape(turned_weights.shape, F32),
        ),
        in_specs=[smem, vmem, vmem, vmem, vmem, anywhere],
        out_specs=(vmem,) * 6,
        compiler_params=SMALL,
        name="near_plan",
    )(
        place,
        row_ids[None, :],
        turned_ids,
        turned_weights,
        jnp.exp2(block_exps.T.astype(F32)),
        fetched,
    )
    far_pick, far_of, far_columns = pl.pallas_call(
        far_plan_kernel,
        out_shape=(pick_shape, shape(square, jnp.int32), shape(square, F32)),
        in_specs=[smem, vmem, vmem],
        out_specs=(vmem,) * 3,
        compiler_params=SMALL,
        name="far_plan",
    )(place, mirrored(sent_ids), mirrored(sent_weights))

    sent_shape = pltpu.HBM((slots, features), BF16)
    sent_scratch = [VMEM((slots, features), BF16), pltpu.SemaphoreType.DMA((4,))]
    state, near_sent = pl.pallas_call(
        state_kernel,
        out_shape=(shape((tok_rows, features), BF16), sent_shape),
        in_specs=[vmem] * 5 + [anywhere],
        out_specs=(vmem, anywhere),
        scratch_shapes=sent_scratch,
        compiler_params=SMALL,
        name="token_state",
    )(
        put,
        near_pick,
        returned.reshape(device_count * look_cap, features),
        block_values,
        near_columns,
        far_pick,
    )
    far_sent = pl.pallas_call(
        pick_kernel,
        out_shape=sent_shape,
        in_specs=[vmem, vmem],
        out_specs=anywhere,
        scratch_shapes=sent_scratch,
        compiler_params=SMALL,
        name="far_slots",
    )(far_pick, mirrored(state))
    rows_shape = (half, 2 * PAIR, features)
    far_rows = swap(far_sent.reshape(rows_shape), halves)
    near_sent, sent_grad = pl.pallas_call(
        after_far_kernel,
        out_shape=(shape(rows_shape, BF16), shape((tok_rows, features), BF16)),
        in_specs=[anywhere, anywhere, vmem],
        out_specs=(anywhere, vmem),
        input_output_aliases={0: 0},
        compiler_params=SMALL,
        name="after_far",
    )(in_hbm(near_sent.reshape(rows_shape)), in_hbm(far_rows), out_grad)
    near_rows = swap(near_sent, halves)

    weights = (w_gate, w_up, w_down)
    other_grad = mirrored(sent_grad)
    far_out = expert_call("far_experts", far_rows, weights)
    far_out = ordered(in_hbm(far_out), in_hbm(near_rows), other_grad)
    near_out = expert_call("near_experts", near_rows, weights, after=(far_out,))
    far_back = swap(far_out, halves)

    def mixed_rows(name, slot_of, columns, back, grad, lines, more=(), after=()):
        return pl.pallas_call(
            functools.partial(mix_kernel, len(after)),
            out_shape=(shape((tok_rows, features), BF16), shape((lines, tok_rows), F32)),
            in_specs=[vmem] * 4 + [anywhere] * len(after) + [vmem] * len(more),
            out_specs=(vmem, vmem),
            compiler_params=SMALL,
            name=name,
        )(slot_of, columns, back.reshape(slots, features), grad, *after, *more)

    far_mixed, far_grads = mixed_rows(
        "mix_far", far_of, far_columns, far_back, other_grad, 2 * TOP, after=(in_hbm(near_out),)
    )
    near_back = swap(ordered(in_hbm(near_out), far_mixed), halves)
    mixed, grads = mixed_rows(
        "mix_near",
        near_of,
        near_columns,
        near_back,
        out_grad,
        TOP,
        more=(ordered(mirrored(far_mixed), flops=400_000_000_000), mirrored(far_grads)),
    )
    return mixed, grads.T


def expert_work(arrived, w_gate, w_up, w_down):
    gate_act = jnp.einsum("sjcd,jdf->sjcf", arrived, w_gate, preferred_element_type=jnp.float32)
    up_act = jnp.einsum("sjcd,jdf->sjcf", arrived, w_up, preferred_element_type=jnp.float32)
    hidden = (jax.nn.silu(gate_act) * up_act).astype(jnp.bfloat16)
    return jnp.einsum("sjcf,jfd->sjcd", hidden, w_down, preferred_element_type=jnp.float32).astype(
        jnp.bfloat16
    )


def full_path(buffer, w_gate, w_up, w_down, device_count, exp_dev, width_split, features):
    group_count = EXPERTS // exp_dev
    grouped = buffer.reshape(group_count, 1, exp_dev, CAP, features)
    outgoing = jnp.broadcast_to(
        grouped, (group_count, width_split, exp_dev, CAP, features)
    ).reshape(device_count, exp_dev, CAP, features)
    returned_out = lax.all_to_all(
        expert_work(
            lax.all_to_all(outgoing, "expert", split_axis=0, concat_axis=0, tiled=True),
            w_gate,
            w_up,
            w_down,
        ),
        "expert",
        split_axis=0,
        concat_axis=0,
        tiled=True,
    )
    pieces = returned_out.reshape(group_count, width_split, exp_dev, CAP, features).astype(
        jnp.float32
    )
    return jnp.sum(pieces, axis=1).astype(jnp.bfloat16).reshape(EXPERTS * CAP, features)


def far_path(
    block_values,
    block_exps,
    row_ids,
    expert_ids,
    gate_weights,
    table,
    w_gate,
    w_up,
    w_down,
    out_grad,
):
    device_count = lax.axis_size("expert")
    tok_rows = block_values.shape[0]
    features = block_values.shape[1]
    rows_held = table.shape[0]
    look_cap = max(2, 2 * tok_rows // device_count)
    exp_dev = w_gate.shape[0]
    width_split = device_count * exp_dev // EXPERTS
    owners = row_ids // rows_held
    local_row = row_ids % rows_held
    owner_hot = (owners[:, None] == jnp.arange(device_count, dtype=jnp.int32)[None, :]).astype(
        jnp.int32
    )
    owner_rank = jnp.sum((jnp.cumsum(owner_hot, axis=0) - 1) * owner_hot, axis=1)
    placed = owners * look_cap + owner_rank
    wanted = jnp.zeros((device_count * look_cap,), jnp.int32).at[placed].set(local_row)
    requested = lax.all_to_all(
        wanted.reshape(device_count, look_cap), "expert", split_axis=0, concat_axis=0, tiled=True
    )
    fetched = jnp.take(table, requested.reshape(-1), axis=0).reshape(
        device_count, look_cap, features
    )
    rows_returned = lax.all_to_all(fetched, "expert", split_axis=0, concat_axis=0, tiled=True)
    embedded = jnp.take(rows_returned.reshape(device_count * look_cap, features), placed, axis=0)
    scales = jnp.exp2(block_exps.astype(jnp.float32))
    blocks = (
        block_values.reshape(tok_rows, scales.shape[1], -1).astype(jnp.float32) * scales[:, :, None]
    )
    token_state = (blocks.reshape(tok_rows, features) + embedded.astype(jnp.float32)).astype(
        jnp.bfloat16
    )
    flat_ids = expert_ids.reshape(-1)
    expert_hot = (flat_ids[:, None] == jnp.arange(EXPERTS, dtype=jnp.int32)[None, :]).astype(
        jnp.int32
    )
    expert_rank = jnp.sum((jnp.cumsum(expert_hot, axis=0) - 1) * expert_hot, axis=1)
    slot_of = flat_ids * CAP + expert_rank
    token_index = jnp.arange(tok_rows * TOP, dtype=jnp.int32) // TOP
    source = jnp.full((EXPERTS * CAP,), tok_rows, jnp.int32).at[slot_of].set(token_index)
    padded = jnp.concatenate([token_state, jnp.zeros((1, features), jnp.bfloat16)], axis=0)
    buffer = jnp.take(padded, source, axis=0)
    expert_out = full_path(
        buffer, w_gate, w_up, w_down, device_count, exp_dev, width_split, features
    )
    chosen = jnp.take(expert_out, slot_of, axis=0).reshape(tok_rows, TOP, features)
    mixed = jnp.sum(gate_weights[:, :, None] * chosen.astype(jnp.float32), axis=1).astype(
        jnp.bfloat16
    )
    gate_grads = jnp.einsum("tkd,td->tk", chosen, out_grad, preferred_element_type=jnp.float32)
    return (mixed, gate_grads)


def local(*arrays):
    if lax.axis_size("expert") == 16 and arrays[6].shape[0] * 16 == EXPERTS:
        return near_path(*arrays)
    return far_path(*arrays)


def solution(mesh):
    return jax.shard_map(
        local,
        mesh=mesh,
        in_specs=(
            P(("groups", "expert"), None),
            P(("groups", "expert"), None),
            P(("groups", "expert")),
            P(("groups", "expert"), None),
            P(("groups", "expert"), None),
            P("expert", None),
            P("expert", None, None),
            P("expert", None, None),
            P("expert", None, None),
            P(("groups", "expert"), None),
        ),
        out_specs=(P(("groups", "expert"), None), P(("groups", "expert"), None)),
        check_vma=False,
    )
```

```python
import functools

import jax
import jax.numpy as jnp
from jax import lax
from jax.experimental import pallas as pl
from jax.experimental.pallas import tpu as pltpu
from jax.sharding import PartitionSpec as P

EXPERTS = 64
TOP = 4
CAP = 12
BLOCK = 128
PAIR = 2 * CAP
VMEM = pltpu.VMEM
F32 = jnp.float32
BF16 = jnp.bfloat16
SMALL = pltpu.CompilerParams(vmem_limit_bytes=16 * 1024 * 1024)


def dot(a, b):
    return jnp.dot(a, b, preferred_element_type=F32)


def in_hbm(array):
    return pltpu.with_memory_space_constraint(array, pltpu.HBM)


def iota(shape, dimension):
    return lax.broadcasted_iota(jnp.int32, shape, dimension)


def flags(mask):
    return mask.astype(F32).astype(BF16)


def earlier(length):
    return flags(iota((length, length), 0) < iota((length, length), 1))


def repeat_kernel(rows_ref, out_ref):
    for n in range(out_ref.shape[0]):
        out_ref[n] = rows_ref[...]


def fetch_kernel(me_ref, rows_ref, table_hbm, out_ref, table_ref, sem):
    copy = pltpu.make_async_copy(table_hbm, table_ref, sem)
    copy.start()
    device_count, _, tok_rows = rows_ref.shape
    held = table_ref.shape[0]
    look_cap = out_ref.shape[0] // device_count
    local = rows_ref[:, 0, :] - me_ref[0] * held
    hit = (local >= 0) & (local < held)
    rank = dot(flags(hit), earlier(tok_rows)).astype(jnp.int32)
    rank = jnp.where(hit, rank, -1)
    slot = iota((look_cap, tok_rows), 0)
    place = iota((look_cap, held), 1)
    picks = []
    for source in range(device_count):
        mine = jnp.where(slot == rank[source : source + 1], local[source : source + 1], 0)
        wanted = jnp.sum(mine, axis=1, keepdims=True)
        picks.append(flags(place == wanted))
    pick = jnp.concatenate(picks, axis=0)
    copy.wait()
    out_ref[...] = dot(pick, table_ref[...]).astype(BF16)


def turned(rows):
    count, length = rows.shape
    return jnp.concatenate([rows, jnp.zeros((length - count, length), F32)], axis=0).T


def plan_slots(me, ids_ref, pick_ref, slots_ref):
    tok_rows = ids_ref.shape[1]
    half = pick_ref.shape[0] // (2 * PAIR)
    exp_dev = EXPERTS // (2 * half)
    flip = me % 2
    inside = iota((half * exp_dev, tok_rows), 0)
    expert = inside + me // half * half * exp_dev
    place = iota((PAIR, tok_rows), 0)
    ids = ids_ref[...]
    chosen = [ids[k : k + 1] == expert for k in range(TOP)]
    hit = functools.reduce(jnp.logical_or, chosen)
    rank = jnp.where(hit, dot(flags(hit), earlier(tok_rows)).astype(jnp.int32), -1000)
    lines = []
    for at in range(0, half * exp_dev, 2):
        one, two = rank[at : at + 1], rank[at + 1 : at + 2]
        upper = jnp.where(flip == 0, one, two)
        lower = jnp.where(flip == 0, two, one) + CAP
        here = ((place < CAP) & (place == upper)) | ((place >= CAP) & (place == lower))
        lines.append(here.astype(F32))
    pick_ref[...] = jnp.concatenate(lines, axis=0).astype(BF16)
    slot = (inside // 2) * PAIR + ((inside + flip) & 1) * CAP + rank
    found = [
        jnp.sum(jnp.where(chosen[k], slot + 1, 0), axis=0, keepdims=True) - 1 for k in range(TOP)
    ]
    slots_ref[...] = turned(jnp.concatenate(found, axis=0).astype(F32)).astype(jnp.int32)


def near_plan_kernel(
    me_ref,
    rows_ref,
    ids_ref,
    weights_ref,
    scales_ref,
    _,
    put_ref,
    pick_ref,
    slots_ref,
    columns_ref,
    ids_out_ref,
    weights_out_ref,
):
    ids_out_ref[...] = ids_ref[...]
    weights_out_ref[...] = weights_ref[...]
    tok_rows = rows_ref.shape[1]
    me, held = me_ref[0], me_ref[1]
    device_count = pick_ref.shape[0] // PAIR
    look_cap = put_ref.shape[1] // device_count
    row = jnp.broadcast_to(rows_ref[...], (device_count, tok_rows))
    low = iota((device_count, tok_rows), 0) * held
    hit = (row >= low) & (row < low + held)
    rank = jnp.where(hit, dot(flags(hit), earlier(tok_rows)).astype(jnp.int32), -1)
    slot = iota((look_cap, tok_rows), 0)
    put = [(slot == rank[o : o + 1]).astype(F32) for o in range(device_count)]
    put_ref[...] = jnp.concatenate(put, axis=0).T.astype(BF16)
    plan_slots(me, ids_ref, pick_ref, slots_ref)
    columns_ref[...] = turned(jnp.concatenate([weights_ref[...], scales_ref[...]], axis=0))


def far_plan_kernel(me_ref, ids_ref, weights_ref, pick_ref, slots_ref, columns_ref):
    plan_slots(me_ref[0], ids_ref, pick_ref, slots_ref)
    columns_ref[...] = turned(weights_ref[...])


def state_kernel(
    me_ref, put_ref, pick_ref, returned_ref, values_ref, columns_ref, _, state_ref, *refs
):
    out_hbms, (sent_ref, sem) = refs[:-2], refs[-2:]
    features = values_ref.shape[1]
    half = len(out_hbms)
    block = sent_ref.shape[0] // half
    width = 512
    for left in range(0, features, width):
        found = dot(put_ref[...], returned_ref[:, left : left + width])
        for b in range(width // BLOCK):
            at = left + b * BLOCK
            scaled = (
                values_ref[:, at : at + BLOCK].astype(F32)
                * columns_ref[:, TOP + at // BLOCK : TOP + at // BLOCK + 1]
            )
            state_ref[:, at : at + BLOCK] = (
                scaled + found[:, b * BLOCK : (b + 1) * BLOCK]
            ).astype(BF16)
        cols = slice(left, left + width)
        sent_ref[:, cols] = dot(pick_ref[...], state_ref[:, cols]).astype(BF16)
    copies = []
    for k in range(half):
        partner = (me_ref[0] & (half - 1)) ^ k
        rows = pl.ds(pl.multiple_of(partner * block, block), block)
        copies.append(pltpu.make_async_copy(sent_ref.at[rows], out_hbms[k], sem.at[k]))
        copies[-1].start()
    for copy in copies:
        copy.wait()


def pick_kernel(
    pick_ref, state_ref, grad_ref, out_hbm, upper_grad_ref, lower_grad_ref, sent_ref, sem
):
    tok_rows, features = state_ref.shape
    width = features // sem.shape[0]
    copies = []
    for n in range(sem.shape[0]):
        cols = pl.ds(n * width, width)
        sent_ref[:, cols] = dot(pick_ref[...], state_ref[:, cols]).astype(BF16)
        copies.append(
            pltpu.make_async_copy(sent_ref.at[:, cols], out_hbm.at[:, cols], sem.at[n])
        )
        copies[-1].start()
    upper_grad_ref[...] = grad_ref[: tok_rows // 2, :]
    lower_grad_ref[...] = grad_ref[tok_rows // 2 :, :]
    for copy in copies:
        copy.wait()


def expert_kernel(parts, after, me_ref, *refs):
    rows_hbms = refs[:parts]
    wg_hbm, wu_hbm, wd_hbm, out_ref = refs[parts + after : parts + after + 4]
    rows_ref, x_ref, wg_ref, wu_ref, wd_ref, hidden_ref, result_ref, sem, rows_sem = refs[
        parts + after + 4 :
    ]
    exp_dev, features, width = wg_hbm.shape
    held = wg_ref.shape[0]
    half = rows_ref.shape[0]
    up_cuts = ((0, 512), (512, 512), (1024, width - 1024))
    down_cuts = tuple((at, 512) for at in range(0, features, 512))

    def weight_copies(j, place):
        copies = []
        for at, size in up_cuts:
            cols = pl.ds(at, size)
            copies.append((wg_hbm.at[j, :, cols], wg_ref.at[place, :, cols]))
            copies.append((wu_hbm.at[j, :, cols], wu_ref.at[place, :, cols]))
        for at, size in down_cuts:
            cols = pl.ds(at, size)
            copies.append((wd_hbm.at[j, :, cols], wd_ref.at[place, :, cols]))
        return [
            pltpu.make_async_copy(src, dst, sem.at[place, n])
            for n, (src, dst) in enumerate(copies)
        ]

    if parts == 1:
        rows_copies = [pltpu.make_async_copy(rows_hbms[0], rows_ref, rows_sem.at[0])]
    else:
        rows_copies = [
            pltpu.make_async_copy(
                rows_hbms[k], rows_ref.at[(me_ref[0] & (half - 1)) ^ k], rows_sem.at[k]
            )
            for k in range(parts)
        ]
    for copy in rows_copies:
        copy.start()
    for j in range(held):
        for copy in weight_copies(j, j):
            copy.start()
    for copy in rows_copies:
        copy.wait()

    low = iota((PAIR, features), 0) < CAP
    for chunk in range(exp_dev // 2):
        here = slice(chunk * PAIR, (chunk + 1) * PAIR)
        for quad in range(half // 4):
            ones, twos = [], []
            for pair in range(2):
                source = 4 * quad + 2 * pair
                even = rows_ref[source, here, :].astype(F32)
                odd = rows_ref[source + 1, here, :].astype(F32)
                ones.append(jnp.where(low, even, odd))
                twos.append(jnp.where(low, odd, even))
            rows = slice(quad * 2 * PAIR, (quad + 1) * 2 * PAIR)
            x_ref[2 * chunk, rows, :] = jnp.concatenate(ones, axis=0).astype(BF16)
            x_ref[2 * chunk + 1, rows, :] = jnp.concatenate(twos, axis=0).astype(BF16)

    @pl.loop(0, exp_dev)
    def _(j):
        place = j % held
        copies = weight_copies(j, place)
        later = weight_copies(jnp.minimum(j + held, exp_dev - 1), place)

        def refill(first, count):
            @pl.when(j + held < exp_dev)
            def _():
                for n in range(first, first + count):
                    later[n].start()

        def hide(gate, up, at):
            hidden = gate / (1.0 + jnp.exp(-gate)) * up
            hidden_ref[:, at : at + gate.shape[1]] = hidden.astype(BF16)

        n = 0
        for at, size in up_cuts:
            copies[n].wait()
            copies[n + 1].wait()
            gate = dot(x_ref[j], wg_ref[place, :, at : at + size])
            up = dot(x_ref[j], wu_ref[place, :, at : at + size])
            hide(gate, up, at)
            refill(n, 2)
            n += 2
        for at, size in down_cuts:
            copies[n].wait()
            result_ref[j, :, at : at + size] = dot(
                hidden_ref[...], wd_ref[place, :, at : at + size]
            )
            refill(n, 1)
            n += 1

    for pair in range(half // 2):
        rows = slice(pair * PAIR, (pair + 1) * PAIR)
        values = [result_ref[j, rows, :] for j in range(exp_dev)]
        for odd in range(2):
            parts = [
                jnp.where(low, values[j + odd], values[j + 1 - odd]) for j in range(0, exp_dev, 2)
            ]
            out_ref[2 * pair + odd] = jnp.concatenate(parts, axis=0).astype(BF16)


def expert_call(name, place, rows_in, weights, after=()):
    w_gate, w_up, w_down = weights
    exp_dev, features, width = w_gate.shape
    parts = len(rows_in)
    half = EXPERTS // exp_dev // 2
    rows = half * CAP
    held = 2
    slots = exp_dev * CAP
    anywhere = pl.BlockSpec(memory_space=pl.ANY)
    hbm = pl.BlockSpec(memory_space=pltpu.HBM)
    operands = [in_hbm(array) for array in (*rows_in, *after, w_gate, w_up, w_down)]
    return pl.pallas_call(
        functools.partial(expert_kernel, parts, len(after)),
        out_shape=pltpu.HBM((half, slots, features), BF16),
        in_specs=[pl.BlockSpec(memory_space=pltpu.SMEM)]
        + [hbm] * parts
        + [anywhere] * len(after)
        + [hbm] * 3,
        out_specs=pl.BlockSpec(memory_space=VMEM),
        scratch_shapes=[
            VMEM((half, slots, features), BF16),
            VMEM((exp_dev, rows, features), BF16),
            VMEM((held, features, width), BF16),
            VMEM((held, features, width), BF16),
            VMEM((held, width, features), BF16),
            VMEM((rows, width), BF16),
            VMEM((exp_dev, rows, features), F32),
            pltpu.SemaphoreType.DMA((held, 10)),
            pltpu.SemaphoreType.DMA((half,)),
        ],
        compiler_params=pltpu.CompilerParams(vmem_limit_bytes=46 * 1024 * 1024),
        cost_estimate=pl.CostEstimate(
            flops=12 * exp_dev * rows * features * width,
            bytes_accessed=6 * exp_dev * features * width,
            transcendentals=exp_dev * rows * width,
        ),
        name=name,
    )(place, *operands)


def mix_kernel(slots_ref, columns_ref, back_ref, *refs):
    mixed_ref, grads_ref = refs[-2:]
    tok_rows = slots_ref.shape[0]
    count, features = back_ref.shape
    grad = jnp.concatenate([ref[...] for ref in refs[:-2]], axis=0)
    column = iota((tok_rows, count), 1)
    inner = lax.dot_general(
        grad, back_ref[...], (((1,), (1,)), ((), ())), preferred_element_type=F32
    )
    total = jnp.zeros((tok_rows, count), F32)
    place = iota((tok_rows, tok_rows), 1)
    wide = jnp.zeros((tok_rows, tok_rows), F32)
    for k in range(TOP):
        here = column == slots_ref[:, k : k + 1]
        total = total + jnp.where(here, columns_ref[:, k : k + 1], 0.0)
        value = jnp.sum(jnp.where(here, inner, 0.0), axis=1, keepdims=True)
        wide = wide + jnp.where(place == k, value, 0.0)
    high = total.astype(BF16)
    rest = (total - high.astype(F32)).astype(BF16)
    width = 512
    for at in range(0, features, width):
        rows = back_ref[:, at : at + width]
        mixed_ref[:, at : at + width] = (dot(high, rows) + dot(rest, rows)).astype(mixed_ref.dtype)
    grads_ref[...] = wide.T[: grads_ref.shape[0], :]


def swap(array, groups=None):
    return lax.all_to_all(
        array, "expert", split_axis=0, concat_axis=0, tiled=True, axis_index_groups=groups
    )


def near_path(
    block_values,
    block_exps,
    row_ids,
    expert_ids,
    gate_weights,
    table,
    w_gate,
    w_up,
    w_down,
    out_grad,
):
    device_count = lax.axis_size("expert")
    half = device_count // 2
    halves = [list(range(half)), list(range(half, device_count))]
    me = lax.axis_index("expert").astype(jnp.int32)
    tok_rows, features = block_values.shape
    rows_held = table.shape[0]
    look_cap = max(2, 2 * tok_rows // device_count)
    slots = half * 2 * PAIR
    vmem = pl.BlockSpec(memory_space=VMEM)
    smem = pl.BlockSpec(memory_space=pltpu.SMEM)
    anywhere = pl.BlockSpec(memory_space=pl.ANY)
    place = jnp.stack([me, jnp.int32(rows_held)])

    def shape(dims, kind):
        return jax.ShapeDtypeStruct(dims, kind)

    def mirrored(array):
        pairs = [(i, (i + half) % device_count) for i in range(device_count)]
        return lax.ppermute(array, "expert", pairs)

    def ordered(array, *earlier_arrays, flops=0):
        return pl.pallas_call(
            lambda *refs: None,
            out_shape=shape(array.shape, array.dtype),
            in_specs=[anywhere] * (1 + len(earlier_arrays)),
            out_specs=anywhere,
            input_output_aliases={0: 0},
            compiler_params=SMALL,
            cost_estimate=pl.CostEstimate(flops=flops, bytes_accessed=0, transcendentals=0),
            name="ordered",
        )(array, *earlier_arrays)

    all_rows = pl.pallas_call(
        repeat_kernel,
        out_shape=shape((device_count, 1, tok_rows), jnp.int32),
        in_specs=[vmem],
        out_specs=vmem,
        name="repeat_rows",
    )(row_ids[None, :])
    fetched = pl.pallas_call(
        fetch_kernel,
        out_shape=shape((device_count * look_cap, features), BF16),
        in_specs=[smem, vmem, pl.BlockSpec(memory_space=pltpu.HBM)],
        out_specs=vmem,
        scratch_shapes=[VMEM(table.shape, BF16), pltpu.SemaphoreType.DMA],
        compiler_params=SMALL,
        name="fetch_rows",
    )(place, swap(all_rows), in_hbm(table))
    returned = swap(fetched.reshape(device_count, look_cap, features))
    turned_ids, turned_weights = expert_ids.T, gate_weights.T
    pick_shape = shape((slots, tok_rows), BF16)
    square = (tok_rows, tok_rows)
    put, near_pick, near_of, near_columns, sent_ids, sent_weights = pl.pallas_call(
        near_plan_kernel,
        out_shape=(
            shape((tok_rows, device_count * look_cap), BF16),
            pick_shape,
            shape(square, jnp.int32),
            shape(square, F32),
            shape(turned_ids.shape, jnp.int32),
            shape(turned_weights.shape, F32),
        ),
        in_specs=[smem, vmem, vmem, vmem, vmem, anywhere],
        out_specs=(vmem,) * 6,
        compiler_params=SMALL,
        name="near_plan",
    )(
        place,
        row_ids[None, :],
        turned_ids,
        turned_weights,
        jnp.exp2(block_exps.T.astype(F32)),
        fetched,
    )
    far_pick, far_of, far_columns = pl.pallas_call(
        far_plan_kernel,
        out_shape=(pick_shape, shape(square, jnp.int32), shape(square, F32)),
        in_specs=[smem, vmem, vmem],
        out_specs=(vmem,) * 3,
        compiler_params=SMALL,
        name="far_plan",
    )(place, mirrored(sent_ids), mirrored(sent_weights))

    state, *near_sent = pl.pallas_call(
        state_kernel,
        out_shape=(
            shape((tok_rows, features), BF16),
            *[pltpu.HBM((2 * PAIR, features), BF16)] * half,
        ),
        in_specs=[smem] + [vmem] * 5 + [anywhere],
        out_specs=(vmem,) + (anywhere,) * half,
        scratch_shapes=[VMEM((slots, features), BF16), pltpu.SemaphoreType.DMA((half,))],
        compiler_params=SMALL,
        name="token_state",
    )(
        place,
        put,
        near_pick,
        returned.reshape(device_count * look_cap, features),
        block_values,
        near_columns,
        far_pick,
    )
    split = shape((tok_rows // 2, features), BF16)
    far_sent, *grad_halves = pl.pallas_call(
        pick_kernel,
        out_shape=(pltpu.HBM((slots, features), BF16), split, split),
        in_specs=[vmem, vmem, vmem],
        out_specs=(anywhere, vmem, vmem),
        scratch_shapes=[VMEM((slots, features), BF16), pltpu.SemaphoreType.DMA((4,))],
        compiler_params=SMALL,
        cost_estimate=pl.CostEstimate(
            flops=400_000_000_000, bytes_accessed=4 * slots * features, transcendentals=0
        ),
        name="far_slots",
    )(far_pick, mirrored(state), out_grad)
    near_rows = near_sent[:1] + [
        lax.ppermute(
            near_sent[k],
            "expert",
            [(i, i // half * half + (i % half ^ k)) for i in range(device_count)],
        )
        for k in range(1, half)
    ]
    far_sent = far_sent.reshape(half, 2 * PAIR, features)
    far_rows = swap(far_sent, halves)
    other_grads = [mirrored(array) for array in grad_halves]

    weights = (w_gate, w_up, w_down)
    near_out = expert_call("near_experts", place, near_rows, weights, after=(far_sent,))
    near_out = ordered(in_hbm(near_out), other_grads[0])
    far_out = expert_call("far_experts", place, [far_rows], weights, after=(near_out,))
    near_back = swap(near_out, halves)
    far_back = swap(ordered(in_hbm(far_out), near_back, other_grads[1]), halves)

    def mixed_rows(name, slot_of, columns, back, grads, kind):
        return pl.pallas_call(
            mix_kernel,
            out_shape=(shape((tok_rows, features), kind), shape((2 * TOP, tok_rows), F32)),
            in_specs=[vmem] * (3 + len(grads)),
            out_specs=(vmem, vmem),
            compiler_params=SMALL,
            name=name,
        )(slot_of, columns, back.reshape(slots, features), *grads)

    near_mixed, near_grads = mixed_rows(
        "mix_near", near_of, near_columns, near_back, (out_grad,), F32
    )
    far_mixed, far_grads = mixed_rows(
        "mix_far", far_of, far_columns, far_back, other_grads, BF16
    )
    mixed = (near_mixed + mirrored(far_mixed).astype(F32)).astype(BF16)
    grads = (near_grads + mirrored(far_grads))[:TOP]
    return mixed, grads.T


def expert_work(arrived, w_gate, w_up, w_down):
    gate_act = jnp.einsum("sjcd,jdf->sjcf", arrived, w_gate, preferred_element_type=jnp.float32)
    up_act = jnp.einsum("sjcd,jdf->sjcf", arrived, w_up, preferred_element_type=jnp.float32)
    hidden = (jax.nn.silu(gate_act) * up_act).astype(jnp.bfloat16)
    return jnp.einsum("sjcf,jfd->sjcd", hidden, w_down, preferred_element_type=jnp.float32).astype(
        jnp.bfloat16
    )


def full_path(buffer, w_gate, w_up, w_down, device_count, exp_dev, width_split, features):
    group_count = EXPERTS // exp_dev
    grouped = buffer.reshape(group_count, 1, exp_dev, CAP, features)
    outgoing = jnp.broadcast_to(
        grouped, (group_count, width_split, exp_dev, CAP, features)
    ).reshape(device_count, exp_dev, CAP, features)
    returned_out = lax.all_to_all(
        expert_work(
            lax.all_to_all(outgoing, "expert", split_axis=0, concat_axis=0, tiled=True),
            w_gate,
            w_up,
            w_down,
        ),
        "expert",
        split_axis=0,
        concat_axis=0,
        tiled=True,
    )
    pieces = returned_out.reshape(group_count, width_split, exp_dev, CAP, features).astype(
        jnp.float32
    )
    return jnp.sum(pieces, axis=1).astype(jnp.bfloat16).reshape(EXPERTS * CAP, features)


def far_path(
    block_values,
    block_exps,
    row_ids,
    expert_ids,
    gate_weights,
    table,
    w_gate,
    w_up,
    w_down,
    out_grad,
):
    device_count = lax.axis_size("expert")
    tok_rows = block_values.shape[0]
    features = block_values.shape[1]
    rows_held = table.shape[0]
    look_cap = max(2, 2 * tok_rows // device_count)
    exp_dev = w_gate.shape[0]
    width_split = device_count * exp_dev // EXPERTS
    owners = row_ids // rows_held
    local_row = row_ids % rows_held
    owner_hot = (owners[:, None] == jnp.arange(device_count, dtype=jnp.int32)[None, :]).astype(
        jnp.int32
    )
    owner_rank = jnp.sum((jnp.cumsum(owner_hot, axis=0) - 1) * owner_hot, axis=1)
    placed = owners * look_cap + owner_rank
    wanted = jnp.zeros((device_count * look_cap,), jnp.int32).at[placed].set(local_row)
    requested = lax.all_to_all(
        wanted.reshape(device_count, look_cap), "expert", split_axis=0, concat_axis=0, tiled=True
    )
    fetched = jnp.take(table, requested.reshape(-1), axis=0).reshape(
        device_count, look_cap, features
    )
    rows_returned = lax.all_to_all(fetched, "expert", split_axis=0, concat_axis=0, tiled=True)
    embedded = jnp.take(rows_returned.reshape(device_count * look_cap, features), placed, axis=0)
    scales = jnp.exp2(block_exps.astype(jnp.float32))
    blocks = (
        block_values.reshape(tok_rows, scales.shape[1], -1).astype(jnp.float32) * scales[:, :, None]
    )
    token_state = (blocks.reshape(tok_rows, features) + embedded.astype(jnp.float32)).astype(
        jnp.bfloat16
    )
    flat_ids = expert_ids.reshape(-1)
    expert_hot = (flat_ids[:, None] == jnp.arange(EXPERTS, dtype=jnp.int32)[None, :]).astype(
        jnp.int32
    )
    expert_rank = jnp.sum((jnp.cumsum(expert_hot, axis=0) - 1) * expert_hot, axis=1)
    slot_of = flat_ids * CAP + expert_rank
    token_index = jnp.arange(tok_rows * TOP, dtype=jnp.int32) // TOP
    source = jnp.full((EXPERTS * CAP,), tok_rows, jnp.int32).at[slot_of].set(token_index)
    padded = jnp.concatenate([token_state, jnp.zeros((1, features), jnp.bfloat16)], axis=0)
    buffer = jnp.take(padded, source, axis=0)
    expert_out = full_path(
        buffer, w_gate, w_up, w_down, device_count, exp_dev, width_split, features
    )
    chosen = jnp.take(expert_out, slot_of, axis=0).reshape(tok_rows, TOP, features)
    mixed = jnp.sum(gate_weights[:, :, None] * chosen.astype(jnp.float32), axis=1).astype(
        jnp.bfloat16
    )
    gate_grads = jnp.einsum("tkd,td->tk", chosen, out_grad, preferred_element_type=jnp.float32)
    return (mixed, gate_grads)


def local(*arrays):
    if lax.axis_size("expert") == 16 and arrays[6].shape[0] * 16 == EXPERTS:
        return near_path(*arrays)
    return far_path(*arrays)


def solution(mesh):
    return jax.shard_map(
        local,
        mesh=mesh,
        in_specs=(
            P(("groups", "expert"), None),
            P(("groups", "expert"), None),
            P(("groups", "expert")),
            P(("groups", "expert"), None),
            P(("groups", "expert"), None),
            P("expert", None),
            P("expert", None, None),
            P("expert", None, None),
            P("expert", None, None),
            P(("groups", "expert"), None),
        ),
        out_specs=(P(("groups", "expert"), None), P(("groups", "expert"), None)),
        check_vma=False,
    )
```

```python
import functools

import jax
import jax.numpy as jnp
from jax import lax
from jax.experimental import pallas as pl
from jax.experimental.pallas import tpu as pltpu
from jax.sharding import PartitionSpec as P

EXPERTS = 64
TOP = 4
CAP = 12
BLOCK = 128
PAIR = 2 * CAP
VMEM = pltpu.VMEM
F32 = jnp.float32
BF16 = jnp.bfloat16
SMALL = pltpu.CompilerParams(vmem_limit_bytes=16 * 1024 * 1024)


def dot(a, b):
    return jnp.dot(a, b, preferred_element_type=F32)


def in_hbm(array):
    return pltpu.with_memory_space_constraint(array, pltpu.HBM)


def iota(shape, dimension):
    return lax.broadcasted_iota(jnp.int32, shape, dimension)


def flags(mask):
    return mask.astype(F32).astype(BF16)


def earlier(length):
    return flags(iota((length, length), 0) < iota((length, length), 1))


def repeat_kernel(rows_ref, out_ref):
    for n in range(out_ref.shape[0]):
        out_ref[n] = rows_ref[...]


def fetch_kernel(me_ref, rows_ref, table_hbm, out_ref, table_ref, sem):
    copy = pltpu.make_async_copy(table_hbm, table_ref, sem)
    copy.start()
    device_count, _, tok_rows = rows_ref.shape
    held = table_ref.shape[0]
    look_cap = out_ref.shape[0] // device_count
    local = rows_ref[:, 0, :] - me_ref[0] * held
    hit = (local >= 0) & (local < held)
    rank = dot(flags(hit), earlier(tok_rows)).astype(jnp.int32)
    rank = jnp.where(hit, rank, -1)
    slot = iota((look_cap, tok_rows), 0)
    place = iota((look_cap, held), 1)
    picks = []
    for source in range(device_count):
        mine = jnp.where(slot == rank[source : source + 1], local[source : source + 1], 0)
        wanted = jnp.sum(mine, axis=1, keepdims=True)
        picks.append(flags(place == wanted))
    pick = jnp.concatenate(picks, axis=0)
    copy.wait()
    out_ref[...] = dot(pick, table_ref[...]).astype(BF16)


def turned(rows):
    count, length = rows.shape
    return jnp.concatenate([rows, jnp.zeros((length - count, length), F32)], axis=0).T


def plan_slots(me, ids_ref, pick_ref, slots_ref):
    tok_rows = ids_ref.shape[1]
    half = pick_ref.shape[0] // (2 * PAIR)
    exp_dev = EXPERTS // (2 * half)
    flip = me % 2
    inside = iota((half * exp_dev, tok_rows), 0)
    expert = inside + me // half * half * exp_dev
    place = iota((PAIR, tok_rows), 0)
    ids = ids_ref[...]
    chosen = [ids[k : k + 1] == expert for k in range(TOP)]
    hit = functools.reduce(jnp.logical_or, chosen)
    rank = jnp.where(hit, dot(flags(hit), earlier(tok_rows)).astype(jnp.int32), -1000)
    lines = []
    for at in range(0, half * exp_dev, 2):
        one, two = rank[at : at + 1], rank[at + 1 : at + 2]
        upper = jnp.where(flip == 0, one, two)
        lower = jnp.where(flip == 0, two, one) + CAP
        here = ((place < CAP) & (place == upper)) | ((place >= CAP) & (place == lower))
        lines.append(here.astype(F32))
    pick_ref[...] = jnp.concatenate(lines, axis=0).astype(BF16)
    slot = (inside // 2) * PAIR + ((inside + flip) & 1) * CAP + rank
    found = [
        jnp.sum(jnp.where(chosen[k], slot + 1, 0), axis=0, keepdims=True) - 1 for k in range(TOP)
    ]
    slots_ref[...] = turned(jnp.concatenate(found, axis=0).astype(F32)).astype(jnp.int32)


def near_plan_kernel(
    me_ref,
    rows_ref,
    ids_ref,
    weights_ref,
    scales_ref,
    _,
    put_ref,
    pick_ref,
    slots_ref,
    columns_ref,
    ids_out_ref,
    weights_out_ref,
):
    ids_out_ref[...] = ids_ref[...]
    weights_out_ref[...] = weights_ref[...]
    tok_rows = rows_ref.shape[1]
    me, held = me_ref[0], me_ref[1]
    device_count = pick_ref.shape[0] // PAIR
    look_cap = put_ref.shape[1] // device_count
    row = jnp.broadcast_to(rows_ref[...], (device_count, tok_rows))
    low = iota((device_count, tok_rows), 0) * held
    hit = (row >= low) & (row < low + held)
    rank = jnp.where(hit, dot(flags(hit), earlier(tok_rows)).astype(jnp.int32), -1)
    slot = iota((look_cap, tok_rows), 0)
    put = [(slot == rank[o : o + 1]).astype(F32) for o in range(device_count)]
    put_ref[...] = jnp.concatenate(put, axis=0).T.astype(BF16)
    plan_slots(me, ids_ref, pick_ref, slots_ref)
    columns_ref[...] = turned(jnp.concatenate([weights_ref[...], scales_ref[...]], axis=0))


def far_plan_kernel(me_ref, ids_ref, weights_ref, pick_ref, slots_ref, columns_ref):
    plan_slots(me_ref[0], ids_ref, pick_ref, slots_ref)
    columns_ref[...] = turned(weights_ref[...])


def state_kernel(
    put_ref, pick_ref, returned_ref, values_ref, columns_ref, _, state_ref, out_hbm, sent_ref, sem
):
    features = values_ref.shape[1]
    width = features // sem.shape[0]
    copies = []
    for n in range(sem.shape[0]):
        left = n * width
        found = dot(put_ref[...], returned_ref[:, left : left + width])
        for b in range(width // BLOCK):
            at = left + b * BLOCK
            scaled = (
                values_ref[:, at : at + BLOCK].astype(F32)
                * columns_ref[:, TOP + at // BLOCK : TOP + at // BLOCK + 1]
            )
            state_ref[:, at : at + BLOCK] = (
                scaled + found[:, b * BLOCK : (b + 1) * BLOCK]
            ).astype(BF16)
        cols = pl.ds(left, width)
        sent_ref[:, cols] = dot(pick_ref[...], state_ref[:, cols]).astype(BF16)
        copies.append(
            pltpu.make_async_copy(sent_ref.at[:, cols], out_hbm.at[:, cols], sem.at[n])
        )
        copies[-1].start()
    for copy in copies:
        copy.wait()


def pick_kernel(
    pick_ref, state_ref, grad_ref, out_hbm, upper_grad_ref, lower_grad_ref, sent_ref, sem
):
    tok_rows, features = state_ref.shape
    width = features // sem.shape[0]
    copies = []
    for n in range(sem.shape[0]):
        cols = pl.ds(n * width, width)
        sent_ref[:, cols] = dot(pick_ref[...], state_ref[:, cols]).astype(BF16)
        copies.append(
            pltpu.make_async_copy(sent_ref.at[:, cols], out_hbm.at[:, cols], sem.at[n])
        )
        copies[-1].start()
    upper_grad_ref[...] = grad_ref[: tok_rows // 2, :]
    lower_grad_ref[...] = grad_ref[tok_rows // 2 :, :]
    for copy in copies:
        copy.wait()


def expert_kernel(after, rows_hbm, *refs):
    wg_hbm, wu_hbm, wd_hbm, out_ref = refs[after : after + 4]
    rows_ref, x_ref, wg_ref, wu_ref, wd_ref, hidden_ref, result_ref, sem, rows_sem = refs[
        after + 4 :
    ]
    exp_dev, features, width = wg_hbm.shape
    half = rows_ref.shape[0]
    up_cuts = ((0, 256), (256, 256), (512, 512), (1024, width - 1024))
    down_cuts = tuple((at, 512) for at in range(0, features, 512))
    ahead = 4

    def part_copies(j, n):
        if n < len(up_cuts):
            at, size = up_cuts[n]
            cols = pl.ds(at, size)
            pairs = ((wg_hbm, wg_ref), (wu_hbm, wu_ref))
        else:
            at, size = down_cuts[n - len(up_cuts)]
            cols = pl.ds(at, size)
            pairs = ((wd_hbm, wd_ref),)
        return [
            pltpu.make_async_copy(hbm.at[j, :, cols], ref.at[:, cols], sem.at[n, m])
            for m, (hbm, ref) in enumerate(pairs)
        ]

    part_count = len(up_cuts) + len(down_cuts)

    rows_copy = pltpu.make_async_copy(rows_hbm, rows_ref, rows_sem)
    rows_copy.start()
    for copy in part_copies(0, 0):
        copy.start()
    rows_copy.wait()
    for n in range(1, ahead):
        for copy in part_copies(0, n):
            copy.start()

    low = iota((PAIR, features), 0) < CAP
    for chunk in range(exp_dev // 2):
        here = slice(chunk * PAIR, (chunk + 1) * PAIR)
        for quad in range(half // 4):
            ones, twos = [], []
            for pair in range(2):
                source = 4 * quad + 2 * pair
                even = rows_ref[source, here, :].astype(F32)
                odd = rows_ref[source + 1, here, :].astype(F32)
                ones.append(jnp.where(low, even, odd))
                twos.append(jnp.where(low, odd, even))
            rows = slice(quad * 2 * PAIR, (quad + 1) * 2 * PAIR)
            x_ref[2 * chunk, rows, :] = jnp.concatenate(ones, axis=0).astype(BF16)
            x_ref[2 * chunk + 1, rows, :] = jnp.concatenate(twos, axis=0).astype(BF16)

    @pl.loop(0, exp_dev)
    def _(j):
        def arrive(n):
            for copy in part_copies(j, n):
                copy.wait()
            if n + ahead < part_count:
                for copy in part_copies(j, n + ahead):
                    copy.start()
            else:

                @pl.when(j + 1 < exp_dev)
                def _():
                    for copy in part_copies(j + 1, n + ahead - part_count):
                        copy.start()

        n = 0
        for at, size in up_cuts:
            arrive(n)
            gate = dot(x_ref[j], wg_ref[:, at : at + size])
            up = dot(x_ref[j], wu_ref[:, at : at + size])
            hidden = gate / (1.0 + jnp.exp(-gate)) * up
            hidden_ref[:, at : at + size] = hidden.astype(BF16)
            n += 1
        for at, size in down_cuts:
            arrive(n)
            result_ref[j, :, at : at + size] = dot(hidden_ref[...], wd_ref[:, at : at + size])
            n += 1

    for pair in range(half // 2):
        rows = slice(pair * PAIR, (pair + 1) * PAIR)
        values = [result_ref[j, rows, :] for j in range(exp_dev)]
        for odd in range(2):
            parts = [
                jnp.where(low, values[j + odd], values[j + 1 - odd]) for j in range(0, exp_dev, 2)
            ]
            out_ref[2 * pair + odd] = jnp.concatenate(parts, axis=0).astype(BF16)


def expert_call(name, rows_in, weights, after=()):
    w_gate, w_up, w_down = weights
    exp_dev, features, width = w_gate.shape
    half = rows_in.shape[0]
    rows = half * CAP
    anywhere = pl.BlockSpec(memory_space=pl.ANY)
    hbm = pl.BlockSpec(memory_space=pltpu.HBM)
    operands = [in_hbm(array) for array in (rows_in, *after, w_gate, w_up, w_down)]
    return pl.pallas_call(
        functools.partial(expert_kernel, len(after)),
        out_shape=pltpu.HBM(rows_in.shape, BF16),
        in_specs=[hbm] + [anywhere] * len(after) + [hbm] * 3,
        out_specs=pl.BlockSpec(memory_space=VMEM),
        scratch_shapes=[
            VMEM(rows_in.shape, BF16),
            VMEM((exp_dev, rows, features), BF16),
            VMEM((features, width), BF16),
            VMEM((features, width), BF16),
            VMEM((width, features), BF16),
            VMEM((rows, width), BF16),
            VMEM((exp_dev, rows, features), F32),
            pltpu.SemaphoreType.DMA((8, 2)),
            pltpu.SemaphoreType.DMA,
        ],
        compiler_params=pltpu.CompilerParams(vmem_limit_bytes=30 * 1024 * 1024),
        cost_estimate=pl.CostEstimate(
            flops=12 * exp_dev * rows * features * width,
            bytes_accessed=6 * exp_dev * features * width,
            transcendentals=exp_dev * rows * width,
        ),
        name=name,
    )(*operands)


def mix_kernel(slots_ref, columns_ref, back_ref, *refs):
    mixed_ref, grads_ref = refs[-2:]
    tok_rows = slots_ref.shape[0]
    count, features = back_ref.shape
    grad = jnp.concatenate([ref[...] for ref in refs[:-2]], axis=0)
    column = iota((tok_rows, count), 1)
    inner = lax.dot_general(
        grad, back_ref[...], (((1,), (1,)), ((), ())), preferred_element_type=F32
    )
    total = jnp.zeros((tok_rows, count), F32)
    place = iota((tok_rows, tok_rows), 1)
    wide = jnp.zeros((tok_rows, tok_rows), F32)
    for k in range(TOP):
        here = column == slots_ref[:, k : k + 1]
        total = total + jnp.where(here, columns_ref[:, k : k + 1], 0.0)
        value = jnp.sum(jnp.where(here, inner, 0.0), axis=1, keepdims=True)
        wide = wide + jnp.where(place == k, value, 0.0)
    high = total.astype(BF16)
    rest = (total - high.astype(F32)).astype(BF16)
    width = 512
    for at in range(0, features, width):
        rows = back_ref[:, at : at + width]
        mixed_ref[:, at : at + width] = (dot(high, rows) + dot(rest, rows)).astype(mixed_ref.dtype)
    grads_ref[...] = wide.T[: grads_ref.shape[0], :]


def swap(array, groups=None):
    return lax.all_to_all(
        array, "expert", split_axis=0, concat_axis=0, tiled=True, axis_index_groups=groups
    )


def near_path(
    block_values,
    block_exps,
    row_ids,
    expert_ids,
    gate_weights,
    table,
    w_gate,
    w_up,
    w_down,
    out_grad,
):
    device_count = lax.axis_size("expert")
    half = device_count // 2
    halves = [list(range(half)), list(range(half, device_count))]
    me = lax.axis_index("expert").astype(jnp.int32)
    tok_rows, features = block_values.shape
    rows_held = table.shape[0]
    look_cap = max(2, 2 * tok_rows // device_count)
    slots = half * 2 * PAIR
    vmem = pl.BlockSpec(memory_space=VMEM)
    smem = pl.BlockSpec(memory_space=pltpu.SMEM)
    anywhere = pl.BlockSpec(memory_space=pl.ANY)
    place = jnp.stack([me, jnp.int32(rows_held)])

    def shape(dims, kind):
        return jax.ShapeDtypeStruct(dims, kind)

    def mirrored(array):
        pairs = [(i, (i + half) % device_count) for i in range(device_count)]
        return lax.ppermute(array, "expert", pairs)

    def ordered(array, *earlier_arrays, flops=0):
        return pl.pallas_call(
            lambda *refs: None,
            out_shape=shape(array.shape, array.dtype),
            in_specs=[anywhere] * (1 + len(earlier_arrays)),
            out_specs=anywhere,
            input_output_aliases={0: 0},
            compiler_params=SMALL,
            cost_estimate=pl.CostEstimate(flops=flops, bytes_accessed=0, transcendentals=0),
            name="ordered",
        )(array, *earlier_arrays)

    all_rows = pl.pallas_call(
        repeat_kernel,
        out_shape=shape((device_count, 1, tok_rows), jnp.int32),
        in_specs=[vmem],
        out_specs=vmem,
        name="repeat_rows",
    )(row_ids[None, :])
    fetched = pl.pallas_call(
        fetch_kernel,
        out_shape=shape((device_count * look_cap, features), BF16),
        in_specs=[smem, vmem, pl.BlockSpec(memory_space=pltpu.HBM)],
        out_specs=vmem,
        scratch_shapes=[VMEM(table.shape, BF16), pltpu.SemaphoreType.DMA],
        compiler_params=SMALL,
        name="fetch_rows",
    )(place, swap(all_rows), in_hbm(table))
    returned = swap(fetched.reshape(device_count, look_cap, features))
    turned_ids, turned_weights = expert_ids.T, gate_weights.T
    pick_shape = shape((slots, tok_rows), BF16)
    square = (tok_rows, tok_rows)
    put, near_pick, near_of, near_columns, sent_ids, sent_weights = pl.pallas_call(
        near_plan_kernel,
        out_shape=(
            shape((tok_rows, device_count * look_cap), BF16),
            pick_shape,
            shape(square, jnp.int32),
            shape(square, F32),
            shape(turned_ids.shape, jnp.int32),
            shape(turned_weights.shape, F32),
        ),
        in_specs=[smem, vmem, vmem, vmem, vmem, anywhere],
        out_specs=(vmem,) * 6,
        compiler_params=SMALL,
        name="near_plan",
    )(
        place,
        row_ids[None, :],
        turned_ids,
        turned_weights,
        jnp.exp2(block_exps.T.astype(F32)),
        fetched,
    )
    far_pick, far_of, far_columns = pl.pallas_call(
        far_plan_kernel,
        out_shape=(pick_shape, shape(square, jnp.int32), shape(square, F32)),
        in_specs=[smem, vmem, vmem],
        out_specs=(vmem,) * 3,
        compiler_params=SMALL,
        name="far_plan",
    )(place, mirrored(sent_ids), mirrored(sent_weights))

    sent_shape = pltpu.HBM((slots, features), BF16)
    sent_scratch = [VMEM((slots, features), BF16), pltpu.SemaphoreType.DMA((4,))]
    state, near_sent = pl.pallas_call(
        state_kernel,
        out_shape=(shape((tok_rows, features), BF16), sent_shape),
        in_specs=[vmem] * 5 + [anywhere],
        out_specs=(vmem, anywhere),
        scratch_shapes=sent_scratch,
        compiler_params=SMALL,
        name="token_state",
    )(
        put,
        near_pick,
        returned.reshape(device_count * look_cap, features),
        block_values,
        near_columns,
        far_pick,
    )
    split = shape((tok_rows // 2, features), BF16)
    far_sent, *grad_halves = pl.pallas_call(
        pick_kernel,
        out_shape=(sent_shape, split, split),
        in_specs=[vmem, vmem, vmem],
        out_specs=(anywhere, vmem, vmem),
        scratch_shapes=sent_scratch,
        compiler_params=SMALL,
        cost_estimate=pl.CostEstimate(
            flops=400_000_000_000, bytes_accessed=4 * slots * features, transcendentals=0
        ),
        name="far_slots",
    )(far_pick, mirrored(state), out_grad)
    near_rows = swap(near_sent.reshape(half, 2 * PAIR, features), halves)
    far_sent = far_sent.reshape(half, 2 * PAIR, features)
    far_rows = swap(far_sent, halves)
    other_grads = [mirrored(array) for array in grad_halves]

    weights = (w_gate, w_up, w_down)
    near_out = expert_call("near_experts", near_rows, weights, after=(far_sent,))
    near_out = ordered(in_hbm(near_out), other_grads[0])
    far_out = expert_call("far_experts", far_rows, weights, after=(near_out,))
    near_back = swap(near_out, halves)
    far_back = swap(ordered(in_hbm(far_out), near_back, other_grads[1]), halves)

    def mixed_rows(name, slot_of, columns, back, grads, kind):
        return pl.pallas_call(
            mix_kernel,
            out_shape=(shape((tok_rows, features), kind), shape((2 * TOP, tok_rows), F32)),
            in_specs=[vmem] * (3 + len(grads)),
            out_specs=(vmem, vmem),
            compiler_params=SMALL,
            name=name,
        )(slot_of, columns, back.reshape(slots, features), *grads)

    near_mixed, near_grads = mixed_rows(
        "mix_near", near_of, near_columns, near_back, (out_grad,), F32
    )
    far_mixed, far_grads = mixed_rows(
        "mix_far", far_of, far_columns, far_back, other_grads, BF16
    )
    mixed = (near_mixed + mirrored(far_mixed).astype(F32)).astype(BF16)
    grads = (near_grads + mirrored(far_grads))[:TOP]
    return mixed, grads.T


def expert_work(arrived, w_gate, w_up, w_down):
    gate_act = jnp.einsum("sjcd,jdf->sjcf", arrived, w_gate, preferred_element_type=jnp.float32)
    up_act = jnp.einsum("sjcd,jdf->sjcf", arrived, w_up, preferred_element_type=jnp.float32)
    hidden = (jax.nn.silu(gate_act) * up_act).astype(jnp.bfloat16)
    return jnp.einsum("sjcf,jfd->sjcd", hidden, w_down, preferred_element_type=jnp.float32).astype(
        jnp.bfloat16
    )


def full_path(buffer, w_gate, w_up, w_down, device_count, exp_dev, width_split, features):
    group_count = EXPERTS // exp_dev
    grouped = buffer.reshape(group_count, 1, exp_dev, CAP, features)
    outgoing = jnp.broadcast_to(
        grouped, (group_count, width_split, exp_dev, CAP, features)
    ).reshape(device_count, exp_dev, CAP, features)
    returned_out = lax.all_to_all(
        expert_work(
            lax.all_to_all(outgoing, "expert", split_axis=0, concat_axis=0, tiled=True),
            w_gate,
            w_up,
            w_down,
        ),
        "expert",
        split_axis=0,
        concat_axis=0,
        tiled=True,
    )
    pieces = returned_out.reshape(group_count, width_split, exp_dev, CAP, features).astype(
        jnp.float32
    )
    return jnp.sum(pieces, axis=1).astype(jnp.bfloat16).reshape(EXPERTS * CAP, features)


def far_path(
    block_values,
    block_exps,
    row_ids,
    expert_ids,
    gate_weights,
    table,
    w_gate,
    w_up,
    w_down,
    out_grad,
):
    device_count = lax.axis_size("expert")
    tok_rows = block_values.shape[0]
    features = block_values.shape[1]
    rows_held = table.shape[0]
    look_cap = max(2, 2 * tok_rows // device_count)
    exp_dev = w_gate.shape[0]
    width_split = device_count * exp_dev // EXPERTS
    owners = row_ids // rows_held
    local_row = row_ids % rows_held
    owner_hot = (owners[:, None] == jnp.arange(device_count, dtype=jnp.int32)[None, :]).astype(
        jnp.int32
    )
    owner_rank = jnp.sum((jnp.cumsum(owner_hot, axis=0) - 1) * owner_hot, axis=1)
    placed = owners * look_cap + owner_rank
    wanted = jnp.zeros((device_count * look_cap,), jnp.int32).at[placed].set(local_row)
    requested = lax.all_to_all(
        wanted.reshape(device_count, look_cap), "expert", split_axis=0, concat_axis=0, tiled=True
    )
    fetched = jnp.take(table, requested.reshape(-1), axis=0).reshape(
        device_count, look_cap, features
    )
    rows_returned = lax.all_to_all(fetched, "expert", split_axis=0, concat_axis=0, tiled=True)
    embedded = jnp.take(rows_returned.reshape(device_count * look_cap, features), placed, axis=0)
    scales = jnp.exp2(block_exps.astype(jnp.float32))
    blocks = (
        block_values.reshape(tok_rows, scales.shape[1], -1).astype(jnp.float32) * scales[:, :, None]
    )
    token_state = (blocks.reshape(tok_rows, features) + embedded.astype(jnp.float32)).astype(
        jnp.bfloat16
    )
    flat_ids = expert_ids.reshape(-1)
    expert_hot = (flat_ids[:, None] == jnp.arange(EXPERTS, dtype=jnp.int32)[None, :]).astype(
        jnp.int32
    )
    expert_rank = jnp.sum((jnp.cumsum(expert_hot, axis=0) - 1) * expert_hot, axis=1)
    slot_of = flat_ids * CAP + expert_rank
    token_index = jnp.arange(tok_rows * TOP, dtype=jnp.int32) // TOP
    source = jnp.full((EXPERTS * CAP,), tok_rows, jnp.int32).at[slot_of].set(token_index)
    padded = jnp.concatenate([token_state, jnp.zeros((1, features), jnp.bfloat16)], axis=0)
    buffer = jnp.take(padded, source, axis=0)
    expert_out = full_path(
        buffer, w_gate, w_up, w_down, device_count, exp_dev, width_split, features
    )
    chosen = jnp.take(expert_out, slot_of, axis=0).reshape(tok_rows, TOP, features)
    mixed = jnp.sum(gate_weights[:, :, None] * chosen.astype(jnp.float32), axis=1).astype(
        jnp.bfloat16
    )
    gate_grads = jnp.einsum("tkd,td->tk", chosen, out_grad, preferred_element_type=jnp.float32)
    return (mixed, gate_grads)


def local(*arrays):
    if lax.axis_size("expert") == 16 and arrays[6].shape[0] * 16 == EXPERTS:
        return near_path(*arrays)
    return far_path(*arrays)


def solution(mesh):
    return jax.shard_map(
        local,
        mesh=mesh,
        in_specs=(
            P(("groups", "expert"), None),
            P(("groups", "expert"), None),
            P(("groups", "expert")),
            P(("groups", "expert"), None),
            P(("groups", "expert"), None),
            P("expert", None),
            P("expert", None, None),
            P("expert", None, None),
            P("expert", None, None),
            P(("groups", "expert"), None),
        ),
        out_specs=(P(("groups", "expert"), None), P(("groups", "expert"), None)),
        check_vma=False,
    )
```

```python
import functools

import jax
import jax.numpy as jnp
from jax import lax
from jax.experimental import pallas as pl
from jax.experimental.pallas import tpu as pltpu
from jax.sharding import PartitionSpec as P

EXPERTS = 64
TOP = 4
CAP = 12
BLOCK = 128
PAIR = 2 * CAP
VMEM = pltpu.VMEM
F32 = jnp.float32
BF16 = jnp.bfloat16
SMALL = pltpu.CompilerParams(vmem_limit_bytes=16 * 1024 * 1024)


def dot(a, b):
    return jnp.dot(a, b, preferred_element_type=F32)


def in_hbm(array):
    return pltpu.with_memory_space_constraint(array, pltpu.HBM)


def iota(shape, dimension):
    return lax.broadcasted_iota(jnp.int32, shape, dimension)


def flags(mask):
    return mask.astype(F32).astype(BF16)


def earlier(length):
    return flags(iota((length, length), 0) < iota((length, length), 1))


def repeat_kernel(rows_ref, out_ref):
    for n in range(out_ref.shape[0]):
        out_ref[n] = rows_ref[...]


def fetch_kernel(me_ref, rows_ref, table_hbm, out_ref, table_ref, sem):
    copy = pltpu.make_async_copy(table_hbm, table_ref, sem)
    copy.start()
    device_count, _, tok_rows = rows_ref.shape
    held = table_ref.shape[0]
    look_cap = out_ref.shape[0] // device_count
    local = rows_ref[:, 0, :] - me_ref[0] * held
    hit = (local >= 0) & (local < held)
    rank = dot(flags(hit), earlier(tok_rows)).astype(jnp.int32)
    rank = jnp.where(hit, rank, -1)
    slot = iota((look_cap, tok_rows), 0)
    place = iota((look_cap, held), 1)
    picks = []
    for source in range(device_count):
        mine = jnp.where(slot == rank[source : source + 1], local[source : source + 1], 0)
        wanted = jnp.sum(mine, axis=1, keepdims=True)
        picks.append(flags(place == wanted))
    pick = jnp.concatenate(picks, axis=0)
    copy.wait()
    out_ref[...] = dot(pick, table_ref[...]).astype(BF16)


def turned(rows):
    count, length = rows.shape
    return jnp.concatenate([rows, jnp.zeros((length - count, length), F32)], axis=0).T


def plan_slots(me, ids_ref, pick_refs, slots_ref):
    tok_rows = ids_ref.shape[1]
    half = sum(ref.shape[0] for ref in pick_refs) // (2 * PAIR)
    exp_dev = EXPERTS // (2 * half)
    flip = me % 2
    inside = iota((half * exp_dev, tok_rows), 0)
    expert = inside + me // half * half * exp_dev
    place = iota((PAIR, tok_rows), 0)
    ids = ids_ref[...]
    chosen = [ids[k : k + 1] == expert for k in range(TOP)]
    hit = functools.reduce(jnp.logical_or, chosen)
    rank = jnp.where(hit, dot(flags(hit), earlier(tok_rows)).astype(jnp.int32), -1000)
    lines = []
    for at in range(0, half * exp_dev, 2):
        one, two = rank[at : at + 1], rank[at + 1 : at + 2]
        upper = jnp.where(flip == 0, one, two)
        lower = jnp.where(flip == 0, two, one) + CAP
        here = ((place < CAP) & (place == upper)) | ((place >= CAP) & (place == lower))
        lines.append(here.astype(F32))
    pairs = exp_dev // 2
    slot = ((inside + flip) & 1) * CAP + rank
    if len(pick_refs) == 1:
        pick_refs[0][...] = jnp.concatenate(lines, axis=0).astype(BF16)
        slot = slot + (inside // 2) * PAIR
    else:
        for n, ref in enumerate(pick_refs):
            ref[...] = jnp.concatenate(lines[n::pairs], axis=0).astype(BF16)
        device = inside // exp_dev
        first = device * (2 * PAIR) + PAIR
        second = half * 2 * PAIR + device * PAIR
        slot = slot + jnp.where((inside & 2) == 0, first, second)
    found = [
        jnp.sum(jnp.where(chosen[k], slot + 1, 0), axis=0, keepdims=True) - 1 for k in range(TOP)
    ]
    slots_ref[...] = turned(jnp.concatenate(found, axis=0).astype(F32)).astype(jnp.int32)


def near_plan_kernel(
    me_ref,
    rows_ref,
    ids_ref,
    weights_ref,
    scales_ref,
    _,
    put_ref,
    first_pick_ref,
    second_pick_ref,
    slots_ref,
    columns_ref,
    ids_out_ref,
    weights_out_ref,
):
    ids_out_ref[...] = ids_ref[...]
    weights_out_ref[...] = weights_ref[...]
    tok_rows = rows_ref.shape[1]
    me, held = me_ref[0], me_ref[1]
    device_count = first_pick_ref.shape[0] // PAIR * 2
    look_cap = put_ref.shape[1] // device_count
    row = jnp.broadcast_to(rows_ref[...], (device_count, tok_rows))
    low = iota((device_count, tok_rows), 0) * held
    hit = (row >= low) & (row < low + held)
    rank = jnp.where(hit, dot(flags(hit), earlier(tok_rows)).astype(jnp.int32), -1)
    slot = iota((look_cap, tok_rows), 0)
    put = [(slot == rank[o : o + 1]).astype(F32) for o in range(device_count)]
    put_ref[...] = jnp.concatenate(put, axis=0).T.astype(BF16)
    plan_slots(me, ids_ref, (first_pick_ref, second_pick_ref), slots_ref)
    columns_ref[...] = turned(jnp.concatenate([weights_ref[...], scales_ref[...]], axis=0))


def far_plan_kernel(me_ref, ids_ref, weights_ref, pick_ref, slots_ref, columns_ref):
    plan_slots(me_ref[0], ids_ref, (pick_ref,), slots_ref)
    columns_ref[...] = turned(weights_ref[...])


def state_kernel(
    put_ref, pick_ref, returned_ref, values_ref, columns_ref, _, state_ref, out_hbm, sent_ref, sem
):
    features = values_ref.shape[1]
    width = features // sem.shape[0]
    copies = []
    for n in range(sem.shape[0]):
        left = n * width
        found = dot(put_ref[...], returned_ref[:, left : left + width])
        for b in range(width // BLOCK):
            at = left + b * BLOCK
            scaled = (
                values_ref[:, at : at + BLOCK].astype(F32)
                * columns_ref[:, TOP + at // BLOCK : TOP + at // BLOCK + 1]
            )
            state_ref[:, at : at + BLOCK] = (
                scaled + found[:, b * BLOCK : (b + 1) * BLOCK]
            ).astype(BF16)
        cols = pl.ds(left, width)
        sent_ref[:, cols] = dot(pick_ref[...], state_ref[:, cols]).astype(BF16)
        copies.append(
            pltpu.make_async_copy(sent_ref.at[:, cols], out_hbm.at[:, cols], sem.at[n])
        )
        copies[-1].start()
    for copy in copies:
        copy.wait()


def later_kernel(pick_ref, state_ref, _, out_ref):
    out_ref[...] = dot(pick_ref[...], state_ref[...]).astype(BF16)


def pick_kernel(
    pick_ref, state_ref, grad_ref, out_hbm, upper_grad_ref, lower_grad_ref, sent_ref, sem
):
    tok_rows, features = state_ref.shape
    width = features // sem.shape[0]
    copies = []
    for n in range(sem.shape[0]):
        cols = pl.ds(n * width, width)
        sent_ref[:, cols] = dot(pick_ref[...], state_ref[:, cols]).astype(BF16)
        copies.append(
            pltpu.make_async_copy(sent_ref.at[:, cols], out_hbm.at[:, cols], sem.at[n])
        )
        copies[-1].start()
    upper_grad_ref[...] = grad_ref[: tok_rows // 2, :]
    lower_grad_ref[...] = grad_ref[tok_rows // 2 :, :]
    for copy in copies:
        copy.wait()


def expert_kernel(first, count, join, after, rows_ref, *refs):
    if join:
        front_ref, refs = refs[0], refs[1:]
    wg_hbm, wu_hbm, wd_hbm, out_ref = refs[after : after + 4]
    x_ref, wg_ref, wu_ref, wd_ref, hidden_ref, result_ref, sem = refs[after + 4 :]
    held, features, width = wg_ref.shape
    half = rows_ref.shape[0]
    up_cuts = ((0, 512), (512, 512), (1024, width - 1024))
    down_cuts = tuple((at, 512) for at in range(0, features, 512))

    def weight_copies(j, place):
        copies = []
        for at, size in up_cuts:
            cols = pl.ds(at, size)
            copies.append((wg_hbm.at[first + j, :, cols], wg_ref.at[place, :, cols]))
            copies.append((wu_hbm.at[first + j, :, cols], wu_ref.at[place, :, cols]))
        for at, size in down_cuts:
            cols = pl.ds(at, size)
            copies.append((wd_hbm.at[first + j, :, cols], wd_ref.at[place, :, cols]))
        return [
            pltpu.make_async_copy(src, dst, sem.at[place, n])
            for n, (src, dst) in enumerate(copies)
        ]

    for j in range(held):
        for copy in weight_copies(j, j):
            copy.start()

    low = iota((PAIR, features), 0) < CAP
    for chunk in range(count // 2):
        here = slice(chunk * PAIR, (chunk + 1) * PAIR)
        for quad in range(half // 4):
            ones, twos = [], []
            for pair in range(2):
                source = 4 * quad + 2 * pair
                even = rows_ref[source, here, :].astype(F32)
                odd = rows_ref[source + 1, here, :].astype(F32)
                ones.append(jnp.where(low, even, odd))
                twos.append(jnp.where(low, odd, even))
            rows = slice(quad * 2 * PAIR, (quad + 1) * 2 * PAIR)
            x_ref[2 * chunk, rows, :] = jnp.concatenate(ones, axis=0).astype(BF16)
            x_ref[2 * chunk + 1, rows, :] = jnp.concatenate(twos, axis=0).astype(BF16)

    @pl.loop(0, count)
    def _(j):
        place = j % held
        copies = weight_copies(j, place)

        def refill(n, parts):
            @pl.when(j + held < count)
            def _():
                for copy in weight_copies(j + held, place)[n : n + parts]:
                    copy.start()

        n = 0
        for at, size in up_cuts:
            copies[n].wait()
            copies[n + 1].wait()
            gate = dot(x_ref[j], wg_ref[place, :, at : at + size])
            up = dot(x_ref[j], wu_ref[place, :, at : at + size])
            hidden = gate / (1.0 + jnp.exp(-gate)) * up
            hidden_ref[:, at : at + size] = hidden.astype(BF16)
            if count > held:
                refill(n, 2)
            n += 2
        for at, size in down_cuts:
            copies[n].wait()
            result_ref[j, :, at : at + size] = dot(
                hidden_ref[...], wd_ref[place, :, at : at + size]
            )
            if count > held:
                refill(n, 1)
            n += 1

    for pair in range(half // 2):
        rows = slice(pair * PAIR, (pair + 1) * PAIR)
        values = [result_ref[j, rows, :] for j in range(count)]
        for odd in range(2):
            parts = [
                jnp.where(low, values[j + odd], values[j + 1 - odd]) for j in range(0, count, 2)
            ]
            if join:
                parts = [front_ref[2 * pair + odd].astype(F32)] + parts
            out_ref[2 * pair + odd] = jnp.concatenate(parts, axis=0).astype(BF16)


def expert_call(name, first, count, rows_in, weights, front=(), after=()):
    w_gate, w_up, w_down = weights
    _, features, width = w_gate.shape
    half = rows_in.shape[0]
    rows = half * CAP
    held = 2
    anywhere = pl.BlockSpec(memory_space=pl.ANY)
    hbm = pl.BlockSpec(memory_space=pltpu.HBM)
    vmem = pl.BlockSpec(memory_space=VMEM)
    return pl.pallas_call(
        functools.partial(expert_kernel, first, count, bool(front), len(after)),
        out_shape=pltpu.HBM((half, count * CAP + len(front) * PAIR, features), BF16),
        in_specs=[vmem] * (1 + len(front)) + [anywhere] * len(after) + [hbm] * 3,
        out_specs=vmem,
        scratch_shapes=[
            VMEM((count, rows, features), BF16),
            VMEM((held, features, width), BF16),
            VMEM((held, features, width), BF16),
            VMEM((held, width, features), BF16),
            VMEM((rows, width), BF16),
            VMEM((count, rows, features), F32),
            pltpu.SemaphoreType.DMA((held, 10)),
        ],
        compiler_params=pltpu.CompilerParams(vmem_limit_bytes=46 * 1024 * 1024),
        cost_estimate=pl.CostEstimate(
            flops=12 * count * rows * features * width,
            bytes_accessed=6 * count * features * width,
            transcendentals=count * rows * width,
        ),
        name=name,
    )(
        *[in_hbm(array) for array in (rows_in, *front, *after, w_gate, w_up, w_down)],
    )


def mix_kernel(parts, grads, slots_ref, columns_ref, *refs):
    mixed_ref, grads_ref = refs[-2:]
    back_refs, grad_refs = refs[:parts], refs[parts : parts + grads]
    tok_rows = slots_ref.shape[0]
    features = back_refs[0].shape[1]
    grad = jnp.concatenate([ref[...] for ref in grad_refs], axis=0)
    place = iota((tok_rows, tok_rows), 1)
    wide = jnp.zeros((tok_rows, tok_rows), F32)
    spread = []
    start = 0
    for ref in back_refs:
        count = ref.shape[0]
        column = iota((tok_rows, count), 1) + start
        start += count
        inner = lax.dot_general(
            grad, ref[...], (((1,), (1,)), ((), ())), preferred_element_type=F32
        )
        total = jnp.zeros((tok_rows, count), F32)
        for k in range(TOP):
            here = column == slots_ref[:, k : k + 1]
            total = total + jnp.where(here, columns_ref[:, k : k + 1], 0.0)
            value = jnp.sum(jnp.where(here, inner, 0.0), axis=1, keepdims=True)
            wide = wide + jnp.where(place == k, value, 0.0)
        high = total.astype(BF16)
        spread.append((high, (total - high.astype(F32)).astype(BF16)))
    width = 512
    for at in range(0, features, width):
        cols = slice(at, at + width)
        value = jnp.zeros((tok_rows, width), F32)
        for (high, rest), ref in zip(spread, back_refs):
            value = value + dot(high, ref[:, cols]) + dot(rest, ref[:, cols])
        mixed_ref[:, cols] = value.astype(mixed_ref.dtype)
    grads_ref[...] = wide.T[: grads_ref.shape[0], :]


def swap(array, groups=None):
    return lax.all_to_all(
        array, "expert", split_axis=0, concat_axis=0, tiled=True, axis_index_groups=groups
    )


def near_path(
    block_values,
    block_exps,
    row_ids,
    expert_ids,
    gate_weights,
    table,
    w_gate,
    w_up,
    w_down,
    out_grad,
):
    device_count = lax.axis_size("expert")
    half = device_count // 2
    halves = [list(range(half)), list(range(half, device_count))]
    me = lax.axis_index("expert").astype(jnp.int32)
    tok_rows, features = block_values.shape
    rows_held = table.shape[0]
    look_cap = max(2, 2 * tok_rows // device_count)
    slots = half * 2 * PAIR
    vmem = pl.BlockSpec(memory_space=VMEM)
    smem = pl.BlockSpec(memory_space=pltpu.SMEM)
    anywhere = pl.BlockSpec(memory_space=pl.ANY)
    place = jnp.stack([me, jnp.int32(rows_held)])

    def shape(dims, kind):
        return jax.ShapeDtypeStruct(dims, kind)

    def mirrored(array):
        pairs = [(i, (i + half) % device_count) for i in range(device_count)]
        return lax.ppermute(array, "expert", pairs)

    def ordered(array, *earlier_arrays, flops=0):
        return pl.pallas_call(
            lambda *refs: None,
            out_shape=shape(array.shape, array.dtype),
            in_specs=[anywhere] * (1 + len(earlier_arrays)),
            out_specs=anywhere,
            input_output_aliases={0: 0},
            compiler_params=SMALL,
            cost_estimate=pl.CostEstimate(flops=flops, bytes_accessed=0, transcendentals=0),
            name="ordered",
        )(array, *earlier_arrays)

    all_rows = pl.pallas_call(
        repeat_kernel,
        out_shape=shape((device_count, 1, tok_rows), jnp.int32),
        in_specs=[vmem],
        out_specs=vmem,
        name="repeat_rows",
    )(row_ids[None, :])
    fetched = pl.pallas_call(
        fetch_kernel,
        out_shape=shape((device_count * look_cap, features), BF16),
        in_specs=[smem, vmem, pl.BlockSpec(memory_space=pltpu.HBM)],
        out_specs=vmem,
        scratch_shapes=[VMEM(table.shape, BF16), pltpu.SemaphoreType.DMA],
        compiler_params=SMALL,
        name="fetch_rows",
    )(place, swap(all_rows), in_hbm(table))
    returned = swap(fetched.reshape(device_count, look_cap, features))
    turned_ids, turned_weights = expert_ids.T, gate_weights.T
    pick_shape = shape((slots, tok_rows), BF16)
    pair_shape = shape((slots // 2, tok_rows), BF16)
    square = (tok_rows, tok_rows)
    put, first_pick, second_pick, near_of, near_columns, sent_ids, sent_weights = pl.pallas_call(
        near_plan_kernel,
        out_shape=(
            shape((tok_rows, device_count * look_cap), BF16),
            pair_shape,
            pair_shape,
            shape(square, jnp.int32),
            shape(square, F32),
            shape(turned_ids.shape, jnp.int32),
            shape(turned_weights.shape, F32),
        ),
        in_specs=[smem, vmem, vmem, vmem, vmem, anywhere],
        out_specs=(vmem,) * 7,
        compiler_params=SMALL,
        name="near_plan",
    )(
        place,
        row_ids[None, :],
        turned_ids,
        turned_weights,
        jnp.exp2(block_exps.T.astype(F32)),
        fetched,
    )
    far_pick, far_of, far_columns = pl.pallas_call(
        far_plan_kernel,
        out_shape=(pick_shape, shape(square, jnp.int32), shape(square, F32)),
        in_specs=[smem, vmem, vmem],
        out_specs=(vmem,) * 3,
        compiler_params=SMALL,
        name="far_plan",
    )(place, mirrored(sent_ids), mirrored(sent_weights))

    def sent_scratch(count):
        return [VMEM((count, features), BF16), pltpu.SemaphoreType.DMA((4,))]

    state, near_sent = pl.pallas_call(
        state_kernel,
        out_shape=(shape((tok_rows, features), BF16), pltpu.HBM((slots // 2, features), BF16)),
        in_specs=[vmem] * 5 + [anywhere],
        out_specs=(vmem, anywhere),
        scratch_shapes=sent_scratch(slots // 2),
        compiler_params=SMALL,
        name="token_state",
    )(
        put,
        first_pick,
        returned.reshape(device_count * look_cap, features),
        block_values,
        near_columns,
        far_pick,
    )
    split = shape((tok_rows // 2, features), BF16)
    far_sent, *grad_halves = pl.pallas_call(
        pick_kernel,
        out_shape=(pltpu.HBM((slots, features), BF16), split, split),
        in_specs=[vmem, vmem, vmem],
        out_specs=(anywhere, vmem, vmem),
        scratch_shapes=sent_scratch(slots),
        compiler_params=SMALL,
        cost_estimate=pl.CostEstimate(
            flops=400_000_000_000, bytes_accessed=4 * slots * features, transcendentals=0
        ),
        name="far_slots",
    )(far_pick, mirrored(state), out_grad)
    pair_rows = (half, PAIR, features)
    near_rows = swap(near_sent.reshape(pair_rows), halves)
    far_sent = far_sent.reshape(half, 2 * PAIR, features)
    far_rows = swap(far_sent, halves)
    later_sent = pl.pallas_call(
        later_kernel,
        out_shape=pltpu.HBM((slots // 2, features), BF16),
        in_specs=[vmem, vmem, anywhere],
        out_specs=vmem,
        compiler_params=SMALL,
        name="later_slots",
    )(second_pick, state, in_hbm(far_sent)).reshape(pair_rows)
    other_grads = [mirrored(array) for array in grad_halves]

    weights = (w_gate, w_up, w_down)
    sent_both = expert_call(
        "near_first", 0, 2, near_rows, weights, front=(later_sent,), after=(far_sent,)
    )
    sent_both = ordered(in_hbm(sent_both), other_grads[0])
    far_out = expert_call("far_experts", 0, 4, far_rows, weights, after=(sent_both,))
    both = swap(sent_both, halves)
    far_back = swap(ordered(in_hbm(far_out), in_hbm(both), other_grads[1]), halves)
    near_out = expert_call("near_second", 2, 2, both, weights)

    def mixed_rows(name, slot_of, columns, backs, grads, kind, after=()):
        backs = [back.reshape(-1, features) for back in backs]
        return pl.pallas_call(
            functools.partial(mix_kernel, len(backs), len(grads)),
            out_shape=(shape((tok_rows, features), kind), shape((2 * TOP, tok_rows), F32)),
            in_specs=[vmem] * (2 + len(backs) + len(grads)) + [anywhere] * len(after),
            out_specs=(vmem, vmem),
            compiler_params=SMALL,
            name=name,
        )(slot_of, columns, *backs, *grads, *after)

    far_mixed, far_grads = mixed_rows(
        "mix_far", far_of, far_columns, (far_back,), other_grads, BF16, after=(in_hbm(near_out),)
    )
    near_back = swap(ordered(in_hbm(near_out), far_mixed), halves)
    near_mixed, near_grads = mixed_rows(
        "mix_near", near_of, near_columns, (both, near_back), (out_grad,), F32
    )
    arrived = ordered(mirrored(far_mixed), flops=400_000_000_000)
    mixed = (near_mixed + arrived.astype(F32)).astype(BF16)
    grads = (near_grads + mirrored(far_grads))[:TOP]
    return mixed, grads.T


def expert_work(arrived, w_gate, w_up, w_down):
    gate_act = jnp.einsum("sjcd,jdf->sjcf", arrived, w_gate, preferred_element_type=jnp.float32)
    up_act = jnp.einsum("sjcd,jdf->sjcf", arrived, w_up, preferred_element_type=jnp.float32)
    hidden = (jax.nn.silu(gate_act) * up_act).astype(jnp.bfloat16)
    return jnp.einsum("sjcf,jfd->sjcd", hidden, w_down, preferred_element_type=jnp.float32).astype(
        jnp.bfloat16
    )


def full_path(buffer, w_gate, w_up, w_down, device_count, exp_dev, width_split, features):
    group_count = EXPERTS // exp_dev
    grouped = buffer.reshape(group_count, 1, exp_dev, CAP, features)
    outgoing = jnp.broadcast_to(
        grouped, (group_count, width_split, exp_dev, CAP, features)
    ).reshape(device_count, exp_dev, CAP, features)
    returned_out = lax.all_to_all(
        expert_work(
            lax.all_to_all(outgoing, "expert", split_axis=0, concat_axis=0, tiled=True),
            w_gate,
            w_up,
            w_down,
        ),
        "expert",
        split_axis=0,
        concat_axis=0,
        tiled=True,
    )
    pieces = returned_out.reshape(group_count, width_split, exp_dev, CAP, features).astype(
        jnp.float32
    )
    return jnp.sum(pieces, axis=1).astype(jnp.bfloat16).reshape(EXPERTS * CAP, features)


def far_path(
    block_values,
    block_exps,
    row_ids,
    expert_ids,
    gate_weights,
    table,
    w_gate,
    w_up,
    w_down,
    out_grad,
):
    device_count = lax.axis_size("expert")
    tok_rows = block_values.shape[0]
    features = block_values.shape[1]
    rows_held = table.shape[0]
    look_cap = max(2, 2 * tok_rows // device_count)
    exp_dev = w_gate.shape[0]
    width_split = device_count * exp_dev // EXPERTS
    owners = row_ids // rows_held
    local_row = row_ids % rows_held
    owner_hot = (owners[:, None] == jnp.arange(device_count, dtype=jnp.int32)[None, :]).astype(
        jnp.int32
    )
    owner_rank = jnp.sum((jnp.cumsum(owner_hot, axis=0) - 1) * owner_hot, axis=1)
    placed = owners * look_cap + owner_rank
    wanted = jnp.zeros((device_count * look_cap,), jnp.int32).at[placed].set(local_row)
    requested = lax.all_to_all(
        wanted.reshape(device_count, look_cap), "expert", split_axis=0, concat_axis=0, tiled=True
    )
    fetched = jnp.take(table, requested.reshape(-1), axis=0).reshape(
        device_count, look_cap, features
    )
    rows_returned = lax.all_to_all(fetched, "expert", split_axis=0, concat_axis=0, tiled=True)
    embedded = jnp.take(rows_returned.reshape(device_count * look_cap, features), placed, axis=0)
    scales = jnp.exp2(block_exps.astype(jnp.float32))
    blocks = (
        block_values.reshape(tok_rows, scales.shape[1], -1).astype(jnp.float32) * scales[:, :, None]
    )
    token_state = (blocks.reshape(tok_rows, features) + embedded.astype(jnp.float32)).astype(
        jnp.bfloat16
    )
    flat_ids = expert_ids.reshape(-1)
    expert_hot = (flat_ids[:, None] == jnp.arange(EXPERTS, dtype=jnp.int32)[None, :]).astype(
        jnp.int32
    )
    expert_rank = jnp.sum((jnp.cumsum(expert_hot, axis=0) - 1) * expert_hot, axis=1)
    slot_of = flat_ids * CAP + expert_rank
    token_index = jnp.arange(tok_rows * TOP, dtype=jnp.int32) // TOP
    source = jnp.full((EXPERTS * CAP,), tok_rows, jnp.int32).at[slot_of].set(token_index)
    padded = jnp.concatenate([token_state, jnp.zeros((1, features), jnp.bfloat16)], axis=0)
    buffer = jnp.take(padded, source, axis=0)
    expert_out = full_path(
        buffer, w_gate, w_up, w_down, device_count, exp_dev, width_split, features
    )
    chosen = jnp.take(expert_out, slot_of, axis=0).reshape(tok_rows, TOP, features)
    mixed = jnp.sum(gate_weights[:, :, None] * chosen.astype(jnp.float32), axis=1).astype(
        jnp.bfloat16
    )
    gate_grads = jnp.einsum("tkd,td->tk", chosen, out_grad, preferred_element_type=jnp.float32)
    return (mixed, gate_grads)


def local(*arrays):
    if lax.axis_size("expert") == 16 and arrays[6].shape[0] * 16 == EXPERTS:
        return near_path(*arrays)
    return far_path(*arrays)


def solution(mesh):
    return jax.shard_map(
        local,
        mesh=mesh,
        in_specs=(
            P(("groups", "expert"), None),
            P(("groups", "expert"), None),
            P(("groups", "expert")),
            P(("groups", "expert"), None),
            P(("groups", "expert"), None),
            P("expert", None),
            P("expert", None, None),
            P("expert", None, None),
            P("expert", None, None),
            P(("groups", "expert"), None),
        ),
        out_specs=(P(("groups", "expert"), None), P(("groups", "expert"), None)),
        check_vma=False,
    )
```

```python
import functools

import jax
import jax.numpy as jnp
from jax import lax
from jax.experimental import pallas as pl
from jax.experimental.pallas import tpu as pltpu
from jax.sharding import PartitionSpec as P

EXPERTS = 64
TOP = 4
CAP = 12
BLOCK = 128
PAIR = 2 * CAP
VMEM = pltpu.VMEM
F32 = jnp.float32
BF16 = jnp.bfloat16
SMALL = pltpu.CompilerParams(vmem_limit_bytes=16 * 1024 * 1024)


def dot(a, b):
    return jnp.dot(a, b, preferred_element_type=F32)


def in_hbm(array):
    return pltpu.with_memory_space_constraint(array, pltpu.HBM)


def iota(shape, dimension):
    return lax.broadcasted_iota(jnp.int32, shape, dimension)


def flags(mask):
    return mask.astype(F32).astype(BF16)


def earlier(length):
    return flags(iota((length, length), 0) < iota((length, length), 1))


def repeat_kernel(rows_ref, grad_hbm, out_ref, upper_hbm, sem):
    copy = pltpu.make_async_copy(grad_hbm.at[pl.ds(0, upper_hbm.shape[0])], upper_hbm, sem)
    copy.start()
    for n in range(out_ref.shape[0]):
        out_ref[n] = rows_ref[...]
    copy.wait()


def fetch_kernel(me_ref, rows_ref, table_hbm, _, out_ref, table_ref, sem):
    copy = pltpu.make_async_copy(table_hbm, table_ref, sem)
    copy.start()
    device_count, _, tok_rows = rows_ref.shape
    held = table_ref.shape[0]
    look_cap = out_ref.shape[0] // device_count
    local = rows_ref[:, 0, :] - me_ref[0] * held
    hit = (local >= 0) & (local < held)
    rank = dot(flags(hit), earlier(tok_rows)).astype(jnp.int32)
    rank = jnp.where(hit, rank, -1)
    slot = iota((look_cap, tok_rows), 0)
    place = iota((look_cap, held), 1)
    picks = []
    for source in range(device_count):
        mine = jnp.where(slot == rank[source : source + 1], local[source : source + 1], 0)
        wanted = jnp.sum(mine, axis=1, keepdims=True)
        picks.append(flags(place == wanted))
    pick = jnp.concatenate(picks, axis=0)
    copy.wait()
    out_ref[...] = dot(pick, table_ref[...]).astype(BF16)


def turned(rows):
    count, length = rows.shape
    return jnp.concatenate([rows, jnp.zeros((length - count, length), F32)], axis=0).T


def plan_slots(me, ids_ref, pick_refs, slots_ref):
    tok_rows = ids_ref.shape[1]
    half = sum(ref.shape[0] for ref in pick_refs) // (2 * PAIR)
    exp_dev = EXPERTS // (2 * half)
    flip = me % 2
    inside = iota((half * exp_dev, tok_rows), 0)
    expert = inside + me // half * half * exp_dev
    place = iota((PAIR, tok_rows), 0)
    ids = ids_ref[...]
    chosen = [ids[k : k + 1] == expert for k in range(TOP)]
    hit = functools.reduce(jnp.logical_or, chosen)
    rank = jnp.where(hit, dot(flags(hit), earlier(tok_rows)).astype(jnp.int32), -1000)
    lines = []
    for at in range(0, half * exp_dev, 2):
        one, two = rank[at : at + 1], rank[at + 1 : at + 2]
        upper = jnp.where(flip == 0, one, two)
        lower = jnp.where(flip == 0, two, one) + CAP
        here = ((place < CAP) & (place == upper)) | ((place >= CAP) & (place == lower))
        lines.append(here.astype(F32))
    pairs = exp_dev // 2
    slot = ((inside + flip) & 1) * CAP + rank
    if len(pick_refs) == 1:
        pick_refs[0][...] = jnp.concatenate(lines, axis=0).astype(BF16)
        slot = slot + (inside // 2) * PAIR
    else:
        for n, ref in enumerate(pick_refs):
            ref[...] = jnp.concatenate(lines[n::pairs], axis=0).astype(BF16)
        device = inside // exp_dev
        first = device * (2 * PAIR) + PAIR
        second = half * 2 * PAIR + device * PAIR
        slot = slot + jnp.where((inside & 2) == 0, first, second)
    found = [
        jnp.sum(jnp.where(chosen[k], slot + 1, 0), axis=0, keepdims=True) - 1 for k in range(TOP)
    ]
    slots_ref[...] = turned(jnp.concatenate(found, axis=0).astype(F32)).astype(jnp.int32)


def near_plan_kernel(
    me_ref,
    rows_ref,
    ids_ref,
    weights_ref,
    scales_ref,
    _,
    put_ref,
    first_pick_ref,
    second_pick_ref,
    slots_ref,
    columns_ref,
    ids_out_ref,
    weights_out_ref,
):
    ids_out_ref[...] = ids_ref[...]
    weights_out_ref[...] = weights_ref[...]
    tok_rows = rows_ref.shape[1]
    me, held = me_ref[0], me_ref[1]
    device_count = first_pick_ref.shape[0] // PAIR * 2
    look_cap = put_ref.shape[1] // device_count
    row = jnp.broadcast_to(rows_ref[...], (device_count, tok_rows))
    low = iota((device_count, tok_rows), 0) * held
    hit = (row >= low) & (row < low + held)
    rank = jnp.where(hit, dot(flags(hit), earlier(tok_rows)).astype(jnp.int32), -1)
    slot = iota((look_cap, tok_rows), 0)
    put = [(slot == rank[o : o + 1]).astype(F32) for o in range(device_count)]
    put_ref[...] = jnp.concatenate(put, axis=0).T.astype(BF16)
    plan_slots(me, ids_ref, (first_pick_ref, second_pick_ref), slots_ref)
    columns_ref[...] = turned(jnp.concatenate([weights_ref[...], scales_ref[...]], axis=0))


def far_plan_kernel(me_ref, ids_ref, weights_ref, pick_ref, slots_ref, columns_ref):
    plan_slots(me_ref[0], ids_ref, (pick_ref,), slots_ref)
    columns_ref[...] = turned(weights_ref[...])


def state_kernel(
    put_ref, pick_ref, returned_ref, values_ref, columns_ref, _, state_ref, out_hbm, sent_ref, sem
):
    features = values_ref.shape[1]
    width = features // sem.shape[0]
    copies = []
    for n in range(sem.shape[0]):
        left = n * width
        found = dot(put_ref[...], returned_ref[:, left : left + width])
        for b in range(width // BLOCK):
            at = left + b * BLOCK
            scaled = (
                values_ref[:, at : at + BLOCK].astype(F32)
                * columns_ref[:, TOP + at // BLOCK : TOP + at // BLOCK + 1]
            )
            state_ref[:, at : at + BLOCK] = (
                scaled + found[:, b * BLOCK : (b + 1) * BLOCK]
            ).astype(BF16)
        cols = pl.ds(left, width)
        sent_ref[:, cols] = dot(pick_ref[...], state_ref[:, cols]).astype(BF16)
        copies.append(
            pltpu.make_async_copy(sent_ref.at[:, cols], out_hbm.at[:, cols], sem.at[n])
        )
        copies[-1].start()
    for copy in copies:
        copy.wait()


def later_kernel(pick_ref, state_ref, _, out_ref):
    out_ref[...] = dot(pick_ref[...], state_ref[...]).astype(BF16)


def pick_kernel(
    pick_ref, state_ref, grad_ref, out_hbm, lower_grad_ref, sent_ref, sem
):
    tok_rows, features = state_ref.shape
    width = features // sem.shape[0]
    copies = []
    for n in range(sem.shape[0]):
        cols = pl.ds(n * width, width)
        sent_ref[:, cols] = dot(pick_ref[...], state_ref[:, cols]).astype(BF16)
        copies.append(
            pltpu.make_async_copy(sent_ref.at[:, cols], out_hbm.at[:, cols], sem.at[n])
        )
        copies[-1].start()
    lower_grad_ref[...] = grad_ref[tok_rows // 2 :, :]
    for copy in copies:
        copy.wait()


def expert_kernel(first, count, join, after, rows_ref, *refs):
    if join:
        front_ref, refs = refs[0], refs[1:]
    wg_hbm, wu_hbm, wd_hbm, out_ref = refs[after : after + 4]
    x_ref, wg_ref, wu_ref, wd_ref, hidden_ref, result_ref, sem = refs[after + 4 :]
    held, features, width = wg_ref.shape
    half = rows_ref.shape[0]
    up_cuts = ((0, 512), (512, 512), (1024, width - 1024))
    down_cuts = tuple((at, 512) for at in range(0, features, 512))

    def weight_copies(j, place):
        copies = []
        for at, size in up_cuts:
            cols = pl.ds(at, size)
            copies.append((wg_hbm.at[first + j, :, cols], wg_ref.at[place, :, cols]))
            copies.append((wu_hbm.at[first + j, :, cols], wu_ref.at[place, :, cols]))
        for at, size in down_cuts:
            cols = pl.ds(at, size)
            copies.append((wd_hbm.at[first + j, :, cols], wd_ref.at[place, :, cols]))
        return [
            pltpu.make_async_copy(src, dst, sem.at[place, n])
            for n, (src, dst) in enumerate(copies)
        ]

    for j in range(held):
        for copy in weight_copies(j, j):
            copy.start()

    low = iota((PAIR, features), 0) < CAP
    for chunk in range(count // 2):
        here = slice(chunk * PAIR, (chunk + 1) * PAIR)
        for quad in range(half // 4):
            ones, twos = [], []
            for pair in range(2):
                source = 4 * quad + 2 * pair
                even = rows_ref[source, here, :].astype(F32)
                odd = rows_ref[source + 1, here, :].astype(F32)
                ones.append(jnp.where(low, even, odd))
                twos.append(jnp.where(low, odd, even))
            rows = slice(quad * 2 * PAIR, (quad + 1) * 2 * PAIR)
            x_ref[2 * chunk, rows, :] = jnp.concatenate(ones, axis=0).astype(BF16)
            x_ref[2 * chunk + 1, rows, :] = jnp.concatenate(twos, axis=0).astype(BF16)

    @pl.loop(0, count)
    def _(j):
        place = j % held
        copies = weight_copies(j, place)

        def refill(n, parts):
            @pl.when(j + held < count)
            def _():
                for copy in weight_copies(j + held, place)[n : n + parts]:
                    copy.start()

        n = 0
        for at, size in up_cuts:
            copies[n].wait()
            copies[n + 1].wait()
            gate = dot(x_ref[j], wg_ref[place, :, at : at + size])
            up = dot(x_ref[j], wu_ref[place, :, at : at + size])
            hidden = gate / (1.0 + jnp.exp(-gate)) * up
            hidden_ref[:, at : at + size] = hidden.astype(BF16)
            if count > held:
                refill(n, 2)
            n += 2
        for at, size in down_cuts:
            copies[n].wait()
            result_ref[j, :, at : at + size] = dot(
                hidden_ref[...], wd_ref[place, :, at : at + size]
            )
            if count > held:
                refill(n, 1)
            n += 1

    for pair in range(half // 2):
        rows = slice(pair * PAIR, (pair + 1) * PAIR)
        values = [result_ref[j, rows, :] for j in range(count)]
        for odd in range(2):
            parts = [
                jnp.where(low, values[j + odd], values[j + 1 - odd]) for j in range(0, count, 2)
            ]
            if join:
                parts = [front_ref[2 * pair + odd].astype(F32)] + parts
            out_ref[2 * pair + odd] = jnp.concatenate(parts, axis=0).astype(BF16)


def expert_call(name, first, count, rows_in, weights, front=(), after=()):
    w_gate, w_up, w_down = weights
    _, features, width = w_gate.shape
    half = rows_in.shape[0]
    rows = half * CAP
    held = 2
    anywhere = pl.BlockSpec(memory_space=pl.ANY)
    hbm = pl.BlockSpec(memory_space=pltpu.HBM)
    vmem = pl.BlockSpec(memory_space=VMEM)
    return pl.pallas_call(
        functools.partial(expert_kernel, first, count, bool(front), len(after)),
        out_shape=pltpu.HBM((half, count * CAP + len(front) * PAIR, features), BF16),
        in_specs=[vmem] * (1 + len(front)) + [anywhere] * len(after) + [hbm] * 3,
        out_specs=vmem,
        scratch_shapes=[
            VMEM((count, rows, features), BF16),
            VMEM((held, features, width), BF16),
            VMEM((held, features, width), BF16),
            VMEM((held, width, features), BF16),
            VMEM((rows, width), BF16),
            VMEM((count, rows, features), F32),
            pltpu.SemaphoreType.DMA((held, 10)),
        ],
        compiler_params=pltpu.CompilerParams(vmem_limit_bytes=46 * 1024 * 1024),
        cost_estimate=pl.CostEstimate(
            flops=12 * count * rows * features * width,
            bytes_accessed=6 * count * features * width,
            transcendentals=count * rows * width,
        ),
        name=name,
    )(
        *[in_hbm(array) for array in (rows_in, *front, *after, w_gate, w_up, w_down)],
    )


def mix_kernel(grads, added, start, slots_ref, columns_ref, back_ref, *refs):
    mixed_ref, grads_ref = refs[-2:]
    grad_refs, added_refs = refs[:grads], refs[grads : grads + 2 * added]
    tok_rows = slots_ref.shape[0]
    count, features = back_ref.shape
    grad = jnp.concatenate([ref[...] for ref in grad_refs], axis=0)
    place = iota((tok_rows, tok_rows), 1)
    wide = jnp.zeros((tok_rows, tok_rows), F32)
    column = iota((tok_rows, count), 1) + start
    inner = lax.dot_general(
        grad, back_ref[...], (((1,), (1,)), ((), ())), preferred_element_type=F32
    )
    total = jnp.zeros((tok_rows, count), F32)
    for k in range(TOP):
        here = column == slots_ref[:, k : k + 1]
        total = total + jnp.where(here, columns_ref[:, k : k + 1], 0.0)
        value = jnp.sum(jnp.where(here, inner, 0.0), axis=1, keepdims=True)
        wide = wide + jnp.where(place == k, value, 0.0)
    high = total.astype(BF16)
    rest = (total - high.astype(F32)).astype(BF16)
    width = 512
    for at in range(0, features, width):
        cols = slice(at, at + width)
        value = dot(high, back_ref[:, cols]) + dot(rest, back_ref[:, cols])
        for ref in added_refs[::2]:
            value = value + ref[:, cols].astype(F32)
        mixed_ref[:, cols] = value.astype(mixed_ref.dtype)
    lines = grads_ref.shape[0]
    sums = wide.T[:lines, :]
    for ref in added_refs[1::2]:
        sums = sums + ref[:lines, :]
    grads_ref[...] = sums


def swap(array, groups=None):
    return lax.all_to_all(
        array, "expert", split_axis=0, concat_axis=0, tiled=True, axis_index_groups=groups
    )


def near_path(
    block_values,
    block_exps,
    row_ids,
    expert_ids,
    gate_weights,
    table,
    w_gate,
    w_up,
    w_down,
    out_grad,
):
    device_count = lax.axis_size("expert")
    half = device_count // 2
    halves = [list(range(half)), list(range(half, device_count))]
    me = lax.axis_index("expert").astype(jnp.int32)
    tok_rows, features = block_values.shape
    rows_held = table.shape[0]
    look_cap = max(2, 2 * tok_rows // device_count)
    slots = half * 2 * PAIR
    vmem = pl.BlockSpec(memory_space=VMEM)
    smem = pl.BlockSpec(memory_space=pltpu.SMEM)
    anywhere = pl.BlockSpec(memory_space=pl.ANY)
    place = jnp.stack([me, jnp.int32(rows_held)])

    def shape(dims, kind):
        return jax.ShapeDtypeStruct(dims, kind)

    def mirrored(array):
        pairs = [(i, (i + half) % device_count) for i in range(device_count)]
        return lax.ppermute(array, "expert", pairs)

    def ordered(array, *earlier_arrays, flops=0):
        return pl.pallas_call(
            lambda *refs: None,
            out_shape=shape(array.shape, array.dtype),
            in_specs=[anywhere] * (1 + len(earlier_arrays)),
            out_specs=anywhere,
            input_output_aliases={0: 0},
            compiler_params=SMALL,
            cost_estimate=pl.CostEstimate(flops=flops, bytes_accessed=0, transcendentals=0),
            name="ordered",
        )(array, *earlier_arrays)

    upper = tok_rows // 2
    all_rows, upper_grad = pl.pallas_call(
        repeat_kernel,
        out_shape=(
            shape((device_count, 1, tok_rows), jnp.int32),
            pltpu.HBM((upper, features), BF16),
        ),
        in_specs=[vmem, anywhere],
        out_specs=(vmem, anywhere),
        scratch_shapes=[pltpu.SemaphoreType.DMA],
        name="repeat_rows",
    )(row_ids[None, :], in_hbm(out_grad))
    other_upper = mirrored(upper_grad)
    fetched = pl.pallas_call(
        fetch_kernel,
        out_shape=shape((device_count * look_cap, features), BF16),
        in_specs=[smem, vmem, pl.BlockSpec(memory_space=pltpu.HBM), anywhere],
        out_specs=vmem,
        scratch_shapes=[VMEM(table.shape, BF16), pltpu.SemaphoreType.DMA],
        compiler_params=SMALL,
        name="fetch_rows",
    )(place, swap(all_rows), in_hbm(table), in_hbm(other_upper))
    returned = swap(fetched.reshape(device_count, look_cap, features))
    turned_ids, turned_weights = expert_ids.T, gate_weights.T
    pick_shape = shape((slots, tok_rows), BF16)
    pair_shape = shape((slots // 2, tok_rows), BF16)
    square = (tok_rows, tok_rows)
    put, first_pick, second_pick, near_of, near_columns, sent_ids, sent_weights = pl.pallas_call(
        near_plan_kernel,
        out_shape=(
            shape((tok_rows, device_count * look_cap), BF16),
            pair_shape,
            pair_shape,
            shape(square, jnp.int32),
            shape(square, F32),
            shape(turned_ids.shape, jnp.int32),
            shape(turned_weights.shape, F32),
        ),
        in_specs=[smem, vmem, vmem, vmem, vmem, anywhere],
        out_specs=(vmem,) * 7,
        compiler_params=SMALL,
        name="near_plan",
    )(
        place,
        row_ids[None, :],
        turned_ids,
        turned_weights,
        jnp.exp2(block_exps.T.astype(F32)),
        fetched,
    )
    far_pick, far_of, far_columns = pl.pallas_call(
        far_plan_kernel,
        out_shape=(pick_shape, shape(square, jnp.int32), shape(square, F32)),
        in_specs=[smem, vmem, vmem],
        out_specs=(vmem,) * 3,
        compiler_params=SMALL,
        name="far_plan",
    )(place, mirrored(sent_ids), mirrored(sent_weights))

    def sent_scratch(count):
        return [VMEM((count, features), BF16), pltpu.SemaphoreType.DMA((4,))]

    state, near_sent = pl.pallas_call(
        state_kernel,
        out_shape=(shape((tok_rows, features), BF16), pltpu.HBM((slots // 2, features), BF16)),
        in_specs=[vmem] * 5 + [anywhere],
        out_specs=(vmem, anywhere),
        scratch_shapes=sent_scratch(slots // 2),
        compiler_params=SMALL,
        name="token_state",
    )(
        put,
        first_pick,
        returned.reshape(device_count * look_cap, features),
        block_values,
        near_columns,
        far_pick,
    )
    far_sent, lower_grad = pl.pallas_call(
        pick_kernel,
        out_shape=(
            pltpu.HBM((slots, features), BF16),
            shape((tok_rows - upper, features), BF16),
        ),
        in_specs=[vmem, vmem, vmem],
        out_specs=(anywhere, vmem),
        scratch_shapes=sent_scratch(slots),
        compiler_params=SMALL,
        cost_estimate=pl.CostEstimate(
            flops=400_000_000_000, bytes_accessed=4 * slots * features, transcendentals=0
        ),
        name="far_slots",
    )(far_pick, mirrored(state), out_grad)
    pair_rows = (half, PAIR, features)
    near_rows = swap(near_sent.reshape(pair_rows), halves)
    far_sent = far_sent.reshape(half, 2 * PAIR, features)
    far_rows = swap(far_sent, halves)
    later_sent = pl.pallas_call(
        later_kernel,
        out_shape=pltpu.HBM((slots // 2, features), BF16),
        in_specs=[vmem, vmem, anywhere],
        out_specs=vmem,
        compiler_params=SMALL,
        name="later_slots",
    )(second_pick, state, in_hbm(far_sent)).reshape(pair_rows)
    other_grads = (in_hbm(other_upper), mirrored(lower_grad))

    weights = (w_gate, w_up, w_down)
    sent_both = expert_call(
        "near_first", 0, 2, near_rows, weights, front=(later_sent,), after=(far_sent,)
    )
    far_out = expert_call("far_experts", 0, 4, far_rows, weights, after=(sent_both,))
    both = swap(sent_both, halves)
    far_back = swap(ordered(in_hbm(far_out), in_hbm(both), other_grads[1]), halves)
    near_out = expert_call("near_second", 2, 2, both, weights)

    def mixed_rows(
        name, slot_of, columns, back, grads, kind, start=0, lines=2 * TOP, added=(), after=()
    ):
        return pl.pallas_call(
            functools.partial(mix_kernel, len(grads), len(added) // 2, start),
            out_shape=(shape((tok_rows, features), kind), shape((lines, tok_rows), F32)),
            in_specs=[vmem] * (3 + len(grads) + len(added)) + [anywhere] * len(after),
            out_specs=(vmem, vmem),
            compiler_params=SMALL,
            name=name,
        )(slot_of, columns, back.reshape(-1, features), *grads, *added, *after)

    far_mixed, far_grads = mixed_rows(
        "mix_far", far_of, far_columns, far_back, other_grads, BF16, after=(in_hbm(near_out),)
    )
    near_back = swap(ordered(in_hbm(near_out), far_mixed), halves)
    near_sums = mixed_rows(
        "mix_first", near_of, near_columns, in_hbm(both.reshape(slots, features)), (out_grad,), F32
    )
    far_sums = (ordered(mirrored(far_mixed), flops=400_000_000_000), mirrored(far_grads))
    mixed, grads = mixed_rows(
        "mix_second",
        near_of,
        near_columns,
        near_back,
        (out_grad,),
        BF16,
        start=slots,
        lines=TOP,
        added=(*near_sums, *far_sums),
    )
    return mixed, grads.T


def expert_work(arrived, w_gate, w_up, w_down):
    gate_act = jnp.einsum("sjcd,jdf->sjcf", arrived, w_gate, preferred_element_type=jnp.float32)
    up_act = jnp.einsum("sjcd,jdf->sjcf", arrived, w_up, preferred_element_type=jnp.float32)
    hidden = (jax.nn.silu(gate_act) * up_act).astype(jnp.bfloat16)
    return jnp.einsum("sjcf,jfd->sjcd", hidden, w_down, preferred_element_type=jnp.float32).astype(
        jnp.bfloat16
    )


def full_path(buffer, w_gate, w_up, w_down, device_count, exp_dev, width_split, features):
    group_count = EXPERTS // exp_dev
    grouped = buffer.reshape(group_count, 1, exp_dev, CAP, features)
    outgoing = jnp.broadcast_to(
        grouped, (group_count, width_split, exp_dev, CAP, features)
    ).reshape(device_count, exp_dev, CAP, features)
    returned_out = lax.all_to_all(
        expert_work(
            lax.all_to_all(outgoing, "expert", split_axis=0, concat_axis=0, tiled=True),
            w_gate,
            w_up,
            w_down,
        ),
        "expert",
        split_axis=0,
        concat_axis=0,
        tiled=True,
    )
    pieces = returned_out.reshape(group_count, width_split, exp_dev, CAP, features).astype(
        jnp.float32
    )
    return jnp.sum(pieces, axis=1).astype(jnp.bfloat16).reshape(EXPERTS * CAP, features)


def far_path(
    block_values,
    block_exps,
    row_ids,
    expert_ids,
    gate_weights,
    table,
    w_gate,
    w_up,
    w_down,
    out_grad,
):
    device_count = lax.axis_size("expert")
    tok_rows = block_values.shape[0]
    features = block_values.shape[1]
    rows_held = table.shape[0]
    look_cap = max(2, 2 * tok_rows // device_count)
    exp_dev = w_gate.shape[0]
    width_split = device_count * exp_dev // EXPERTS
    owners = row_ids // rows_held
    local_row = row_ids % rows_held
    owner_hot = (owners[:, None] == jnp.arange(device_count, dtype=jnp.int32)[None, :]).astype(
        jnp.int32
    )
    owner_rank = jnp.sum((jnp.cumsum(owner_hot, axis=0) - 1) * owner_hot, axis=1)
    placed = owners * look_cap + owner_rank
    wanted = jnp.zeros((device_count * look_cap,), jnp.int32).at[placed].set(local_row)
    requested = lax.all_to_all(
        wanted.reshape(device_count, look_cap), "expert", split_axis=0, concat_axis=0, tiled=True
    )
    fetched = jnp.take(table, requested.reshape(-1), axis=0).reshape(
        device_count, look_cap, features
    )
    rows_returned = lax.all_to_all(fetched, "expert", split_axis=0, concat_axis=0, tiled=True)
    embedded = jnp.take(rows_returned.reshape(device_count * look_cap, features), placed, axis=0)
    scales = jnp.exp2(block_exps.astype(jnp.float32))
    blocks = (
        block_values.reshape(tok_rows, scales.shape[1], -1).astype(jnp.float32) * scales[:, :, None]
    )
    token_state = (blocks.reshape(tok_rows, features) + embedded.astype(jnp.float32)).astype(
        jnp.bfloat16
    )
    flat_ids = expert_ids.reshape(-1)
    expert_hot = (flat_ids[:, None] == jnp.arange(EXPERTS, dtype=jnp.int32)[None, :]).astype(
        jnp.int32
    )
    expert_rank = jnp.sum((jnp.cumsum(expert_hot, axis=0) - 1) * expert_hot, axis=1)
    slot_of = flat_ids * CAP + expert_rank
    token_index = jnp.arange(tok_rows * TOP, dtype=jnp.int32) // TOP
    source = jnp.full((EXPERTS * CAP,), tok_rows, jnp.int32).at[slot_of].set(token_index)
    padded = jnp.concatenate([token_state, jnp.zeros((1, features), jnp.bfloat16)], axis=0)
    buffer = jnp.take(padded, source, axis=0)
    expert_out = full_path(
        buffer, w_gate, w_up, w_down, device_count, exp_dev, width_split, features
    )
    chosen = jnp.take(expert_out, slot_of, axis=0).reshape(tok_rows, TOP, features)
    mixed = jnp.sum(gate_weights[:, :, None] * chosen.astype(jnp.float32), axis=1).astype(
        jnp.bfloat16
    )
    gate_grads = jnp.einsum("tkd,td->tk", chosen, out_grad, preferred_element_type=jnp.float32)
    return (mixed, gate_grads)


def local(*arrays):
    if lax.axis_size("expert") == 16 and arrays[6].shape[0] * 16 == EXPERTS:
        return near_path(*arrays)
    return far_path(*arrays)


def solution(mesh):
    return jax.shard_map(
        local,
        mesh=mesh,
        in_specs=(
            P(("groups", "expert"), None),
            P(("groups", "expert"), None),
            P(("groups", "expert")),
            P(("groups", "expert"), None),
            P(("groups", "expert"), None),
            P("expert", None),
            P("expert", None, None),
            P("expert", None, None),
            P("expert", None, None),
            P(("groups", "expert"), None),
        ),
        out_specs=(P(("groups", "expert"), None), P(("groups", "expert"), None)),
        check_vma=False,
    )
```

```python
import functools

import jax
import jax.numpy as jnp
from jax import lax
from jax.experimental import pallas as pl
from jax.experimental.pallas import tpu as pltpu
from jax.sharding import PartitionSpec as P

EXPERTS = 64
TOP = 4
CAP = 12
BLOCK = 128
PAIR = 2 * CAP
VMEM = pltpu.VMEM
F32 = jnp.float32
BF16 = jnp.bfloat16
SMALL = pltpu.CompilerParams(vmem_limit_bytes=16 * 1024 * 1024)


def dot(a, b):
    return jnp.dot(a, b, preferred_element_type=F32)


def in_hbm(array):
    return pltpu.with_memory_space_constraint(array, pltpu.HBM)


def iota(shape, dimension):
    return lax.broadcasted_iota(jnp.int32, shape, dimension)


def flags(mask):
    return mask.astype(F32).astype(BF16)


def earlier(length):
    return flags(iota((length, length), 0) < iota((length, length), 1))


def repeat_kernel(rows_ref, grad_ref, out_ref, upper_ref):
    for n in range(out_ref.shape[0]):
        out_ref[n] = rows_ref[...]
    upper_ref[...] = grad_ref[...]


def fetch_kernel(me_ref, rows_ref, table_hbm, _, out_ref, table_ref, sem):
    copy = pltpu.make_async_copy(table_hbm, table_ref, sem)
    copy.start()
    device_count, _, tok_rows = rows_ref.shape
    held = table_ref.shape[0]
    look_cap = out_ref.shape[0] // device_count
    local = rows_ref[:, 0, :] - me_ref[0] * held
    hit = (local >= 0) & (local < held)
    rank = dot(flags(hit), earlier(tok_rows)).astype(jnp.int32)
    rank = jnp.where(hit, rank, -1)
    slot = iota((look_cap, tok_rows), 0)
    place = iota((look_cap, held), 1)
    picks = []
    for source in range(device_count):
        mine = jnp.where(slot == rank[source : source + 1], local[source : source + 1], 0)
        wanted = jnp.sum(mine, axis=1, keepdims=True)
        picks.append(flags(place == wanted))
    pick = jnp.concatenate(picks, axis=0)
    copy.wait()
    out_ref[...] = dot(pick, table_ref[...]).astype(BF16)


def turned(rows):
    count, length = rows.shape
    return jnp.concatenate([rows, jnp.zeros((length - count, length), F32)], axis=0).T


def plan_slots(me, ids_ref, pick_refs, slots_ref):
    tok_rows = ids_ref.shape[1]
    half = sum(ref.shape[0] for ref in pick_refs) // (2 * PAIR)
    exp_dev = EXPERTS // (2 * half)
    flip = me % 2
    inside = iota((half * exp_dev, tok_rows), 0)
    expert = inside + me // half * half * exp_dev
    place = iota((PAIR, tok_rows), 0)
    ids = ids_ref[...]
    chosen = [ids[k : k + 1] == expert for k in range(TOP)]
    hit = functools.reduce(jnp.logical_or, chosen)
    rank = jnp.where(hit, dot(flags(hit), earlier(tok_rows)).astype(jnp.int32), -1000)
    lines = []
    for at in range(0, half * exp_dev, 2):
        one, two = rank[at : at + 1], rank[at + 1 : at + 2]
        upper = jnp.where(flip == 0, one, two)
        lower = jnp.where(flip == 0, two, one) + CAP
        here = ((place < CAP) & (place == upper)) | ((place >= CAP) & (place == lower))
        lines.append(here.astype(F32))
    pairs = exp_dev // 2
    slot = ((inside + flip) & 1) * CAP + rank
    if len(pick_refs) == 1:
        pick_refs[0][...] = jnp.concatenate(lines, axis=0).astype(BF16)
        slot = slot + (inside // 2) * PAIR
    else:
        for n, ref in enumerate(pick_refs):
            ref[...] = jnp.concatenate(lines[n::pairs], axis=0).astype(BF16)
        device = inside // exp_dev
        first = device * (2 * PAIR) + PAIR
        second = half * 2 * PAIR + device * PAIR
        slot = slot + jnp.where((inside & 2) == 0, first, second)
    found = [
        jnp.sum(jnp.where(chosen[k], slot + 1, 0), axis=0, keepdims=True) - 1 for k in range(TOP)
    ]
    slots_ref[...] = turned(jnp.concatenate(found, axis=0).astype(F32)).astype(jnp.int32)


def near_plan_kernel(
    me_ref,
    rows_ref,
    ids_ref,
    weights_ref,
    scales_ref,
    _,
    put_ref,
    first_pick_ref,
    second_pick_ref,
    slots_ref,
    columns_ref,
    ids_out_ref,
    weights_out_ref,
):
    ids_out_ref[...] = ids_ref[...]
    weights_out_ref[...] = weights_ref[...]
    tok_rows = rows_ref.shape[1]
    me, held = me_ref[0], me_ref[1]
    device_count = first_pick_ref.shape[0] // PAIR * 2
    look_cap = put_ref.shape[1] // device_count
    row = jnp.broadcast_to(rows_ref[...], (device_count, tok_rows))
    low = iota((device_count, tok_rows), 0) * held
    hit = (row >= low) & (row < low + held)
    rank = jnp.where(hit, dot(flags(hit), earlier(tok_rows)).astype(jnp.int32), -1)
    slot = iota((look_cap, tok_rows), 0)
    put = [(slot == rank[o : o + 1]).astype(F32) for o in range(device_count)]
    put_ref[...] = jnp.concatenate(put, axis=0).T.astype(BF16)
    plan_slots(me, ids_ref, (first_pick_ref, second_pick_ref), slots_ref)
    columns_ref[...] = turned(jnp.concatenate([weights_ref[...], scales_ref[...]], axis=0))


def far_plan_kernel(me_ref, ids_ref, weights_ref, _, pick_ref, slots_ref, columns_ref):
    plan_slots(me_ref[0], ids_ref, (pick_ref,), slots_ref)
    columns_ref[...] = turned(weights_ref[...])


def state_kernel(
    put_ref,
    pick_ref,
    returned_ref,
    values_ref,
    columns_ref,
    ids_ref,
    weights_ref,
    state_ref,
    out_hbm,
    sent_ref,
    sem,
):
    features = values_ref.shape[1]
    width = features // sem.shape[0]
    copies = []
    for n in range(sem.shape[0]):
        left = n * width
        found = dot(put_ref[...], returned_ref[:, left : left + width])
        for b in range(width // BLOCK):
            at = left + b * BLOCK
            scaled = (
                values_ref[:, at : at + BLOCK].astype(F32)
                * columns_ref[:, TOP + at // BLOCK : TOP + at // BLOCK + 1]
            )
            state_ref[:, at : at + BLOCK] = (
                scaled + found[:, b * BLOCK : (b + 1) * BLOCK]
            ).astype(BF16)
        cols = pl.ds(left, width)
        sent_ref[:, cols] = dot(pick_ref[...], state_ref[:, cols]).astype(BF16)
        copies.append(
            pltpu.make_async_copy(sent_ref.at[:, cols], out_hbm.at[:, cols], sem.at[n])
        )
        copies[-1].start()
    for copy in copies:
        copy.wait()


def later_kernel(pick_ref, state_ref, _, out_ref):
    out_ref[...] = dot(pick_ref[...], state_ref[...]).astype(BF16)


def pick_kernel(
    pick_ref, state_ref, grad_ref, out_hbm, lower_grad_ref, sent_ref, sem
):
    tok_rows, features = state_ref.shape
    width = features // sem.shape[0]
    copies = []
    for n in range(sem.shape[0]):
        cols = pl.ds(n * width, width)
        sent_ref[:, cols] = dot(pick_ref[...], state_ref[:, cols]).astype(BF16)
        copies.append(
            pltpu.make_async_copy(sent_ref.at[:, cols], out_hbm.at[:, cols], sem.at[n])
        )
        copies[-1].start()
    lower_grad_ref[...] = grad_ref[tok_rows // 2 :, :]
    for copy in copies:
        copy.wait()


def expert_kernel(first, count, join, after, rows_hbm, *refs):
    if join:
        front_ref, refs = refs[0], refs[1:]
    wg_hbm, wu_hbm, wd_hbm, out_ref = refs[after : after + 4]
    rows_ref, x_ref, wg_ref, wu_ref, wd_ref, hidden_ref, result_ref, sem, rows_sem = refs[
        after + 4 :
    ]
    held, features, width = wg_ref.shape
    half = rows_ref.shape[0]
    up_cuts = ((0, 512), (512, 512), (1024, width - 1024))
    down_cuts = tuple((at, 512) for at in range(0, features, 512))

    def weight_copies(j, place):
        copies = []
        for at, size in up_cuts:
            cols = pl.ds(at, size)
            copies.append((wg_hbm.at[first + j, :, cols], wg_ref.at[place, :, cols]))
            copies.append((wu_hbm.at[first + j, :, cols], wu_ref.at[place, :, cols]))
        for at, size in down_cuts:
            cols = pl.ds(at, size)
            copies.append((wd_hbm.at[first + j, :, cols], wd_ref.at[place, :, cols]))
        return [
            pltpu.make_async_copy(src, dst, sem.at[place, n])
            for n, (src, dst) in enumerate(copies)
        ]

    rows_copy = pltpu.make_async_copy(rows_hbm, rows_ref, rows_sem)
    rows_copy.start()
    weights = weight_copies(0, 0) + weight_copies(1, 1)
    for copy in weights[:4]:
        copy.start()
    rows_copy.wait()
    for copy in weights[4:]:
        copy.start()

    low = iota((PAIR, features), 0) < CAP
    for chunk in range(count // 2):
        here = slice(chunk * PAIR, (chunk + 1) * PAIR)
        for quad in range(half // 4):
            ones, twos = [], []
            for pair in range(2):
                source = 4 * quad + 2 * pair
                even = rows_ref[source, here, :].astype(F32)
                odd = rows_ref[source + 1, here, :].astype(F32)
                ones.append(jnp.where(low, even, odd))
                twos.append(jnp.where(low, odd, even))
            rows = slice(quad * 2 * PAIR, (quad + 1) * 2 * PAIR)
            x_ref[2 * chunk, rows, :] = jnp.concatenate(ones, axis=0).astype(BF16)
            x_ref[2 * chunk + 1, rows, :] = jnp.concatenate(twos, axis=0).astype(BF16)

    @pl.loop(0, count)
    def _(j):
        place = j % held
        copies = weight_copies(j, place)

        def refill(n, parts):
            @pl.when(j + held < count)
            def _():
                for copy in weight_copies(j + held, place)[n : n + parts]:
                    copy.start()

        n = 0
        for at, size in up_cuts:
            copies[n].wait()
            copies[n + 1].wait()
            gate = dot(x_ref[j], wg_ref[place, :, at : at + size])
            up = dot(x_ref[j], wu_ref[place, :, at : at + size])
            hidden = gate / (1.0 + jnp.exp(-gate)) * up
            hidden_ref[:, at : at + size] = hidden.astype(BF16)
            if count > held:
                refill(n, 2)
            n += 2
        for at, size in down_cuts:
            copies[n].wait()
            result_ref[j, :, at : at + size] = dot(
                hidden_ref[...], wd_ref[place, :, at : at + size]
            )
            if count > held:
                refill(n, 1)
            n += 1

    for pair in range(half // 2):
        rows = slice(pair * PAIR, (pair + 1) * PAIR)
        values = [result_ref[j, rows, :] for j in range(count)]
        for odd in range(2):
            parts = [
                jnp.where(low, values[j + odd], values[j + 1 - odd]) for j in range(0, count, 2)
            ]
            if join:
                parts = [front_ref[2 * pair + odd].astype(F32)] + parts
            out_ref[2 * pair + odd] = jnp.concatenate(parts, axis=0).astype(BF16)


def expert_call(name, first, count, rows_in, weights, front=(), after=()):
    w_gate, w_up, w_down = weights
    _, features, width = w_gate.shape
    half = rows_in.shape[0]
    rows = half * CAP
    held = 2
    anywhere = pl.BlockSpec(memory_space=pl.ANY)
    hbm = pl.BlockSpec(memory_space=pltpu.HBM)
    vmem = pl.BlockSpec(memory_space=VMEM)
    return pl.pallas_call(
        functools.partial(expert_kernel, first, count, bool(front), len(after)),
        out_shape=pltpu.HBM((half, count * CAP + len(front) * PAIR, features), BF16),
        in_specs=[hbm] + [vmem] * len(front) + [anywhere] * len(after) + [hbm] * 3,
        out_specs=vmem,
        scratch_shapes=[
            VMEM(rows_in.shape, BF16),
            VMEM((count, rows, features), BF16),
            VMEM((held, features, width), BF16),
            VMEM((held, features, width), BF16),
            VMEM((held, width, features), BF16),
            VMEM((rows, width), BF16),
            VMEM((count, rows, features), F32),
            pltpu.SemaphoreType.DMA((held, 10)),
            pltpu.SemaphoreType.DMA,
        ],
        compiler_params=pltpu.CompilerParams(vmem_limit_bytes=46 * 1024 * 1024),
        cost_estimate=pl.CostEstimate(
            flops=12 * count * rows * features * width,
            bytes_accessed=6 * count * features * width,
            transcendentals=count * rows * width,
        ),
        name=name,
    )(
        *[in_hbm(array) for array in (rows_in, *front, *after, w_gate, w_up, w_down)],
    )


def mix_kernel(grads, added, start, slots_ref, columns_ref, back_ref, *refs):
    mixed_ref, grads_ref = refs[-2:]
    grad_refs, added_refs = refs[:grads], refs[grads : grads + 2 * added]
    tok_rows = slots_ref.shape[0]
    count, features = back_ref.shape
    grad = jnp.concatenate([ref[...] for ref in grad_refs], axis=0)
    place = iota((tok_rows, tok_rows), 1)
    wide = jnp.zeros((tok_rows, tok_rows), F32)
    column = iota((tok_rows, count), 1) + start
    inner = lax.dot_general(
        grad, back_ref[...], (((1,), (1,)), ((), ())), preferred_element_type=F32
    )
    total = jnp.zeros((tok_rows, count), F32)
    for k in range(TOP):
        here = column == slots_ref[:, k : k + 1]
        total = total + jnp.where(here, columns_ref[:, k : k + 1], 0.0)
        value = jnp.sum(jnp.where(here, inner, 0.0), axis=1, keepdims=True)
        wide = wide + jnp.where(place == k, value, 0.0)
    high = total.astype(BF16)
    rest = (total - high.astype(F32)).astype(BF16)
    width = 512
    for at in range(0, features, width):
        cols = slice(at, at + width)
        value = dot(high, back_ref[:, cols]) + dot(rest, back_ref[:, cols])
        for ref in added_refs[::2]:
            value = value + ref[:, cols].astype(F32)
        mixed_ref[:, cols] = value.astype(mixed_ref.dtype)
    lines = grads_ref.shape[0]
    sums = wide.T[:lines, :]
    for ref in added_refs[1::2]:
        sums = sums + ref[:lines, :]
    grads_ref[...] = sums


def swap(array, groups=None):
    return lax.all_to_all(
        array, "expert", split_axis=0, concat_axis=0, tiled=True, axis_index_groups=groups
    )


def near_path(
    block_values,
    block_exps,
    row_ids,
    expert_ids,
    gate_weights,
    table,
    w_gate,
    w_up,
    w_down,
    out_grad,
):
    device_count = lax.axis_size("expert")
    half = device_count // 2
    halves = [list(range(half)), list(range(half, device_count))]
    me = lax.axis_index("expert").astype(jnp.int32)
    tok_rows, features = block_values.shape
    rows_held = table.shape[0]
    look_cap = max(2, 2 * tok_rows // device_count)
    slots = half * 2 * PAIR
    vmem = pl.BlockSpec(memory_space=VMEM)
    smem = pl.BlockSpec(memory_space=pltpu.SMEM)
    anywhere = pl.BlockSpec(memory_space=pl.ANY)
    place = jnp.stack([me, jnp.int32(rows_held)])

    def shape(dims, kind):
        return jax.ShapeDtypeStruct(dims, kind)

    def mirrored(array):
        pairs = [(i, (i + half) % device_count) for i in range(device_count)]
        return lax.ppermute(array, "expert", pairs)

    def ordered(array, *earlier_arrays, flops=0):
        return pl.pallas_call(
            lambda *refs: None,
            out_shape=shape(array.shape, array.dtype),
            in_specs=[anywhere] * (1 + len(earlier_arrays)),
            out_specs=anywhere,
            input_output_aliases={0: 0},
            compiler_params=SMALL,
            cost_estimate=pl.CostEstimate(flops=flops, bytes_accessed=0, transcendentals=0),
            name="ordered",
        )(array, *earlier_arrays)

    upper = tok_rows // 2
    all_rows, upper_grad = pl.pallas_call(
        repeat_kernel,
        out_shape=(
            shape((device_count, 1, tok_rows), jnp.int32),
            shape((upper, features), BF16),
        ),
        grid=(1,),
        in_specs=[
            pl.BlockSpec((1, tok_rows), lambda i: (0, 0)),
            pl.BlockSpec((upper, features), lambda i: (0, 0)),
        ],
        out_specs=(
            pl.BlockSpec((device_count, 1, tok_rows), lambda i: (0, 0, 0)),
            pl.BlockSpec((upper, features), lambda i: (0, 0)),
        ),
        name="repeat_rows",
    )(row_ids[None, :], out_grad)
    other_upper = mirrored(upper_grad)
    fetched = pl.pallas_call(
        fetch_kernel,
        out_shape=shape((device_count * look_cap, features), BF16),
        in_specs=[smem, vmem, pl.BlockSpec(memory_space=pltpu.HBM), anywhere],
        out_specs=vmem,
        scratch_shapes=[VMEM(table.shape, BF16), pltpu.SemaphoreType.DMA],
        compiler_params=SMALL,
        name="fetch_rows",
    )(place, swap(all_rows), in_hbm(table), other_upper)
    returned = swap(fetched.reshape(device_count, look_cap, features))
    turned_ids, turned_weights = expert_ids.T, gate_weights.T
    pick_shape = shape((slots, tok_rows), BF16)
    pair_shape = shape((slots // 2, tok_rows), BF16)
    square = (tok_rows, tok_rows)
    put, first_pick, second_pick, near_of, near_columns, sent_ids, sent_weights = pl.pallas_call(
        near_plan_kernel,
        out_shape=(
            shape((tok_rows, device_count * look_cap), BF16),
            pair_shape,
            pair_shape,
            shape(square, jnp.int32),
            shape(square, F32),
            shape(turned_ids.shape, jnp.int32),
            shape(turned_weights.shape, F32),
        ),
        in_specs=[smem, vmem, vmem, vmem, vmem, anywhere],
        out_specs=(vmem,) * 7,
        compiler_params=SMALL,
        name="near_plan",
    )(
        place,
        row_ids[None, :],
        turned_ids,
        turned_weights,
        jnp.exp2(block_exps.T.astype(F32)),
        fetched,
    )
    other_ids, other_weights = mirrored(sent_ids), mirrored(sent_weights)

    def sent_scratch(count):
        return [VMEM((count, features), BF16), pltpu.SemaphoreType.DMA((4,))]

    state, near_sent = pl.pallas_call(
        state_kernel,
        out_shape=(shape((tok_rows, features), BF16), pltpu.HBM((slots // 2, features), BF16)),
        in_specs=[vmem] * 5 + [anywhere] * 2,
        out_specs=(vmem, anywhere),
        scratch_shapes=sent_scratch(slots // 2),
        compiler_params=SMALL,
        name="token_state",
    )(
        put,
        first_pick,
        returned.reshape(device_count * look_cap, features),
        block_values,
        near_columns,
        other_ids,
        other_weights,
    )
    far_pick, far_of, far_columns = pl.pallas_call(
        far_plan_kernel,
        out_shape=(pick_shape, shape(square, jnp.int32), shape(square, F32)),
        in_specs=[smem, vmem, vmem, anywhere],
        out_specs=(vmem,) * 3,
        compiler_params=SMALL,
        name="far_plan",
    )(place, other_ids, other_weights, state)
    far_sent, lower_grad = pl.pallas_call(
        pick_kernel,
        out_shape=(
            pltpu.HBM((slots, features), BF16),
            shape((tok_rows - upper, features), BF16),
        ),
        in_specs=[vmem, vmem, vmem],
        out_specs=(anywhere, vmem),
        scratch_shapes=sent_scratch(slots),
        compiler_params=SMALL,
        cost_estimate=pl.CostEstimate(
            flops=400_000_000_000, bytes_accessed=4 * slots * features, transcendentals=0
        ),
        name="far_slots",
    )(far_pick, mirrored(state), out_grad)
    pair_rows = (half, PAIR, features)
    near_rows = swap(near_sent.reshape(pair_rows), halves)
    far_sent = far_sent.reshape(half, 2 * PAIR, features)
    far_rows = swap(far_sent, halves)
    later_sent = pl.pallas_call(
        later_kernel,
        out_shape=pltpu.HBM((slots // 2, features), BF16),
        in_specs=[vmem, vmem, anywhere],
        out_specs=vmem,
        compiler_params=SMALL,
        name="later_slots",
    )(second_pick, state, in_hbm(far_sent)).reshape(pair_rows)
    other_grads = (other_upper, mirrored(lower_grad))

    weights = (w_gate, w_up, w_down)
    sent_both = expert_call(
        "near_first", 0, 2, near_rows, weights, front=(later_sent,), after=(far_sent,)
    )
    far_out = expert_call("far_experts", 0, 4, far_rows, weights, after=(sent_both,))
    both = swap(sent_both, halves)
    far_back = swap(ordered(in_hbm(far_out), in_hbm(both), other_grads[1]), halves)
    near_out = expert_call("near_second", 2, 2, both, weights)

    def mixed_rows(
        name, slot_of, columns, back, grads, kind, start=0, lines=2 * TOP, added=(), after=()
    ):
        return pl.pallas_call(
            functools.partial(mix_kernel, len(grads), len(added) // 2, start),
            out_shape=(shape((tok_rows, features), kind), shape((lines, tok_rows), F32)),
            in_specs=[vmem] * (3 + len(grads) + len(added)) + [anywhere] * len(after),
            out_specs=(vmem, vmem),
            compiler_params=SMALL,
            name=name,
        )(slot_of, columns, back.reshape(-1, features), *grads, *added, *after)

    far_mixed, far_grads = mixed_rows(
        "mix_far", far_of, far_columns, far_back, other_grads, BF16, after=(in_hbm(near_out),)
    )
    near_back = swap(ordered(in_hbm(near_out), far_mixed), halves)
    far_sums = (ordered(mirrored(far_mixed), flops=400_000_000_000), mirrored(far_grads))
    sums = mixed_rows(
        "mix_first",
        near_of,
        near_columns,
        in_hbm(both.reshape(slots, features)),
        (out_grad,),
        F32,
        added=far_sums,
    )
    mixed, grads = mixed_rows(
        "mix_second",
        near_of,
        near_columns,
        near_back,
        (out_grad,),
        BF16,
        start=slots,
        lines=TOP,
        added=sums,
    )
    return mixed, grads.T


def expert_work(arrived, w_gate, w_up, w_down):
    gate_act = jnp.einsum("sjcd,jdf->sjcf", arrived, w_gate, preferred_element_type=jnp.float32)
    up_act = jnp.einsum("sjcd,jdf->sjcf", arrived, w_up, preferred_element_type=jnp.float32)
    hidden = (jax.nn.silu(gate_act) * up_act).astype(jnp.bfloat16)
    return jnp.einsum("sjcf,jfd->sjcd", hidden, w_down, preferred_element_type=jnp.float32).astype(
        jnp.bfloat16
    )


def full_path(buffer, w_gate, w_up, w_down, device_count, exp_dev, width_split, features):
    group_count = EXPERTS // exp_dev
    grouped = buffer.reshape(group_count, 1, exp_dev, CAP, features)
    outgoing = jnp.broadcast_to(
        grouped, (group_count, width_split, exp_dev, CAP, features)
    ).reshape(device_count, exp_dev, CAP, features)
    returned_out = lax.all_to_all(
        expert_work(
            lax.all_to_all(outgoing, "expert", split_axis=0, concat_axis=0, tiled=True),
            w_gate,
            w_up,
            w_down,
        ),
        "expert",
        split_axis=0,
        concat_axis=0,
        tiled=True,
    )
    pieces = returned_out.reshape(group_count, width_split, exp_dev, CAP, features).astype(
        jnp.float32
    )
    return jnp.sum(pieces, axis=1).astype(jnp.bfloat16).reshape(EXPERTS * CAP, features)


def far_path(
    block_values,
    block_exps,
    row_ids,
    expert_ids,
    gate_weights,
    table,
    w_gate,
    w_up,
    w_down,
    out_grad,
):
    device_count = lax.axis_size("expert")
    tok_rows = block_values.shape[0]
    features = block_values.shape[1]
    rows_held = table.shape[0]
    look_cap = max(2, 2 * tok_rows // device_count)
    exp_dev = w_gate.shape[0]
    width_split = device_count * exp_dev // EXPERTS
    owners = row_ids // rows_held
    local_row = row_ids % rows_held
    owner_hot = (owners[:, None] == jnp.arange(device_count, dtype=jnp.int32)[None, :]).astype(
        jnp.int32
    )
    owner_rank = jnp.sum((jnp.cumsum(owner_hot, axis=0) - 1) * owner_hot, axis=1)
    placed = owners * look_cap + owner_rank
    wanted = jnp.zeros((device_count * look_cap,), jnp.int32).at[placed].set(local_row)
    requested = lax.all_to_all(
        wanted.reshape(device_count, look_cap), "expert", split_axis=0, concat_axis=0, tiled=True
    )
    fetched = jnp.take(table, requested.reshape(-1), axis=0).reshape(
        device_count, look_cap, features
    )
    rows_returned = lax.all_to_all(fetched, "expert", split_axis=0, concat_axis=0, tiled=True)
    embedded = jnp.take(rows_returned.reshape(device_count * look_cap, features), placed, axis=0)
    scales = jnp.exp2(block_exps.astype(jnp.float32))
    blocks = (
        block_values.reshape(tok_rows, scales.shape[1], -1).astype(jnp.float32) * scales[:, :, None]
    )
    token_state = (blocks.reshape(tok_rows, features) + embedded.astype(jnp.float32)).astype(
        jnp.bfloat16
    )
    flat_ids = expert_ids.reshape(-1)
    expert_hot = (flat_ids[:, None] == jnp.arange(EXPERTS, dtype=jnp.int32)[None, :]).astype(
        jnp.int32
    )
    expert_rank = jnp.sum((jnp.cumsum(expert_hot, axis=0) - 1) * expert_hot, axis=1)
    slot_of = flat_ids * CAP + expert_rank
    token_index = jnp.arange(tok_rows * TOP, dtype=jnp.int32) // TOP
    source = jnp.full((EXPERTS * CAP,), tok_rows, jnp.int32).at[slot_of].set(token_index)
    padded = jnp.concatenate([token_state, jnp.zeros((1, features), jnp.bfloat16)], axis=0)
    buffer = jnp.take(padded, source, axis=0)
    expert_out = full_path(
        buffer, w_gate, w_up, w_down, device_count, exp_dev, width_split, features
    )
    chosen = jnp.take(expert_out, slot_of, axis=0).reshape(tok_rows, TOP, features)
    mixed = jnp.sum(gate_weights[:, :, None] * chosen.astype(jnp.float32), axis=1).astype(
        jnp.bfloat16
    )
    gate_grads = jnp.einsum("tkd,td->tk", chosen, out_grad, preferred_element_type=jnp.float32)
    return (mixed, gate_grads)


def local(*arrays):
    if lax.axis_size("expert") == 16 and arrays[6].shape[0] * 16 == EXPERTS:
        return near_path(*arrays)
    return far_path(*arrays)


def solution(mesh):
    return jax.shard_map(
        local,
        mesh=mesh,
        in_specs=(
            P(("groups", "expert"), None),
            P(("groups", "expert"), None),
            P(("groups", "expert")),
            P(("groups", "expert"), None),
            P(("groups", "expert"), None),
            P("expert", None),
            P("expert", None, None),
            P("expert", None, None),
            P("expert", None, None),
            P(("groups", "expert"), None),
        ),
        out_specs=(P(("groups", "expert"), None), P(("groups", "expert"), None)),
        check_vma=False,
    )
```

```python
import functools

import jax
import jax.numpy as jnp
from jax import lax
from jax.experimental import pallas as pl
from jax.experimental.pallas import tpu as pltpu
from jax.sharding import PartitionSpec as P

EXPERTS = 64
TOP = 4
CAP = 12
BLOCK = 128
PAIR = 2 * CAP
VMEM = pltpu.VMEM
F32 = jnp.float32
BF16 = jnp.bfloat16
SMALL = pltpu.CompilerParams(vmem_limit_bytes=16 * 1024 * 1024)


def dot(a, b):
    return jnp.dot(a, b, preferred_element_type=F32)


def in_hbm(array):
    return pltpu.with_memory_space_constraint(array, pltpu.HBM)


def iota(shape, dimension):
    return lax.broadcasted_iota(jnp.int32, shape, dimension)


def flags(mask):
    return mask.astype(F32).astype(BF16)


def earlier(length):
    return flags(iota((length, length), 0) < iota((length, length), 1))


def repeat_kernel(rows_ref, grad_ref, out_ref, upper_ref):
    for n in range(out_ref.shape[0]):
        out_ref[n] = rows_ref[...]
    upper_ref[...] = grad_ref[...]


def fetch_kernel(me_ref, rows_ref, table_hbm, _, out_hbm, table_ref, out_ref, sem, out_sem):
    copy = pltpu.make_async_copy(table_hbm, table_ref, sem)
    copy.start()
    device_count, _, tok_rows = rows_ref.shape
    held = table_ref.shape[0]
    look_cap = out_ref.shape[0] // device_count
    local = rows_ref[:, 0, :] - me_ref[0] * held
    hit = (local >= 0) & (local < held)
    rank = dot(flags(hit), earlier(tok_rows)).astype(jnp.int32)
    rank = jnp.where(hit, rank, -1)
    slot = iota((look_cap, tok_rows), 0)
    place = iota((look_cap, held), 1)
    picks = []
    for source in range(device_count):
        mine = jnp.where(slot == rank[source : source + 1], local[source : source + 1], 0)
        wanted = jnp.sum(mine, axis=1, keepdims=True)
        picks.append(flags(place == wanted))
    pick = jnp.concatenate(picks, axis=0)
    copy.wait()
    width = out_ref.shape[1] // out_sem.shape[0]
    copies = []
    for n in range(out_sem.shape[0]):
        cols = pl.ds(n * width, width)
        out_ref[:, cols] = dot(pick, table_ref[:, cols]).astype(BF16)
        copies.append(
            pltpu.make_async_copy(out_ref.at[:, cols], out_hbm.at[:, cols], out_sem.at[n])
        )
        copies[-1].start()
    for copy in copies:
        copy.wait()


def turned(rows):
    count, length = rows.shape
    return jnp.concatenate([rows, jnp.zeros((length - count, length), F32)], axis=0).T


def plan_slots(me, ids_ref, pick_refs, slots_ref):
    tok_rows = ids_ref.shape[1]
    half = sum(ref.shape[0] for ref in pick_refs) // (2 * PAIR)
    exp_dev = EXPERTS // (2 * half)
    flip = me % 2
    inside = iota((half * exp_dev, tok_rows), 0)
    expert = inside + me // half * half * exp_dev
    place = iota((PAIR, tok_rows), 0)
    ids = ids_ref[...]
    chosen = [ids[k : k + 1] == expert for k in range(TOP)]
    hit = functools.reduce(jnp.logical_or, chosen)
    rank = jnp.where(hit, dot(flags(hit), earlier(tok_rows)).astype(jnp.int32), -1000)
    lines = []
    for at in range(0, half * exp_dev, 2):
        one, two = rank[at : at + 1], rank[at + 1 : at + 2]
        upper = jnp.where(flip == 0, one, two)
        lower = jnp.where(flip == 0, two, one) + CAP
        here = ((place < CAP) & (place == upper)) | ((place >= CAP) & (place == lower))
        lines.append(here.astype(F32))
    pairs = exp_dev // 2
    slot = ((inside + flip) & 1) * CAP + rank
    if len(pick_refs) == 1:
        pick_refs[0][...] = jnp.concatenate(lines, axis=0).astype(BF16)
        slot = slot + (inside // 2) * PAIR
    else:
        for n, ref in enumerate(pick_refs):
            ref[...] = jnp.concatenate(lines[n::pairs], axis=0).astype(BF16)
        device = inside // exp_dev
        first = device * (2 * PAIR) + PAIR
        second = half * 2 * PAIR + device * PAIR
        slot = slot + jnp.where((inside & 2) == 0, first, second)
    found = [
        jnp.sum(jnp.where(chosen[k], slot + 1, 0), axis=0, keepdims=True) - 1 for k in range(TOP)
    ]
    slots_ref[...] = turned(jnp.concatenate(found, axis=0).astype(F32)).astype(jnp.int32)


def near_plan_kernel(
    me_ref,
    rows_ref,
    ids_ref,
    weights_ref,
    scales_ref,
    _,
    put_ref,
    first_pick_ref,
    second_pick_ref,
    slots_ref,
    columns_ref,
    ids_out_ref,
    weights_out_ref,
):
    ids_out_ref[...] = ids_ref[...]
    weights_out_ref[...] = weights_ref[...]
    tok_rows = rows_ref.shape[1]
    me, held = me_ref[0], me_ref[1]
    device_count = first_pick_ref.shape[0] // PAIR * 2
    look_cap = put_ref.shape[1] // device_count
    row = jnp.broadcast_to(rows_ref[...], (device_count, tok_rows))
    low = iota((device_count, tok_rows), 0) * held
    hit = (row >= low) & (row < low + held)
    rank = jnp.where(hit, dot(flags(hit), earlier(tok_rows)).astype(jnp.int32), -1)
    slot = iota((look_cap, tok_rows), 0)
    put = [(slot == rank[o : o + 1]).astype(F32) for o in range(device_count)]
    put_ref[...] = jnp.concatenate(put, axis=0).T.astype(BF16)
    plan_slots(me, ids_ref, (first_pick_ref, second_pick_ref), slots_ref)
    columns_ref[...] = turned(jnp.concatenate([weights_ref[...], scales_ref[...]], axis=0))


def far_plan_kernel(me_ref, ids_ref, weights_ref, _, pick_ref, slots_ref, columns_ref):
    plan_slots(me_ref[0], ids_ref, (pick_ref,), slots_ref)
    columns_ref[...] = turned(weights_ref[...])


def state_kernel(
    put_ref, returned_ref, values_ref, columns_ref, ids_ref, weights_ref, state_ref
):
    features = values_ref.shape[1]
    width = 512
    for left in range(0, features, width):
        found = dot(put_ref[...], returned_ref[:, left : left + width])
        for b in range(width // BLOCK):
            at = left + b * BLOCK
            scaled = (
                values_ref[:, at : at + BLOCK].astype(F32)
                * columns_ref[:, TOP + at // BLOCK : TOP + at // BLOCK + 1]
            )
            state_ref[:, at : at + BLOCK] = (
                scaled + found[:, b * BLOCK : (b + 1) * BLOCK]
            ).astype(BF16)


def pair_kernel(pick_ref, state_ref, *refs):
    out_ref = refs[-1]
    out_ref[...] = dot(pick_ref[...], state_ref[...]).astype(BF16)


def pick_kernel(
    pick_ref, state_ref, grad_ref, out_hbm, lower_grad_ref, sent_ref, sem
):
    tok_rows, features = state_ref.shape
    width = features // sem.shape[0]
    copies = []
    for n in range(sem.shape[0]):
        cols = pl.ds(n * width, width)
        sent_ref[:, cols] = dot(pick_ref[...], state_ref[:, cols]).astype(BF16)
        copies.append(
            pltpu.make_async_copy(sent_ref.at[:, cols], out_hbm.at[:, cols], sem.at[n])
        )
        copies[-1].start()
    lower_grad_ref[...] = grad_ref[tok_rows // 2 :, :]
    for copy in copies:
        copy.wait()


def expert_kernel(first, count, join, after, rows_hbm, *refs):
    if join:
        front_ref, refs = refs[0], refs[1:]
    wg_hbm, wu_hbm, wd_hbm, out_ref = refs[after : after + 4]
    rows_ref, x_ref, wg_ref, wu_ref, wd_ref, hidden_ref, result_ref, sem, rows_sem = refs[
        after + 4 :
    ]
    held, features, width = wg_ref.shape
    half = rows_ref.shape[0]
    up_cuts = ((0, 512), (512, 512), (1024, width - 1024))
    down_cuts = tuple((at, 512) for at in range(0, features, 512))

    def weight_copies(j, place):
        copies = []
        for at, size in up_cuts:
            cols = pl.ds(at, size)
            copies.append((wg_hbm.at[first + j, :, cols], wg_ref.at[place, :, cols]))
            copies.append((wu_hbm.at[first + j, :, cols], wu_ref.at[place, :, cols]))
        for at, size in down_cuts:
            cols = pl.ds(at, size)
            copies.append((wd_hbm.at[first + j, :, cols], wd_ref.at[place, :, cols]))
        return [
            pltpu.make_async_copy(src, dst, sem.at[place, n])
            for n, (src, dst) in enumerate(copies)
        ]

    rows_copy = pltpu.make_async_copy(rows_hbm, rows_ref, rows_sem)
    rows_copy.start()
    weights = weight_copies(0, 0) + weight_copies(1, 1)
    for copy in weights[:4]:
        copy.start()
    rows_copy.wait()
    for copy in weights[4:]:
        copy.start()

    low = iota((PAIR, features), 0) < CAP
    for chunk in range(count // 2):
        here = slice(chunk * PAIR, (chunk + 1) * PAIR)
        for quad in range(half // 4):
            ones, twos = [], []
            for pair in range(2):
                source = 4 * quad + 2 * pair
                even = rows_ref[source, here, :].astype(F32)
                odd = rows_ref[source + 1, here, :].astype(F32)
                ones.append(jnp.where(low, even, odd))
                twos.append(jnp.where(low, odd, even))
            rows = slice(quad * 2 * PAIR, (quad + 1) * 2 * PAIR)
            x_ref[2 * chunk, rows, :] = jnp.concatenate(ones, axis=0).astype(BF16)
            x_ref[2 * chunk + 1, rows, :] = jnp.concatenate(twos, axis=0).astype(BF16)

    @pl.loop(0, count)
    def _(j):
        place = j % held
        copies = weight_copies(j, place)

        def refill(n, parts):
            @pl.when(j + held < count)
            def _():
                for copy in weight_copies(j + held, place)[n : n + parts]:
                    copy.start()

        n = 0
        for at, size in up_cuts:
            copies[n].wait()
            copies[n + 1].wait()
            gate = dot(x_ref[j], wg_ref[place, :, at : at + size])
            up = dot(x_ref[j], wu_ref[place, :, at : at + size])
            hidden = gate / (1.0 + jnp.exp(-gate)) * up
            hidden_ref[:, at : at + size] = hidden.astype(BF16)
            if count > held:
                refill(n, 2)
            n += 2
        for at, size in down_cuts:
            copies[n].wait()
            result_ref[j, :, at : at + size] = dot(
                hidden_ref[...], wd_ref[place, :, at : at + size]
            )
            if count > held:
                refill(n, 1)
            n += 1

    for pair in range(half // 2):
        rows = slice(pair * PAIR, (pair + 1) * PAIR)
        values = [result_ref[j, rows, :] for j in range(count)]
        for odd in range(2):
            parts = [
                jnp.where(low, values[j + odd], values[j + 1 - odd]) for j in range(0, count, 2)
            ]
            if join:
                parts = [front_ref[2 * pair + odd].astype(F32)] + parts
            out_ref[2 * pair + odd] = jnp.concatenate(parts, axis=0).astype(BF16)


def expert_call(name, first, count, rows_in, weights, front=(), after=()):
    w_gate, w_up, w_down = weights
    _, features, width = w_gate.shape
    half = rows_in.shape[0]
    rows = half * CAP
    held = 2
    anywhere = pl.BlockSpec(memory_space=pl.ANY)
    hbm = pl.BlockSpec(memory_space=pltpu.HBM)
    vmem = pl.BlockSpec(memory_space=VMEM)
    return pl.pallas_call(
        functools.partial(expert_kernel, first, count, bool(front), len(after)),
        out_shape=pltpu.HBM((half, count * CAP + len(front) * PAIR, features), BF16),
        in_specs=[hbm] + [vmem] * len(front) + [anywhere] * len(after) + [hbm] * 3,
        out_specs=vmem,
        scratch_shapes=[
            VMEM(rows_in.shape, BF16),
            VMEM((count, rows, features), BF16),
            VMEM((held, features, width), BF16),
            VMEM((held, features, width), BF16),
            VMEM((held, width, features), BF16),
            VMEM((rows, width), BF16),
            VMEM((count, rows, features), F32),
            pltpu.SemaphoreType.DMA((held, 10)),
            pltpu.SemaphoreType.DMA,
        ],
        compiler_params=pltpu.CompilerParams(vmem_limit_bytes=46 * 1024 * 1024),
        cost_estimate=pl.CostEstimate(
            flops=12 * count * rows * features * width,
            bytes_accessed=6 * count * features * width,
            transcendentals=count * rows * width,
        ),
        name=name,
    )(
        *[in_hbm(array) for array in (rows_in, *front, *after, w_gate, w_up, w_down)],
    )


def mix_kernel(grads, added, added_grads, start, slots_ref, columns_ref, back_ref, *refs):
    mixed_ref, grads_ref = refs[-2:]
    grad_refs = refs[:grads]
    added_refs = refs[grads : grads + added]
    added_grad_refs = refs[grads + added : grads + added + added_grads]
    tok_rows = slots_ref.shape[0]
    count, features = back_ref.shape
    grad = jnp.concatenate([ref[...] for ref in grad_refs], axis=0)
    place = iota((tok_rows, tok_rows), 1)
    wide = jnp.zeros((tok_rows, tok_rows), F32)
    column = iota((tok_rows, count), 1) + start
    inner = lax.dot_general(
        grad, back_ref[...], (((1,), (1,)), ((), ())), preferred_element_type=F32
    )
    total = jnp.zeros((tok_rows, count), F32)
    for k in range(TOP):
        here = column == slots_ref[:, k : k + 1]
        total = total + jnp.where(here, columns_ref[:, k : k + 1], 0.0)
        value = jnp.sum(jnp.where(here, inner, 0.0), axis=1, keepdims=True)
        wide = wide + jnp.where(place == k, value, 0.0)
    high = total.astype(BF16)
    rest = (total - high.astype(F32)).astype(BF16)
    width = 512
    for at in range(0, features, width):
        cols = slice(at, at + width)
        value = dot(high, back_ref[:, cols]) + dot(rest, back_ref[:, cols])
        for ref in added_refs:
            value = value + ref[:, cols].astype(F32)
        mixed_ref[:, cols] = value.astype(mixed_ref.dtype)
    lines = grads_ref.shape[0]
    sums = wide.T[:lines, :]
    for ref in added_grad_refs:
        sums = sums + ref[:lines, :]
    grads_ref[...] = sums


def swap(array, groups=None):
    return lax.all_to_all(
        array, "expert", split_axis=0, concat_axis=0, tiled=True, axis_index_groups=groups
    )


def near_path(
    block_values,
    block_exps,
    row_ids,
    expert_ids,
    gate_weights,
    table,
    w_gate,
    w_up,
    w_down,
    out_grad,
):
    device_count = lax.axis_size("expert")
    half = device_count // 2
    halves = [list(range(half)), list(range(half, device_count))]
    me = lax.axis_index("expert").astype(jnp.int32)
    tok_rows, features = block_values.shape
    rows_held = table.shape[0]
    look_cap = max(2, 2 * tok_rows // device_count)
    slots = half * 2 * PAIR
    vmem = pl.BlockSpec(memory_space=VMEM)
    smem = pl.BlockSpec(memory_space=pltpu.SMEM)
    anywhere = pl.BlockSpec(memory_space=pl.ANY)
    place = jnp.stack([me, jnp.int32(rows_held)])

    def shape(dims, kind):
        return jax.ShapeDtypeStruct(dims, kind)

    def mirrored(array):
        pairs = [(i, (i + half) % device_count) for i in range(device_count)]
        return lax.ppermute(array, "expert", pairs)

    def ordered(array, *earlier_arrays, flops=0):
        return pl.pallas_call(
            lambda *refs: None,
            out_shape=shape(array.shape, array.dtype),
            in_specs=[anywhere] * (1 + len(earlier_arrays)),
            out_specs=anywhere,
            input_output_aliases={0: 0},
            compiler_params=SMALL,
            cost_estimate=pl.CostEstimate(flops=flops, bytes_accessed=0, transcendentals=0),
            name="ordered",
        )(array, *earlier_arrays)

    upper = tok_rows // 2
    all_rows, upper_grad = pl.pallas_call(
        repeat_kernel,
        out_shape=(
            shape((device_count, 1, tok_rows), jnp.int32),
            shape((upper, features), BF16),
        ),
        grid=(1,),
        in_specs=[
            pl.BlockSpec((1, tok_rows), lambda i: (0, 0)),
            pl.BlockSpec((upper, features), lambda i: (0, 0)),
        ],
        out_specs=(
            pl.BlockSpec((device_count, 1, tok_rows), lambda i: (0, 0, 0)),
            pl.BlockSpec((upper, features), lambda i: (0, 0)),
        ),
        name="repeat_rows",
    )(row_ids[None, :], out_grad)
    other_upper = mirrored(upper_grad)
    fetched = pl.pallas_call(
        fetch_kernel,
        out_shape=pltpu.HBM((device_count * look_cap, features), BF16),
        in_specs=[smem, vmem, pl.BlockSpec(memory_space=pltpu.HBM), anywhere],
        out_specs=anywhere,
        scratch_shapes=[
            VMEM(table.shape, BF16),
            VMEM((device_count * look_cap, features), BF16),
            pltpu.SemaphoreType.DMA,
            pltpu.SemaphoreType.DMA((4,)),
        ],
        compiler_params=SMALL,
        name="fetch_rows",
    )(place, swap(all_rows), in_hbm(table), other_upper)
    returned = swap(fetched.reshape(device_count, look_cap, features))
    turned_ids, turned_weights = expert_ids.T, gate_weights.T
    pick_shape = shape((slots, tok_rows), BF16)
    pair_shape = shape((slots // 2, tok_rows), BF16)
    square = (tok_rows, tok_rows)
    put, first_pick, second_pick, near_of, near_columns, sent_ids, sent_weights = pl.pallas_call(
        near_plan_kernel,
        out_shape=(
            shape((tok_rows, device_count * look_cap), BF16),
            pair_shape,
            pair_shape,
            shape(square, jnp.int32),
            shape(square, F32),
            shape(turned_ids.shape, jnp.int32),
            shape(turned_weights.shape, F32),
        ),
        in_specs=[smem, vmem, vmem, vmem, vmem, anywhere],
        out_specs=(vmem,) * 7,
        compiler_params=SMALL,
        name="near_plan",
    )(
        place,
        row_ids[None, :],
        turned_ids,
        turned_weights,
        jnp.exp2(block_exps.T.astype(F32)),
        in_hbm(fetched),
    )
    other_ids, other_weights = mirrored(sent_ids), mirrored(sent_weights)

    def sent_scratch(count):
        return [VMEM((count, features), BF16), pltpu.SemaphoreType.DMA((4,))]

    state = pl.pallas_call(
        state_kernel,
        out_shape=shape((tok_rows, features), BF16),
        in_specs=[vmem] * 4 + [anywhere] * 2,
        out_specs=vmem,
        compiler_params=SMALL,
        name="token_state",
    )(
        put,
        returned.reshape(device_count * look_cap, features),
        block_values,
        near_columns,
        other_ids,
        other_weights,
    )

    def pair_sent(name, pick, *after):
        return pl.pallas_call(
            pair_kernel,
            out_shape=pltpu.HBM((slots // 2, features), BF16),
            in_specs=[vmem, vmem] + [anywhere] * len(after),
            out_specs=vmem,
            compiler_params=SMALL,
            name=name,
        )(pick, state, *after).reshape(half, PAIR, features)

    far_pick, far_of, far_columns = pl.pallas_call(
        far_plan_kernel,
        out_shape=(pick_shape, shape(square, jnp.int32), shape(square, F32)),
        in_specs=[smem, vmem, vmem, anywhere],
        out_specs=(vmem,) * 3,
        compiler_params=SMALL,
        name="far_plan",
    )(place, other_ids, other_weights, state)
    far_sent, lower_grad = pl.pallas_call(
        pick_kernel,
        out_shape=(
            pltpu.HBM((slots, features), BF16),
            shape((tok_rows - upper, features), BF16),
        ),
        in_specs=[vmem, vmem, vmem],
        out_specs=(anywhere, vmem),
        scratch_shapes=sent_scratch(slots),
        compiler_params=SMALL,
        cost_estimate=pl.CostEstimate(
            flops=400_000_000_000, bytes_accessed=4 * slots * features, transcendentals=0
        ),
        name="far_slots",
    )(far_pick, mirrored(state), out_grad)
    near_rows = swap(pair_sent("first_slots", first_pick), halves)
    far_sent = far_sent.reshape(half, 2 * PAIR, features)
    far_rows = swap(far_sent, halves)
    later_sent = pair_sent("later_slots", second_pick, in_hbm(far_sent))
    other_grads = (other_upper, mirrored(lower_grad))

    weights = (w_gate, w_up, w_down)
    sent_both = expert_call(
        "near_first", 0, 2, near_rows, weights, front=(later_sent,), after=(far_sent,)
    )
    far_out = expert_call("far_experts", 0, 4, far_rows, weights, after=(sent_both,))
    both = swap(sent_both, halves)
    far_back = swap(ordered(in_hbm(far_out), in_hbm(both), other_grads[1]), halves)
    near_out = expert_call("near_second", 2, 2, both, weights)

    def mixed_rows(
        name,
        slot_of,
        columns,
        back,
        grads,
        kind,
        start=0,
        lines=2 * TOP,
        added=(),
        added_grads=(),
        after=(),
    ):
        operands = (*grads, *added, *added_grads)

        return pl.pallas_call(
            functools.partial(mix_kernel, len(grads), len(added), len(added_grads), start),
            out_shape=(shape((tok_rows, features), kind), shape((lines, tok_rows), F32)),
            in_specs=[vmem] * (3 + len(operands)) + [anywhere] * len(after),
            out_specs=(vmem, vmem),
            compiler_params=SMALL,
            name=name,
        )(slot_of, columns, back.reshape(-1, features), *operands, *after)

    far_mixed, far_grads = mixed_rows(
        "mix_far", far_of, far_columns, far_back, other_grads, BF16, after=(in_hbm(near_out),)
    )
    near_back = swap(ordered(in_hbm(near_out), far_mixed), halves)
    far_sums = ordered(mirrored(far_mixed), flops=400_000_000_000)
    sums, sum_grads = mixed_rows(
        "mix_first",
        near_of,
        near_columns,
        in_hbm(both.reshape(slots, features)),
        (out_grad,),
        F32,
        added=(far_sums,),
    )
    mixed, grads = mixed_rows(
        "mix_second",
        near_of,
        near_columns,
        near_back,
        (out_grad,),
        BF16,
        start=slots,
        lines=TOP,
        added=(sums,),
        added_grads=(sum_grads, mirrored(far_grads)),
    )
    return mixed, grads.T


def expert_work(arrived, w_gate, w_up, w_down):
    gate_act = jnp.einsum("sjcd,jdf->sjcf", arrived, w_gate, preferred_element_type=jnp.float32)
    up_act = jnp.einsum("sjcd,jdf->sjcf", arrived, w_up, preferred_element_type=jnp.float32)
    hidden = (jax.nn.silu(gate_act) * up_act).astype(jnp.bfloat16)
    return jnp.einsum("sjcf,jfd->sjcd", hidden, w_down, preferred_element_type=jnp.float32).astype(
        jnp.bfloat16
    )


def full_path(buffer, w_gate, w_up, w_down, device_count, exp_dev, width_split, features):
    group_count = EXPERTS // exp_dev
    grouped = buffer.reshape(group_count, 1, exp_dev, CAP, features)
    outgoing = jnp.broadcast_to(
        grouped, (group_count, width_split, exp_dev, CAP, features)
    ).reshape(device_count, exp_dev, CAP, features)
    returned_out = lax.all_to_all(
        expert_work(
            lax.all_to_all(outgoing, "expert", split_axis=0, concat_axis=0, tiled=True),
            w_gate,
            w_up,
            w_down,
        ),
        "expert",
        split_axis=0,
        concat_axis=0,
        tiled=True,
    )
    pieces = returned_out.reshape(group_count, width_split, exp_dev, CAP, features).astype(
        jnp.float32
    )
    return jnp.sum(pieces, axis=1).astype(jnp.bfloat16).reshape(EXPERTS * CAP, features)


def far_path(
    block_values,
    block_exps,
    row_ids,
    expert_ids,
    gate_weights,
    table,
    w_gate,
    w_up,
    w_down,
    out_grad,
):
    device_count = lax.axis_size("expert")
    tok_rows = block_values.shape[0]
    features = block_values.shape[1]
    rows_held = table.shape[0]
    look_cap = max(2, 2 * tok_rows // device_count)
    exp_dev = w_gate.shape[0]
    width_split = device_count * exp_dev // EXPERTS
    owners = row_ids // rows_held
    local_row = row_ids % rows_held
    owner_hot = (owners[:, None] == jnp.arange(device_count, dtype=jnp.int32)[None, :]).astype(
        jnp.int32
    )
    owner_rank = jnp.sum((jnp.cumsum(owner_hot, axis=0) - 1) * owner_hot, axis=1)
    placed = owners * look_cap + owner_rank
    wanted = jnp.zeros((device_count * look_cap,), jnp.int32).at[placed].set(local_row)
    requested = lax.all_to_all(
        wanted.reshape(device_count, look_cap), "expert", split_axis=0, concat_axis=0, tiled=True
    )
    fetched = jnp.take(table, requested.reshape(-1), axis=0).reshape(
        device_count, look_cap, features
    )
    rows_returned = lax.all_to_all(fetched, "expert", split_axis=0, concat_axis=0, tiled=True)
    embedded = jnp.take(rows_returned.reshape(device_count * look_cap, features), placed, axis=0)
    scales = jnp.exp2(block_exps.astype(jnp.float32))
    blocks = (
        block_values.reshape(tok_rows, scales.shape[1], -1).astype(jnp.float32) * scales[:, :, None]
    )
    token_state = (blocks.reshape(tok_rows, features) + embedded.astype(jnp.float32)).astype(
        jnp.bfloat16
    )
    flat_ids = expert_ids.reshape(-1)
    expert_hot = (flat_ids[:, None] == jnp.arange(EXPERTS, dtype=jnp.int32)[None, :]).astype(
        jnp.int32
    )
    expert_rank = jnp.sum((jnp.cumsum(expert_hot, axis=0) - 1) * expert_hot, axis=1)
    slot_of = flat_ids * CAP + expert_rank
    token_index = jnp.arange(tok_rows * TOP, dtype=jnp.int32) // TOP
    source = jnp.full((EXPERTS * CAP,), tok_rows, jnp.int32).at[slot_of].set(token_index)
    padded = jnp.concatenate([token_state, jnp.zeros((1, features), jnp.bfloat16)], axis=0)
    buffer = jnp.take(padded, source, axis=0)
    expert_out = full_path(
        buffer, w_gate, w_up, w_down, device_count, exp_dev, width_split, features
    )
    chosen = jnp.take(expert_out, slot_of, axis=0).reshape(tok_rows, TOP, features)
    mixed = jnp.sum(gate_weights[:, :, None] * chosen.astype(jnp.float32), axis=1).astype(
        jnp.bfloat16
    )
    gate_grads = jnp.einsum("tkd,td->tk", chosen, out_grad, preferred_element_type=jnp.float32)
    return (mixed, gate_grads)


def local(*arrays):
    if lax.axis_size("expert") == 16 and arrays[6].shape[0] * 16 == EXPERTS:
        return near_path(*arrays)
    return far_path(*arrays)


def solution(mesh):
    return jax.shard_map(
        local,
        mesh=mesh,
        in_specs=(
            P(("groups", "expert"), None),
            P(("groups", "expert"), None),
            P(("groups", "expert")),
            P(("groups", "expert"), None),
            P(("groups", "expert"), None),
            P("expert", None),
            P("expert", None, None),
            P("expert", None, None),
            P("expert", None, None),
            P(("groups", "expert"), None),
        ),
        out_specs=(P(("groups", "expert"), None), P(("groups", "expert"), None)),
        check_vma=False,
    )
```

```python
import functools

import jax
import jax.numpy as jnp
from jax import lax
from jax.experimental import pallas as pl
from jax.experimental.pallas import tpu as pltpu
from jax.sharding import PartitionSpec as P

EXPERTS = 64
TOP = 4
CAP = 12
BLOCK = 128
PAIR = 2 * CAP
VMEM = pltpu.VMEM
F32 = jnp.float32
BF16 = jnp.bfloat16
SMALL = pltpu.CompilerParams(vmem_limit_bytes=16 * 1024 * 1024)


def dot(a, b):
    return jnp.dot(a, b, preferred_element_type=F32)


def in_hbm(array):
    return pltpu.with_memory_space_constraint(array, pltpu.HBM)


def iota(shape, dimension):
    return lax.broadcasted_iota(jnp.int32, shape, dimension)


def flags(mask):
    return mask.astype(F32).astype(BF16)


def earlier(length):
    return flags(iota((length, length), 0) < iota((length, length), 1))


def repeat_kernel(rows_ref, grad_ref, out_ref, upper_ref):
    for n in range(out_ref.shape[0]):
        out_ref[n] = rows_ref[...]
    upper_ref[...] = grad_ref[...]


def fetch_kernel(me_ref, rows_ref, table_hbm, _, out_hbm, table_ref, out_ref, sem, out_sem):
    copy = pltpu.make_async_copy(table_hbm, table_ref, sem)
    copy.start()
    device_count, _, tok_rows = rows_ref.shape
    held = table_ref.shape[0]
    look_cap = out_ref.shape[0] // device_count
    local = rows_ref[:, 0, :] - me_ref[0] * held
    hit = (local >= 0) & (local < held)
    rank = dot(flags(hit), earlier(tok_rows)).astype(jnp.int32)
    rank = jnp.where(hit, rank, -1)
    slot = iota((look_cap, tok_rows), 0)
    place = iota((look_cap, held), 1)
    picks = []
    for source in range(device_count):
        mine = jnp.where(slot == rank[source : source + 1], local[source : source + 1], 0)
        wanted = jnp.sum(mine, axis=1, keepdims=True)
        picks.append(flags(place == wanted))
    pick = jnp.concatenate(picks, axis=0)
    copy.wait()
    width = out_ref.shape[1] // out_sem.shape[0]
    copies = []
    for n in range(out_sem.shape[0]):
        cols = pl.ds(n * width, width)
        out_ref[:, cols] = dot(pick, table_ref[:, cols]).astype(BF16)
        copies.append(
            pltpu.make_async_copy(out_ref.at[:, cols], out_hbm.at[:, cols], out_sem.at[n])
        )
        copies[-1].start()
    for copy in copies:
        copy.wait()


def turned(rows):
    count, length = rows.shape
    return jnp.concatenate([rows, jnp.zeros((length - count, length), F32)], axis=0).T


def plan_slots(me, ids_ref, pick_refs, slots_ref):
    tok_rows = ids_ref.shape[1]
    half = sum(ref.shape[0] for ref in pick_refs) // (2 * PAIR)
    exp_dev = EXPERTS // (2 * half)
    flip = me % 2
    inside = iota((half * exp_dev, tok_rows), 0)
    expert = inside + me // half * half * exp_dev
    place = iota((PAIR, tok_rows), 0)
    ids = ids_ref[...]
    chosen = [ids[k : k + 1] == expert for k in range(TOP)]
    hit = functools.reduce(jnp.logical_or, chosen)
    rank = jnp.where(hit, dot(flags(hit), earlier(tok_rows)).astype(jnp.int32), -1000)
    lines = []
    for at in range(0, half * exp_dev, 2):
        one, two = rank[at : at + 1], rank[at + 1 : at + 2]
        upper = jnp.where(flip == 0, one, two)
        lower = jnp.where(flip == 0, two, one) + CAP
        here = ((place < CAP) & (place == upper)) | ((place >= CAP) & (place == lower))
        lines.append(here.astype(F32))
    pairs = exp_dev // 2
    slot = ((inside + flip) & 1) * CAP + rank
    if len(pick_refs) == 1:
        pick_refs[0][...] = jnp.concatenate(lines, axis=0).astype(BF16)
        slot = slot + (inside // 2) * PAIR
    else:
        for n, ref in enumerate(pick_refs):
            ref[...] = jnp.concatenate(lines[n::pairs], axis=0).astype(BF16)
        device = inside // exp_dev
        first = device * (2 * PAIR) + PAIR
        second = half * 2 * PAIR + device * PAIR
        slot = slot + jnp.where((inside & 2) == 0, first, second)
    found = [
        jnp.sum(jnp.where(chosen[k], slot + 1, 0), axis=0, keepdims=True) - 1 for k in range(TOP)
    ]
    slots_ref[...] = turned(jnp.concatenate(found, axis=0).astype(F32)).astype(jnp.int32)


def near_plan_kernel(
    me_ref,
    rows_ref,
    ids_ref,
    weights_ref,
    scales_ref,
    _,
    put_ref,
    first_pick_ref,
    second_pick_ref,
    slots_ref,
    columns_ref,
    ids_out_ref,
    weights_out_ref,
):
    ids_out_ref[...] = ids_ref[...]
    weights_out_ref[...] = weights_ref[...]
    tok_rows = rows_ref.shape[1]
    me, held = me_ref[0], me_ref[1]
    device_count = first_pick_ref.shape[0] // PAIR * 2
    look_cap = put_ref.shape[1] // device_count
    row = jnp.broadcast_to(rows_ref[...], (device_count, tok_rows))
    low = iota((device_count, tok_rows), 0) * held
    hit = (row >= low) & (row < low + held)
    rank = jnp.where(hit, dot(flags(hit), earlier(tok_rows)).astype(jnp.int32), -1)
    slot = iota((look_cap, tok_rows), 0)
    put = [(slot == rank[o : o + 1]).astype(F32) for o in range(device_count)]
    put_ref[...] = jnp.concatenate(put, axis=0).T.astype(BF16)
    plan_slots(me, ids_ref, (first_pick_ref, second_pick_ref), slots_ref)
    columns_ref[...] = turned(jnp.concatenate([weights_ref[...], scales_ref[...]], axis=0))


def far_plan_kernel(me_ref, ids_ref, weights_ref, _, pick_ref, slots_ref, columns_ref):
    plan_slots(me_ref[0], ids_ref, (pick_ref,), slots_ref)
    columns_ref[...] = turned(weights_ref[...])


def state_kernel(
    put_ref, returned_ref, values_ref, columns_ref, ids_ref, weights_ref, state_ref
):
    features = values_ref.shape[1]
    width = 512
    for left in range(0, features, width):
        found = dot(put_ref[...], returned_ref[:, left : left + width])
        for b in range(width // BLOCK):
            at = left + b * BLOCK
            scaled = (
                values_ref[:, at : at + BLOCK].astype(F32)
                * columns_ref[:, TOP + at // BLOCK : TOP + at // BLOCK + 1]
            )
            state_ref[:, at : at + BLOCK] = (
                scaled + found[:, b * BLOCK : (b + 1) * BLOCK]
            ).astype(BF16)


def pair_kernel(pick_ref, state_ref, *refs):
    out_ref = refs[-1]
    out_ref[...] = dot(pick_ref[...], state_ref[...]).astype(BF16)


def pick_kernel(
    pick_ref, state_ref, grad_ref, out_hbm, lower_grad_ref, sent_ref, sem
):
    tok_rows, features = state_ref.shape
    width = features // sem.shape[0]
    copies = []
    for n in range(sem.shape[0]):
        cols = pl.ds(n * width, width)
        sent_ref[:, cols] = dot(pick_ref[...], state_ref[:, cols]).astype(BF16)
        copies.append(
            pltpu.make_async_copy(sent_ref.at[:, cols], out_hbm.at[:, cols], sem.at[n])
        )
        copies[-1].start()
    lower_grad_ref[...] = grad_ref[tok_rows // 2 :, :]
    for copy in copies:
        copy.wait()


def expert_kernel(first, count, join, after, rows_hbm, *refs):
    if join:
        front_ref, refs = refs[0], refs[1:]
    wg_hbm, wu_hbm, wd_hbm, out_ref = refs[after : after + 4]
    rows_ref, x_ref, wg_ref, wu_ref, wd_ref, hidden_ref, result_ref, sem, rows_sem = refs[
        after + 4 :
    ]
    held, features, width = wg_ref.shape
    half = rows_ref.shape[0]
    up_cuts = ((0, 512), (512, 512), (1024, width - 1024))
    down_cuts = tuple((at, 512) for at in range(0, features, 512))

    def weight_copies(j, place):
        copies = []
        for at, size in up_cuts:
            cols = pl.ds(at, size)
            copies.append((wg_hbm.at[first + j, :, cols], wg_ref.at[place, :, cols]))
            copies.append((wu_hbm.at[first + j, :, cols], wu_ref.at[place, :, cols]))
        for at, size in down_cuts:
            cols = pl.ds(at, size)
            copies.append((wd_hbm.at[first + j, :, cols], wd_ref.at[place, :, cols]))
        return [
            pltpu.make_async_copy(src, dst, sem.at[place, n])
            for n, (src, dst) in enumerate(copies)
        ]

    rows_copy = pltpu.make_async_copy(rows_hbm, rows_ref, rows_sem)
    rows_copy.start()
    weights = weight_copies(0, 0) + weight_copies(1, 1)
    for copy in weights[:4]:
        copy.start()
    rows_copy.wait()
    for copy in weights[4:]:
        copy.start()

    low = iota((PAIR, features), 0) < CAP
    for chunk in range(count // 2):
        here = slice(chunk * PAIR, (chunk + 1) * PAIR)
        for quad in range(half // 4):
            ones, twos = [], []
            for pair in range(2):
                source = 4 * quad + 2 * pair
                even = rows_ref[source, here, :].astype(F32)
                odd = rows_ref[source + 1, here, :].astype(F32)
                ones.append(jnp.where(low, even, odd))
                twos.append(jnp.where(low, odd, even))
            rows = slice(quad * 2 * PAIR, (quad + 1) * 2 * PAIR)
            x_ref[2 * chunk, rows, :] = jnp.concatenate(ones, axis=0).astype(BF16)
            x_ref[2 * chunk + 1, rows, :] = jnp.concatenate(twos, axis=0).astype(BF16)

    @pl.loop(0, count)
    def _(j):
        place = j % held
        copies = weight_copies(j, place)

        def refill(n, parts):
            @pl.when(j + held < count)
            def _():
                for copy in weight_copies(j + held, place)[n : n + parts]:
                    copy.start()

        n = 0
        for at, size in up_cuts:
            copies[n].wait()
            copies[n + 1].wait()
            gate = dot(x_ref[j], wg_ref[place, :, at : at + size])
            up = dot(x_ref[j], wu_ref[place, :, at : at + size])
            hidden = gate / (1.0 + jnp.exp(-gate)) * up
            hidden_ref[:, at : at + size] = hidden.astype(BF16)
            if count > held:
                refill(n, 2)
            n += 2
        for at, size in down_cuts:
            copies[n].wait()
            result_ref[j, :, at : at + size] = dot(
                hidden_ref[...], wd_ref[place, :, at : at + size]
            )
            if count > held:
                refill(n, 1)
            n += 1

    for pair in range(half // 2):
        rows = slice(pair * PAIR, (pair + 1) * PAIR)
        values = [result_ref[j, rows, :] for j in range(count)]
        for odd in range(2):
            parts = [
                jnp.where(low, values[j + odd], values[j + 1 - odd]) for j in range(0, count, 2)
            ]
            if join:
                parts = [front_ref[2 * pair + odd].astype(F32)] + parts
            out_ref[2 * pair + odd] = jnp.concatenate(parts, axis=0).astype(BF16)


def expert_call(name, first, count, rows_in, weights, front=(), after=(), grant=46):
    w_gate, w_up, w_down = weights
    _, features, width = w_gate.shape
    half = rows_in.shape[0]
    rows = half * CAP
    held = 2
    anywhere = pl.BlockSpec(memory_space=pl.ANY)
    hbm = pl.BlockSpec(memory_space=pltpu.HBM)
    vmem = pl.BlockSpec(memory_space=VMEM)
    return pl.pallas_call(
        functools.partial(expert_kernel, first, count, bool(front), len(after)),
        out_shape=pltpu.HBM((half, count * CAP + len(front) * PAIR, features), BF16),
        in_specs=[hbm] + [vmem] * len(front) + [anywhere] * len(after) + [hbm] * 3,
        out_specs=vmem,
        scratch_shapes=[
            VMEM(rows_in.shape, BF16),
            VMEM((count, rows, features), BF16),
            VMEM((held, features, width), BF16),
            VMEM((held, features, width), BF16),
            VMEM((held, width, features), BF16),
            VMEM((rows, width), BF16),
            VMEM((count, rows, features), F32),
            pltpu.SemaphoreType.DMA((held, 10)),
            pltpu.SemaphoreType.DMA,
        ],
        compiler_params=pltpu.CompilerParams(vmem_limit_bytes=grant * 1024 * 1024),
        cost_estimate=pl.CostEstimate(
            flops=12 * count * rows * features * width,
            bytes_accessed=6 * count * features * width,
            transcendentals=count * rows * width,
        ),
        name=name,
    )(
        *[in_hbm(array) for array in (rows_in, *front, *after, w_gate, w_up, w_down)],
    )


def mix_kernel(grads, added, added_grads, start, slots_ref, columns_ref, back_ref, *refs):
    mixed_ref, grads_ref = refs[-2:]
    grad_refs = refs[:grads]
    added_refs = refs[grads : grads + added]
    added_grad_refs = refs[grads + added : grads + added + added_grads]
    tok_rows = slots_ref.shape[0]
    count, features = back_ref.shape
    grad = jnp.concatenate([ref[...] for ref in grad_refs], axis=0)
    place = iota((tok_rows, tok_rows), 1)
    wide = jnp.zeros((tok_rows, tok_rows), F32)
    column = iota((tok_rows, count), 1) + start
    inner = lax.dot_general(
        grad, back_ref[...], (((1,), (1,)), ((), ())), preferred_element_type=F32
    )
    total = jnp.zeros((tok_rows, count), F32)
    for k in range(TOP):
        here = column == slots_ref[:, k : k + 1]
        total = total + jnp.where(here, columns_ref[:, k : k + 1], 0.0)
        value = jnp.sum(jnp.where(here, inner, 0.0), axis=1, keepdims=True)
        wide = wide + jnp.where(place == k, value, 0.0)
    high = total.astype(BF16)
    rest = (total - high.astype(F32)).astype(BF16)
    width = 512
    for at in range(0, features, width):
        cols = slice(at, at + width)
        value = dot(high, back_ref[:, cols]) + dot(rest, back_ref[:, cols])
        for ref in added_refs:
            value = value + ref[:, cols].astype(F32)
        mixed_ref[:, cols] = value.astype(mixed_ref.dtype)
    lines = grads_ref.shape[0]
    sums = wide.T[:lines, :]
    for ref in added_grad_refs:
        sums = sums + ref[:lines, :]
    grads_ref[...] = sums


def swap(array, groups=None):
    return lax.all_to_all(
        array, "expert", split_axis=0, concat_axis=0, tiled=True, axis_index_groups=groups
    )


def near_path(
    block_values,
    block_exps,
    row_ids,
    expert_ids,
    gate_weights,
    table,
    w_gate,
    w_up,
    w_down,
    out_grad,
):
    device_count = lax.axis_size("expert")
    half = device_count // 2
    halves = [list(range(half)), list(range(half, device_count))]
    me = lax.axis_index("expert").astype(jnp.int32)
    tok_rows, features = block_values.shape
    rows_held = table.shape[0]
    look_cap = max(2, 2 * tok_rows // device_count)
    slots = half * 2 * PAIR
    vmem = pl.BlockSpec(memory_space=VMEM)
    smem = pl.BlockSpec(memory_space=pltpu.SMEM)
    anywhere = pl.BlockSpec(memory_space=pl.ANY)
    place = jnp.stack([me, jnp.int32(rows_held)])

    def shape(dims, kind):
        return jax.ShapeDtypeStruct(dims, kind)

    def mirrored(array):
        pairs = [(i, (i + half) % device_count) for i in range(device_count)]
        return lax.ppermute(array, "expert", pairs)

    def ordered(array, *earlier_arrays, flops=0):
        return pl.pallas_call(
            lambda *refs: None,
            out_shape=shape(array.shape, array.dtype),
            in_specs=[anywhere] * (1 + len(earlier_arrays)),
            out_specs=anywhere,
            input_output_aliases={0: 0},
            compiler_params=SMALL,
            cost_estimate=pl.CostEstimate(flops=flops, bytes_accessed=0, transcendentals=0),
            name="ordered",
        )(array, *earlier_arrays)

    upper = tok_rows // 2
    all_rows, upper_grad = pl.pallas_call(
        repeat_kernel,
        out_shape=(
            shape((device_count, 1, tok_rows), jnp.int32),
            shape((upper, features), BF16),
        ),
        grid=(1,),
        in_specs=[
            pl.BlockSpec((1, tok_rows), lambda i: (0, 0)),
            pl.BlockSpec((upper, features), lambda i: (0, 0)),
        ],
        out_specs=(
            pl.BlockSpec((device_count, 1, tok_rows), lambda i: (0, 0, 0)),
            pl.BlockSpec((upper, features), lambda i: (0, 0)),
        ),
        name="repeat_rows",
    )(row_ids[None, :], out_grad)
    other_upper = mirrored(upper_grad)
    fetched = pl.pallas_call(
        fetch_kernel,
        out_shape=pltpu.HBM((device_count * look_cap, features), BF16),
        in_specs=[smem, vmem, pl.BlockSpec(memory_space=pltpu.HBM), anywhere],
        out_specs=anywhere,
        scratch_shapes=[
            VMEM(table.shape, BF16),
            VMEM((device_count * look_cap, features), BF16),
            pltpu.SemaphoreType.DMA,
            pltpu.SemaphoreType.DMA((4,)),
        ],
        compiler_params=SMALL,
        name="fetch_rows",
    )(place, swap(all_rows), in_hbm(table), other_upper)
    returned = swap(fetched.reshape(device_count, look_cap, features))
    turned_ids, turned_weights = expert_ids.T, gate_weights.T
    pick_shape = shape((slots, tok_rows), BF16)
    pair_shape = shape((slots // 2, tok_rows), BF16)
    square = (tok_rows, tok_rows)
    put, first_pick, second_pick, near_of, near_columns, sent_ids, sent_weights = pl.pallas_call(
        near_plan_kernel,
        out_shape=(
            shape((tok_rows, device_count * look_cap), BF16),
            pair_shape,
            pair_shape,
            shape(square, jnp.int32),
            shape(square, F32),
            shape(turned_ids.shape, jnp.int32),
            shape(turned_weights.shape, F32),
        ),
        in_specs=[smem, vmem, vmem, vmem, vmem, anywhere],
        out_specs=(vmem,) * 7,
        compiler_params=SMALL,
        name="near_plan",
    )(
        place,
        row_ids[None, :],
        turned_ids,
        turned_weights,
        jnp.exp2(block_exps.T.astype(F32)),
        in_hbm(fetched),
    )
    other_ids, other_weights = mirrored(sent_ids), mirrored(sent_weights)

    def sent_scratch(count):
        return [VMEM((count, features), BF16), pltpu.SemaphoreType.DMA((4,))]

    state = pl.pallas_call(
        state_kernel,
        out_shape=shape((tok_rows, features), BF16),
        in_specs=[vmem] * 4 + [anywhere] * 2,
        out_specs=vmem,
        compiler_params=SMALL,
        name="token_state",
    )(
        put,
        returned.reshape(device_count * look_cap, features),
        block_values,
        near_columns,
        other_ids,
        other_weights,
    )

    def pair_sent(name, pick, *after):
        return pl.pallas_call(
            pair_kernel,
            out_shape=pltpu.HBM((slots // 2, features), BF16),
            in_specs=[vmem, vmem] + [anywhere] * len(after),
            out_specs=vmem,
            compiler_params=SMALL,
            name=name,
        )(pick, state, *after).reshape(half, PAIR, features)

    far_pick, far_of, far_columns = pl.pallas_call(
        far_plan_kernel,
        out_shape=(pick_shape, shape(square, jnp.int32), shape(square, F32)),
        in_specs=[smem, vmem, vmem, anywhere],
        out_specs=(vmem,) * 3,
        compiler_params=SMALL,
        name="far_plan",
    )(place, other_ids, other_weights, state)
    far_sent, lower_grad = pl.pallas_call(
        pick_kernel,
        out_shape=(
            pltpu.HBM((slots, features), BF16),
            shape((tok_rows - upper, features), BF16),
        ),
        in_specs=[vmem, vmem, vmem],
        out_specs=(anywhere, vmem),
        scratch_shapes=sent_scratch(slots),
        compiler_params=SMALL,
        cost_estimate=pl.CostEstimate(
            flops=400_000_000_000, bytes_accessed=4 * slots * features, transcendentals=0
        ),
        name="far_slots",
    )(far_pick, mirrored(state), out_grad)
    near_rows = swap(pair_sent("first_slots", first_pick), halves)
    far_sent = far_sent.reshape(half, 2 * PAIR, features)
    far_rows = swap(far_sent, halves)
    later_sent = pair_sent("later_slots", second_pick, in_hbm(far_sent))
    other_grads = (other_upper, mirrored(lower_grad))

    weights = (w_gate, w_up, w_down)
    sent_both = expert_call(
        "near_first", 0, 2, near_rows, weights, front=(later_sent,), after=(far_sent,), grant=63
    )
    far_out = expert_call("far_experts", 0, 4, far_rows, weights, after=(sent_both,), grant=63)
    both = swap(sent_both, halves)
    far_back = swap(ordered(in_hbm(far_out), in_hbm(both), other_grads[1]), halves)
    near_out = expert_call("near_second", 2, 2, both, weights)

    def mixed_rows(
        name,
        slot_of,
        columns,
        back,
        grads,
        kind,
        start=0,
        lines=2 * TOP,
        added=(),
        added_grads=(),
        after=(),
    ):
        operands = (*grads, *added, *added_grads)

        return pl.pallas_call(
            functools.partial(mix_kernel, len(grads), len(added), len(added_grads), start),
            out_shape=(shape((tok_rows, features), kind), shape((lines, tok_rows), F32)),
            in_specs=[vmem] * (3 + len(operands)) + [anywhere] * len(after),
            out_specs=(vmem, vmem),
            compiler_params=SMALL,
            name=name,
        )(slot_of, columns, back.reshape(-1, features), *operands, *after)

    sums, sum_grads = mixed_rows(
        "mix_first",
        near_of,
        near_columns,
        in_hbm(both.reshape(slots, features)),
        (out_grad,),
        F32,
    )
    far_mixed, far_grads = mixed_rows(
        "mix_far",
        far_of,
        far_columns,
        far_back,
        other_grads,
        BF16,
        after=(in_hbm(near_out), sum_grads),
    )
    near_back = swap(ordered(in_hbm(near_out), far_mixed), halves)
    mixed, grads = mixed_rows(
        "mix_second",
        near_of,
        near_columns,
        near_back,
        (out_grad,),
        BF16,
        start=slots,
        lines=TOP,
        added=(sums, ordered(mirrored(far_mixed), flops=400_000_000_000)),
        added_grads=(sum_grads, mirrored(far_grads)),
    )
    return mixed, grads.T


def expert_work(arrived, w_gate, w_up, w_down):
    gate_act = jnp.einsum("sjcd,jdf->sjcf", arrived, w_gate, preferred_element_type=jnp.float32)
    up_act = jnp.einsum("sjcd,jdf->sjcf", arrived, w_up, preferred_element_type=jnp.float32)
    hidden = (jax.nn.silu(gate_act) * up_act).astype(jnp.bfloat16)
    return jnp.einsum("sjcf,jfd->sjcd", hidden, w_down, preferred_element_type=jnp.float32).astype(
        jnp.bfloat16
    )


def full_path(buffer, w_gate, w_up, w_down, device_count, exp_dev, width_split, features):
    group_count = EXPERTS // exp_dev
    grouped = buffer.reshape(group_count, 1, exp_dev, CAP, features)
    outgoing = jnp.broadcast_to(
        grouped, (group_count, width_split, exp_dev, CAP, features)
    ).reshape(device_count, exp_dev, CAP, features)
    returned_out = lax.all_to_all(
        expert_work(
            lax.all_to_all(outgoing, "expert", split_axis=0, concat_axis=0, tiled=True),
            w_gate,
            w_up,
            w_down,
        ),
        "expert",
        split_axis=0,
        concat_axis=0,
        tiled=True,
    )
    pieces = returned_out.reshape(group_count, width_split, exp_dev, CAP, features).astype(
        jnp.float32
    )
    return jnp.sum(pieces, axis=1).astype(jnp.bfloat16).reshape(EXPERTS * CAP, features)


def far_path(
    block_values,
    block_exps,
    row_ids,
    expert_ids,
    gate_weights,
    table,
    w_gate,
    w_up,
    w_down,
    out_grad,
):
    device_count = lax.axis_size("expert")
    tok_rows = block_values.shape[0]
    features = block_values.shape[1]
    rows_held = table.shape[0]
    look_cap = max(2, 2 * tok_rows // device_count)
    exp_dev = w_gate.shape[0]
    width_split = device_count * exp_dev // EXPERTS
    owners = row_ids // rows_held
    local_row = row_ids % rows_held
    owner_hot = (owners[:, None] == jnp.arange(device_count, dtype=jnp.int32)[None, :]).astype(
        jnp.int32
    )
    owner_rank = jnp.sum((jnp.cumsum(owner_hot, axis=0) - 1) * owner_hot, axis=1)
    placed = owners * look_cap + owner_rank
    wanted = jnp.zeros((device_count * look_cap,), jnp.int32).at[placed].set(local_row)
    requested = lax.all_to_all(
        wanted.reshape(device_count, look_cap), "expert", split_axis=0, concat_axis=0, tiled=True
    )
    fetched = jnp.take(table, requested.reshape(-1), axis=0).reshape(
        device_count, look_cap, features
    )
    rows_returned = lax.all_to_all(fetched, "expert", split_axis=0, concat_axis=0, tiled=True)
    embedded = jnp.take(rows_returned.reshape(device_count * look_cap, features), placed, axis=0)
    scales = jnp.exp2(block_exps.astype(jnp.float32))
    blocks = (
        block_values.reshape(tok_rows, scales.shape[1], -1).astype(jnp.float32) * scales[:, :, None]
    )
    token_state = (blocks.reshape(tok_rows, features) + embedded.astype(jnp.float32)).astype(
        jnp.bfloat16
    )
    flat_ids = expert_ids.reshape(-1)
    expert_hot = (flat_ids[:, None] == jnp.arange(EXPERTS, dtype=jnp.int32)[None, :]).astype(
        jnp.int32
    )
    expert_rank = jnp.sum((jnp.cumsum(expert_hot, axis=0) - 1) * expert_hot, axis=1)
    slot_of = flat_ids * CAP + expert_rank
    token_index = jnp.arange(tok_rows * TOP, dtype=jnp.int32) // TOP
    source = jnp.full((EXPERTS * CAP,), tok_rows, jnp.int32).at[slot_of].set(token_index)
    padded = jnp.concatenate([token_state, jnp.zeros((1, features), jnp.bfloat16)], axis=0)
    buffer = jnp.take(padded, source, axis=0)
    expert_out = full_path(
        buffer, w_gate, w_up, w_down, device_count, exp_dev, width_split, features
    )
    chosen = jnp.take(expert_out, slot_of, axis=0).reshape(tok_rows, TOP, features)
    mixed = jnp.sum(gate_weights[:, :, None] * chosen.astype(jnp.float32), axis=1).astype(
        jnp.bfloat16
    )
    gate_grads = jnp.einsum("tkd,td->tk", chosen, out_grad, preferred_element_type=jnp.float32)
    return (mixed, gate_grads)


def local(*arrays):
    if lax.axis_size("expert") == 16 and arrays[6].shape[0] * 16 == EXPERTS:
        return near_path(*arrays)
    return far_path(*arrays)


def solution(mesh):
    return jax.shard_map(
        local,
        mesh=mesh,
        in_specs=(
            P(("groups", "expert"), None),
            P(("groups", "expert"), None),
            P(("groups", "expert")),
            P(("groups", "expert"), None),
            P(("groups", "expert"), None),
            P("expert", None),
            P("expert", None, None),
            P("expert", None, None),
            P("expert", None, None),
            P(("groups", "expert"), None),
        ),
        out_specs=(P(("groups", "expert"), None), P(("groups", "expert"), None)),
        check_vma=False,
    )
```

```python
import functools

import jax
import jax.numpy as jnp
from jax import lax
from jax.experimental import pallas as pl
from jax.experimental.pallas import tpu as pltpu
from jax.sharding import PartitionSpec as P

EXPERTS = 64
TOP = 4
CAP = 12
BLOCK = 128
PAIR = 2 * CAP
VMEM = pltpu.VMEM
F32 = jnp.float32
BF16 = jnp.bfloat16
SMALL = pltpu.CompilerParams(vmem_limit_bytes=16 * 1024 * 1024)


def dot(a, b):
    return jnp.dot(a, b, preferred_element_type=F32)


def in_hbm(array):
    return pltpu.with_memory_space_constraint(array, pltpu.HBM)


def iota(shape, dimension):
    return lax.broadcasted_iota(jnp.int32, shape, dimension)


def flags(mask):
    return mask.astype(F32).astype(BF16)


def earlier(length):
    return flags(iota((length, length), 0) < iota((length, length), 1))


def repeat_kernel(rows_ref, grad_ref, out_ref, upper_ref):
    for n in range(out_ref.shape[0]):
        out_ref[n] = rows_ref[...]
    upper_ref[...] = grad_ref[...]


def fetch_kernel(me_ref, rows_ref, table_hbm, _, out_hbm, table_ref, out_ref, sem, out_sem):
    copy = pltpu.make_async_copy(table_hbm, table_ref, sem)
    copy.start()
    device_count, _, tok_rows = rows_ref.shape
    held = table_ref.shape[0]
    look_cap = out_ref.shape[0] // device_count
    local = rows_ref[:, 0, :] - me_ref[0] * held
    hit = (local >= 0) & (local < held)
    rank = dot(flags(hit), earlier(tok_rows)).astype(jnp.int32)
    rank = jnp.where(hit, rank, -1)
    slot = iota((look_cap, tok_rows), 0)
    place = iota((look_cap, held), 1)
    picks = []
    for source in range(device_count):
        mine = jnp.where(slot == rank[source : source + 1], local[source : source + 1], 0)
        wanted = jnp.sum(mine, axis=1, keepdims=True)
        picks.append(flags(place == wanted))
    pick = jnp.concatenate(picks, axis=0)
    copy.wait()
    width = out_ref.shape[1] // out_sem.shape[0]
    copies = []
    for n in range(out_sem.shape[0]):
        cols = pl.ds(n * width, width)
        out_ref[:, cols] = dot(pick, table_ref[:, cols]).astype(BF16)
        copies.append(
            pltpu.make_async_copy(out_ref.at[:, cols], out_hbm.at[:, cols], out_sem.at[n])
        )
        copies[-1].start()
    for copy in copies:
        copy.wait()


def turned(rows):
    count, length = rows.shape
    return jnp.concatenate([rows, jnp.zeros((length - count, length), F32)], axis=0).T


def plan_slots(me, ids_ref, pick_refs, slots_ref):
    tok_rows = ids_ref.shape[1]
    half = sum(ref.shape[0] for ref in pick_refs) // (2 * PAIR)
    exp_dev = EXPERTS // (2 * half)
    flip = me % 2
    inside = iota((half * exp_dev, tok_rows), 0)
    expert = inside + me // half * half * exp_dev
    place = iota((PAIR, tok_rows), 0)
    ids = ids_ref[...]
    chosen = [ids[k : k + 1] == expert for k in range(TOP)]
    hit = functools.reduce(jnp.logical_or, chosen)
    rank = jnp.where(hit, dot(flags(hit), earlier(tok_rows)).astype(jnp.int32), -1000)
    lines = []
    for at in range(0, half * exp_dev, 2):
        one, two = rank[at : at + 1], rank[at + 1 : at + 2]
        upper = jnp.where(flip == 0, one, two)
        lower = jnp.where(flip == 0, two, one) + CAP
        here = ((place < CAP) & (place == upper)) | ((place >= CAP) & (place == lower))
        lines.append(here.astype(F32))
    pairs = exp_dev // 2
    slot = ((inside + flip) & 1) * CAP + rank
    if len(pick_refs) == 1:
        pick_refs[0][...] = jnp.concatenate(lines, axis=0).astype(BF16)
        slot = slot + (inside // 2) * PAIR
    else:
        for n, ref in enumerate(pick_refs):
            ref[...] = jnp.concatenate(lines[n::pairs], axis=0).astype(BF16)
        device = inside // exp_dev
        first = device * (2 * PAIR) + PAIR
        second = half * 2 * PAIR + device * PAIR
        slot = slot + jnp.where((inside & 2) == 0, first, second)
    found = [
        jnp.sum(jnp.where(chosen[k], slot + 1, 0), axis=0, keepdims=True) - 1 for k in range(TOP)
    ]
    slots_ref[...] = turned(jnp.concatenate(found, axis=0).astype(F32)).astype(jnp.int32)


def near_plan_kernel(
    me_ref,
    rows_ref,
    ids_ref,
    weights_ref,
    scales_ref,
    _,
    put_ref,
    first_pick_ref,
    second_pick_ref,
    slots_ref,
    columns_ref,
    ids_out_ref,
    weights_out_ref,
):
    ids_out_ref[...] = ids_ref[...]
    weights_out_ref[...] = weights_ref[...]
    tok_rows = rows_ref.shape[1]
    me, held = me_ref[0], me_ref[1]
    device_count = first_pick_ref.shape[0] // PAIR * 2
    look_cap = put_ref.shape[1] // device_count
    row = jnp.broadcast_to(rows_ref[...], (device_count, tok_rows))
    low = iota((device_count, tok_rows), 0) * held
    hit = (row >= low) & (row < low + held)
    rank = jnp.where(hit, dot(flags(hit), earlier(tok_rows)).astype(jnp.int32), -1)
    slot = iota((look_cap, tok_rows), 0)
    put = [(slot == rank[o : o + 1]).astype(F32) for o in range(device_count)]
    put_ref[...] = jnp.concatenate(put, axis=0).T.astype(BF16)
    plan_slots(me, ids_ref, (first_pick_ref, second_pick_ref), slots_ref)
    columns_ref[...] = turned(jnp.concatenate([weights_ref[...], scales_ref[...]], axis=0))


def far_plan_kernel(me_ref, ids_ref, weights_ref, _, pick_ref, slots_ref, columns_ref):
    plan_slots(me_ref[0], ids_ref, (pick_ref,), slots_ref)
    columns_ref[...] = turned(weights_ref[...])


def state_kernel(
    put_ref, returned_ref, values_ref, columns_ref, ids_ref, weights_ref, state_ref
):
    features = values_ref.shape[1]
    width = 512
    for left in range(0, features, width):
        found = dot(put_ref[...], returned_ref[:, left : left + width])
        for b in range(width // BLOCK):
            at = left + b * BLOCK
            scaled = (
                values_ref[:, at : at + BLOCK].astype(F32)
                * columns_ref[:, TOP + at // BLOCK : TOP + at // BLOCK + 1]
            )
            state_ref[:, at : at + BLOCK] = (
                scaled + found[:, b * BLOCK : (b + 1) * BLOCK]
            ).astype(BF16)


def pair_kernel(pick_ref, state_ref, *refs):
    out_ref = refs[-1]
    out_ref[...] = dot(pick_ref[...], state_ref[...]).astype(BF16)


def pick_kernel(
    pick_ref, state_ref, grad_ref, out_hbm, lower_grad_ref, sent_ref, sem
):
    tok_rows, features = state_ref.shape
    width = features // sem.shape[0]
    copies = []
    for n in range(sem.shape[0]):
        cols = pl.ds(n * width, width)
        sent_ref[:, cols] = dot(pick_ref[...], state_ref[:, cols]).astype(BF16)
        copies.append(
            pltpu.make_async_copy(sent_ref.at[:, cols], out_hbm.at[:, cols], sem.at[n])
        )
        copies[-1].start()
    lower_grad_ref[...] = grad_ref[tok_rows // 2 :, :]
    for copy in copies:
        copy.wait()


def expert_kernel(first, count, join, after, rows_hbm, *refs):
    if join:
        front_ref, refs = refs[0], refs[1:]
    wg_hbm, wu_hbm, wd_hbm, out_ref = refs[after : after + 4]
    rows_ref, x_ref, wg_ref, wu_ref, wd_ref, hidden_ref, result_ref, sem, rows_sem = refs[
        after + 4 :
    ]
    held, features, width = wg_ref.shape
    half = x_ref.shape[1] // CAP
    up_cuts = ((0, 512), (512, 512), (1024, width - 1024))
    down_cuts = tuple((at, 512) for at in range(0, features, 512))

    def weight_copies(j, place):
        copies = []
        for at, size in up_cuts:
            cols = pl.ds(at, size)
            copies.append((wg_hbm.at[first + j, :, cols], wg_ref.at[place, :, cols]))
            copies.append((wu_hbm.at[first + j, :, cols], wu_ref.at[place, :, cols]))
        for at, size in down_cuts:
            cols = pl.ds(at, size)
            copies.append((wd_hbm.at[first + j, :, cols], wd_ref.at[place, :, cols]))
        return [
            pltpu.make_async_copy(src, dst, sem.at[place, n])
            for n, (src, dst) in enumerate(copies)
        ]

    rows_copy = pltpu.make_async_copy(rows_hbm, rows_ref, rows_sem)
    rows_copy.start()
    weights = weight_copies(0, 0) + weight_copies(1, 1)
    for copy in weights[:4]:
        copy.start()
    rows_copy.wait()
    for copy in weights[4:]:
        copy.start()

    low = iota((PAIR, features), 0) < CAP
    lines = rows_ref.shape[0] // half

    def pair_rows(ref, pair):
        block = 2 * PAIR
        return ref[pair * block : (pair + 1) * block, :].astype(F32)

    for chunk in range(count // 2):
        for quad in range(half // 4):
            ones, twos = [], []
            for pair in (2 * quad, 2 * quad + 1):
                if lines == PAIR:
                    rows = pair_rows(rows_ref, pair)
                    even, odd = rows[:PAIR], rows[PAIR:]
                else:
                    here = slice(chunk * PAIR, (chunk + 1) * PAIR)
                    even = pair_rows(rows_ref, 2 * pair)[here]
                    odd = pair_rows(rows_ref, 2 * pair + 1)[here]
                ones.append(jnp.where(low, even, odd))
                twos.append(jnp.where(low, odd, even))
            rows = slice(quad * 2 * PAIR, (quad + 1) * 2 * PAIR)
            x_ref[2 * chunk, rows, :] = jnp.concatenate(ones, axis=0).astype(BF16)
            x_ref[2 * chunk + 1, rows, :] = jnp.concatenate(twos, axis=0).astype(BF16)

    @pl.loop(0, count)
    def _(j):
        place = j % held
        copies = weight_copies(j, place)

        def refill(n, parts):
            @pl.when(j + held < count)
            def _():
                for copy in weight_copies(j + held, place)[n : n + parts]:
                    copy.start()

        n = 0
        for at, size in up_cuts:
            copies[n].wait()
            copies[n + 1].wait()
            gate = dot(x_ref[j], wg_ref[place, :, at : at + size])
            up = dot(x_ref[j], wu_ref[place, :, at : at + size])
            hidden = gate / (1.0 + jnp.exp(-gate)) * up
            hidden_ref[:, at : at + size] = hidden.astype(BF16)
            if count > held:
                refill(n, 2)
            n += 2
        for at, size in down_cuts:
            copies[n].wait()
            result_ref[j, :, at : at + size] = dot(
                hidden_ref[...], wd_ref[place, :, at : at + size]
            )
            if count > held:
                refill(n, 1)
            n += 1

    block = 2 * PAIR
    for pair in range(half // 2):
        rows = slice(pair * PAIR, (pair + 1) * PAIR)
        values = [result_ref[j, rows, :] for j in range(count)]
        results = []
        for odd in range(2):
            parts = [
                jnp.where(low, values[j + odd], values[j + 1 - odd]) for j in range(0, count, 2)
            ]
            if join:
                parts = [pair_rows(front_ref, pair)[odd * PAIR : (odd + 1) * PAIR]] + parts
            results += parts
        for n in range(0, len(results), 2):
            at = (pair * len(results) + n) * PAIR
            two = jnp.concatenate(results[n : n + 2], axis=0)
            out_ref[at : at + block, :] = two.astype(BF16)


def expert_call(name, first, count, rows_in, weights, front=(), after=(), grant=46):
    w_gate, w_up, w_down = weights
    _, features, width = w_gate.shape
    half = rows_in.shape[0]
    rows = half * CAP
    lines = count * CAP + len(front) * PAIR
    rows_in, *front = [array.reshape(-1, features) for array in (rows_in, *front)]
    held = 2
    anywhere = pl.BlockSpec(memory_space=pl.ANY)
    hbm = pl.BlockSpec(memory_space=pltpu.HBM)
    vmem = pl.BlockSpec(memory_space=VMEM)
    return pl.pallas_call(
        functools.partial(expert_kernel, first, count, bool(front), len(after)),
        out_shape=pltpu.HBM((half * lines, features), BF16),
        in_specs=[hbm] + [vmem] * len(front) + [anywhere] * len(after) + [hbm] * 3,
        out_specs=vmem,
        scratch_shapes=[
            VMEM(rows_in.shape, BF16),
            VMEM((count, rows, features), BF16),
            VMEM((held, features, width), BF16),
            VMEM((held, features, width), BF16),
            VMEM((held, width, features), BF16),
            VMEM((rows, width), BF16),
            VMEM((count, rows, features), F32),
            pltpu.SemaphoreType.DMA((held, 10)),
            pltpu.SemaphoreType.DMA,
        ],
        compiler_params=pltpu.CompilerParams(vmem_limit_bytes=grant * 1024 * 1024),
        cost_estimate=pl.CostEstimate(
            flops=12 * count * rows * features * width,
            bytes_accessed=6 * count * features * width,
            transcendentals=count * rows * width,
        ),
        name=name,
    )(
        *[in_hbm(array) for array in (rows_in, *front, *after, w_gate, w_up, w_down)],
    ).reshape(half, lines, features)


def mix_kernel(grads, added, added_grads, start, slots_ref, columns_ref, back_ref, *refs):
    mixed_ref, grads_ref = refs[-2:]
    grad_refs = refs[:grads]
    added_refs = refs[grads : grads + added]
    added_grad_refs = refs[grads + added : grads + added + added_grads]
    tok_rows = slots_ref.shape[0]
    count, features = back_ref.shape
    grad = jnp.concatenate([ref[...] for ref in grad_refs], axis=0)
    place = iota((tok_rows, tok_rows), 1)
    wide = jnp.zeros((tok_rows, tok_rows), F32)
    column = iota((tok_rows, count), 1) + start
    inner = lax.dot_general(
        grad, back_ref[...], (((1,), (1,)), ((), ())), preferred_element_type=F32
    )
    total = jnp.zeros((tok_rows, count), F32)
    for k in range(TOP):
        here = column == slots_ref[:, k : k + 1]
        total = total + jnp.where(here, columns_ref[:, k : k + 1], 0.0)
        value = jnp.sum(jnp.where(here, inner, 0.0), axis=1, keepdims=True)
        wide = wide + jnp.where(place == k, value, 0.0)
    high = total.astype(BF16)
    rest = (total - high.astype(F32)).astype(BF16)
    width = 512
    for at in range(0, features, width):
        cols = slice(at, at + width)
        value = dot(high, back_ref[:, cols]) + dot(rest, back_ref[:, cols])
        for ref in added_refs:
            value = value + ref[:, cols].astype(F32)
        mixed_ref[:, cols] = value.astype(mixed_ref.dtype)
    lines = grads_ref.shape[0]
    sums = wide.T[:lines, :]
    for ref in added_grad_refs:
        sums = sums + ref[:lines, :]
    grads_ref[...] = sums


def swap(array, groups=None):
    return lax.all_to_all(
        array, "expert", split_axis=0, concat_axis=0, tiled=True, axis_index_groups=groups
    )


def near_path(
    block_values,
    block_exps,
    row_ids,
    expert_ids,
    gate_weights,
    table,
    w_gate,
    w_up,
    w_down,
    out_grad,
):
    device_count = lax.axis_size("expert")
    half = device_count // 2
    halves = [list(range(half)), list(range(half, device_count))]
    me = lax.axis_index("expert").astype(jnp.int32)
    tok_rows, features = block_values.shape
    rows_held = table.shape[0]
    look_cap = max(2, 2 * tok_rows // device_count)
    slots = half * 2 * PAIR
    vmem = pl.BlockSpec(memory_space=VMEM)
    smem = pl.BlockSpec(memory_space=pltpu.SMEM)
    anywhere = pl.BlockSpec(memory_space=pl.ANY)
    place = jnp.stack([me, jnp.int32(rows_held)])

    def shape(dims, kind):
        return jax.ShapeDtypeStruct(dims, kind)

    def mirrored(array):
        pairs = [(i, (i + half) % device_count) for i in range(device_count)]
        return lax.ppermute(array, "expert", pairs)

    def ordered(array, *earlier_arrays, flops=0):
        return pl.pallas_call(
            lambda *refs: None,
            out_shape=shape(array.shape, array.dtype),
            in_specs=[anywhere] * (1 + len(earlier_arrays)),
            out_specs=anywhere,
            input_output_aliases={0: 0},
            compiler_params=SMALL,
            cost_estimate=pl.CostEstimate(flops=flops, bytes_accessed=0, transcendentals=0),
            name="ordered",
        )(array, *earlier_arrays)

    upper = tok_rows // 2
    all_rows, upper_grad = pl.pallas_call(
        repeat_kernel,
        out_shape=(
            shape((device_count, 1, tok_rows), jnp.int32),
            shape((upper, features), BF16),
        ),
        grid=(1,),
        in_specs=[
            pl.BlockSpec((1, tok_rows), lambda i: (0, 0)),
            pl.BlockSpec((upper, features), lambda i: (0, 0)),
        ],
        out_specs=(
            pl.BlockSpec((device_count, 1, tok_rows), lambda i: (0, 0, 0)),
            pl.BlockSpec((upper, features), lambda i: (0, 0)),
        ),
        name="repeat_rows",
    )(row_ids[None, :], out_grad)
    other_upper = mirrored(upper_grad)
    fetched = pl.pallas_call(
        fetch_kernel,
        out_shape=pltpu.HBM((device_count * look_cap, features), BF16),
        in_specs=[smem, vmem, pl.BlockSpec(memory_space=pltpu.HBM), anywhere],
        out_specs=anywhere,
        scratch_shapes=[
            VMEM(table.shape, BF16),
            VMEM((device_count * look_cap, features), BF16),
            pltpu.SemaphoreType.DMA,
            pltpu.SemaphoreType.DMA((4,)),
        ],
        compiler_params=SMALL,
        name="fetch_rows",
    )(place, swap(all_rows), in_hbm(table), other_upper)
    returned = swap(fetched.reshape(device_count, look_cap, features))
    turned_ids, turned_weights = expert_ids.T, gate_weights.T
    pick_shape = shape((slots, tok_rows), BF16)
    pair_shape = shape((slots // 2, tok_rows), BF16)
    square = (tok_rows, tok_rows)
    put, first_pick, second_pick, near_of, near_columns, sent_ids, sent_weights = pl.pallas_call(
        near_plan_kernel,
        out_shape=(
            shape((tok_rows, device_count * look_cap), BF16),
            pair_shape,
            pair_shape,
            shape(square, jnp.int32),
            shape(square, F32),
            shape(turned_ids.shape, jnp.int32),
            shape(turned_weights.shape, F32),
        ),
        in_specs=[smem, vmem, vmem, vmem, vmem, anywhere],
        out_specs=(vmem,) * 7,
        compiler_params=SMALL,
        name="near_plan",
    )(
        place,
        row_ids[None, :],
        turned_ids,
        turned_weights,
        jnp.exp2(block_exps.T.astype(F32)),
        in_hbm(fetched),
    )
    other_ids, other_weights = mirrored(sent_ids), mirrored(sent_weights)

    def sent_scratch(count):
        return [VMEM((count, features), BF16), pltpu.SemaphoreType.DMA((4,))]

    state = pl.pallas_call(
        state_kernel,
        out_shape=shape((tok_rows, features), BF16),
        in_specs=[vmem] * 4 + [anywhere] * 2,
        out_specs=vmem,
        compiler_params=SMALL,
        name="token_state",
    )(
        put,
        returned.reshape(device_count * look_cap, features),
        block_values,
        near_columns,
        other_ids,
        other_weights,
    )

    def pair_sent(name, pick, *after):
        return pl.pallas_call(
            pair_kernel,
            out_shape=pltpu.HBM((slots // 2, features), BF16),
            in_specs=[vmem, vmem] + [anywhere] * len(after),
            out_specs=vmem,
            compiler_params=SMALL,
            name=name,
        )(pick, state, *after).reshape(half, PAIR, features)

    far_pick, far_of, far_columns = pl.pallas_call(
        far_plan_kernel,
        out_shape=(pick_shape, shape(square, jnp.int32), shape(square, F32)),
        in_specs=[smem, vmem, vmem, anywhere],
        out_specs=(vmem,) * 3,
        compiler_params=SMALL,
        name="far_plan",
    )(place, other_ids, other_weights, state)
    far_sent, lower_grad = pl.pallas_call(
        pick_kernel,
        out_shape=(
            pltpu.HBM((slots, features), BF16),
            shape((tok_rows - upper, features), BF16),
        ),
        in_specs=[vmem, vmem, vmem],
        out_specs=(anywhere, vmem),
        scratch_shapes=sent_scratch(slots),
        compiler_params=SMALL,
        cost_estimate=pl.CostEstimate(
            flops=400_000_000_000, bytes_accessed=4 * slots * features, transcendentals=0
        ),
        name="far_slots",
    )(far_pick, mirrored(state), out_grad)
    near_rows = swap(pair_sent("first_slots", first_pick), halves)
    far_sent = far_sent.reshape(half, 2 * PAIR, features)
    far_rows = swap(far_sent, halves)
    later_sent = pair_sent("later_slots", second_pick, in_hbm(far_sent))
    other_grads = (other_upper, mirrored(lower_grad))

    weights = (w_gate, w_up, w_down)
    sent_both = expert_call(
        "near_first", 0, 2, near_rows, weights, front=(later_sent,), after=(far_sent,), grant=63
    )
    far_out = expert_call("far_experts", 0, 4, far_rows, weights, after=(sent_both,), grant=63)
    both = swap(sent_both, halves)
    far_back = swap(ordered(in_hbm(far_out), in_hbm(both), other_grads[1]), halves)
    near_out = expert_call("near_second", 2, 2, both, weights)

    def mixed_rows(
        name,
        slot_of,
        columns,
        back,
        grads,
        kind,
        start=0,
        lines=2 * TOP,
        added=(),
        added_grads=(),
        after=(),
    ):
        operands = (*grads, *added, *added_grads)

        return pl.pallas_call(
            functools.partial(mix_kernel, len(grads), len(added), len(added_grads), start),
            out_shape=(shape((tok_rows, features), kind), shape((lines, tok_rows), F32)),
            in_specs=[vmem] * (3 + len(operands)) + [anywhere] * len(after),
            out_specs=(vmem, vmem),
            compiler_params=SMALL,
            name=name,
        )(slot_of, columns, back.reshape(-1, features), *operands, *after)

    sums, sum_grads = mixed_rows(
        "mix_first",
        near_of,
        near_columns,
        in_hbm(both.reshape(slots, features)),
        (out_grad,),
        F32,
    )
    far_mixed, far_grads = mixed_rows(
        "mix_far",
        far_of,
        far_columns,
        far_back,
        other_grads,
        BF16,
        after=(in_hbm(near_out), sum_grads),
    )
    near_back = swap(ordered(in_hbm(near_out), far_mixed), halves)
    mixed, grads = mixed_rows(
        "mix_second",
        near_of,
        near_columns,
        near_back,
        (out_grad,),
        BF16,
        start=slots,
        lines=TOP,
        added=(sums, ordered(mirrored(far_mixed), flops=400_000_000_000)),
        added_grads=(sum_grads, mirrored(far_grads)),
    )
    return mixed, grads.T


def expert_work(arrived, w_gate, w_up, w_down):
    gate_act = jnp.einsum("sjcd,jdf->sjcf", arrived, w_gate, preferred_element_type=jnp.float32)
    up_act = jnp.einsum("sjcd,jdf->sjcf", arrived, w_up, preferred_element_type=jnp.float32)
    hidden = (jax.nn.silu(gate_act) * up_act).astype(jnp.bfloat16)
    return jnp.einsum("sjcf,jfd->sjcd", hidden, w_down, preferred_element_type=jnp.float32).astype(
        jnp.bfloat16
    )


def full_path(buffer, w_gate, w_up, w_down, device_count, exp_dev, width_split, features):
    group_count = EXPERTS // exp_dev
    grouped = buffer.reshape(group_count, 1, exp_dev, CAP, features)
    outgoing = jnp.broadcast_to(
        grouped, (group_count, width_split, exp_dev, CAP, features)
    ).reshape(device_count, exp_dev, CAP, features)
    returned_out = lax.all_to_all(
        expert_work(
            lax.all_to_all(outgoing, "expert", split_axis=0, concat_axis=0, tiled=True),
            w_gate,
            w_up,
            w_down,
        ),
        "expert",
        split_axis=0,
        concat_axis=0,
        tiled=True,
    )
    pieces = returned_out.reshape(group_count, width_split, exp_dev, CAP, features).astype(
        jnp.float32
    )
    return jnp.sum(pieces, axis=1).astype(jnp.bfloat16).reshape(EXPERTS * CAP, features)


def far_path(
    block_values,
    block_exps,
    row_ids,
    expert_ids,
    gate_weights,
    table,
    w_gate,
    w_up,
    w_down,
    out_grad,
):
    device_count = lax.axis_size("expert")
    tok_rows = block_values.shape[0]
    features = block_values.shape[1]
    rows_held = table.shape[0]
    look_cap = max(2, 2 * tok_rows // device_count)
    exp_dev = w_gate.shape[0]
    width_split = device_count * exp_dev // EXPERTS
    owners = row_ids // rows_held
    local_row = row_ids % rows_held
    owner_hot = (owners[:, None] == jnp.arange(device_count, dtype=jnp.int32)[None, :]).astype(
        jnp.int32
    )
    owner_rank = jnp.sum((jnp.cumsum(owner_hot, axis=0) - 1) * owner_hot, axis=1)
    placed = owners * look_cap + owner_rank
    wanted = jnp.zeros((device_count * look_cap,), jnp.int32).at[placed].set(local_row)
    requested = lax.all_to_all(
        wanted.reshape(device_count, look_cap), "expert", split_axis=0, concat_axis=0, tiled=True
    )
    fetched = jnp.take(table, requested.reshape(-1), axis=0).reshape(
        device_count, look_cap, features
    )
    rows_returned = lax.all_to_all(fetched, "expert", split_axis=0, concat_axis=0, tiled=True)
    embedded = jnp.take(rows_returned.reshape(device_count * look_cap, features), placed, axis=0)
    scales = jnp.exp2(block_exps.astype(jnp.float32))
    blocks = (
        block_values.reshape(tok_rows, scales.shape[1], -1).astype(jnp.float32) * scales[:, :, None]
    )
    token_state = (blocks.reshape(tok_rows, features) + embedded.astype(jnp.float32)).astype(
        jnp.bfloat16
    )
    flat_ids = expert_ids.reshape(-1)
    expert_hot = (flat_ids[:, None] == jnp.arange(EXPERTS, dtype=jnp.int32)[None, :]).astype(
        jnp.int32
    )
    expert_rank = jnp.sum((jnp.cumsum(expert_hot, axis=0) - 1) * expert_hot, axis=1)
    slot_of = flat_ids * CAP + expert_rank
    token_index = jnp.arange(tok_rows * TOP, dtype=jnp.int32) // TOP
    source = jnp.full((EXPERTS * CAP,), tok_rows, jnp.int32).at[slot_of].set(token_index)
    padded = jnp.concatenate([token_state, jnp.zeros((1, features), jnp.bfloat16)], axis=0)
    buffer = jnp.take(padded, source, axis=0)
    expert_out = full_path(
        buffer, w_gate, w_up, w_down, device_count, exp_dev, width_split, features
    )
    chosen = jnp.take(expert_out, slot_of, axis=0).reshape(tok_rows, TOP, features)
    mixed = jnp.sum(gate_weights[:, :, None] * chosen.astype(jnp.float32), axis=1).astype(
        jnp.bfloat16
    )
    gate_grads = jnp.einsum("tkd,td->tk", chosen, out_grad, preferred_element_type=jnp.float32)
    return (mixed, gate_grads)


def local(*arrays):
    if lax.axis_size("expert") == 16 and arrays[6].shape[0] * 16 == EXPERTS:
        return near_path(*arrays)
    return far_path(*arrays)


def solution(mesh):
    return jax.shard_map(
        local,
        mesh=mesh,
        in_specs=(
            P(("groups", "expert"), None),
            P(("groups", "expert"), None),
            P(("groups", "expert")),
            P(("groups", "expert"), None),
            P(("groups", "expert"), None),
            P("expert", None),
            P("expert", None, None),
            P("expert", None, None),
            P("expert", None, None),
            P(("groups", "expert"), None),
        ),
        out_specs=(P(("groups", "expert"), None), P(("groups", "expert"), None)),
        check_vma=False,
    )
```

```python
import functools

import jax
import jax.numpy as jnp
from jax import lax
from jax.experimental import pallas as pl
from jax.experimental.pallas import tpu as pltpu
from jax.sharding import PartitionSpec as P

EXPERTS = 64
TOP = 4
CAP = 12
BLOCK = 128
PAIR = 2 * CAP
VMEM = pltpu.VMEM
F32 = jnp.float32
BF16 = jnp.bfloat16
SMALL = pltpu.CompilerParams(vmem_limit_bytes=16 * 1024 * 1024)


def dot(a, b):
    return jnp.dot(a, b, preferred_element_type=F32)


def in_hbm(array):
    return pltpu.with_memory_space_constraint(array, pltpu.HBM)


def iota(shape, dimension):
    return lax.broadcasted_iota(jnp.int32, shape, dimension)


def flags(mask):
    return mask.astype(F32).astype(BF16)


def earlier(length):
    return flags(iota((length, length), 0) < iota((length, length), 1))


def repeat_kernel(rows_ref, grad_ref, out_ref, upper_ref):
    for n in range(out_ref.shape[0]):
        out_ref[n] = rows_ref[...]
    upper_ref[...] = grad_ref[...]


def fetch_kernel(me_ref, rows_ref, table_hbm, _, out_hbm, table_ref, out_ref, sem, out_sem):
    copy = pltpu.make_async_copy(table_hbm, table_ref, sem)
    copy.start()
    device_count, _, tok_rows = rows_ref.shape
    held = table_ref.shape[0]
    look_cap = out_ref.shape[0] // device_count
    local = rows_ref[:, 0, :] - me_ref[0] * held
    hit = (local >= 0) & (local < held)
    rank = dot(flags(hit), earlier(tok_rows)).astype(jnp.int32)
    rank = jnp.where(hit, rank, -1)
    slot = iota((look_cap, tok_rows), 0)
    place = iota((look_cap, held), 1)
    picks = []
    for source in range(device_count):
        mine = jnp.where(slot == rank[source : source + 1], local[source : source + 1], 0)
        wanted = jnp.sum(mine, axis=1, keepdims=True)
        picks.append(flags(place == wanted))
    pick = jnp.concatenate(picks, axis=0)
    copy.wait()
    width = out_ref.shape[1] // out_sem.shape[0]
    copies = []
    for n in range(out_sem.shape[0]):
        cols = pl.ds(n * width, width)
        out_ref[:, cols] = dot(pick, table_ref[:, cols]).astype(BF16)
        copies.append(
            pltpu.make_async_copy(out_ref.at[:, cols], out_hbm.at[:, cols], out_sem.at[n])
        )
        copies[-1].start()
    for copy in copies:
        copy.wait()


def turned(rows):
    count, length = rows.shape
    return jnp.concatenate([rows, jnp.zeros((length - count, length), F32)], axis=0).T


def plan_slots(me, ids_ref, pick_refs, slots_ref):
    tok_rows = ids_ref.shape[1]
    half = sum(ref.shape[0] for ref in pick_refs) // (2 * PAIR)
    exp_dev = EXPERTS // (2 * half)
    flip = me % 2
    inside = iota((half * exp_dev, tok_rows), 0)
    expert = inside + me // half * half * exp_dev
    place = iota((PAIR, tok_rows), 0)
    ids = ids_ref[...]
    chosen = [ids[k : k + 1] == expert for k in range(TOP)]
    hit = functools.reduce(jnp.logical_or, chosen)
    rank = jnp.where(hit, dot(flags(hit), earlier(tok_rows)).astype(jnp.int32), -1000)
    lines = []
    for at in range(0, half * exp_dev, 2):
        one, two = rank[at : at + 1], rank[at + 1 : at + 2]
        upper = jnp.where(flip == 0, one, two)
        lower = jnp.where(flip == 0, two, one) + CAP
        here = ((place < CAP) & (place == upper)) | ((place >= CAP) & (place == lower))
        lines.append(here.astype(F32))
    pairs = exp_dev // 2
    slot = ((inside + flip) & 1) * CAP + rank
    if len(pick_refs) == 1:
        pick_refs[0][...] = jnp.concatenate(lines, axis=0).astype(BF16)
        slot = slot + (inside // 2) * PAIR
    else:
        for n, ref in enumerate(pick_refs):
            ref[...] = jnp.concatenate(lines[n::pairs], axis=0).astype(BF16)
        device = inside // exp_dev
        first = device * (2 * PAIR) + PAIR
        second = half * 2 * PAIR + device * PAIR
        slot = slot + jnp.where((inside & 2) == 0, first, second)
    found = [
        jnp.sum(jnp.where(chosen[k], slot + 1, 0), axis=0, keepdims=True) - 1 for k in range(TOP)
    ]
    slots_ref[...] = turned(jnp.concatenate(found, axis=0).astype(F32)).astype(jnp.int32)


def near_plan_kernel(
    me_ref,
    rows_ref,
    ids_ref,
    weights_ref,
    scales_ref,
    _,
    put_ref,
    first_pick_ref,
    second_pick_ref,
    slots_ref,
    columns_ref,
    ids_out_ref,
    weights_out_ref,
):
    ids_out_ref[...] = ids_ref[...]
    weights_out_ref[...] = weights_ref[...]
    tok_rows = rows_ref.shape[1]
    me, held = me_ref[0], me_ref[1]
    device_count = first_pick_ref.shape[0] // PAIR * 2
    look_cap = put_ref.shape[1] // device_count
    row = jnp.broadcast_to(rows_ref[...], (device_count, tok_rows))
    low = iota((device_count, tok_rows), 0) * held
    hit = (row >= low) & (row < low + held)
    rank = jnp.where(hit, dot(flags(hit), earlier(tok_rows)).astype(jnp.int32), -1)
    slot = iota((look_cap, tok_rows), 0)
    put = [(slot == rank[o : o + 1]).astype(F32) for o in range(device_count)]
    put_ref[...] = jnp.concatenate(put, axis=0).T.astype(BF16)
    plan_slots(me, ids_ref, (first_pick_ref, second_pick_ref), slots_ref)
    columns_ref[...] = turned(jnp.concatenate([weights_ref[...], scales_ref[...]], axis=0))


def far_plan_kernel(me_ref, ids_ref, weights_ref, _, pick_ref, slots_ref, columns_ref):
    plan_slots(me_ref[0], ids_ref, (pick_ref,), slots_ref)
    columns_ref[...] = turned(weights_ref[...])


def state_kernel(
    put_ref, returned_ref, values_ref, columns_ref, ids_ref, weights_ref, state_ref
):
    features = values_ref.shape[1]
    width = 512
    for left in range(0, features, width):
        found = dot(put_ref[...], returned_ref[:, left : left + width])
        for b in range(width // BLOCK):
            at = left + b * BLOCK
            scaled = (
                values_ref[:, at : at + BLOCK].astype(F32)
                * columns_ref[:, TOP + at // BLOCK : TOP + at // BLOCK + 1]
            )
            state_ref[:, at : at + BLOCK] = (
                scaled + found[:, b * BLOCK : (b + 1) * BLOCK]
            ).astype(BF16)


def pair_kernel(pick_ref, state_ref, *refs):
    out_ref = refs[-1]
    out_ref[...] = dot(pick_ref[...], state_ref[...]).astype(BF16)


def pick_kernel(
    pick_ref, state_ref, grad_ref, out_hbm, lower_grad_ref, sent_ref, sem
):
    tok_rows, features = state_ref.shape
    width = features // sem.shape[0]
    copies = []
    for n in range(sem.shape[0]):
        cols = pl.ds(n * width, width)
        sent_ref[:, cols] = dot(pick_ref[...], state_ref[:, cols]).astype(BF16)
        copies.append(
            pltpu.make_async_copy(sent_ref.at[:, cols], out_hbm.at[:, cols], sem.at[n])
        )
        copies[-1].start()
    lower_grad_ref[...] = grad_ref[tok_rows - lower_grad_ref.shape[0] :, :]
    for copy in copies:
        copy.wait()


def expert_kernel(first, count, join, after, rows_hbm, *refs):
    if join:
        front_ref, refs = refs[0], refs[1:]
    wg_hbm, wu_hbm, wd_hbm, out_ref = refs[after : after + 4]
    rows_ref, x_ref, wg_ref, wu_ref, wd_ref, hidden_ref, result_ref, sem, rows_sem = refs[
        after + 4 :
    ]
    held, features, width = wg_ref.shape
    half = x_ref.shape[1] // CAP
    up_cuts = ((0, 512), (512, 512), (1024, width - 1024))
    down_cuts = tuple((at, 512) for at in range(0, features, 512))

    def weight_copies(j, place):
        copies = []
        for at, size in up_cuts:
            cols = pl.ds(at, size)
            copies.append((wg_hbm.at[first + j, :, cols], wg_ref.at[place, :, cols]))
            copies.append((wu_hbm.at[first + j, :, cols], wu_ref.at[place, :, cols]))
        for at, size in down_cuts:
            cols = pl.ds(at, size)
            copies.append((wd_hbm.at[first + j, :, cols], wd_ref.at[place, :, cols]))
        return [
            pltpu.make_async_copy(src, dst, sem.at[place, n])
            for n, (src, dst) in enumerate(copies)
        ]

    rows_copy = pltpu.make_async_copy(rows_hbm, rows_ref, rows_sem)
    rows_copy.start()
    weights = weight_copies(0, 0) + weight_copies(1, 1)
    for copy in weights[:4]:
        copy.start()
    rows_copy.wait()
    for copy in weights[4:]:
        copy.start()

    low = iota((PAIR, features), 0) < CAP
    lines = rows_ref.shape[0] // half

    def pair_rows(ref, pair):
        block = 2 * PAIR
        return ref[pair * block : (pair + 1) * block, :].astype(F32)

    for chunk in range(count // 2):
        for quad in range(half // 4):
            ones, twos = [], []
            for pair in (2 * quad, 2 * quad + 1):
                if lines == PAIR:
                    rows = pair_rows(rows_ref, pair)
                    even, odd = rows[:PAIR], rows[PAIR:]
                else:
                    here = slice(chunk * PAIR, (chunk + 1) * PAIR)
                    even = pair_rows(rows_ref, 2 * pair)[here]
                    odd = pair_rows(rows_ref, 2 * pair + 1)[here]
                ones.append(jnp.where(low, even, odd))
                twos.append(jnp.where(low, odd, even))
            rows = slice(quad * 2 * PAIR, (quad + 1) * 2 * PAIR)
            x_ref[2 * chunk, rows, :] = jnp.concatenate(ones, axis=0).astype(BF16)
            x_ref[2 * chunk + 1, rows, :] = jnp.concatenate(twos, axis=0).astype(BF16)

    @pl.loop(0, count)
    def _(j):
        place = j % held
        copies = weight_copies(j, place)

        def refill(n, parts):
            @pl.when(j + held < count)
            def _():
                for copy in weight_copies(j + held, place)[n : n + parts]:
                    copy.start()

        n = 0
        for at, size in up_cuts:
            copies[n].wait()
            copies[n + 1].wait()
            gate = dot(x_ref[j], wg_ref[place, :, at : at + size])
            up = dot(x_ref[j], wu_ref[place, :, at : at + size])
            hidden = gate / (1.0 + jnp.exp(-gate)) * up
            hidden_ref[:, at : at + size] = hidden.astype(BF16)
            if count > held:
                refill(n, 2)
            n += 2
        for at, size in down_cuts:
            copies[n].wait()
            result_ref[j, :, at : at + size] = dot(
                hidden_ref[...], wd_ref[place, :, at : at + size]
            )
            if count > held:
                refill(n, 1)
            n += 1

    block = 2 * PAIR
    for pair in range(half // 2):
        rows = slice(pair * PAIR, (pair + 1) * PAIR)
        values = [result_ref[j, rows, :] for j in range(count)]
        results = []
        for odd in range(2):
            parts = [
                jnp.where(low, values[j + odd], values[j + 1 - odd]) for j in range(0, count, 2)
            ]
            if join:
                parts = [pair_rows(front_ref, pair)[odd * PAIR : (odd + 1) * PAIR]] + parts
            results += parts
        for n in range(0, len(results), 2):
            at = (pair * len(results) + n) * PAIR
            two = jnp.concatenate(results[n : n + 2], axis=0)
            out_ref[at : at + block, :] = two.astype(BF16)


def expert_call(name, first, count, rows_in, weights, front=(), after=(), grant=46):
    w_gate, w_up, w_down = weights
    _, features, width = w_gate.shape
    half = rows_in.shape[0]
    rows = half * CAP
    lines = count * CAP + len(front) * PAIR
    rows_in, *front = [array.reshape(-1, features) for array in (rows_in, *front)]
    held = 2
    anywhere = pl.BlockSpec(memory_space=pl.ANY)
    hbm = pl.BlockSpec(memory_space=pltpu.HBM)
    vmem = pl.BlockSpec(memory_space=VMEM)
    return pl.pallas_call(
        functools.partial(expert_kernel, first, count, bool(front), len(after)),
        out_shape=pltpu.HBM((half * lines, features), BF16),
        in_specs=[hbm] + [vmem] * len(front) + [anywhere] * len(after) + [hbm] * 3,
        out_specs=vmem,
        scratch_shapes=[
            VMEM(rows_in.shape, BF16),
            VMEM((count, rows, features), BF16),
            VMEM((held, features, width), BF16),
            VMEM((held, features, width), BF16),
            VMEM((held, width, features), BF16),
            VMEM((rows, width), BF16),
            VMEM((count, rows, features), F32),
            pltpu.SemaphoreType.DMA((held, 10)),
            pltpu.SemaphoreType.DMA,
        ],
        compiler_params=pltpu.CompilerParams(vmem_limit_bytes=grant * 1024 * 1024),
        cost_estimate=pl.CostEstimate(
            flops=12 * count * rows * features * width,
            bytes_accessed=6 * count * features * width,
            transcendentals=count * rows * width,
        ),
        name=name,
    )(
        *[in_hbm(array) for array in (rows_in, *front, *after, w_gate, w_up, w_down)],
    ).reshape(half, lines, features)


def mix_kernel(grads, added, added_grads, start, slots_ref, columns_ref, back_ref, *refs):
    mixed_ref, grads_ref = refs[-2:]
    grad_refs = refs[:grads]
    added_refs = refs[grads : grads + added]
    added_grad_refs = refs[grads + added : grads + added + added_grads]
    tok_rows = slots_ref.shape[0]
    count, features = back_ref.shape
    grad = jnp.concatenate([ref[...] for ref in grad_refs], axis=0)
    place = iota((tok_rows, tok_rows), 1)
    wide = jnp.zeros((tok_rows, tok_rows), F32)
    column = iota((tok_rows, count), 1) + start
    inner = lax.dot_general(
        grad, back_ref[...], (((1,), (1,)), ((), ())), preferred_element_type=F32
    )
    total = jnp.zeros((tok_rows, count), F32)
    for k in range(TOP):
        here = column == slots_ref[:, k : k + 1]
        total = total + jnp.where(here, columns_ref[:, k : k + 1], 0.0)
        value = jnp.sum(jnp.where(here, inner, 0.0), axis=1, keepdims=True)
        wide = wide + jnp.where(place == k, value, 0.0)
    high = total.astype(BF16)
    rest = (total - high.astype(F32)).astype(BF16)
    width = 512
    for at in range(0, features, width):
        cols = slice(at, at + width)
        value = dot(high, back_ref[:, cols]) + dot(rest, back_ref[:, cols])
        for ref in added_refs:
            value = value + ref[:, cols].astype(F32)
        mixed_ref[:, cols] = value.astype(mixed_ref.dtype)
    lines = grads_ref.shape[0]
    sums = wide.T[:lines, :]
    for ref in added_grad_refs:
        sums = sums + ref[:lines, :]
    grads_ref[...] = sums


def swap(array, groups=None):
    return lax.all_to_all(
        array, "expert", split_axis=0, concat_axis=0, tiled=True, axis_index_groups=groups
    )


def near_path(
    block_values,
    block_exps,
    row_ids,
    expert_ids,
    gate_weights,
    table,
    w_gate,
    w_up,
    w_down,
    out_grad,
):
    device_count = lax.axis_size("expert")
    half = device_count // 2
    halves = [list(range(half)), list(range(half, device_count))]
    me = lax.axis_index("expert").astype(jnp.int32)
    tok_rows, features = block_values.shape
    rows_held = table.shape[0]
    look_cap = max(2, 2 * tok_rows // device_count)
    slots = half * 2 * PAIR
    vmem = pl.BlockSpec(memory_space=VMEM)
    smem = pl.BlockSpec(memory_space=pltpu.SMEM)
    anywhere = pl.BlockSpec(memory_space=pl.ANY)
    place = jnp.stack([me, jnp.int32(rows_held)])

    def shape(dims, kind):
        return jax.ShapeDtypeStruct(dims, kind)

    def mirrored(array):
        pairs = [(i, (i + half) % device_count) for i in range(device_count)]
        return lax.ppermute(array, "expert", pairs)

    def ordered(array, *earlier_arrays, flops=0):
        return pl.pallas_call(
            lambda *refs: None,
            out_shape=shape(array.shape, array.dtype),
            in_specs=[anywhere] * (1 + len(earlier_arrays)),
            out_specs=anywhere,
            input_output_aliases={0: 0},
            compiler_params=SMALL,
            cost_estimate=pl.CostEstimate(flops=flops, bytes_accessed=0, transcendentals=0),
            name="ordered",
        )(array, *earlier_arrays)

    upper = 3 * tok_rows // 8
    all_rows, upper_grad = pl.pallas_call(
        repeat_kernel,
        out_shape=(
            shape((device_count, 1, tok_rows), jnp.int32),
            shape((upper, features), BF16),
        ),
        grid=(1,),
        in_specs=[
            pl.BlockSpec((1, tok_rows), lambda i: (0, 0)),
            pl.BlockSpec((upper, features), lambda i: (0, 0)),
        ],
        out_specs=(
            pl.BlockSpec((device_count, 1, tok_rows), lambda i: (0, 0, 0)),
            pl.BlockSpec((upper, features), lambda i: (0, 0)),
        ),
        name="repeat_rows",
    )(row_ids[None, :], out_grad)
    other_upper = mirrored(upper_grad)
    fetched = pl.pallas_call(
        fetch_kernel,
        out_shape=pltpu.HBM((device_count * look_cap, features), BF16),
        in_specs=[smem, vmem, pl.BlockSpec(memory_space=pltpu.HBM), anywhere],
        out_specs=anywhere,
        scratch_shapes=[
            VMEM(table.shape, BF16),
            VMEM((device_count * look_cap, features), BF16),
            pltpu.SemaphoreType.DMA,
            pltpu.SemaphoreType.DMA((4,)),
        ],
        compiler_params=SMALL,
        name="fetch_rows",
    )(place, swap(all_rows), in_hbm(table), other_upper)
    returned = swap(fetched.reshape(device_count, look_cap, features))
    turned_ids, turned_weights = expert_ids.T, gate_weights.T
    pick_shape = shape((slots, tok_rows), BF16)
    pair_shape = shape((slots // 2, tok_rows), BF16)
    square = (tok_rows, tok_rows)
    put, first_pick, second_pick, near_of, near_columns, sent_ids, sent_weights = pl.pallas_call(
        near_plan_kernel,
        out_shape=(
            shape((tok_rows, device_count * look_cap), BF16),
            pair_shape,
            pair_shape,
            shape(square, jnp.int32),
            shape(square, F32),
            shape(turned_ids.shape, jnp.int32),
            shape(turned_weights.shape, F32),
        ),
        in_specs=[smem, vmem, vmem, vmem, vmem, anywhere],
        out_specs=(vmem,) * 7,
        compiler_params=SMALL,
        name="near_plan",
    )(
        place,
        row_ids[None, :],
        turned_ids,
        turned_weights,
        jnp.exp2(block_exps.T.astype(F32)),
        in_hbm(fetched),
    )
    other_ids, other_weights = mirrored(sent_ids), mirrored(sent_weights)

    def sent_scratch(count):
        return [VMEM((count, features), BF16), pltpu.SemaphoreType.DMA((4,))]

    state = pl.pallas_call(
        state_kernel,
        out_shape=shape((tok_rows, features), BF16),
        in_specs=[vmem] * 4 + [anywhere] * 2,
        out_specs=vmem,
        compiler_params=SMALL,
        name="token_state",
    )(
        put,
        returned.reshape(device_count * look_cap, features),
        block_values,
        near_columns,
        other_ids,
        other_weights,
    )

    def pair_sent(name, pick, *after):
        return pl.pallas_call(
            pair_kernel,
            out_shape=pltpu.HBM((slots // 2, features), BF16),
            in_specs=[vmem, vmem] + [anywhere] * len(after),
            out_specs=vmem,
            compiler_params=SMALL,
            name=name,
        )(pick, state, *after).reshape(half, PAIR, features)

    far_pick, far_of, far_columns = pl.pallas_call(
        far_plan_kernel,
        out_shape=(pick_shape, shape(square, jnp.int32), shape(square, F32)),
        in_specs=[smem, vmem, vmem, anywhere],
        out_specs=(vmem,) * 3,
        compiler_params=SMALL,
        name="far_plan",
    )(place, other_ids, other_weights, state)
    far_sent, lower_grad = pl.pallas_call(
        pick_kernel,
        out_shape=(
            pltpu.HBM((slots, features), BF16),
            shape((tok_rows - upper, features), BF16),
        ),
        in_specs=[vmem, vmem, vmem],
        out_specs=(anywhere, vmem),
        scratch_shapes=sent_scratch(slots),
        compiler_params=SMALL,
        cost_estimate=pl.CostEstimate(
            flops=400_000_000_000, bytes_accessed=4 * slots * features, transcendentals=0
        ),
        name="far_slots",
    )(far_pick, mirrored(state), out_grad)
    near_rows = swap(pair_sent("first_slots", first_pick), halves)
    far_sent = far_sent.reshape(half, 2 * PAIR, features)
    far_rows = swap(far_sent, halves)
    later_sent = pair_sent("later_slots", second_pick, in_hbm(far_sent))
    other_grads = (other_upper, mirrored(lower_grad))

    weights = (w_gate, w_up, w_down)
    sent_both = expert_call(
        "near_first", 0, 2, near_rows, weights, front=(later_sent,), after=(far_sent,), grant=63
    )
    far_out = expert_call("far_experts", 0, 4, far_rows, weights, after=(sent_both,), grant=63)
    both = swap(sent_both, halves)
    far_back = swap(ordered(in_hbm(far_out), in_hbm(both), other_grads[1]), halves)
    near_out = expert_call("near_second", 2, 2, both, weights)

    def mixed_rows(
        name,
        slot_of,
        columns,
        back,
        grads,
        kind,
        start=0,
        lines=2 * TOP,
        added=(),
        added_grads=(),
        after=(),
    ):
        operands = (*grads, *added, *added_grads)

        return pl.pallas_call(
            functools.partial(mix_kernel, len(grads), len(added), len(added_grads), start),
            out_shape=(shape((tok_rows, features), kind), shape((lines, tok_rows), F32)),
            in_specs=[vmem] * (3 + len(operands)) + [anywhere] * len(after),
            out_specs=(vmem, vmem),
            compiler_params=SMALL,
            name=name,
        )(slot_of, columns, back.reshape(-1, features), *operands, *after)

    sums, sum_grads = mixed_rows(
        "mix_first",
        near_of,
        near_columns,
        in_hbm(both.reshape(slots, features)),
        (out_grad,),
        F32,
    )
    far_mixed, far_grads = mixed_rows(
        "mix_far",
        far_of,
        far_columns,
        far_back,
        other_grads,
        BF16,
        after=(in_hbm(near_out), sum_grads),
    )
    near_back = swap(ordered(in_hbm(near_out), far_mixed), halves)
    mixed, grads = mixed_rows(
        "mix_second",
        near_of,
        near_columns,
        near_back,
        (out_grad,),
        BF16,
        start=slots,
        lines=TOP,
        added=(sums, ordered(mirrored(far_mixed), flops=400_000_000_000)),
        added_grads=(sum_grads, mirrored(far_grads)),
    )
    return mixed, grads.T


def expert_work(arrived, w_gate, w_up, w_down):
    gate_act = jnp.einsum("sjcd,jdf->sjcf", arrived, w_gate, preferred_element_type=jnp.float32)
    up_act = jnp.einsum("sjcd,jdf->sjcf", arrived, w_up, preferred_element_type=jnp.float32)
    hidden = (jax.nn.silu(gate_act) * up_act).astype(jnp.bfloat16)
    return jnp.einsum("sjcf,jfd->sjcd", hidden, w_down, preferred_element_type=jnp.float32).astype(
        jnp.bfloat16
    )


def full_path(buffer, w_gate, w_up, w_down, device_count, exp_dev, width_split, features):
    group_count = EXPERTS // exp_dev
    grouped = buffer.reshape(group_count, 1, exp_dev, CAP, features)
    outgoing = jnp.broadcast_to(
        grouped, (group_count, width_split, exp_dev, CAP, features)
    ).reshape(device_count, exp_dev, CAP, features)
    returned_out = lax.all_to_all(
        expert_work(
            lax.all_to_all(outgoing, "expert", split_axis=0, concat_axis=0, tiled=True),
            w_gate,
            w_up,
            w_down,
        ),
        "expert",
        split_axis=0,
        concat_axis=0,
        tiled=True,
    )
    pieces = returned_out.reshape(group_count, width_split, exp_dev, CAP, features).astype(
        jnp.float32
    )
    return jnp.sum(pieces, axis=1).astype(jnp.bfloat16).reshape(EXPERTS * CAP, features)


def far_path(
    block_values,
    block_exps,
    row_ids,
    expert_ids,
    gate_weights,
    table,
    w_gate,
    w_up,
    w_down,
    out_grad,
):
    device_count = lax.axis_size("expert")
    tok_rows = block_values.shape[0]
    features = block_values.shape[1]
    rows_held = table.shape[0]
    look_cap = max(2, 2 * tok_rows // device_count)
    exp_dev = w_gate.shape[0]
    width_split = device_count * exp_dev // EXPERTS
    owners = row_ids // rows_held
    local_row = row_ids % rows_held
    owner_hot = (owners[:, None] == jnp.arange(device_count, dtype=jnp.int32)[None, :]).astype(
        jnp.int32
    )
    owner_rank = jnp.sum((jnp.cumsum(owner_hot, axis=0) - 1) * owner_hot, axis=1)
    placed = owners * look_cap + owner_rank
    wanted = jnp.zeros((device_count * look_cap,), jnp.int32).at[placed].set(local_row)
    requested = lax.all_to_all(
        wanted.reshape(device_count, look_cap), "expert", split_axis=0, concat_axis=0, tiled=True
    )
    fetched = jnp.take(table, requested.reshape(-1), axis=0).reshape(
        device_count, look_cap, features
    )
    rows_returned = lax.all_to_all(fetched, "expert", split_axis=0, concat_axis=0, tiled=True)
    embedded = jnp.take(rows_returned.reshape(device_count * look_cap, features), placed, axis=0)
    scales = jnp.exp2(block_exps.astype(jnp.float32))
    blocks = (
        block_values.reshape(tok_rows, scales.shape[1], -1).astype(jnp.float32) * scales[:, :, None]
    )
    token_state = (blocks.reshape(tok_rows, features) + embedded.astype(jnp.float32)).astype(
        jnp.bfloat16
    )
    flat_ids = expert_ids.reshape(-1)
    expert_hot = (flat_ids[:, None] == jnp.arange(EXPERTS, dtype=jnp.int32)[None, :]).astype(
        jnp.int32
    )
    expert_rank = jnp.sum((jnp.cumsum(expert_hot, axis=0) - 1) * expert_hot, axis=1)
    slot_of = flat_ids * CAP + expert_rank
    token_index = jnp.arange(tok_rows * TOP, dtype=jnp.int32) // TOP
    source = jnp.full((EXPERTS * CAP,), tok_rows, jnp.int32).at[slot_of].set(token_index)
    padded = jnp.concatenate([token_state, jnp.zeros((1, features), jnp.bfloat16)], axis=0)
    buffer = jnp.take(padded, source, axis=0)
    expert_out = full_path(
        buffer, w_gate, w_up, w_down, device_count, exp_dev, width_split, features
    )
    chosen = jnp.take(expert_out, slot_of, axis=0).reshape(tok_rows, TOP, features)
    mixed = jnp.sum(gate_weights[:, :, None] * chosen.astype(jnp.float32), axis=1).astype(
        jnp.bfloat16
    )
    gate_grads = jnp.einsum("tkd,td->tk", chosen, out_grad, preferred_element_type=jnp.float32)
    return (mixed, gate_grads)


def local(*arrays):
    if lax.axis_size("expert") == 16 and arrays[6].shape[0] * 16 == EXPERTS:
        return near_path(*arrays)
    return far_path(*arrays)


def solution(mesh):
    return jax.shard_map(
        local,
        mesh=mesh,
        in_specs=(
            P(("groups", "expert"), None),
            P(("groups", "expert"), None),
            P(("groups", "expert")),
            P(("groups", "expert"), None),
            P(("groups", "expert"), None),
            P("expert", None),
            P("expert", None, None),
            P("expert", None, None),
            P("expert", None, None),
            P(("groups", "expert"), None),
        ),
        out_specs=(P(("groups", "expert"), None), P(("groups", "expert"), None)),
        check_vma=False,
    )
```
